32 devices in a mesh: dp: 8 (over y, x, core), section: 4 (over z).
Axes of the slice: x: 2, y: 2, z: 4, core: 2. Of those that a mesh axis runs over, the one named last changes fastest.
Arguments:
- hidden_in: bfloat16 [4, 1024, 2048], P('section', 'dp'), may hold values from -80 to 80
- queries: bfloat16 [4, 1024, 2048], P('section', 'dp'), may hold values from -20 to 20
- keys: bfloat16 [4, 1024, 512], P('section', 'dp'), may hold values from -6 to 6
- segments: int32 [8, 128], P('dp'), may hold values from 0 to 3, as said below
- value_weight: bfloat16 [4, 2048, 512], P('section'), may hold values from -0.125 to 0.125
- norm_gain: float32 [4, 2048], P('section'), may hold values from 0.25 to 1.75
- upstream: bfloat16 [1024, 2048], P('dp'), may hold values from -6 to 6
Outputs:
- input_grads: bfloat16 [4, 1024, 2048], P('section', 'dp')
- value_weight_grads: float32 [4, 2048, 512], P('section', 'dp')
- gain_grads: float32 [4, 2048], P('section', 'dp')
The draws below stay inside these ranges and needn't reach their ends.
Inputs may be any that keep to these rules, and one draw needn't show every extreme that they name: `segments`: within each aligned block of 64 list-order tokens of a replica the list ids run from 0 to 3 in order, never falling; each of the 4 lists has 1 to 48 tokens and one has exactly 48.
All inputs are finite; a program needn't handle non-finite values.
Results may differ from the reference program's by a relative error of at most 0.03.
Values may be sent and summed in bfloat16 or wider, within the bound.
No kernel may reach another device: no remote copies, remote signals or barrier semaphores. Data moves between devices by JAX's collectives and lax.ppermute only.
A program may use at most 64 MiB of HBM per device.

```python
import math
import jax
import jax.numpy as jnp
from jax import lax

QUERY_HEADS = 16
KEY_VALUE_HEADS = 4
HEAD_FEATURES = 128
D = 2048
KW = 512
MICRO_ROWS = 64
MICRO = 2
LISTS = 4
LIST_MAX = 48
TOK_DEV = 128
REPLICAS = 8
PIECE = 16
TOKEN_COUNT = 1024
LAYER_COUNT = 4


def block_lists(block_key):
    first_key, second_key = jax.random.split(block_key)
    remainder = MICRO_ROWS - LIST_MAX
    cut_points = jnp.sort(jax.random.permutation(first_key, remainder - 1)[:LISTS - 2] + 1).astype(jnp.int32)
    edge_list = jnp.concatenate([jnp.zeros((1,), jnp.int32), cut_points, jnp.full((1,), remainder, jnp.int32)])
    short_lengths = edge_list[1:] - edge_list[:-1]
    position = jax.random.randint(second_key, (), 0, LISTS)
    list_index = jnp.arange(LISTS, dtype=jnp.int32)
    source = jnp.clip(list_index - (list_index > position).astype(jnp.int32), 0, LISTS - 2)
    lengths = jnp.where(list_index == position, LIST_MAX, short_lengths[source]).astype(jnp.int32)
    list_ends = jnp.cumsum(lengths).astype(jnp.int32)
    rows_here = jnp.arange(MICRO_ROWS, dtype=jnp.int32)
    return jnp.sum((rows_here[:, None] >= list_ends[None, :LISTS - 1]).astype(jnp.int32), axis=1)


def list_table(key):
    base_key = jax.random.fold_in(key, 7001)
    block_keys = jax.random.split(base_key, REPLICAS * MICRO)
    return jax.vmap(block_lists)(block_keys).reshape(REPLICAS, TOK_DEV).astype(jnp.int32)


def draw_segments(key, part):
    return list_table(key)


def to_loader(values):
    width = values.shape[-1]
    shaped = values.reshape(LAYER_COUNT, REPLICAS, REPLICAS, PIECE, width)
    return shaped.transpose(0, 2, 1, 3, 4).reshape(LAYER_COUNT, TOKEN_COUNT, width)


def draw_keys(key, part):
    noise_key = jax.random.fold_in(key, 7004)
    target_shape = (LAYER_COUNT, TOKEN_COUNT, KEY_VALUE_HEADS, HEAD_FEATURES)
    values = jnp.clip(jax.random.normal(noise_key, target_shape, jnp.float32), -6.0, 6.0)
    return to_loader(values.reshape(LAYER_COUNT, TOKEN_COUNT, KW)).astype(jnp.bfloat16)


def draw_queries(key, part):
    noise_key = jax.random.fold_in(key, 7005)
    group_width = QUERY_HEADS // KEY_VALUE_HEADS
    target_shape = (LAYER_COUNT, TOKEN_COUNT, KEY_VALUE_HEADS, group_width, HEAD_FEATURES)
    values = jnp.clip(jax.random.normal(noise_key, target_shape, jnp.float32), -6.0, 6.0)
    return to_loader(values.reshape(LAYER_COUNT, TOKEN_COUNT, D)).astype(jnp.bfloat16)


def draw_hidden_in(key, part):
    base_key = jax.random.fold_in(key, 7011)
    row_key = jax.random.fold_in(key, 7012)
    column_key = jax.random.fold_in(key, 7013)
    values = jnp.clip(jax.random.normal(base_key, (LAYER_COUNT, TOKEN_COUNT, D), jnp.float32), -6.0, 6.0)
    row_scale = jnp.exp(jax.random.uniform(row_key, (LAYER_COUNT, TOKEN_COUNT, 1), jnp.float32) * math.log(10.0))
    column_scale = jnp.exp(jax.random.uniform(column_key, (LAYER_COUNT, 1, D), jnp.float32) * math.log(10.0))
    return (values * row_scale * column_scale * 0.1).astype(jnp.bfloat16)


def steps_of(key, shape, cuts, smallest, top_value):
    level = 1.0
    for axis_at, shards_of in cuts:
        heights = jax.random.uniform(jax.random.fold_in(jax.random.fold_in(key, 6), axis_at), (shards_of,), jnp.float32, smallest / len(cuts), top_value / len(cuts))
        level = level * jnp.repeat(jnp.exp(heights), shape[axis_at] // shards_of).reshape((-1,) + (1,) * (len(shape) - 1 - axis_at))
    return level


def normal_values(stream_key, shape, scale, bound, cuts=(), kind=jnp.bfloat16):
    level = steps_of(stream_key, shape, cuts, -0.22, 0.18) if cuts else 1.0
    entries = jax.random.normal(stream_key, shape, jnp.float32) * scale * level
    return jnp.minimum(jnp.maximum(entries, -bound), bound).astype(kind)


def setup_inputs(seed: int = 0) -> dict:
    key_of = jax.random.split(jax.random.key(seed), 8)
    hidden_in = draw_hidden_in(jax.random.fold_in(key_of[7], 71), 0)
    queries = draw_queries(jax.random.fold_in(key_of[7], 71), 0)
    keys = draw_keys(jax.random.fold_in(key_of[7], 71), 0)
    segments = draw_segments(jax.random.fold_in(key_of[7], 71), 0)
    value_weight = normal_values(key_of[4], (LAYER_COUNT, D, KW), D ** -0.5, 0.125, ((0, 4),))
    norm_gain = jnp.clip(1.0 + 0.15 * jax.random.normal(key_of[5], (LAYER_COUNT, D), jnp.float32), 0.25, 1.75)
    upstream = normal_values(key_of[6], (TOKEN_COUNT, D), 1.0, 6.0, ((0, 8),))
    return dict(hidden_in=hidden_in, queries=queries, keys=keys, segments=segments, value_weight=value_weight, norm_gain=norm_gain, upstream=upstream)


epsilon = 1e-06
masked_score = -1e+30

def reorder(rows):
    width = rows.shape[-1]
    return rows.reshape(REPLICAS, REPLICAS, PIECE, width).transpose(1, 0, 2, 3).reshape(TOKEN_COUNT, width)

def block_values(query_tile_block, key_tile_block, gradient_block, list_block):
    group_width = QUERY_HEADS // KEY_VALUE_HEADS
    query_grid4 = query_tile_block.astype(jnp.float32).reshape(MICRO_ROWS, KEY_VALUE_HEADS, group_width, HEAD_FEATURES)
    key_grid3 = key_tile_block.astype(jnp.float32).reshape(MICRO_ROWS, KEY_VALUE_HEADS, HEAD_FEATURES)
    scores = jnp.einsum('ikgd,jkd->kgij', query_grid4, key_grid3) * HEAD_FEATURES ** (-0.5)
    positions = jnp.arange(MICRO_ROWS, dtype=jnp.int32)
    allowed = (list_block[:, None] == list_block[None, :]) & (positions[None, :] <= positions[:, None])
    scores = jnp.where(allowed, scores, masked_score)
    exp_scores = jnp.exp(scores - lax.optimization_barrier(jnp.max(scores, axis=-1, keepdims=True)))
    block_weights = (exp_scores / lax.optimization_barrier(jnp.sum(exp_scores, axis=-1, keepdims=True))).astype(jnp.bfloat16)
    gradient_grid4 = gradient_block.astype(jnp.float32).reshape(MICRO_ROWS, KEY_VALUE_HEADS, group_width, HEAD_FEATURES)
    value_gradient = jnp.einsum('kgij,ikgd->jkd', block_weights.astype(jnp.float32), gradient_grid4)
    return value_gradient.reshape(MICRO_ROWS, KEY_VALUE_HEADS * HEAD_FEATURES).astype(jnp.bfloat16)

def block_entry(inputs):
    return block_values(inputs[0], inputs[1], inputs[2], inputs[3])

def reference(hidden_in, queries, keys, segments, value_weight, norm_gain, upstream):
    block_count = TOKEN_COUNT // MICRO_ROWS
    list_blocks = segments.reshape(block_count, MICRO_ROWS)
    scale_total = TOKEN_COUNT ** (-0.5)
    grad_now = upstream
    input_list = []
    weight_list = []
    gain_list = []
    for layer_index in range(LAYER_COUNT - 1, -1, -1):
        x_wide = reorder(hidden_in[layer_index]).astype(jnp.float32)
        inv_rms = lax.rsqrt(lax.optimization_barrier(jnp.mean(x_wide * x_wide, axis=1, keepdims=True)) + epsilon)
        x_norm = x_wide * inv_rms
        gain_row = norm_gain[layer_index]
        normed = (x_norm * gain_row).astype(jnp.bfloat16)
        inputs = (reorder(queries[layer_index]).reshape(block_count, MICRO_ROWS, D), reorder(keys[layer_index]).reshape(block_count, MICRO_ROWS, KW), grad_now.reshape(block_count, MICRO_ROWS, D), list_blocks)
        value_gradient = lax.map(block_entry, inputs).reshape(TOKEN_COUNT, KW)
        normed_grad = jnp.dot(value_gradient, value_weight[layer_index].T, preferred_element_type=jnp.float32)
        scaled = normed_grad * gain_row
        inner_mean = lax.optimization_barrier(jnp.mean(x_norm * scaled, axis=1, keepdims=True))
        input_grad = (grad_now.astype(jnp.float32) + inv_rms * (scaled - x_norm * inner_mean)).astype(jnp.bfloat16)
        weight_grad = jnp.dot(normed.T, value_gradient, preferred_element_type=jnp.float32) * scale_total
        gain_grad = lax.optimization_barrier(jnp.sum(x_norm * normed_grad, axis=0)) * scale_total
        input_list.append(reorder(input_grad))
        weight_list.append(weight_grad)
        gain_list.append(gain_grad)
        grad_now = input_grad
    return (jnp.stack(input_list[::-1]), jnp.stack(weight_list[::-1]), jnp.stack(gain_list[::-1]))
```

```python
import functools

import jax
import jax.numpy as jnp
from jax import lax
from jax.experimental import pallas as pl
from jax.experimental.pallas import tpu as pltpu
from jax.sharding import PartitionSpec as P

HEAD_FEATURES = 128
BLOCK = 64
EPSILON = 1e-06
MASKED = -1e30
UNROLLED = 8
VMEM = pl.BlockSpec(memory_space=pltpu.VMEM)
SMEM = pl.BlockSpec(memory_space=pltpu.SMEM)


def probs_kernel(model_width, kv_width, rows_ref, seg_row_ref, seg_column_ref, probs_ref, inv_ref):
    heads = model_width // kv_width
    shape = (BLOCK, heads * BLOCK)
    key_at = lax.broadcasted_iota(jnp.int32, shape, 0)
    query_at = lax.rem(lax.broadcasted_iota(jnp.int32, shape, 1), BLOCK)
    allowed = (seg_column_ref[...] == seg_row_ref[...]) & (key_at <= query_at)
    for c in range(kv_width // HEAD_FEATURES):
        first = c * heads * HEAD_FEATURES
        query_stack = jnp.concatenate(
            [
                rows_ref[:, first + h * HEAD_FEATURES : first + (h + 1) * HEAD_FEATURES]
                for h in range(heads)
            ],
            axis=0,
        )
        key_first = model_width + c * HEAD_FEATURES
        keys = rows_ref[:, key_first : key_first + HEAD_FEATURES]
        scores = lax.dot_general(
            keys, query_stack, (((1,), (1,)), ((), ())), preferred_element_type=jnp.float32
        ) * HEAD_FEATURES ** (-0.5)
        scores = jnp.where(allowed, scores, MASKED)
        exp_scores = jnp.exp(scores - jnp.max(scores, axis=0, keepdims=True))
        total = jnp.sum(exp_scores, axis=0, keepdims=True)
        probs_ref[c] = (exp_scores / total).astype(jnp.bfloat16)
    x = rows_ref[:, model_width + kv_width :].astype(jnp.float32)
    mean_square = jnp.mean(x * x, axis=1, keepdims=True)
    inv_ref[...] = jnp.broadcast_to(lax.rsqrt(mean_square + EPSILON), inv_ref.shape)


def block_probs(rows, seg, model_width, kv_width):
    heads = model_width // kv_width
    return pl.pallas_call(
        functools.partial(probs_kernel, model_width, kv_width),
        out_shape=(
            jax.ShapeDtypeStruct(
                (kv_width // HEAD_FEATURES, BLOCK, heads * BLOCK), jnp.bfloat16
            ),
            jax.ShapeDtypeStruct((BLOCK, 128), jnp.float32),
        ),
        in_specs=[VMEM, VMEM, VMEM],
        out_specs=(VMEM, VMEM),
        name="probs",
    )(rows, jnp.tile(seg, heads)[None, :], seg[:, None])


def layer_kernel(
    kv_width, live_ref, grad_ref, rows_ref, probs_ref, inv_ref, weight_ref, gain_ref, *rest
):
    out_ref, value_ref = rest[-2:]
    if len(rest) == 4:

        @pl.when(live_ref[0] == 0)
        def _():
            out_ref[...] = rest[0][...]
            value_ref[...] = rest[1][...]

    @pl.when(live_ref[0] == 1)
    def _():
        model_width = grad_ref.shape[1]
        heads = model_width // kv_width
        inv = inv_ref[:, :1]
        values = []
        for c in range(kv_width // HEAD_FEATURES):
            first = c * heads * HEAD_FEATURES
            grad_stack = jnp.concatenate(
                [
                    grad_ref[:, first + h * HEAD_FEATURES : first + (h + 1) * HEAD_FEATURES]
                    for h in range(heads)
                ],
                axis=0,
            )
            values.append(
                jnp.dot(probs_ref[c], grad_stack, preferred_element_type=jnp.float32).astype(
                    jnp.bfloat16
                )
            )
        value = jnp.concatenate(values, axis=1)
        value_ref[...] = (value.astype(jnp.float32) * inv).astype(jnp.bfloat16)
        normed_grad = lax.dot_general(
            value, weight_ref[...], (((1,), (1,)), ((), ())), preferred_element_type=jnp.float32
        )
        scaled = normed_grad * gain_ref[...]
        x_norm = rows_ref[:, model_width + kv_width :].astype(jnp.float32) * inv
        inner_mean = jnp.mean(x_norm * scaled, axis=1, keepdims=True)
        out_ref[...] = (
            grad_ref[...].astype(jnp.float32) + inv * (scaled - x_norm * inner_mean)
        ).astype(jnp.bfloat16)


def layer_step(live, grad, rows, probs, inv, weight, gain, held):
    kv_width = weight.shape[1]
    operands = [live, grad, rows, probs, inv, weight, gain]
    specs = [SMEM] + [VMEM] * 6
    if held is not None:
        operands += list(held)
        specs += [VMEM] * 2
    return pl.pallas_call(
        functools.partial(layer_kernel, kv_width),
        out_shape=(
            jax.ShapeDtypeStruct(grad.shape, jnp.bfloat16),
            jax.ShapeDtypeStruct((BLOCK, kv_width), jnp.bfloat16),
        ),
        in_specs=specs,
        out_specs=(VMEM, VMEM),
        name="layer",
    )(*operands)


def weight_kernel(scale, columns_ref, value_ref, weight_ref, gain_ref, out_ref, gain_out_ref):
    total = lax.dot_general(
        columns_ref[...], value_ref[...], (((0,), (0,)), ((), ())),
        preferred_element_type=jnp.float32,
    ) * scale
    out_ref[...] = total * gain_ref[...]
    product = total * weight_ref[...].astype(jnp.float32)
    sums = lax.dot_general(
        jnp.ones((8, product.shape[1]), jnp.float32), product, (((1,), (1,)), ((), ())),
        preferred_element_type=jnp.float32, precision=lax.Precision.HIGHEST,
    )
    gain_out_ref[...] = sums[:1]


def on_device(hidden_in, queries, keys, segments, value_weight, norm_gain, upstream):
    hidden, query, key = hidden_in[0], queries[0], keys[0]
    seg, weight = segments[0], value_weight[0]
    tokens, model_width = hidden.shape
    kv_width = key.shape[1]
    replicas = lax.axis_size("dp")
    layers = lax.axis_size("section")
    half = replicas // 2
    me = lax.axis_index("dp")
    section = lax.axis_index("section")
    side = me // half
    groups = [list(range(half)), list(range(half, replicas))]
    across = [(i, (i + half) % replicas) for i in range(replicas)]
    shares = model_width // replicas

    def rows_of(array, which, axis=0):
        at = side if which == 0 else 1 - side
        return lax.dynamic_slice_in_dim(array, at * BLOCK, BLOCK, axis)

    def regroup(array):
        return lax.all_to_all(
            array, "dp", split_axis=0, concat_axis=0, axis_index_groups=groups, tiled=True
        )

    def spread(array):
        return lax.all_to_all(array, "dp", split_axis=0, concat_axis=0, tiled=True)

    rows, probs, inv, grads, segs = [], [], [], [], []
    for which in range(2):
        up = rows_of(upstream, which)
        block_seg = rows_of(seg, which)
        if which == 1:
            up = lax.ppermute(up, "dp", across)
            block_seg = lax.ppermute(block_seg, "dp", across)
        packed = jnp.concatenate(
            [rows_of(query, which), rows_of(key, which), rows_of(hidden, which)], axis=1
        )
        rows.append(regroup(packed))
        block = block_probs(rows[which], block_seg, model_width, kv_width)
        probs.append(block[0])
        inv.append(block[1])
        grads.append(up)

    def layer(tick, which, grad, kept):
        live = (section == layers - 1 - tick).astype(jnp.int32)[None]
        return layer_step(
            live, grad, rows[which], probs[which], inv[which], weight, norm_gain, kept
        )

    held = [layer(0, which, grads[which], None) for which in range(2)]
    if layers <= UNROLLED:
        for tick in range(1, layers):
            hop = [(layers - tick, layers - 1 - tick)]
            for which in range(2):
                grad = lax.ppermute(held[which][0], "section", hop)
                held[which] = layer(tick, which, grad, held[which])
    else:
        hops = [(i, i - 1) for i in range(1, layers)]

        def tick_step(tick, held):
            grads = [lax.ppermute(kept[0], "section", hops) for kept in held]
            return [layer(tick, which, grads[which], held[which]) for which in range(2)]

        held = lax.fori_loop(1, layers, tick_step, held)

    columns, values, stored = [], [], []
    for which in range(2):
        block = rows[which][:, model_width + kv_width :]
        block = block.reshape(BLOCK, replicas, shares).transpose(1, 0, 2)
        columns.append(spread(block.reshape(replicas * BLOCK, shares)))
        out, value = held[which]
        stored.append(regroup(out))
        values.append(spread(jnp.tile(value, (replicas, 1))))
    ordered = jnp.where(
        side == 0, jnp.concatenate(stored, axis=0), jnp.concatenate(stored[::-1], axis=0)
    )
    own_weight = lax.dynamic_slice_in_dim(weight, me * shares, shares, 0)
    own_gain = lax.dynamic_slice_in_dim(norm_gain[0], me * shares, shares, 0)
    scale = float(tokens * replicas) ** (-0.5)
    weight_grad, gain_grad = pl.pallas_call(
        functools.partial(weight_kernel, scale),
        out_shape=(
            jax.ShapeDtypeStruct((shares, kv_width), jnp.float32),
            jax.ShapeDtypeStruct((1, shares), jnp.float32),
        ),
        in_specs=[VMEM] * 4,
        out_specs=(VMEM, VMEM),
        name="weight_grad",
    )(
        jnp.concatenate(columns, axis=0),
        jnp.concatenate(values, axis=0),
        own_weight,
        own_gain[:, None],
    )
    return ordered[None], weight_grad[None], gain_grad


def solution(mesh):
    in_specs = (
        P("section", "dp", None),
        P("section", "dp", None),
        P("section", "dp", None),
        P("dp", None),
        P("section", None, None),
        P("section", None),
        P("dp", None),
    )
    out_specs = (P("section", "dp", None), P("section", "dp", None), P("section", "dp"))
    return jax.shard_map(
        on_device, mesh=mesh, in_specs=in_specs, out_specs=out_specs, check_vma=False
    )
```

```python
import functools

import jax
import jax.numpy as jnp
from jax import lax
from jax.experimental import pallas as pl
from jax.experimental.pallas import tpu as pltpu
from jax.sharding import PartitionSpec as P

HEAD_FEATURES = 128
BLOCK = 64
EPSILON = 1e-06
MASKED = -1e30
VMEM = pl.BlockSpec(memory_space=pltpu.VMEM)
SMEM = pl.BlockSpec(memory_space=pltpu.SMEM)


def params(flops=0, nbytes=1 << 20):
    return dict(
        compiler_params=pltpu.CompilerParams(vmem_limit_bytes=24 << 20),
        cost_estimate=pl.CostEstimate(flops=flops, bytes_accessed=nbytes, transcendentals=0),
    )


def near(array):
    return pltpu.with_memory_space_constraint(array, pltpu.VMEM)


def wide_columns(refs, first, last):
    parts = [ref[:, first:last] for ref in refs]
    return parts[0] if len(parts) == 1 else jnp.concatenate(parts, axis=0)


def probs_kernel(count, model_width, kv_width, *refs):
    pieces = refs[:count]
    code_row_ref, code_column_ref = refs[count : count + 2]
    probs_ref, inv_ref, x_ref = refs[-3:]
    heads = model_width // kv_width
    query_code, key_code = code_row_ref[...], code_column_ref[...]
    list_start = query_code - lax.rem(query_code, BLOCK)
    allowed = (key_code <= query_code) & (key_code >= list_start)
    for c in range(kv_width // HEAD_FEATURES):
        first = c * heads * HEAD_FEATURES
        query_stack = jnp.concatenate(
            [
                wide_columns(pieces, first + h * HEAD_FEATURES, first + (h + 1) * HEAD_FEATURES)
                for h in range(heads)
            ],
            axis=0,
        )
        key_first = model_width + c * HEAD_FEATURES
        keys = wide_columns(pieces, key_first, key_first + HEAD_FEATURES)
        scores = lax.dot_general(
            keys, query_stack, (((1,), (1,)), ((), ())), preferred_element_type=jnp.float32
        ) * HEAD_FEATURES ** (-0.5)
        scores = jnp.where(allowed, scores, MASKED)
        exp_scores = jnp.exp(scores - jnp.max(scores, axis=0, keepdims=True))
        total = jnp.sum(exp_scores, axis=0, keepdims=True)
        probs_ref[c] = (exp_scores / total).astype(jnp.bfloat16)
    rows = BLOCK // count
    for p, piece in enumerate(pieces):
        hidden = piece[:, model_width + kv_width :]
        x_ref[p * rows : (p + 1) * rows, :] = hidden
        x = hidden.astype(jnp.float32)
        mean_square = jnp.mean(x * x, axis=1, keepdims=True)
        inv_ref[p * rows : (p + 1) * rows, :] = jnp.broadcast_to(
            lax.rsqrt(mean_square + EPSILON), (rows, inv_ref.shape[1])
        )


def block_probs(pieces, code, model_width, kv_width, after=None):
    heads = model_width // kv_width
    key_heads = kv_width // HEAD_FEATURES
    operands = [near(piece) for piece in pieces]
    operands += [jnp.tile(code, heads)[None, :], code[:, None]]
    specs = [VMEM] * len(operands)
    if after is not None:
        operands.append(after)
        specs.append(pl.BlockSpec(memory_space=pl.ANY))
    return pl.pallas_call(
        functools.partial(probs_kernel, len(pieces), model_width, kv_width),
        out_shape=(
            jax.ShapeDtypeStruct((key_heads, BLOCK, heads * BLOCK), jnp.bfloat16),
            jax.ShapeDtypeStruct((BLOCK, 128), jnp.float32),
            jax.ShapeDtypeStruct((BLOCK, model_width), jnp.bfloat16),
        ),
        in_specs=specs,
        out_specs=(VMEM,) * 3,
        name="probs",
        **params(4 * BLOCK * BLOCK * model_width),
    )(*operands)


def layer_math(grad_ref, x_ref, probs_ref, inv_ref, weight_ref, gain_ref, scaled_ref, store, value_ref):
    model_width = grad_ref.shape[1]
    kv_width = weight_ref.shape[1]
    heads = model_width // kv_width
    chunk = min(512, model_width)
    inv = inv_ref[:, :1]
    values = []
    for c in range(kv_width // HEAD_FEATURES):
        first = c * heads * HEAD_FEATURES
        grad_stack = jnp.concatenate(
            [
                grad_ref[:, first + h * HEAD_FEATURES : first + (h + 1) * HEAD_FEATURES]
                for h in range(heads)
            ],
            axis=0,
        )
        values.append(
            jnp.dot(probs_ref[c], grad_stack, preferred_element_type=jnp.float32).astype(
                jnp.bfloat16
            )
        )
    value = jnp.concatenate(values, axis=1)
    value_ref[...] = (value.astype(jnp.float32) * inv).astype(jnp.bfloat16)
    inner = jnp.zeros((BLOCK, 1), jnp.float32)
    for first in range(0, model_width, chunk):
        columns = slice(first, first + chunk)
        normed_grad = lax.dot_general(
            value, weight_ref[columns, :], (((1,), (1,)), ((), ())),
            preferred_element_type=jnp.float32,
        )
        scaled = normed_grad * gain_ref[:, columns]
        scaled_ref[:, columns] = scaled
        x = x_ref[:, columns].astype(jnp.float32)
        inner = inner + jnp.sum(x * scaled, axis=1, keepdims=True)
    pull = inner * (inv * inv / model_width)
    for first in range(0, model_width, chunk):
        columns = slice(first, first + chunk)
        x = x_ref[:, columns].astype(jnp.float32)
        change = inv * (scaled_ref[:, columns] - x * pull)
        store(columns, (grad_ref[:, columns].astype(jnp.float32) + change).astype(jnp.bfloat16))


def layer_kernel(live_ref, grad_ref, x_ref, probs_ref, inv_ref, weight_ref, gain_ref, *rest):
    out_ref, value_ref, scaled_ref = rest[-3:]

    def store(columns, part):
        out_ref[:, columns] = part

    @pl.when(live_ref[0] == 1)
    def _():
        layer_math(
            grad_ref, x_ref, probs_ref, inv_ref, weight_ref, gain_ref, scaled_ref, store, value_ref
        )


def last_layer_kernel(
    live_ref, grad_ref, x_ref, probs_ref, inv_ref, weight_ref, gain_ref,
    first_ref, held_ref, held_value_ref, value_ref, *rest
):
    scaled_ref = rest[-1]
    pieces = rest[:-1]
    piece = BLOCK // len(pieces)

    def store(columns, part):
        for k, piece_ref in enumerate(pieces):
            piece_ref[1, :, columns] = part[k * piece : (k + 1) * piece]

    for k, piece_ref in enumerate(pieces):
        piece_ref[0] = first_ref[k * piece : (k + 1) * piece, :]

    @pl.when(live_ref[0] == 0)
    def _():
        value_ref[...] = held_value_ref[...]
        for k, piece_ref in enumerate(pieces):
            piece_ref[1] = held_ref[k * piece : (k + 1) * piece, :]

    @pl.when(live_ref[0] == 1)
    def _():
        layer_math(
            grad_ref, x_ref, probs_ref, inv_ref, weight_ref, gain_ref, scaled_ref, store, value_ref
        )


def layer_step(live, grad, x, probs, inv, weight, gain, held=None, after=None):
    model_width, kv_width = weight.shape
    operands = [live] + [near(array) for array in (grad, x, probs, inv, weight, gain)]
    specs = [SMEM] + [VMEM] * 6
    aliases = {}
    if held is not None:
        aliases = {len(operands): 0, len(operands) + 1: 1}
        operands += [near(array) for array in held]
        specs += [VMEM] * 2
    if after is not None:
        operands.append(after)
        specs.append(pl.BlockSpec(memory_space=pl.ANY))
    return pl.pallas_call(
        layer_kernel,
        out_shape=(
            pltpu.VMEM((BLOCK, model_width), jnp.bfloat16),
            pltpu.VMEM((BLOCK, kv_width), jnp.bfloat16),
        ),
        in_specs=specs,
        out_specs=(VMEM, VMEM),
        scratch_shapes=[pltpu.VMEM((BLOCK, model_width), jnp.float32)],
        input_output_aliases=aliases,
        name="layer",
        **params(2 * BLOCK * model_width * kv_width),
    )(*operands)


def last_layer_step(live, grad, x, probs, inv, weight, gain, first, held, count):
    model_width, kv_width = weight.shape
    operands = [live]
    operands += [near(array) for array in (grad, x, probs, inv, weight, gain, first, *held)]
    piece = jax.ShapeDtypeStruct((2, BLOCK // count, model_width), jnp.bfloat16)
    return pl.pallas_call(
        last_layer_kernel,
        out_shape=(jax.ShapeDtypeStruct((BLOCK, kv_width), jnp.bfloat16),) + (piece,) * count,
        in_specs=[SMEM] + [VMEM] * (len(operands) - 1),
        out_specs=(VMEM,) * (1 + count),
        scratch_shapes=[pltpu.VMEM((BLOCK, model_width), jnp.float32)],
        name="last_layer",
        **params(2 * BLOCK * model_width * kv_width),
    )(*operands)


def pack_kernel(half, piece, me_ref, query_ref, key_ref, hidden_ref, up_ref, *rest):
    sems = rest[-1]
    ups = rest[-3:-1]
    packed = rest[:-3]
    side, at = me_ref[0], me_ref[1]
    copies = []

    def copy(source, target):
        made = pltpu.make_async_copy(source, target, sems.at[len(copies)])
        made.start()
        copies.append(made)

    for block in range(2):
        for k in range(half):
            replica = (side if block == 0 else 1 - side) * half + lax.bitwise_xor(at, k)
            rows = pl.ds(pl.multiple_of(replica * piece, piece), piece)
            target = packed[block * half + k]
            first = 0
            for source in (query_ref, key_ref, hidden_ref):
                width = source.shape[1]
                copy(source.at[rows], target.at[:, pl.ds(first, width)])
                first += width
    for block in range(2):
        for k in range(half):
            replica = (side if block == 0 else 1 - side) * half + lax.bitwise_xor(at, k)
            rows = pl.ds(pl.multiple_of(replica * piece, piece), piece)
            copy(up_ref.at[rows], ups[block].at[pl.ds(k * piece, piece)])
    for made in copies:
        made.wait()


def columns_kernel(width, me_ref, first_ref, second_ref, *outs):
    pair = me_ref[0]
    for k, out_ref in enumerate(outs):
        start = pl.multiple_of(lax.bitwise_xor(pair, k) * width, width)
        out_ref[:BLOCK, :] = first_ref[:, pl.ds(start, width)]
        out_ref[BLOCK:, :] = second_ref[:, pl.ds(start, width)]


def partial_kernel(count, shares, me_ref, *refs):
    columns, first, second = refs[:count], refs[count : 2 * count], refs[2 * count : 3 * count]
    own_ref, other_ref = refs[-2:]
    value = jnp.concatenate(
        [ref[...] for pair in zip(first, second) for ref in pair], axis=0
    )
    for ref, core in ((other_ref, 1 - me_ref[0]), (own_ref, me_ref[0])):
        at = pl.ds(pl.multiple_of(core * shares, shares), shares)
        rows = jnp.concatenate([part[:, at] for part in columns], axis=0)
        ref[...] = lax.dot_general(
            rows, value, (((0,), (0,)), ((), ())), preferred_element_type=jnp.float32
        )


def finish_kernel(
    half, scale, me_ref, own_ref, other_ref, weight_ref, gain_ref, *refs
):
    pieces = refs[:half]
    rows_ref, out_ref, gain_out_ref, sems = refs[half:]
    side, at = me_ref[0], me_ref[1]
    piece = pieces[0].shape[1]
    copies = []
    for block in range(2):
        for k in range(half):
            replica = (side if block == 0 else 1 - side) * half + lax.bitwise_xor(at, k)
            rows = pl.ds(pl.multiple_of(replica * piece, piece), piece)
            made = pltpu.make_async_copy(
                pieces[k].at[block], rows_ref.at[rows], sems.at[block * half + k]
            )
            made.start()
            copies.append(made)
    shares = own_ref.shape[0]
    first = pl.multiple_of(me_ref[2] * shares, shares)
    gain = gain_ref[:, pl.ds(first, shares)]
    eye = lax.broadcasted_iota(jnp.int32, (shares, shares), 0) == lax.broadcasted_iota(
        jnp.int32, (shares, shares), 1
    )
    gain_column = jnp.sum(jnp.where(eye, gain, 0.0), axis=1, keepdims=True)
    total = (own_ref[...] + other_ref[...]) * scale
    out_ref[...] = total * gain_column
    product = total * weight_ref[pl.ds(first, shares), :].astype(jnp.float32)
    sums = lax.dot_general(
        jnp.ones((8, product.shape[1]), jnp.float32), product, (((1,), (1,)), ((), ())),
        preferred_element_type=jnp.float32, precision=lax.Precision.HIGHEST,
    )
    gain_out_ref[...] = sums[:1]
    for made in copies:
        made.wait()


def direct(hidden, query, key, seg, weight, norm_gain, upstream):
    tokens, model_width = hidden.shape
    kv_width = key.shape[1]
    replicas = lax.axis_size("dp")
    layers = lax.axis_size("section")
    half = replicas // 2
    piece = tokens // replicas
    shares = model_width // replicas
    me = lax.axis_index("dp")
    section = lax.axis_index("section")
    side, at = me // half, me % half
    place = jnp.stack([side, at, me]).astype(jnp.int32)

    def swap(array, k):
        return lax.ppermute(array, "dp", [(i, i ^ k) for i in range(replicas)])

    count = 2 * half
    bf16 = jnp.bfloat16
    packed = pl.pallas_call(
        functools.partial(pack_kernel, half, piece),
        out_shape=(jax.ShapeDtypeStruct((piece, 2 * model_width + kv_width), bf16),) * count
        + (jax.ShapeDtypeStruct((BLOCK, model_width), bf16),) * 2,
        in_specs=[SMEM] + [pl.BlockSpec(memory_space=pl.ANY)] * 4,
        out_specs=(VMEM,) * (count + 2),
        scratch_shapes=[pltpu.SemaphoreType.DMA((4 * count,))],
        name="pack",
        **params(0, 3 << 20),
    )(place, query, key, hidden, upstream)
    ups = packed[-2:]
    seg_pieces = seg.reshape(2, half, piece)
    order = jnp.bitwise_xor(at, jnp.arange(half, dtype=jnp.int32))
    place_in_block = (order[:, None] * piece + jnp.arange(piece, dtype=jnp.int32)).reshape(-1)

    def seg_of(which):
        return seg_pieces[which][order].reshape(-1)

    segs = [seg_of(side), swap(seg_of(1 - side), half)]
    codes = [block_seg * BLOCK + place_in_block for block_seg in segs]
    pieces = [
        [packed[b * half]] + [swap(packed[b * half + k], k) for k in range(1, half)]
        for b in range(2)
    ]
    grads = [ups[0], swap(ups[1], half)]
    lives = [(section == layers - 1 - tick).astype(jnp.int32)[None] for tick in range(layers)]

    blocks, held = [], []
    for b in range(2):
        after = held[0][0] if b else None
        blocks.append(block_probs(pieces[b], codes[b], model_width, kv_width, after))
        probs, inv, x = blocks[b]
        held.append(layer_step(lives[0], grads[b], x, probs, inv, weight, norm_gain))

    columns = pl.pallas_call(
        functools.partial(columns_kernel, 2 * shares),
        out_shape=(jax.ShapeDtypeStruct((2 * BLOCK, 2 * shares), bf16),) * half,
        in_specs=[SMEM, VMEM, VMEM],
        out_specs=(VMEM,) * half,
        name="columns",
        **params(0, 1 << 20),
    )((me // 2)[None], blocks[0][2], blocks[1][2])
    columns = [columns[0]] + [swap(columns[k], 2 * k) for k in range(1, half)]

    for tick in range(1, layers):
        hop = [(layers - tick, layers - 1 - tick)]
        for b in range(2):
            probs, inv, x = blocks[b]
            grad = lax.ppermute(held[b][0], "section", hop)
            if tick == layers - 1 and b == 1:
                last = last_layer_step(
                    lives[tick], grad, x, probs, inv, weight, norm_gain, held[0][0], held[1], half
                )
            else:
                after = held[0][0] if b else None
                held[b] = layer_step(
                    lives[tick], grad, x, probs, inv, weight, norm_gain, held[b], after
                )
    values = [held[0][1], last[0]]
    gathered = [[value] + [swap(value, 2 * k) for k in range(1, half)] for value in values]
    rows = [last[1]] + [swap(last[1 + k], k) for k in range(1, half)]
    own, other = pl.pallas_call(
        functools.partial(partial_kernel, half, shares),
        out_shape=(jax.ShapeDtypeStruct((shares, kv_width), jnp.float32),) * 2,
        in_specs=[SMEM] + [VMEM] * (3 * half),
        out_specs=(VMEM, VMEM),
        name="weight_partial",
        **params(4 * tokens * half * shares * kv_width),
    )((me % 2)[None], *columns, *gathered[0], *gathered[1])
    other = swap(other, 1)
    scale = float(tokens * replicas) ** (-0.5)
    input_grad, weight_grad, gain_grad = pl.pallas_call(
        functools.partial(finish_kernel, half, scale),
        out_shape=(
            jax.ShapeDtypeStruct((tokens, model_width), bf16),
            jax.ShapeDtypeStruct((shares, kv_width), jnp.float32),
            jax.ShapeDtypeStruct((1, shares), jnp.float32),
        ),
        in_specs=[SMEM] + [VMEM] * (4 + half),
        out_specs=(pl.BlockSpec(memory_space=pl.ANY), VMEM, VMEM),
        scratch_shapes=[pltpu.SemaphoreType.DMA((count,))],
        name="finish",
        **params(),
    )(place, own, other, weight, norm_gain, *rows)
    return input_grad[None], weight_grad[None], gain_grad


def weight_kernel(scale, columns_ref, value_ref, weight_ref, gain_ref, out_ref, gain_out_ref):
    total = lax.dot_general(
        columns_ref[...], value_ref[...], (((0,), (0,)), ((), ())),
        preferred_element_type=jnp.float32,
    ) * scale
    out_ref[...] = total * gain_ref[...]
    product = total * weight_ref[...].astype(jnp.float32)
    sums = lax.dot_general(
        jnp.ones((8, product.shape[1]), jnp.float32), product, (((1,), (1,)), ((), ())),
        preferred_element_type=jnp.float32, precision=lax.Precision.HIGHEST,
    )
    gain_out_ref[...] = sums[:1]


def grouped(hidden, query, key, seg, weight, norm_gain, upstream):
    tokens, model_width = hidden.shape
    kv_width = key.shape[1]
    replicas = lax.axis_size("dp")
    layers = lax.axis_size("section")
    half = replicas // 2
    me = lax.axis_index("dp")
    section = lax.axis_index("section")
    side = me // half
    groups = [list(range(half)), list(range(half, replicas))]
    across = [(i, (i + half) % replicas) for i in range(replicas)]
    shares = model_width // replicas

    def rows_of(array, which, axis=0):
        at = side if which == 0 else 1 - side
        return lax.dynamic_slice_in_dim(array, at * BLOCK, BLOCK, axis)

    def regroup(array):
        return lax.all_to_all(
            array, "dp", split_axis=0, concat_axis=0, axis_index_groups=groups, tiled=True
        )

    def spread(array):
        return lax.all_to_all(array, "dp", split_axis=0, concat_axis=0, tiled=True)

    blocks, grads = [], []
    for which in range(2):
        up = rows_of(upstream, which)
        block_seg = rows_of(seg, which)
        if which == 1:
            up = lax.ppermute(up, "dp", across)
            block_seg = lax.ppermute(block_seg, "dp", across)
        packed = jnp.concatenate(
            [rows_of(query, which), rows_of(key, which), rows_of(hidden, which)], axis=1
        )
        code = block_seg * BLOCK + jnp.arange(BLOCK, dtype=jnp.int32)
        blocks.append(block_probs([regroup(packed)], code, model_width, kv_width))
        grads.append(up)

    def layer(tick, which, grad, kept):
        live = (section == layers - 1 - tick).astype(jnp.int32)[None]
        probs, inv, x = blocks[which]
        return layer_step(live, grad, x, probs, inv, weight, norm_gain, kept)

    held = [layer(0, which, grads[which], None) for which in range(2)]
    hops = [(i, i - 1) for i in range(1, layers)]

    def tick_step(tick, held):
        grads = [lax.ppermute(kept[0], "section", hops) for kept in held]
        return [layer(tick, which, grads[which], held[which]) for which in range(2)]

    held = lax.fori_loop(1, layers, tick_step, held)

    columns, values, stored = [], [], []
    for which in range(2):
        block = blocks[which][2].reshape(BLOCK, replicas, shares).transpose(1, 0, 2)
        columns.append(spread(block.reshape(replicas * BLOCK, shares)))
        out, value = held[which]
        stored.append(regroup(out))
        values.append(spread(jnp.tile(value, (replicas, 1))))
    ordered = jnp.where(
        side == 0, jnp.concatenate(stored, axis=0), jnp.concatenate(stored[::-1], axis=0)
    )
    own_weight = lax.dynamic_slice_in_dim(weight, me * shares, shares, 0)
    own_gain = lax.dynamic_slice_in_dim(norm_gain[0], me * shares, shares, 0)
    scale = float(tokens * replicas) ** (-0.5)
    weight_grad, gain_grad = pl.pallas_call(
        functools.partial(weight_kernel, scale),
        out_shape=(
            jax.ShapeDtypeStruct((shares, kv_width), jnp.float32),
            jax.ShapeDtypeStruct((1, shares), jnp.float32),
        ),
        in_specs=[VMEM] * 4,
        out_specs=(VMEM, VMEM),
        name="weight_grad",
    )(
        jnp.concatenate(columns, axis=0),
        jnp.concatenate(values, axis=0),
        own_weight,
        own_gain[:, None],
    )
    return ordered[None], weight_grad[None], gain_grad


def on_device(hidden_in, queries, keys, segments, value_weight, norm_gain, upstream):
    replicas = lax.axis_size("dp")
    piece = hidden_in.shape[1] // replicas
    plan = direct if piece % 16 == 0 and replicas in (4, 8) else grouped
    return plan(
        hidden_in[0], queries[0], keys[0], segments[0], value_weight[0], norm_gain, upstream
    )


def solution(mesh):
    in_specs = (
        P("section", "dp", None),
        P("section", "dp", None),
        P("section", "dp", None),
        P("dp", None),
        P("section", None, None),
        P("section", None),
        P("dp", None),
    )
    out_specs = (P("section", "dp", None), P("section", "dp", None), P("section", "dp"))
    return jax.shard_map(
        on_device, mesh=mesh, in_specs=in_specs, out_specs=out_specs, check_vma=False
    )
```

```python
import functools

import jax
import jax.numpy as jnp
from jax import lax
from jax.experimental import pallas as pl
from jax.experimental.pallas import tpu as pltpu
from jax.sharding import PartitionSpec as P

HEAD_FEATURES = 128
BLOCK = 64
EPSILON = 1e-06
MASKED = -1e30
VMEM = pl.BlockSpec(memory_space=pltpu.VMEM)
SMEM = pl.BlockSpec(memory_space=pltpu.SMEM)


ANY = pl.BlockSpec(memory_space=pl.ANY)


def params(flops=0, nbytes=1 << 20):
    return dict(
        compiler_params=pltpu.CompilerParams(vmem_limit_bytes=16 << 20),
        cost_estimate=pl.CostEstimate(flops=flops, bytes_accessed=nbytes, transcendentals=0),
    )


def near(array):
    return pltpu.with_memory_space_constraint(array, pltpu.VMEM)


def wide_columns(refs, first, last):
    parts = [ref[:, first:last] for ref in refs]
    return parts[0] if len(parts) == 1 else jnp.concatenate(parts, axis=0)


def probs_kernel(count, shuffled, model_width, kv_width, *refs):
    pieces, seg_ref = refs[:count], refs[count]
    probs_ref, inv_ref, x_ref = refs[-3:]
    heads = model_width // kv_width
    rows = BLOCK // count
    half = lax.axis_size("dp") // 2
    me = lax.axis_index("dp")
    turn = lax.rem(me, half) * rows if shuffled else 0

    def iota(shape, axis):
        return lax.broadcasted_iota(jnp.int32, shape, axis)

    shape = (BLOCK, seg_ref.shape[1])
    wanted = lax.div(me, half) * BLOCK + lax.bitwise_xor(iota(shape, 0), turn)
    seg = seg_ref[...].astype(jnp.float32)
    ids = jnp.sum(jnp.where(iota(shape, 1) == wanted, seg, 0.0), axis=1, keepdims=True)
    place = lax.bitwise_xor(iota((BLOCK, 1), 0), turn)
    key_code = ids * BLOCK + place.astype(jnp.float32)
    list_start = ids * BLOCK
    shape = (BLOCK, heads * BLOCK)
    same = iota(shape, 0) == lax.rem(iota(shape, 1), BLOCK)
    query_code = jnp.sum(jnp.where(same, key_code, 0.0), axis=0, keepdims=True)
    query_start = jnp.sum(jnp.where(same, list_start, 0.0), axis=0, keepdims=True)
    allowed = (key_code <= query_code) & (key_code >= query_start)
    for c in range(kv_width // HEAD_FEATURES):
        first = c * heads * HEAD_FEATURES
        query_stack = jnp.concatenate(
            [
                wide_columns(pieces, first + h * HEAD_FEATURES, first + (h + 1) * HEAD_FEATURES)
                for h in range(heads)
            ],
            axis=0,
        )
        key_first = model_width + c * HEAD_FEATURES
        keys = wide_columns(pieces, key_first, key_first + HEAD_FEATURES)
        scores = lax.dot_general(
            keys, query_stack, (((1,), (1,)), ((), ())), preferred_element_type=jnp.float32
        ) * HEAD_FEATURES ** (-0.5)
        scores = jnp.where(allowed, scores, MASKED)
        exp_scores = jnp.exp(scores - jnp.max(scores, axis=0, keepdims=True))
        total = jnp.sum(exp_scores, axis=0, keepdims=True)
        probs_ref[c] = (exp_scores / total).astype(jnp.bfloat16)
    for p, piece in enumerate(pieces):
        hidden = piece[:, model_width + kv_width :]
        x_ref[p * rows : (p + 1) * rows, :] = hidden
        x = hidden.astype(jnp.float32)
        mean_square = jnp.mean(x * x, axis=1, keepdims=True)
        inv_ref[p * rows : (p + 1) * rows, :] = jnp.broadcast_to(
            lax.rsqrt(mean_square + EPSILON), (rows, inv_ref.shape[1])
        )


def block_probs(pieces, seg, shuffled, model_width, kv_width, after=None):
    heads = model_width // kv_width
    key_heads = kv_width // HEAD_FEATURES
    operands = [near(piece) for piece in pieces] + [seg]
    specs = [VMEM] * len(operands)
    if after is not None:
        operands.append(after)
        specs.append(ANY)
    return pl.pallas_call(
        functools.partial(probs_kernel, len(pieces), shuffled, model_width, kv_width),
        out_shape=(
            jax.ShapeDtypeStruct((key_heads, BLOCK, heads * BLOCK), jnp.bfloat16),
            jax.ShapeDtypeStruct((BLOCK, 128), jnp.float32),
            jax.ShapeDtypeStruct((BLOCK, model_width), jnp.bfloat16),
        ),
        in_specs=specs,
        out_specs=(VMEM,) * 3,
        name="probs",
        **params(4 * BLOCK * BLOCK * model_width),
    )(*operands)


def layer_math(grad_ref, x_ref, probs_ref, inv_ref, weight_ref, gain_ref, scaled_ref, store, value_ref):
    model_width = grad_ref.shape[1]
    kv_width = weight_ref.shape[1]
    heads = model_width // kv_width
    chunk = min(512, model_width)
    inv = inv_ref[:, :1]
    values = []
    for c in range(kv_width // HEAD_FEATURES):
        first = c * heads * HEAD_FEATURES
        grad_stack = jnp.concatenate(
            [
                grad_ref[:, first + h * HEAD_FEATURES : first + (h + 1) * HEAD_FEATURES]
                for h in range(heads)
            ],
            axis=0,
        )
        values.append(
            jnp.dot(probs_ref[c], grad_stack, preferred_element_type=jnp.float32).astype(
                jnp.bfloat16
            )
        )
    value = jnp.concatenate(values, axis=1)
    value_ref[...] = (value.astype(jnp.float32) * inv).astype(jnp.bfloat16)
    inner = jnp.zeros((BLOCK, 1), jnp.float32)
    for first in range(0, model_width, chunk):
        columns = slice(first, first + chunk)
        normed_grad = lax.dot_general(
            value, weight_ref[columns, :], (((1,), (1,)), ((), ())),
            preferred_element_type=jnp.float32,
        )
        scaled = normed_grad * gain_ref[:, columns]
        scaled_ref[:, columns] = scaled
        x = x_ref[:, columns].astype(jnp.float32)
        inner = inner + jnp.sum(x * scaled, axis=1, keepdims=True)
    pull = inner * (inv * inv / model_width)
    for first in range(0, model_width, chunk):
        columns = slice(first, first + chunk)
        x = x_ref[:, columns].astype(jnp.float32)
        change = inv * (scaled_ref[:, columns] - x * pull)
        store(columns, (grad_ref[:, columns].astype(jnp.float32) + change).astype(jnp.bfloat16))


def layer_kernel(live_ref, grad_ref, x_ref, probs_ref, inv_ref, weight_ref, gain_ref, *rest):
    out_ref, value_ref, scaled_ref = rest[-3:]

    def store(columns, part):
        out_ref[:, columns] = part

    if len(rest) == 5:

        @pl.when(live_ref[0] == 0)
        def _():
            out_ref[...] = rest[0][...]
            value_ref[...] = rest[1][...]

    @pl.when(live_ref[0] == 1)
    def _():
        layer_math(
            grad_ref, x_ref, probs_ref, inv_ref, weight_ref, gain_ref, scaled_ref, store, value_ref
        )


def layer_step(live, grad, x, probs, inv, weight, gain, held=()):
    model_width, kv_width = weight.shape
    operands = [live, grad, x, probs, inv, weight, gain, *held]
    return pl.pallas_call(
        layer_kernel,
        out_shape=(
            jax.ShapeDtypeStruct((BLOCK, model_width), jnp.bfloat16),
            jax.ShapeDtypeStruct((BLOCK, kv_width), jnp.bfloat16),
        ),
        in_specs=[SMEM] + [VMEM] * (len(operands) - 1),
        out_specs=(VMEM, VMEM),
        scratch_shapes=[pltpu.VMEM((BLOCK, model_width), jnp.float32)],
        name="layer",
        **params(2 * BLOCK * model_width * kv_width),
    )(*operands)


def tick_kernel(tick, kept, pieces, *refs):
    operands, refs = refs[:6], refs[6:]
    earlier, refs = refs[: 2 * kept], refs[2 * kept :]
    scaled_ref = refs[-1]
    turn = lax.axis_size("section") - 1 - lax.axis_index("section")
    if pieces:
        first_ref, value_ref, outs = refs[0], refs[-2 - pieces], refs[-1 - pieces : -1]
        rows = BLOCK // pieces
        for k, out_ref in enumerate(outs):
            out_ref[0] = first_ref[k * rows : (k + 1) * rows, :]

        def store(columns, part):
            for k, out_ref in enumerate(outs):
                out_ref[1, :, columns] = part[k * rows : (k + 1) * rows]

    else:
        out_ref, value_ref = refs[-3:-1]

        def store(columns, part):
            out_ref[:, columns] = part

    @pl.when(turn == tick)
    def _():
        layer_math(*operands, scaled_ref, store, value_ref)

    for at in range(kept):

        @pl.when(turn == at)
        def _(at=at):
            store(slice(None), earlier[2 * at][...])
            value_ref[...] = earlier[2 * at + 1][...]


def tick_step(tick, grad, block, weight, gain, kept=(), first=None, pieces=0, after=None):
    model_width, kv_width = weight.shape
    probs, inv, x = block
    operands = [near(array) for array in (grad, x, probs, inv, weight, gain)]
    operands += [near(array) for pair in kept for array in pair]
    if first is not None:
        operands.append(near(first))
    specs = [VMEM] * len(operands)
    if after is not None:
        operands.append(after)
        specs.append(ANY)
    rows = jax.ShapeDtypeStruct((BLOCK, model_width), jnp.bfloat16)
    value = jax.ShapeDtypeStruct((BLOCK, kv_width), jnp.bfloat16)
    if pieces:
        piece = jax.ShapeDtypeStruct((2, BLOCK // pieces, model_width), jnp.bfloat16)
        outs = (value,) + (piece,) * pieces
    else:
        outs = (rows, value)
    return pl.pallas_call(
        functools.partial(tick_kernel, tick, len(kept), pieces),
        out_shape=outs,
        in_specs=specs,
        out_specs=(VMEM,) * len(outs),
        scratch_shapes=[pltpu.VMEM((BLOCK, model_width), jnp.float32)],
        name="tick",
        **params(2 * BLOCK * model_width * kv_width),
    )(*operands)


def place():
    half = lax.axis_size("dp") // 2
    me = lax.axis_index("dp")
    return lax.div(me, half), lax.rem(me, half), me


def pack_kernel(half, piece, query_ref, key_ref, hidden_ref, up_ref, *rest):
    sems = rest[-1]
    ups = rest[-3:-1]
    packed = rest[:-3]
    side, at, _ = place()
    copies = []

    def copy(source, target):
        made = pltpu.make_async_copy(source, target, sems.at[len(copies)])
        made.start()
        copies.append(made)

    for block in range(2):
        for k in range(half):
            replica = (side if block == 0 else 1 - side) * half + lax.bitwise_xor(at, k)
            rows = pl.ds(pl.multiple_of(replica * piece, piece), piece)
            target = packed[block * half + k]
            first = 0
            for source in (query_ref, key_ref, hidden_ref):
                width = source.shape[1]
                copy(source.at[rows], target.at[:, pl.ds(first, width)])
                first += width
    for block in range(2):
        for k in range(half):
            replica = (side if block == 0 else 1 - side) * half + lax.bitwise_xor(at, k)
            rows = pl.ds(pl.multiple_of(replica * piece, piece), piece)
            copy(up_ref.at[rows], ups[block].at[pl.ds(k * piece, piece)])
    for made in copies:
        made.wait()


def columns_kernel(width, first_ref, second_ref, *outs):
    pair = lax.div(place()[2], 2)
    for k, out_ref in enumerate(outs):
        start = pl.multiple_of(lax.bitwise_xor(pair, k) * width, width)
        out_ref[:BLOCK, :] = first_ref[:, pl.ds(start, width)]
        out_ref[BLOCK:, :] = second_ref[:, pl.ds(start, width)]


def partial_kernel(count, shares, *refs):
    columns, first, second = refs[:count], refs[count : 2 * count], refs[2 * count : 3 * count]
    own_ref, other_ref = refs[-2:]
    value = jnp.concatenate(
        [ref[...] for pair in zip(first, second) for ref in pair], axis=0
    )
    mine = lax.rem(place()[2], 2)
    for ref, core in ((other_ref, 1 - mine), (own_ref, mine)):
        at = pl.ds(pl.multiple_of(core * shares, shares), shares)
        rows = jnp.concatenate([part[:, at] for part in columns], axis=0)
        ref[...] = lax.dot_general(
            rows, value, (((0,), (0,)), ((), ())), preferred_element_type=jnp.float32
        )


def finish_kernel(
    half, scale, own_ref, other_ref, weight_ref, gain_ref, *refs
):
    pieces = refs[:half]
    rows_ref, out_ref, gain_out_ref, sems = refs[half:]
    side, at, me = place()
    piece = pieces[0].shape[1]
    copies = []
    for block in range(2):
        for k in range(half):
            replica = (side if block == 0 else 1 - side) * half + lax.bitwise_xor(at, k)
            rows = pl.ds(pl.multiple_of(replica * piece, piece), piece)
            made = pltpu.make_async_copy(
                pieces[k].at[block], rows_ref.at[rows], sems.at[block * half + k]
            )
            made.start()
            copies.append(made)
    shares = own_ref.shape[0]
    first = pl.multiple_of(me * shares, shares)
    gain = gain_ref[:, pl.ds(first, shares)]
    eye = lax.broadcasted_iota(jnp.int32, (shares, shares), 0) == lax.broadcasted_iota(
        jnp.int32, (shares, shares), 1
    )
    gain_column = jnp.sum(jnp.where(eye, gain, 0.0), axis=1, keepdims=True)
    total = (own_ref[...] + other_ref[...]) * scale
    out_ref[...] = total * gain_column
    product = total * weight_ref[pl.ds(first, shares), :].astype(jnp.float32)
    sums = lax.dot_general(
        jnp.ones((8, product.shape[1]), jnp.float32), product, (((1,), (1,)), ((), ())),
        preferred_element_type=jnp.float32, precision=lax.Precision.HIGHEST,
    )
    gain_out_ref[...] = sums[:1]
    for made in copies:
        made.wait()


def direct(hidden, query, key, segments, weight, norm_gain, upstream):
    tokens, model_width = hidden.shape
    kv_width = key.shape[1]
    replicas = lax.axis_size("dp")
    layers = lax.axis_size("section")
    half = replicas // 2
    piece = tokens // replicas
    shares = model_width // replicas

    def swap(array, k):
        return lax.ppermute(array, "dp", [(i, i ^ k) for i in range(replicas)])

    def far(array):
        return pltpu.with_memory_space_constraint(array, pltpu.HBM)

    count = 2 * half
    bf16 = jnp.bfloat16
    packed = pl.pallas_call(
        functools.partial(pack_kernel, half, piece),
        out_shape=(jax.ShapeDtypeStruct((piece, 2 * model_width + kv_width), bf16),) * count
        + (jax.ShapeDtypeStruct((BLOCK, model_width), bf16),) * 2,
        in_specs=[pl.BlockSpec(memory_space=pltpu.HBM)] * 4,
        out_specs=(VMEM,) * (count + 2),
        scratch_shapes=[pltpu.SemaphoreType.DMA((4 * count,))],
        name="pack",
        **params(0, 3 << 20),
    )(far(query), far(key), far(hidden), far(upstream))
    ups = packed[-2:]
    segs = [segments, swap(segments, half)]
    pieces = [
        [packed[b * half]] + [swap(packed[b * half + k], k) for k in range(1, half)]
        for b in range(2)
    ]
    grads = [ups[0], swap(ups[1], half)]
    blocks, kept = [], [[], []]
    for b in range(2):
        after = kept[0][0][0] if b else None
        blocks.append(block_probs(pieces[b], segs[b], True, model_width, kv_width, after))
        kept[b].append(tick_step(0, grads[b], blocks[b], weight, norm_gain))

    columns = pl.pallas_call(
        functools.partial(columns_kernel, 2 * shares),
        out_shape=(jax.ShapeDtypeStruct((2 * BLOCK, 2 * shares), bf16),) * half,
        in_specs=[VMEM, VMEM],
        out_specs=(VMEM,) * half,
        name="columns",
        **params(0, 1 << 20),
    )(blocks[0][2], blocks[1][2])
    columns = [columns[0]] + [swap(columns[k], 2 * k) for k in range(1, half)]

    for tick in range(1, layers):
        hop = [(layers - tick, layers - 1 - tick)]
        grads = [lax.ppermute(kept[b][-1][0], "section", hop) for b in range(2)]
        if tick < layers - 1:
            kept[0].append(tick_step(tick, grads[0], blocks[0], weight, norm_gain))
            after = kept[0][-1][0]
            kept[1].append(tick_step(tick, grads[1], blocks[1], weight, norm_gain, after=after))
    first, first_value = tick_step(layers - 1, grads[0], blocks[0], weight, norm_gain, kept[0])
    last_value, *rows = tick_step(
        layers - 1, grads[1], blocks[1], weight, norm_gain, kept[1], first, half
    )
    gathered = [
        [value] + [swap(value, 2 * k) for k in range(1, half)]
        for value in (first_value, last_value)
    ]
    rows = [rows[0]] + [swap(rows[k], k) for k in range(1, half)]
    own, other = pl.pallas_call(
        functools.partial(partial_kernel, half, shares),
        out_shape=(jax.ShapeDtypeStruct((shares, kv_width), jnp.float32),) * 2,
        in_specs=[VMEM] * (3 * half),
        out_specs=(VMEM, VMEM),
        name="weight_partial",
        **params(20 << 30),
    )(*columns, *gathered[0], *gathered[1])
    other = swap(other, 1)
    scale = float(tokens * replicas) ** (-0.5)
    input_grad, weight_grad, gain_grad = pl.pallas_call(
        functools.partial(finish_kernel, half, scale),
        out_shape=(
            jax.ShapeDtypeStruct((tokens, model_width), bf16),
            jax.ShapeDtypeStruct((shares, kv_width), jnp.float32),
            jax.ShapeDtypeStruct((1, shares), jnp.float32),
        ),
        in_specs=[VMEM] * (4 + half),
        out_specs=(ANY, VMEM, VMEM),
        scratch_shapes=[pltpu.SemaphoreType.DMA((count,))],
        name="finish",
        **params(),
    )(own, other, weight, norm_gain, *rows)
    return input_grad[None], weight_grad[None], gain_grad


def weight_kernel(scale, columns_ref, value_ref, weight_ref, gain_ref, out_ref, gain_out_ref):
    total = lax.dot_general(
        columns_ref[...], value_ref[...], (((0,), (0,)), ((), ())),
        preferred_element_type=jnp.float32,
    ) * scale
    out_ref[...] = total * gain_ref[...]
    product = total * weight_ref[...].astype(jnp.float32)
    sums = lax.dot_general(
        jnp.ones((8, product.shape[1]), jnp.float32), product, (((1,), (1,)), ((), ())),
        preferred_element_type=jnp.float32, precision=lax.Precision.HIGHEST,
    )
    gain_out_ref[...] = sums[:1]


def grouped(hidden, query, key, segments, weight, norm_gain, upstream):
    tokens, model_width = hidden.shape
    kv_width = key.shape[1]
    replicas = lax.axis_size("dp")
    layers = lax.axis_size("section")
    half = replicas // 2
    me = lax.axis_index("dp")
    section = lax.axis_index("section")
    side = me // half
    groups = [list(range(half)), list(range(half, replicas))]
    across = [(i, (i + half) % replicas) for i in range(replicas)]
    shares = model_width // replicas

    def rows_of(array, which, axis=0):
        at = side if which == 0 else 1 - side
        return lax.dynamic_slice_in_dim(array, at * BLOCK, BLOCK, axis)

    def regroup(array):
        return lax.all_to_all(
            array, "dp", split_axis=0, concat_axis=0, axis_index_groups=groups, tiled=True
        )

    def spread(array):
        return lax.all_to_all(array, "dp", split_axis=0, concat_axis=0, tiled=True)

    blocks, grads = [], []
    for which in range(2):
        up = rows_of(upstream, which)
        seg = segments
        if which == 1:
            up = lax.ppermute(up, "dp", across)
            seg = lax.ppermute(seg, "dp", across)
        packed = jnp.concatenate(
            [rows_of(query, which), rows_of(key, which), rows_of(hidden, which)], axis=1
        )
        blocks.append(block_probs([regroup(packed)], seg, False, model_width, kv_width))
        grads.append(up)

    def layer(tick, which, grad, kept):
        live = (section == layers - 1 - tick).astype(jnp.int32)[None]
        probs, inv, x = blocks[which]
        return layer_step(live, grad, x, probs, inv, weight, norm_gain, kept)

    held = [layer(0, which, grads[which], ()) for which in range(2)]
    hops = [(i, i - 1) for i in range(1, layers)]

    def step(tick, held):
        grads = [lax.ppermute(kept[0], "section", hops) for kept in held]
        return [layer(tick, which, grads[which], held[which]) for which in range(2)]

    held = lax.fori_loop(1, layers, step, held)

    columns, values, stored = [], [], []
    for which in range(2):
        block = blocks[which][2].reshape(BLOCK, replicas, shares).transpose(1, 0, 2)
        columns.append(spread(block.reshape(replicas * BLOCK, shares)))
        out, value = held[which]
        stored.append(regroup(out))
        values.append(spread(jnp.tile(value, (replicas, 1))))
    ordered = jnp.where(
        side == 0, jnp.concatenate(stored, axis=0), jnp.concatenate(stored[::-1], axis=0)
    )
    own_weight = lax.dynamic_slice_in_dim(weight, me * shares, shares, 0)
    own_gain = lax.dynamic_slice_in_dim(norm_gain[0], me * shares, shares, 0)
    scale = float(tokens * replicas) ** (-0.5)
    weight_grad, gain_grad = pl.pallas_call(
        functools.partial(weight_kernel, scale),
        out_shape=(
            jax.ShapeDtypeStruct((shares, kv_width), jnp.float32),
            jax.ShapeDtypeStruct((1, shares), jnp.float32),
        ),
        in_specs=[VMEM] * 4,
        out_specs=(VMEM, VMEM),
        name="weight_grad",
    )(
        jnp.concatenate(columns, axis=0),
        jnp.concatenate(values, axis=0),
        own_weight,
        own_gain[:, None],
    )
    return ordered[None], weight_grad[None], gain_grad


def on_device(hidden_in, queries, keys, segments, value_weight, norm_gain, upstream):
    replicas = lax.axis_size("dp")
    piece = hidden_in.shape[1] // replicas
    plan = direct if piece % 16 == 0 and replicas in (4, 8) else grouped
    return plan(
        hidden_in[0], queries[0], keys[0], segments, value_weight[0], norm_gain, upstream
    )


def solution(mesh):
    in_specs = (
        P("section", "dp", None),
        P("section", "dp", None),
        P("section", "dp", None),
        P("dp", None),
        P("section", None, None),
        P("section", None),
        P("dp", None),
    )
    out_specs = (P("section", "dp", None), P("section", "dp", None), P("section", "dp"))
    return jax.shard_map(
        on_device, mesh=mesh, in_specs=in_specs, out_specs=out_specs, check_vma=False
    )
```

```python
import functools

import jax
import jax.numpy as jnp
from jax import lax
from jax.experimental import pallas as pl
from jax.experimental.pallas import tpu as pltpu
from jax.sharding import PartitionSpec as P

HEAD_FEATURES = 128
BLOCK = 64
UNIT = 32
EPSILON = 1e-06
MASKED = -1e30
VMEM = pl.BlockSpec(memory_space=pltpu.VMEM)
SMEM = pl.BlockSpec(memory_space=pltpu.SMEM)


ANY = pl.BlockSpec(memory_space=pl.ANY)


LATE, EARLY = slice(UNIT, BLOCK), slice(0, UNIT)


def params(flops=0, nbytes=1 << 20):
    return dict(
        compiler_params=pltpu.CompilerParams(vmem_limit_bytes=16 << 20),
        cost_estimate=pl.CostEstimate(flops=flops, bytes_accessed=nbytes, transcendentals=0),
    )


def near(array):
    return pltpu.with_memory_space_constraint(array, pltpu.VMEM)


def place():
    half = lax.axis_size("dp") // 2
    me = lax.axis_index("dp")
    return lax.div(me, half), lax.rem(me, half), me


def probs_kernel(count, seg_row, model_width, kv_width, *refs):
    pieces, seg_ref = refs[:count], refs[count]
    late_ref, early_ref, inv_ref, x_ref, rows_ref = refs[-5:]
    heads = model_width // kv_width
    rows = BLOCK // count
    side, at, _ = place()
    for k, piece in enumerate(pieces):
        if count == 1:
            rows_ref[...] = piece[...]
        else:
            first = pl.multiple_of(lax.bitwise_xor(at, k) * rows, rows)
            rows_ref[pl.ds(first, rows), :] = piece[...]

    def iota(shape, axis):
        return lax.broadcasted_iota(jnp.int32, shape, axis)

    seg = seg_ref[seg_row : seg_row + 16, : 2 * BLOCK].astype(jnp.float32)[:1]
    shape = (BLOCK, 2 * BLOCK)
    wanted = iota(shape, 1) == side * BLOCK + iota(shape, 0)
    ids = jnp.sum(jnp.where(wanted, seg, 0.0), axis=1, keepdims=True)
    key_code = ids * BLOCK + iota((BLOCK, 1), 0).astype(jnp.float32)
    list_start = ids * BLOCK
    shape = (BLOCK, heads * BLOCK)
    column = iota(shape, 1)
    query_at = lax.rem(column, UNIT) + jnp.where(column < heads * UNIT, UNIT, 0)
    same = iota(shape, 0) == query_at
    query_code = jnp.sum(jnp.where(same, key_code, 0.0), axis=0, keepdims=True)
    query_start = jnp.sum(jnp.where(same, list_start, 0.0), axis=0, keepdims=True)
    allowed = (key_code <= query_code) & (key_code >= query_start)
    for c in range(kv_width // HEAD_FEATURES):
        first = c * heads * HEAD_FEATURES
        query_stack = jnp.concatenate(
            [
                rows_ref[part, first + h * HEAD_FEATURES : first + (h + 1) * HEAD_FEATURES]
                for part in (LATE, EARLY)
                for h in range(heads)
            ],
            axis=0,
        )
        key_first = model_width + c * HEAD_FEATURES
        keys = rows_ref[:, key_first : key_first + HEAD_FEATURES]
        scores = lax.dot_general(
            keys, query_stack, (((1,), (1,)), ((), ())), preferred_element_type=jnp.float32
        ) * HEAD_FEATURES ** (-0.5)
        scores = jnp.where(allowed, scores, MASKED)
        exp_scores = jnp.exp(scores - jnp.max(scores, axis=0, keepdims=True))
        total = jnp.sum(exp_scores, axis=0, keepdims=True)
        probs = (exp_scores / total).astype(jnp.bfloat16)
        late_ref[c] = probs[LATE, : heads * UNIT]
        early_ref[c] = probs[EARLY]
    hidden = rows_ref[:, model_width + kv_width :]
    x_ref[...] = hidden
    x = hidden.astype(jnp.float32)
    mean_square = jnp.mean(x * x, axis=1, keepdims=True)
    inv_ref[...] = jnp.broadcast_to(lax.rsqrt(mean_square + EPSILON), inv_ref.shape)


def block_probs(pieces, seg, seg_row, model_width, kv_width, after=None):
    heads = model_width // kv_width
    key_heads = kv_width // HEAD_FEATURES
    operands = [near(piece) for piece in pieces] + [near(seg)]
    specs = [VMEM] * len(operands)
    if after is not None:
        operands.append(after)
        specs.append(ANY)
    return pl.pallas_call(
        functools.partial(probs_kernel, len(pieces), seg_row, model_width, kv_width),
        out_shape=(
            jax.ShapeDtypeStruct((key_heads, UNIT, heads * UNIT), jnp.bfloat16),
            jax.ShapeDtypeStruct((key_heads, UNIT, heads * BLOCK), jnp.bfloat16),
            jax.ShapeDtypeStruct((BLOCK, 128), jnp.float32),
            jax.ShapeDtypeStruct((BLOCK, model_width), jnp.bfloat16),
        ),
        in_specs=specs,
        out_specs=(VMEM,) * 4,
        scratch_shapes=[pltpu.VMEM((BLOCK, 2 * model_width + kv_width), jnp.bfloat16)],
        name="probs",
        **params(4 * BLOCK * BLOCK * model_width),
    )(*operands)


def unit_math(rows, grads, probs_ref, x_ref, inv_ref, weight_ref, gain_ref, scaled_ref, store, value_ref):
    model_width = x_ref.shape[1]
    kv_width = weight_ref.shape[1]
    heads = model_width // kv_width
    chunk = min(512, model_width)
    inv = inv_ref[rows, :1]
    values = []
    for c in range(kv_width // HEAD_FEATURES):
        first = c * heads * HEAD_FEATURES
        grad_stack = jnp.concatenate(
            [
                grad_ref[part, first + h * HEAD_FEATURES : first + (h + 1) * HEAD_FEATURES]
                for grad_ref, part in grads
                for h in range(heads)
            ],
            axis=0,
        )
        values.append(
            jnp.dot(probs_ref[c], grad_stack, preferred_element_type=jnp.float32).astype(
                jnp.bfloat16
            )
        )
    value = jnp.concatenate(values, axis=1)
    value_ref[...] = (value.astype(jnp.float32) * inv).astype(jnp.bfloat16)
    inner = jnp.zeros((UNIT, 1), jnp.float32)
    for first in range(0, model_width, chunk):
        columns = slice(first, first + chunk)
        normed_grad = lax.dot_general(
            value, weight_ref[columns, :], (((1,), (1,)), ((), ())),
            preferred_element_type=jnp.float32,
        )
        scaled = normed_grad * gain_ref[:, columns]
        scaled_ref[:, columns] = scaled
        x = x_ref[rows, columns].astype(jnp.float32)
        inner = inner + jnp.sum(x * scaled, axis=1, keepdims=True)
    pull = inner * (inv * inv / model_width)
    grad_ref, part = grads[-1]
    for first in range(0, model_width, chunk):
        columns = slice(first, first + chunk)
        x = x_ref[rows, columns].astype(jnp.float32)
        change = inv * (scaled_ref[:, columns] - x * pull)
        grad = grad_ref[part, columns].astype(jnp.float32)
        store(columns, (grad + change).astype(jnp.bfloat16))


def layer_kernel(
    live_ref, grad_ref, late_ref, early_ref, inv_ref, x_ref, weight_ref, gain_ref, *rest
):
    out_ref, value_ref, scaled_ref = rest[-3:]
    if len(rest) == 5:

        @pl.when(live_ref[0] == 0)
        def _():
            out_ref[...] = rest[0][...]
            value_ref[...] = rest[1][...]

    @pl.when(live_ref[0] == 1)
    def _():
        for rows, parts, probs_ref in ((LATE, [LATE], late_ref), (EARLY, [LATE, EARLY], early_ref)):

            def store(columns, part, rows=rows):
                out_ref[rows, columns] = part

            grads = [(grad_ref, part) for part in parts]
            unit_math(
                rows, grads, probs_ref, x_ref, inv_ref, weight_ref, gain_ref, scaled_ref, store,
                value_ref.at[rows],
            )


def layer_step(live, grad, block, weight, gain, held=()):
    model_width, kv_width = weight.shape
    operands = [live, grad, *block, weight, gain, *held]
    return pl.pallas_call(
        layer_kernel,
        out_shape=(
            jax.ShapeDtypeStruct((BLOCK, model_width), jnp.bfloat16),
            jax.ShapeDtypeStruct((BLOCK, kv_width), jnp.bfloat16),
        ),
        in_specs=[SMEM] + [VMEM] * (len(operands) - 1),
        out_specs=(VMEM, VMEM),
        scratch_shapes=[pltpu.VMEM((UNIT, model_width), jnp.float32)],
        name="layer",
        **params(2 * BLOCK * model_width * kv_width),
    )(*operands)


def tick_kernel(tick, rows, parts, kept, final, *refs):
    grads = list(zip(refs, parts))
    probs_ref, inv_ref, x_ref, weight_ref, gain_ref = refs[len(parts) : len(parts) + 5]
    refs = refs[len(parts) + 5 :]
    earlier, refs = refs[: 2 * kept], refs[2 * kept :]
    model_width, kv_width = x_ref.shape[1], weight_ref.shape[1]
    turn = lax.axis_size("section") - 1 - lax.axis_index("section")
    if final:
        late_ref, late_value_ref = refs[:2]
        values_ref, *outs = refs[-8:-3]
        scaled_ref, block_ref, value_ref = refs[-3:]

        def store(columns, part):
            block_ref[EARLY, columns] = part

    else:
        out_ref, value_ref, scaled_ref = refs[-3:]

        def store(columns, part):
            out_ref[:, columns] = part

    @pl.when(turn == tick)
    def _():
        unit_math(
            rows, grads, probs_ref, x_ref, inv_ref, weight_ref, gain_ref, scaled_ref, store,
            value_ref,
        )

    for at in range(kept):

        @pl.when(turn == at)
        def _(at=at):
            store(slice(None), earlier[2 * at][...])
            value_ref[...] = earlier[2 * at + 1][...]

    if final:
        block_ref[LATE, :] = late_ref[...]
        at = place()[1]
        piece = outs[0].shape[0]
        for k, out_ref in enumerate(outs):
            first = pl.multiple_of(lax.bitwise_xor(at, k) * piece, piece)
            out_ref[:piece, :] = block_ref[pl.ds(first, piece), :]
        values = [value_ref[...], late_value_ref[...]]
        if final == 2:
            values = [refs[2][...]] + values
            groups = model_width // kv_width
            whole = jnp.concatenate(values, axis=0)
            values_ref[...] = whole
            share = 2 * BLOCK // groups
            for g in range(groups):
                outs[2][piece:, g * kv_width : (g + 1) * kv_width] = whole[
                    g * share : (g + 1) * share
                ]
        else:
            values_ref[...] = jnp.concatenate(values, axis=0)


def tick_step(tick, grads, block, weight, gain, kept=(), late=(), after=()):
    model_width, kv_width = weight.shape
    low = len(grads) == 2
    final = len(late) - 1 if late else 0
    arrays = [grad for grad, _ in grads]
    arrays += [block[1] if low else block[0], block[2], block[3], weight, gain]
    arrays += [array for pair in kept for array in pair]
    arrays += late
    operands = [near(array) for array in arrays]
    specs = [VMEM] * len(operands) + [ANY] * len(after)
    bf16 = jnp.bfloat16
    scratch = [pltpu.VMEM((UNIT, model_width), jnp.float32)]
    if final:
        scratch += [pltpu.VMEM((BLOCK, model_width), bf16), pltpu.VMEM((UNIT, kv_width), bf16)]
        half = lax.axis_size("dp") // 2
        piece = BLOCK // half
        heights = [piece] * half
        if final == 2:
            heights[2] += 2 * BLOCK * kv_width // model_width
        outs = (jax.ShapeDtypeStruct((final * BLOCK, kv_width), bf16),)
        outs += tuple(jax.ShapeDtypeStruct((rows, model_width), bf16) for rows in heights)
    else:
        outs = (
            jax.ShapeDtypeStruct((UNIT, model_width), bf16),
            jax.ShapeDtypeStruct((UNIT, kv_width), bf16),
        )
    return pl.pallas_call(
        functools.partial(
            tick_kernel, tick, EARLY if low else LATE, [part for _, part in grads], len(kept), final
        ),
        out_shape=outs,
        in_specs=specs,
        out_specs=(VMEM,) * len(outs),
        scratch_shapes=scratch,
        name="tick",
        **params(2 * UNIT * model_width * kv_width),
    )(*operands, *after)


def pack_kernel(half, piece, query_ref, key_ref, hidden_ref, up_ref, seg_ref, *rest):
    sems = rest[-1]
    seg_out_ref, own_up_ref, across_ref = rest[-4:-1]
    packed = rest[:-4]
    side, at, _ = place()
    copies = []

    def copy(source, target):
        made = pltpu.make_async_copy(source, target, sems.at[len(copies)])
        made.start()
        copies.append(made)

    for block in range(2):
        for k in range(half):
            replica = (side if block == 0 else 1 - side) * half + lax.bitwise_xor(at, k)
            rows = pl.ds(pl.multiple_of(replica * piece, piece), piece)
            target = packed[block * half + k]
            first = 0
            for source in (query_ref, key_ref, hidden_ref):
                width = source.shape[1]
                copy(source.at[rows], target.at[:, pl.ds(first, width)])
                first += width
    for there, target in ((side, own_up_ref), (1 - side, across_ref.at[pl.ds(0, BLOCK)])):
        copy(up_ref.at[pl.ds(pl.multiple_of(there * BLOCK, BLOCK), BLOCK)], target)
    ids = jnp.broadcast_to(seg_ref[...].astype(jnp.float32), seg_out_ref.shape).astype(jnp.bfloat16)
    seg_out_ref[...] = ids
    across_ref[BLOCK:, :] = jnp.zeros((16, across_ref.shape[1]), jnp.bfloat16)
    across_ref[BLOCK:, : ids.shape[1]] = ids
    for made in copies:
        made.wait()


def columns_kernel(width, first_ref, second_ref, *outs):
    pair = lax.div(place()[2], 2)
    for k, out_ref in enumerate(outs):
        start = pl.multiple_of(lax.bitwise_xor(pair, k) * width, width)
        out_ref[:BLOCK, :] = first_ref[:, pl.ds(start, width)]
        out_ref[BLOCK:, :] = second_ref[:, pl.ds(start, width)]


def partial_kernel(count, shares, piece, *refs):
    columns, values = refs[:count], refs[count : 2 * count]
    own_ref, other_ref = refs[-2:]
    kv_width = values[0].shape[1]
    parts = []
    for k, ref in enumerate(values):
        if k == 1:
            parts += [
                ref[piece:, first : first + kv_width] for first in range(0, ref.shape[1], kv_width)
            ]
        else:
            parts.append(ref[...])
    value = jnp.concatenate(parts, axis=0)
    mine = lax.rem(place()[2], 2)
    for ref, core in ((other_ref, 1 - mine), (own_ref, mine)):
        at = pl.ds(pl.multiple_of(core * shares, shares), shares)
        rows = jnp.concatenate([part[:, at] for part in columns], axis=0)
        ref[...] = lax.dot_general(
            rows, value, (((0,), (0,)), ((), ())), preferred_element_type=jnp.float32
        )


def finish_kernel(
    half, scale, own_ref, other_ref, weight_ref, gain_ref, *refs
):
    pieces = refs[: 2 * half]
    rows_ref, out_ref, gain_out_ref, sems = refs[2 * half :]
    side, at, me = place()
    piece = pieces[0].shape[0]
    copies = []
    for block in range(2):
        for k in range(half):
            replica = (side if block == 0 else 1 - side) * half + lax.bitwise_xor(at, k)
            rows = pl.ds(pl.multiple_of(replica * piece, piece), piece)
            source = pieces[block * half + k].at[pl.ds(0, piece)]
            made = pltpu.make_async_copy(source, rows_ref.at[rows], sems.at[block * half + k])
            made.start()
            copies.append(made)
    shares = own_ref.shape[0]
    first = pl.multiple_of(me * shares, shares)
    gain = gain_ref[:, pl.ds(first, shares)]
    eye = lax.broadcasted_iota(jnp.int32, (shares, shares), 0) == lax.broadcasted_iota(
        jnp.int32, (shares, shares), 1
    )
    gain_column = jnp.sum(jnp.where(eye, gain, 0.0), axis=1, keepdims=True)
    total = (own_ref[...] + other_ref[...]) * scale
    out_ref[...] = total * gain_column
    product = total * weight_ref[pl.ds(first, shares), :].astype(jnp.float32)
    sums = lax.dot_general(
        jnp.ones((8, product.shape[1]), jnp.float32), product, (((1,), (1,)), ((), ())),
        preferred_element_type=jnp.float32, precision=lax.Precision.HIGHEST,
    )
    gain_out_ref[...] = sums[:1]
    for made in copies:
        made.wait()


def direct(hidden, query, key, segments, weight, norm_gain, upstream):
    tokens, model_width = hidden.shape
    kv_width = key.shape[1]
    replicas = lax.axis_size("dp")
    layers = lax.axis_size("section")
    half = replicas // 2
    piece = tokens // replicas
    shares = model_width // replicas

    def swap(array, k):
        return lax.ppermute(array, "dp", [(i, i ^ k) for i in range(replicas)])

    def far(array):
        return pltpu.with_memory_space_constraint(array, pltpu.HBM)

    count = 2 * half
    bf16 = jnp.bfloat16
    packed = pl.pallas_call(
        functools.partial(pack_kernel, half, piece),
        out_shape=(jax.ShapeDtypeStruct((piece, 2 * model_width + kv_width), bf16),) * count
        + (
            jax.ShapeDtypeStruct((16, segments.shape[1]), bf16),
            jax.ShapeDtypeStruct((BLOCK, model_width), bf16),
            jax.ShapeDtypeStruct((BLOCK + 16, model_width), bf16),
        ),
        in_specs=[pl.BlockSpec(memory_space=pltpu.HBM)] * 4 + [VMEM],
        out_specs=(VMEM,) * (count + 3),
        scratch_shapes=[pltpu.SemaphoreType.DMA((3 * count + 2,))],
        name="pack",
        **params(0, 3 << 20),
    )(far(query), far(key), far(hidden), far(upstream), segments)
    pieces = [
        [packed[b * half]] + [swap(packed[b * half + k], k) for k in range(1, half)]
        for b in range(2)
    ]
    across = swap(packed[-1], half)
    grads, segs = [packed[-2], across], [(packed[-3], 0), (across, BLOCK)]
    blocks, kept, after = [], [], ()
    for b in range(2):
        block = block_probs(pieces[b], *segs[b], model_width, kv_width, *after)
        late, early = (grads[b], LATE), (grads[b], EARLY)
        first = tick_step(0, [late], block, weight, norm_gain)
        second = tick_step(0, [late, early], block, weight, norm_gain, after=[first[0]])
        blocks.append(block)
        kept += [[first], [second]]
        after = [second[0]]

    columns = pl.pallas_call(
        functools.partial(columns_kernel, 2 * shares),
        out_shape=(jax.ShapeDtypeStruct((2 * BLOCK, 2 * shares), bf16),) * half,
        in_specs=[VMEM, VMEM],
        out_specs=(VMEM,) * half,
        name="columns",
        **params(0, 1 << 20),
    )(blocks[0][3], blocks[1][3])
    columns = [columns[0]] + [swap(columns[k], 2 * k) for k in range(1, half)]

    whole = slice(0, UNIT)
    for tick in range(1, layers):
        hop = [(layers - tick, layers - 1 - tick)]
        grads = [(lax.ppermute(unit[-1][0], "section", hop), whole) for unit in kept]
        last = tick == layers - 1
        after, done = [], []
        for u in range(4):
            needs = grads[u - 1 : u + 1] if u % 2 else grads[u : u + 1]
            late = []
            if last and u % 2:
                late = list(done[u - 1]) + ([done[1][0]] if u == 3 else [])
            done.append(
                tick_step(
                    tick, needs, blocks[u // 2], weight, norm_gain, kept[u] if last else (), late,
                    after,
                )
            )
            after = [done[u][0]]
            kept[u].append(done[u])
    first_rows = done[1][1:]
    values, *last_rows = done[3]
    first_rows = [first_rows[0]] + [swap(first_rows[k], k) for k in range(1, half)]
    last_rows = [last_rows[0]] + [swap(last_rows[k], k) for k in range(1, half)]
    gathered = [values, last_rows[2]] + [swap(values, 2 * k) for k in range(2, half)]
    rows = first_rows + last_rows
    own, other = pl.pallas_call(
        functools.partial(partial_kernel, half, shares, piece),
        out_shape=(jax.ShapeDtypeStruct((shares, kv_width), jnp.float32),) * 2,
        in_specs=[VMEM] * (2 * half),
        out_specs=(VMEM, VMEM),
        name="weight_partial",
        **params(4 * tokens * half * shares * kv_width),
    )(*columns, *gathered)
    other = swap(other, 1)
    scale = float(tokens * replicas) ** (-0.5)
    input_grad, weight_grad, gain_grad = pl.pallas_call(
        functools.partial(finish_kernel, half, scale),
        out_shape=(
            jax.ShapeDtypeStruct((tokens, model_width), bf16),
            jax.ShapeDtypeStruct((shares, kv_width), jnp.float32),
            jax.ShapeDtypeStruct((1, shares), jnp.float32),
        ),
        in_specs=[VMEM] * (4 + count),
        out_specs=(ANY, VMEM, VMEM),
        scratch_shapes=[pltpu.SemaphoreType.DMA((count,))],
        name="finish",
        **params(),
    )(own, other, weight, norm_gain, *rows)
    return input_grad[None], weight_grad[None], gain_grad


def weight_kernel(scale, columns_ref, value_ref, weight_ref, gain_ref, out_ref, gain_out_ref):
    total = lax.dot_general(
        columns_ref[...], value_ref[...], (((0,), (0,)), ((), ())),
        preferred_element_type=jnp.float32,
    ) * scale
    out_ref[...] = total * gain_ref[...]
    product = total * weight_ref[...].astype(jnp.float32)
    sums = lax.dot_general(
        jnp.ones((8, product.shape[1]), jnp.float32), product, (((1,), (1,)), ((), ())),
        preferred_element_type=jnp.float32, precision=lax.Precision.HIGHEST,
    )
    gain_out_ref[...] = sums[:1]


def grouped(hidden, query, key, segments, weight, norm_gain, upstream):
    tokens, model_width = hidden.shape
    kv_width = key.shape[1]
    replicas = lax.axis_size("dp")
    layers = lax.axis_size("section")
    half = replicas // 2
    me = lax.axis_index("dp")
    section = lax.axis_index("section")
    side = me // half
    groups = [list(range(half)), list(range(half, replicas))]
    across = [(i, (i + half) % replicas) for i in range(replicas)]
    shares = model_width // replicas

    def rows_of(array, which, axis=0):
        at = side if which == 0 else 1 - side
        return lax.dynamic_slice_in_dim(array, at * BLOCK, BLOCK, axis)

    def regroup(array):
        return lax.all_to_all(
            array, "dp", split_axis=0, concat_axis=0, axis_index_groups=groups, tiled=True
        )

    def spread(array):
        return lax.all_to_all(array, "dp", split_axis=0, concat_axis=0, tiled=True)

    blocks, grads = [], []
    for which in range(2):
        up = rows_of(upstream, which)
        seg = jnp.broadcast_to(segments, (16, 2 * BLOCK)).astype(jnp.bfloat16)
        if which == 1:
            up = lax.ppermute(up, "dp", across)
            seg = lax.ppermute(seg, "dp", across)
        packed = jnp.concatenate(
            [rows_of(query, which), rows_of(key, which), rows_of(hidden, which)], axis=1
        )
        blocks.append(block_probs([regroup(packed)], seg, 0, model_width, kv_width))
        grads.append(up)

    def layer(tick, which, grad, kept):
        live = (section == layers - 1 - tick).astype(jnp.int32)[None]
        return layer_step(live, grad, blocks[which], weight, norm_gain, kept)

    held = [layer(0, which, grads[which], ()) for which in range(2)]
    hops = [(i, i - 1) for i in range(1, layers)]

    def step(tick, held):
        grads = [lax.ppermute(kept[0], "section", hops) for kept in held]
        return [layer(tick, which, grads[which], held[which]) for which in range(2)]

    held = lax.fori_loop(1, layers, step, held)

    columns, values, stored = [], [], []
    for which in range(2):
        block = blocks[which][3].reshape(BLOCK, replicas, shares).transpose(1, 0, 2)
        columns.append(spread(block.reshape(replicas * BLOCK, shares)))
        out, value = held[which]
        stored.append(regroup(out))
        values.append(spread(jnp.tile(value, (replicas, 1))))
    ordered = jnp.where(
        side == 0, jnp.concatenate(stored, axis=0), jnp.concatenate(stored[::-1], axis=0)
    )
    own_weight = lax.dynamic_slice_in_dim(weight, me * shares, shares, 0)
    own_gain = lax.dynamic_slice_in_dim(norm_gain[0], me * shares, shares, 0)
    scale = float(tokens * replicas) ** (-0.5)
    weight_grad, gain_grad = pl.pallas_call(
        functools.partial(weight_kernel, scale),
        out_shape=(
            jax.ShapeDtypeStruct((shares, kv_width), jnp.float32),
            jax.ShapeDtypeStruct((1, shares), jnp.float32),
        ),
        in_specs=[VMEM] * 4,
        out_specs=(VMEM, VMEM),
        name="weight_grad",
    )(
        jnp.concatenate(columns, axis=0),
        jnp.concatenate(values, axis=0),
        own_weight,
        own_gain[:, None],
    )
    return ordered[None], weight_grad[None], gain_grad


def on_device(hidden_in, queries, keys, segments, value_weight, norm_gain, upstream):
    replicas = lax.axis_size("dp")
    piece = hidden_in.shape[1] // replicas
    plan = direct if piece % 16 == 0 and replicas == 8 else grouped
    return plan(
        hidden_in[0], queries[0], keys[0], segments, value_weight[0], norm_gain, upstream
    )


def solution(mesh):
    in_specs = (
        P("section", "dp", None),
        P("section", "dp", None),
        P("section", "dp", None),
        P("dp", None),
        P("section", None, None),
        P("section", None),
        P("dp", None),
    )
    out_specs = (P("section", "dp", None), P("section", "dp", None), P("section", "dp"))
    return jax.shard_map(
        on_device, mesh=mesh, in_specs=in_specs, out_specs=out_specs, check_vma=False
    )
```

```python
import functools

import jax
import jax.numpy as jnp
from jax import lax
from jax.experimental import pallas as pl
from jax.experimental.pallas import tpu as pltpu
from jax.sharding import PartitionSpec as P

HEAD_FEATURES = 128
BLOCK = 64
UNIT = 32
EPSILON = 1e-06
MASKED = -1e30
VMEM = pl.BlockSpec(memory_space=pltpu.VMEM)
SMEM = pl.BlockSpec(memory_space=pltpu.SMEM)


ANY = pl.BlockSpec(memory_space=pl.ANY)


LATE, EARLY = slice(UNIT, BLOCK), slice(0, UNIT)


def params(microseconds):
    flops = int(microseconds * 1.15e9)
    return dict(
        compiler_params=pltpu.CompilerParams(vmem_limit_bytes=16 << 20),
        cost_estimate=pl.CostEstimate(flops=flops, bytes_accessed=0, transcendentals=0),
    )


def near(array):
    return pltpu.with_memory_space_constraint(array, pltpu.VMEM)


def place():
    half = lax.axis_size("dp") // 2
    me = lax.axis_index("dp")
    return lax.div(me, half), lax.rem(me, half), me


def probs_kernel(count, seg_row, model_width, kv_width, *refs):
    pieces, seg_ref = refs[:count], refs[count]
    late_ref, early_ref, inv_ref, x_ref, rows_ref = refs[-5:]
    heads = model_width // kv_width
    rows = BLOCK // count
    side, at, _ = place()
    for k, piece in enumerate(pieces):
        if count == 1:
            rows_ref[...] = piece[...]
        else:
            first = pl.multiple_of(lax.bitwise_xor(at, k) * rows, rows)
            rows_ref[pl.ds(first, rows), :] = piece[...]

    def iota(shape, axis):
        return lax.broadcasted_iota(jnp.int32, shape, axis)

    seg = seg_ref[seg_row : seg_row + 16, : 2 * BLOCK].astype(jnp.float32)[:1]
    shape = (BLOCK, 2 * BLOCK)
    wanted = iota(shape, 1) == side * BLOCK + iota(shape, 0)
    ids = jnp.sum(jnp.where(wanted, seg, 0.0), axis=1, keepdims=True)
    key_code = ids * BLOCK + iota((BLOCK, 1), 0).astype(jnp.float32)
    list_start = ids * BLOCK
    shape = (BLOCK, heads * BLOCK)
    column = iota(shape, 1)
    query_at = lax.rem(column, UNIT) + jnp.where(column < heads * UNIT, UNIT, 0)
    same = iota(shape, 0) == query_at
    query_code = jnp.sum(jnp.where(same, key_code, 0.0), axis=0, keepdims=True)
    query_start = jnp.sum(jnp.where(same, list_start, 0.0), axis=0, keepdims=True)
    allowed = (key_code <= query_code) & (key_code >= query_start)
    for c in range(kv_width // HEAD_FEATURES):
        first = c * heads * HEAD_FEATURES
        query_stack = jnp.concatenate(
            [
                rows_ref[part, first + h * HEAD_FEATURES : first + (h + 1) * HEAD_FEATURES]
                for part in (LATE, EARLY)
                for h in range(heads)
            ],
            axis=0,
        )
        key_first = model_width + c * HEAD_FEATURES
        keys = rows_ref[:, key_first : key_first + HEAD_FEATURES]
        scores = lax.dot_general(
            keys, query_stack, (((1,), (1,)), ((), ())), preferred_element_type=jnp.float32
        ) * HEAD_FEATURES ** (-0.5)
        scores = jnp.where(allowed, scores, MASKED)
        exp_scores = jnp.exp(scores - jnp.max(scores, axis=0, keepdims=True))
        total = jnp.sum(exp_scores, axis=0, keepdims=True)
        probs = (exp_scores / total).astype(jnp.bfloat16)
        late_ref[c] = probs[LATE, : heads * UNIT]
        early_ref[c] = probs[EARLY]
    hidden = rows_ref[:, model_width + kv_width :]
    x_ref[...] = hidden
    x = hidden.astype(jnp.float32)
    mean_square = jnp.mean(x * x, axis=1, keepdims=True)
    inv_ref[...] = jnp.broadcast_to(lax.rsqrt(mean_square + EPSILON), inv_ref.shape)


def block_probs(pieces, seg, seg_row, model_width, kv_width, after=()):
    heads = model_width // kv_width
    key_heads = kv_width // HEAD_FEATURES
    operands = [near(piece) for piece in pieces] + [near(seg)]
    specs = [VMEM] * len(operands) + [ANY] * len(after)
    operands += after
    return pl.pallas_call(
        functools.partial(probs_kernel, len(pieces), seg_row, model_width, kv_width),
        out_shape=(
            jax.ShapeDtypeStruct((key_heads, UNIT, heads * UNIT), jnp.bfloat16),
            jax.ShapeDtypeStruct((key_heads, UNIT, heads * BLOCK), jnp.bfloat16),
            jax.ShapeDtypeStruct((BLOCK, 128), jnp.float32),
            jax.ShapeDtypeStruct((BLOCK, model_width), jnp.bfloat16),
        ),
        in_specs=specs,
        out_specs=(VMEM,) * 4,
        scratch_shapes=[pltpu.VMEM((BLOCK, 2 * model_width + kv_width), jnp.bfloat16)],
        name="probs",
        **params(0.35),
    )(*operands)


def unit_math(rows, grads, probs_ref, x_ref, inv_ref, turned_ref, gain_ref, scaled_ref, store, value_ref):
    kv_width, model_width = turned_ref.shape
    heads = model_width // kv_width
    chunk = min(512, model_width)
    inv = inv_ref[rows, :1]
    values = []
    for c in range(kv_width // HEAD_FEATURES):
        first = c * heads * HEAD_FEATURES
        grad_stack = jnp.concatenate(
            [
                grad_ref[part, first + h * HEAD_FEATURES : first + (h + 1) * HEAD_FEATURES]
                for grad_ref, part in grads
                for h in range(heads)
            ],
            axis=0,
        )
        values.append(
            jnp.dot(probs_ref[c], grad_stack, preferred_element_type=jnp.float32).astype(
                jnp.bfloat16
            )
        )
    value = jnp.concatenate(values, axis=1)
    value_ref[...] = (value.astype(jnp.float32) * inv).astype(jnp.bfloat16)
    inner = jnp.zeros((UNIT, 1), jnp.float32)
    for first in range(0, model_width, chunk):
        columns = slice(first, first + chunk)
        normed_grad = jnp.dot(value, turned_ref[:, columns], preferred_element_type=jnp.float32)
        scaled = normed_grad * gain_ref[:, columns]
        scaled_ref[:, columns] = scaled
        x = x_ref[rows, columns].astype(jnp.float32)
        inner = inner + jnp.sum(x * scaled, axis=1, keepdims=True)
    pull = inner * (inv * inv / model_width)
    grad_ref, part = grads[-1]
    for first in range(0, model_width, chunk):
        columns = slice(first, first + chunk)
        x = x_ref[rows, columns].astype(jnp.float32)
        change = inv * (scaled_ref[:, columns] - x * pull)
        grad = grad_ref[part, columns].astype(jnp.float32)
        store(columns, (grad + change).astype(jnp.bfloat16))


def turn_kernel(weight_ref, *refs):
    turned_ref = refs[-1]
    step = min(256, weight_ref.shape[0])
    for first in range(0, weight_ref.shape[0], step):
        turned_ref[:, first : first + step] = weight_ref[first : first + step, :].T


def turn(weight, after=()):
    return pl.pallas_call(
        turn_kernel,
        out_shape=jax.ShapeDtypeStruct(weight.shape[::-1], weight.dtype),
        in_specs=[VMEM] + [ANY] * len(after),
        out_specs=VMEM,
        name="turn",
        **params(1.5),
    )(near(weight), *after)


def layer_kernel(
    live_ref, grad_ref, late_ref, early_ref, inv_ref, x_ref, turned_ref, gain_ref, *rest
):
    out_ref, value_ref, scaled_ref = rest[-3:]
    if len(rest) == 5:

        @pl.when(live_ref[0] == 0)
        def _():
            out_ref[...] = rest[0][...]
            value_ref[...] = rest[1][...]

    @pl.when(live_ref[0] == 1)
    def _():
        for rows, parts, probs_ref in ((LATE, [LATE], late_ref), (EARLY, [LATE, EARLY], early_ref)):

            def store(columns, part, rows=rows):
                out_ref[rows, columns] = part

            grads = [(grad_ref, part) for part in parts]
            unit_math(
                rows, grads, probs_ref, x_ref, inv_ref, turned_ref, gain_ref, scaled_ref, store,
                value_ref.at[rows],
            )


def layer_step(live, grad, block, turned, gain, held=()):
    kv_width, model_width = turned.shape
    operands = [live, grad, *block, turned, gain, *held]
    return pl.pallas_call(
        layer_kernel,
        out_shape=(
            jax.ShapeDtypeStruct((BLOCK, model_width), jnp.bfloat16),
            jax.ShapeDtypeStruct((BLOCK, kv_width), jnp.bfloat16),
        ),
        in_specs=[SMEM] + [VMEM] * (len(operands) - 1),
        out_specs=(VMEM, VMEM),
        scratch_shapes=[pltpu.VMEM((UNIT, model_width), jnp.float32)],
        name="layer",
        **params(1.1),
    )(*operands)


def tick_kernel(tick, rows, parts, kept, final, *refs):
    grads = list(zip(refs, parts))
    probs_ref, inv_ref, x_ref, turned_ref, gain_ref = refs[len(parts) : len(parts) + 5]
    refs = refs[len(parts) + 5 :]
    earlier, refs = refs[: 2 * kept], refs[2 * kept :]
    kv_width, model_width = turned_ref.shape
    turn = lax.axis_size("section") - 1 - lax.axis_index("section")
    if final:
        late_ref, late_value_ref = refs[:2]
        values_ref, *outs = refs[-8:-3]
        scaled_ref, block_ref, value_ref = refs[-3:]

        def store(columns, part):
            block_ref[EARLY, columns] = part

    else:
        out_ref, value_ref, scaled_ref = refs[-3:]

        def store(columns, part):
            out_ref[:, columns] = part

    @pl.when(turn == tick)
    def _():
        unit_math(
            rows, grads, probs_ref, x_ref, inv_ref, turned_ref, gain_ref, scaled_ref, store,
            value_ref,
        )

    for at in range(kept):

        @pl.when(turn == at)
        def _(at=at):
            store(slice(None), earlier[2 * at][...])
            value_ref[...] = earlier[2 * at + 1][...]

    if final:
        block_ref[LATE, :] = late_ref[...]
        at = place()[1]
        piece = outs[0].shape[0]
        for k, out_ref in enumerate(outs):
            first = pl.multiple_of(lax.bitwise_xor(at, k) * piece, piece)
            out_ref[:piece, :] = block_ref[pl.ds(first, piece), :]
        values = [value_ref[...], late_value_ref[...]]
        if final == 2:
            values = [refs[2][...]] + values
            groups = model_width // kv_width
            whole = jnp.concatenate(values, axis=0)
            values_ref[...] = whole
            share = 2 * BLOCK // groups
            for g in range(groups):
                outs[2][piece:, g * kv_width : (g + 1) * kv_width] = whole[
                    g * share : (g + 1) * share
                ]
        else:
            values_ref[...] = jnp.concatenate(values, axis=0)


def tick_step(tick, grads, block, turned, gain, kept=(), late=(), after=()):
    kv_width, model_width = turned.shape
    low = len(grads) == 2
    final = len(late) - 1 if late else 0
    arrays = [grad for grad, _ in grads]
    arrays += [block[1] if low else block[0], block[2], block[3], turned, gain]
    arrays += [array for pair in kept for array in pair]
    arrays += late
    operands = [near(array) for array in arrays]
    specs = [VMEM] * len(operands) + [ANY] * len(after)
    bf16 = jnp.bfloat16
    scratch = [pltpu.VMEM((UNIT, model_width), jnp.float32)]
    if final:
        scratch += [pltpu.VMEM((BLOCK, model_width), bf16), pltpu.VMEM((UNIT, kv_width), bf16)]
        half = lax.axis_size("dp") // 2
        piece = BLOCK // half
        heights = [piece] * half
        if final == 2:
            heights[2] += 2 * BLOCK * kv_width // model_width
        outs = (jax.ShapeDtypeStruct((final * BLOCK, kv_width), bf16),)
        outs += tuple(jax.ShapeDtypeStruct((rows, model_width), bf16) for rows in heights)
    else:
        outs = (
            jax.ShapeDtypeStruct((UNIT, model_width), bf16),
            jax.ShapeDtypeStruct((UNIT, kv_width), bf16),
        )
    return pl.pallas_call(
        functools.partial(
            tick_kernel, tick, EARLY if low else LATE, [part for _, part in grads], len(kept), final
        ),
        out_shape=outs,
        in_specs=specs,
        out_specs=(VMEM,) * len(outs),
        scratch_shapes=scratch,
        name="tick",
        **params(0.2),
    )(*operands, *after)


def pack_kernel(block, half, piece, query_ref, key_ref, hidden_ref, up_ref, seg_ref, *rest):
    late_ref, early_ref, seg_in_ref, sems = rest[-4:]
    packed = rest[-4 - half : -4]
    side, at, _ = place()
    there = side if block == 0 else 1 - side
    copies = []

    def copy(source, target):
        made = pltpu.make_async_copy(source, target, sems.at[len(copies)])
        made.start()
        copies.append(made)

    copy(seg_ref, seg_in_ref)
    for k in range(half):
        replica = there * half + lax.bitwise_xor(at, k)
        rows = pl.ds(pl.multiple_of(replica * piece, piece), piece)
        first = 0
        for source in (query_ref, key_ref, hidden_ref):
            width = source.shape[1]
            copy(source.at[rows], packed[k].at[:, pl.ds(first, width)])
            first += width
    for first, target in ((0, early_ref), (UNIT, late_ref.at[pl.ds(0, UNIT)])):
        copy(up_ref.at[pl.ds(pl.multiple_of(there * BLOCK + first, UNIT), UNIT)], target)
    late_ref[UNIT:, :] = jnp.zeros((16, late_ref.shape[1]), jnp.bfloat16)
    copies[0].wait()
    ids = seg_in_ref[...].astype(jnp.float32)
    late_ref[UNIT:, : ids.shape[1]] = jnp.broadcast_to(ids, (16, ids.shape[1])).astype(
        jnp.bfloat16
    )
    for made in copies[1:]:
        made.wait()


def pack(block, half, piece, sources):
    model_width = sources[0].shape[1]
    width = sum(source.shape[1] for source in sources[:3])
    bf16 = jnp.bfloat16
    operands = [pltpu.with_memory_space_constraint(array, pltpu.HBM) for array in sources]
    return pl.pallas_call(
        functools.partial(pack_kernel, block, half, piece),
        out_shape=(jax.ShapeDtypeStruct((piece, width), bf16),) * half
        + (
            jax.ShapeDtypeStruct((UNIT + 16, model_width), bf16),
            jax.ShapeDtypeStruct((UNIT, model_width), bf16),
        ),
        in_specs=[pl.BlockSpec(memory_space=pltpu.HBM)] * len(sources),
        out_specs=(VMEM,) * (half + 2),
        scratch_shapes=[
            pltpu.VMEM(sources[-1].shape, jnp.int32),
            pltpu.SemaphoreType.DMA((3 * half + 3,)),
        ],
        name="pack",
        **params(1.2),
    )(*operands)


def columns_kernel(width, first_ref, second_ref, *outs):
    pair = lax.div(place()[2], 2)
    for k, out_ref in enumerate(outs):
        start = pl.multiple_of(lax.bitwise_xor(pair, k) * width, width)
        out_ref[:BLOCK, :] = first_ref[:, pl.ds(start, width)]
        out_ref[BLOCK:, :] = second_ref[:, pl.ds(start, width)]


def partial_kernel(count, shares, piece, *refs):
    columns, values = refs[:count], refs[count : 2 * count]
    own_ref, other_ref = refs[-2:]
    kv_width = values[0].shape[1]
    parts = []
    for k, ref in enumerate(values):
        if k == 1:
            parts += [
                ref[piece:, first : first + kv_width] for first in range(0, ref.shape[1], kv_width)
            ]
        else:
            parts.append(ref[...])
    value = jnp.concatenate(parts, axis=0)
    mine = lax.rem(place()[2], 2)
    for ref, core in ((other_ref, 1 - mine), (own_ref, mine)):
        at = pl.ds(pl.multiple_of(core * shares, shares), shares)
        rows = jnp.concatenate([part[:, at] for part in columns], axis=0)
        ref[...] = lax.dot_general(
            rows, value, (((0,), (0,)), ((), ())), preferred_element_type=jnp.float32
        )


def finish_kernel(
    half, scale, own_ref, other_ref, weight_ref, gain_ref, *refs
):
    pieces = refs[: 2 * half]
    rows_ref, out_ref, gain_out_ref, sems = refs[2 * half :]
    side, at, me = place()
    piece = pieces[0].shape[0]
    copies = []
    for block in range(2):
        for k in range(half):
            replica = (side if block == 0 else 1 - side) * half + lax.bitwise_xor(at, k)
            rows = pl.ds(pl.multiple_of(replica * piece, piece), piece)
            source = pieces[block * half + k].at[pl.ds(0, piece)]
            made = pltpu.make_async_copy(source, rows_ref.at[rows], sems.at[block * half + k])
            made.start()
            copies.append(made)
    shares = own_ref.shape[0]
    first = pl.multiple_of(me * shares, shares)
    gain = gain_ref[:, pl.ds(first, shares)]
    eye = lax.broadcasted_iota(jnp.int32, (shares, shares), 0) == lax.broadcasted_iota(
        jnp.int32, (shares, shares), 1
    )
    gain_column = jnp.sum(jnp.where(eye, gain, 0.0), axis=1, keepdims=True)
    total = (own_ref[...] + other_ref[...]) * scale
    out_ref[...] = total * gain_column
    product = total * weight_ref[pl.ds(first, shares), :].astype(jnp.float32)
    sums = lax.dot_general(
        jnp.ones((8, product.shape[1]), jnp.float32), product, (((1,), (1,)), ((), ())),
        preferred_element_type=jnp.float32, precision=lax.Precision.HIGHEST,
    )
    gain_out_ref[...] = sums[:1]
    for made in copies:
        made.wait()


def direct(hidden, query, key, segments, weight, norm_gain, upstream):
    tokens, model_width = hidden.shape
    kv_width = key.shape[1]
    replicas = lax.axis_size("dp")
    layers = lax.axis_size("section")
    half = replicas // 2
    piece = tokens // replicas
    shares = model_width // replicas

    def swap(array, k):
        return lax.ppermute(array, "dp", [(i, i ^ k) for i in range(replicas)])

    count = 2 * half
    bf16 = jnp.bfloat16
    sources = (query, key, hidden, upstream, segments)
    pieces, ups = [], []
    for b in range(2):
        *packed, late, early = pack(b, half, piece, sources)
        pieces.append([packed[0]] + [swap(packed[k], k) for k in range(1, half)])
        ups.append([swap(part, half) for part in (late, early)] if b else [late, early])
    whole = slice(0, UNIT)
    turned = turn(weight)
    blocks, kept, after = [], [], [turned]
    for b in range(2):
        block = block_probs(pieces[b], ups[b][0], UNIT, model_width, kv_width, after)
        late, early = [(part, whole) for part in ups[b]]
        first = tick_step(0, [late], block, turned, norm_gain)
        second = tick_step(0, [late, early], block, turned, norm_gain, after=[first[0]])
        blocks.append(block)
        kept += [[first], [second]]
        after = [second[0]]

    columns = pl.pallas_call(
        functools.partial(columns_kernel, 2 * shares),
        out_shape=(jax.ShapeDtypeStruct((2 * BLOCK, 2 * shares), bf16),) * half,
        in_specs=[VMEM, VMEM],
        out_specs=(VMEM,) * half,
        name="columns",
        **params(0.4),
    )(blocks[0][3], blocks[1][3])
    columns = [columns[0]] + [swap(columns[k], 2 * k) for k in range(1, half)]

    for tick in range(1, layers):
        hop = [(layers - tick, layers - 1 - tick)]
        grads = [(lax.ppermute(unit[-1][0], "section", hop), whole) for unit in kept]
        last = tick == layers - 1
        after, done = (columns if last else []), []
        for u in range(4):
            needs = grads[u - 1 : u + 1] if u % 2 else grads[u : u + 1]
            late = []
            if last and u % 2:
                late = list(done[u - 1]) + ([done[1][0]] if u == 3 else [])
            if last and u == 3:
                rows = [done[1][1]] + [swap(done[1][1 + k], k) for k in range(1, half)]
                after = after + rows[1:]
            done.append(
                tick_step(
                    tick, needs, blocks[u // 2], turned, norm_gain, kept[u] if last else (), late,
                    after,
                )
            )
            after = [done[u][0]]
            kept[u].append(done[u])
    values, *last_rows = done[3]
    last_rows = [last_rows[0]] + [swap(last_rows[k], k) for k in range(1, half)]
    gathered = [values, last_rows[2]] + [swap(values, 2 * k) for k in range(2, half)]
    own, other = pl.pallas_call(
        functools.partial(partial_kernel, half, shares, piece),
        out_shape=(jax.ShapeDtypeStruct((shares, kv_width), jnp.float32),) * 2,
        in_specs=[VMEM] * (2 * half) + [ANY] * 2,
        out_specs=(VMEM, VMEM),
        name="weight_partial",
        **params(0.5),
    )(*columns, *gathered, last_rows[1], last_rows[3])
    other = swap(other, 1)
    scale = float(tokens * replicas) ** (-0.5)
    input_grad, weight_grad, gain_grad = pl.pallas_call(
        functools.partial(finish_kernel, half, scale),
        out_shape=(
            jax.ShapeDtypeStruct((tokens, model_width), bf16),
            jax.ShapeDtypeStruct((shares, kv_width), jnp.float32),
            jax.ShapeDtypeStruct((1, shares), jnp.float32),
        ),
        in_specs=[VMEM] * (4 + count),
        out_specs=(ANY, VMEM, VMEM),
        scratch_shapes=[pltpu.SemaphoreType.DMA((count,))],
        name="finish",
        **params(2.0),
    )(own, other, weight, norm_gain, *rows, *last_rows)
    return input_grad[None], weight_grad[None], gain_grad


def weight_kernel(scale, columns_ref, value_ref, weight_ref, gain_ref, out_ref, gain_out_ref):
    total = lax.dot_general(
        columns_ref[...], value_ref[...], (((0,), (0,)), ((), ())),
        preferred_element_type=jnp.float32,
    ) * scale
    out_ref[...] = total * gain_ref[...]
    product = total * weight_ref[...].astype(jnp.float32)
    sums = lax.dot_general(
        jnp.ones((8, product.shape[1]), jnp.float32), product, (((1,), (1,)), ((), ())),
        preferred_element_type=jnp.float32, precision=lax.Precision.HIGHEST,
    )
    gain_out_ref[...] = sums[:1]


def grouped(hidden, query, key, segments, weight, norm_gain, upstream):
    tokens, model_width = hidden.shape
    kv_width = key.shape[1]
    replicas = lax.axis_size("dp")
    layers = lax.axis_size("section")
    half = replicas // 2
    me = lax.axis_index("dp")
    section = lax.axis_index("section")
    side = me // half
    groups = [list(range(half)), list(range(half, replicas))]
    across = [(i, (i + half) % replicas) for i in range(replicas)]
    shares = model_width // replicas

    def rows_of(array, which, axis=0):
        at = side if which == 0 else 1 - side
        return lax.dynamic_slice_in_dim(array, at * BLOCK, BLOCK, axis)

    def regroup(array):
        return lax.all_to_all(
            array, "dp", split_axis=0, concat_axis=0, axis_index_groups=groups, tiled=True
        )

    def spread(array):
        return lax.all_to_all(array, "dp", split_axis=0, concat_axis=0, tiled=True)

    turned = turn(weight)
    blocks, grads = [], []
    for which in range(2):
        up = rows_of(upstream, which)
        seg = jnp.broadcast_to(segments, (16, 2 * BLOCK)).astype(jnp.bfloat16)
        if which == 1:
            up = lax.ppermute(up, "dp", across)
            seg = lax.ppermute(seg, "dp", across)
        packed = jnp.concatenate(
            [rows_of(query, which), rows_of(key, which), rows_of(hidden, which)], axis=1
        )
        blocks.append(block_probs([regroup(packed)], seg, 0, model_width, kv_width))
        grads.append(up)

    def layer(tick, which, grad, kept):
        live = (section == layers - 1 - tick).astype(jnp.int32)[None]
        return layer_step(live, grad, blocks[which], turned, norm_gain, kept)

    held = [layer(0, which, grads[which], ()) for which in range(2)]
    hops = [(i, i - 1) for i in range(1, layers)]

    def step(tick, held):
        grads = [lax.ppermute(kept[0], "section", hops) for kept in held]
        return [layer(tick, which, grads[which], held[which]) for which in range(2)]

    held = lax.fori_loop(1, layers, step, held)

    columns, values, stored = [], [], []
    for which in range(2):
        block = blocks[which][3].reshape(BLOCK, replicas, shares).transpose(1, 0, 2)
        columns.append(spread(block.reshape(replicas * BLOCK, shares)))
        out, value = held[which]
        stored.append(regroup(out))
        values.append(spread(jnp.tile(value, (replicas, 1))))
    ordered = jnp.where(
        side == 0, jnp.concatenate(stored, axis=0), jnp.concatenate(stored[::-1], axis=0)
    )
    own_weight = lax.dynamic_slice_in_dim(weight, me * shares, shares, 0)
    own_gain = lax.dynamic_slice_in_dim(norm_gain[0], me * shares, shares, 0)
    scale = float(tokens * replicas) ** (-0.5)
    weight_grad, gain_grad = pl.pallas_call(
        functools.partial(weight_kernel, scale),
        out_shape=(
            jax.ShapeDtypeStruct((shares, kv_width), jnp.float32),
            jax.ShapeDtypeStruct((1, shares), jnp.float32),
        ),
        in_specs=[VMEM] * 4,
        out_specs=(VMEM, VMEM),
        name="weight_grad",
    )(
        jnp.concatenate(columns, axis=0),
        jnp.concatenate(values, axis=0),
        own_weight,
        own_gain[:, None],
    )
    return ordered[None], weight_grad[None], gain_grad


def on_device(hidden_in, queries, keys, segments, value_weight, norm_gain, upstream):
    replicas = lax.axis_size("dp")
    piece = hidden_in.shape[1] // replicas
    plan = direct if piece % 16 == 0 and replicas == 8 else grouped
    return plan(
        hidden_in[0], queries[0], keys[0], segments, value_weight[0], norm_gain, upstream
    )


def solution(mesh):
    in_specs = (
        P("section", "dp", None),
        P("section", "dp", None),
        P("section", "dp", None),
        P("dp", None),
        P("section", None, None),
        P("section", None),
        P("dp", None),
    )
    out_specs = (P("section", "dp", None), P("section", "dp", None), P("section", "dp"))
    return jax.shard_map(
        on_device, mesh=mesh, in_specs=in_specs, out_specs=out_specs, check_vma=False
    )
```

```python
import functools

import jax
import jax.numpy as jnp
from jax import lax
from jax.experimental import pallas as pl
from jax.experimental.pallas import tpu as pltpu
from jax.sharding import PartitionSpec as P

HEAD_FEATURES = 128
BLOCK = 64
UNIT = 32
EPSILON = 1e-06
MASKED = -1e30
VMEM = pl.BlockSpec(memory_space=pltpu.VMEM)
SMEM = pl.BlockSpec(memory_space=pltpu.SMEM)


ANY = pl.BlockSpec(memory_space=pl.ANY)


LATE, EARLY = slice(UNIT, BLOCK), slice(0, UNIT)


def params(microseconds):
    flops = int(microseconds * 1.15e9)
    return dict(
        compiler_params=pltpu.CompilerParams(vmem_limit_bytes=16 << 20),
        cost_estimate=pl.CostEstimate(flops=flops, bytes_accessed=0, transcendentals=0),
    )


def near(array):
    return pltpu.with_memory_space_constraint(array, pltpu.VMEM)


def place():
    half = lax.axis_size("dp") // 2
    me = lax.axis_index("dp")
    return lax.div(me, half), lax.rem(me, half), me


def probs_kernel(count, seg_row, model_width, kv_width, *refs):
    pieces, seg_ref = refs[:count], refs[count]
    late_ref, early_ref, inv_ref, x_ref, rows_ref = refs[-5:]
    heads = model_width // kv_width
    rows = BLOCK // count
    side, at, _ = place()
    for k, piece in enumerate(pieces):
        if count == 1:
            rows_ref[...] = piece[...]
        else:
            first = pl.multiple_of(lax.bitwise_xor(at, k) * rows, rows)
            rows_ref[pl.ds(first, rows), :] = piece[...]

    def iota(shape, axis):
        return lax.broadcasted_iota(jnp.int32, shape, axis)

    seg = seg_ref[seg_row : seg_row + 16, : 2 * BLOCK].astype(jnp.float32)[:1]
    shape = (BLOCK, 2 * BLOCK)
    wanted = iota(shape, 1) == side * BLOCK + iota(shape, 0)
    ids = jnp.sum(jnp.where(wanted, seg, 0.0), axis=1, keepdims=True)
    key_code = ids * BLOCK + iota((BLOCK, 1), 0).astype(jnp.float32)
    list_start = ids * BLOCK
    shape = (BLOCK, heads * BLOCK)
    column = iota(shape, 1)
    query_at = lax.rem(column, UNIT) + jnp.where(column < heads * UNIT, UNIT, 0)
    same = iota(shape, 0) == query_at
    query_code = jnp.sum(jnp.where(same, key_code, 0.0), axis=0, keepdims=True)
    query_start = jnp.sum(jnp.where(same, list_start, 0.0), axis=0, keepdims=True)
    allowed = (key_code <= query_code) & (key_code >= query_start)
    for c in range(kv_width // HEAD_FEATURES):
        first = c * heads * HEAD_FEATURES
        query_stack = jnp.concatenate(
            [
                rows_ref[part, first + h * HEAD_FEATURES : first + (h + 1) * HEAD_FEATURES]
                for part in (LATE, EARLY)
                for h in range(heads)
            ],
            axis=0,
        )
        key_first = model_width + c * HEAD_FEATURES
        keys = rows_ref[:, key_first : key_first + HEAD_FEATURES]
        scores = lax.dot_general(
            keys, query_stack, (((1,), (1,)), ((), ())), preferred_element_type=jnp.float32
        ) * HEAD_FEATURES ** (-0.5)
        scores = jnp.where(allowed, scores, MASKED)
        exp_scores = jnp.exp(scores - jnp.max(scores, axis=0, keepdims=True))
        total = jnp.sum(exp_scores, axis=0, keepdims=True)
        probs = (exp_scores / total).astype(jnp.bfloat16)
        late_ref[c] = probs[LATE, : heads * UNIT]
        early_ref[c] = probs[EARLY]
    hidden = rows_ref[:, model_width + kv_width :]
    x_ref[...] = hidden
    x = hidden.astype(jnp.float32)
    mean_square = jnp.mean(x * x, axis=1, keepdims=True)
    inv_ref[...] = jnp.broadcast_to(lax.rsqrt(mean_square + EPSILON), inv_ref.shape)


def block_probs(pieces, seg, seg_row, model_width, kv_width, after=()):
    heads = model_width // kv_width
    key_heads = kv_width // HEAD_FEATURES
    operands = [near(piece) for piece in pieces] + [near(seg)]
    specs = [VMEM] * len(operands)
    outs = [
        jax.ShapeDtypeStruct((key_heads, UNIT, heads * UNIT), jnp.bfloat16),
        jax.ShapeDtypeStruct((key_heads, UNIT, heads * BLOCK), jnp.bfloat16),
        jax.ShapeDtypeStruct((BLOCK, 128), jnp.float32),
        jax.ShapeDtypeStruct((BLOCK, model_width), jnp.bfloat16),
    ]
    scratch = [pltpu.VMEM((BLOCK, 2 * model_width + kv_width), jnp.bfloat16)]
    operands += after
    specs += [ANY] * len(after)
    return pl.pallas_call(
        functools.partial(probs_kernel, len(pieces), seg_row, model_width, kv_width),
        out_shape=tuple(outs),
        in_specs=specs,
        out_specs=(VMEM,) * len(outs),
        scratch_shapes=scratch,
        name="probs",
        **params(0.35),
    )(*operands)


def unit_math(rows, grads, probs_ref, x_ref, inv_ref, turned_ref, gain_ref, scaled_ref, store, value_ref):
    kv_width, model_width = turned_ref.shape
    heads = model_width // kv_width
    chunk = min(512, model_width)
    inv = inv_ref[rows, :1]
    values = []
    for c in range(kv_width // HEAD_FEATURES):
        first = c * heads * HEAD_FEATURES
        grad_stack = jnp.concatenate(
            [
                grad_ref[part, first + h * HEAD_FEATURES : first + (h + 1) * HEAD_FEATURES]
                for grad_ref, part in grads
                for h in range(heads)
            ],
            axis=0,
        )
        values.append(
            jnp.dot(probs_ref[c], grad_stack, preferred_element_type=jnp.float32).astype(
                jnp.bfloat16
            )
        )
    value = jnp.concatenate(values, axis=1)
    value_ref[...] = (value.astype(jnp.float32) * inv).astype(jnp.bfloat16)
    inner = jnp.zeros((UNIT, 1), jnp.float32)
    for first in range(0, model_width, chunk):
        columns = slice(first, first + chunk)
        normed_grad = jnp.dot(value, turned_ref[:, columns], preferred_element_type=jnp.float32)
        scaled = normed_grad * gain_ref[:, columns]
        scaled_ref[:, columns] = scaled
        x = x_ref[rows, columns].astype(jnp.float32)
        inner = inner + jnp.sum(x * scaled, axis=1, keepdims=True)
    pull = inner * (inv * inv / model_width)
    grad_ref, part = grads[-1]
    for first in range(0, model_width, chunk):
        columns = slice(first, first + chunk)
        x = x_ref[rows, columns].astype(jnp.float32)
        change = inv * (scaled_ref[:, columns] - x * pull)
        grad = grad_ref[part, columns].astype(jnp.float32)
        store(columns, (grad + change).astype(jnp.bfloat16))


def turn_kernel(weight_ref, *refs):
    turned_ref = refs[-1]
    step = min(256, weight_ref.shape[0])
    for first in range(0, weight_ref.shape[0], step):
        turned_ref[:, first : first + step] = weight_ref[first : first + step, :].T


def turn(weight, after=()):
    return pl.pallas_call(
        turn_kernel,
        out_shape=jax.ShapeDtypeStruct(weight.shape[::-1], weight.dtype),
        in_specs=[VMEM] + [ANY] * len(after),
        out_specs=VMEM,
        name="turn",
        **params(1.5),
    )(near(weight), *after)


def layer_kernel(
    live_ref, grad_ref, late_ref, early_ref, inv_ref, x_ref, turned_ref, gain_ref, *rest
):
    out_ref, value_ref, scaled_ref = rest[-3:]
    if len(rest) == 5:

        @pl.when(live_ref[0] == 0)
        def _():
            out_ref[...] = rest[0][...]
            value_ref[...] = rest[1][...]

    @pl.when(live_ref[0] == 1)
    def _():
        for rows, parts, probs_ref in ((LATE, [LATE], late_ref), (EARLY, [LATE, EARLY], early_ref)):

            def store(columns, part, rows=rows):
                out_ref[rows, columns] = part

            grads = [(grad_ref, part) for part in parts]
            unit_math(
                rows, grads, probs_ref, x_ref, inv_ref, turned_ref, gain_ref, scaled_ref, store,
                value_ref.at[rows],
            )


def layer_step(live, grad, block, turned, gain, held=()):
    kv_width, model_width = turned.shape
    operands = [live, grad, *block, turned, gain, *held]
    return pl.pallas_call(
        layer_kernel,
        out_shape=(
            jax.ShapeDtypeStruct((BLOCK, model_width), jnp.bfloat16),
            jax.ShapeDtypeStruct((BLOCK, kv_width), jnp.bfloat16),
        ),
        in_specs=[SMEM] + [VMEM] * (len(operands) - 1),
        out_specs=(VMEM, VMEM),
        scratch_shapes=[pltpu.VMEM((UNIT, model_width), jnp.float32)],
        name="layer",
        **params(1.1),
    )(*operands)


def tick_kernel(tick, rows, parts, kept, final, send, *refs):
    grads = list(zip(refs, parts))
    probs_ref, inv_ref, x_ref, turned_ref, gain_ref = refs[len(parts) : len(parts) + 5]
    refs = refs[len(parts) + 5 :]
    earlier, refs = refs[: 2 * kept], refs[2 * kept :]
    kv_width, model_width = turned_ref.shape
    turn = lax.axis_size("section") - 1 - lax.axis_index("section")
    if final:
        late_ref, late_value_ref = refs[:2]
        values_ref, *outs = refs[-8:-3]
        scaled_ref, block_ref, value_ref = refs[-3:]

        def store(columns, part):
            block_ref[EARLY, columns] = part

    else:
        if send:
            up_ref, across_ref, sem = refs[0], refs[-3], refs[-1]
            refs = refs[:-3] + refs[-2:-1]
            first = pl.multiple_of((1 - place()[0]) * BLOCK, BLOCK)
            made = pltpu.make_async_copy(up_ref.at[pl.ds(first, UNIT)], across_ref, sem)
            made.start()
        out_ref, value_ref, scaled_ref = refs[-3:]

        def store(columns, part):
            out_ref[:, columns] = part

    @pl.when(turn == tick)
    def _():
        unit_math(
            rows, grads, probs_ref, x_ref, inv_ref, turned_ref, gain_ref, scaled_ref, store,
            value_ref,
        )

    if send:
        made.wait()
    for at in range(kept):

        @pl.when(turn == at)
        def _(at=at):
            store(slice(None), earlier[2 * at][...])
            value_ref[...] = earlier[2 * at + 1][...]

    if final:
        block_ref[LATE, :] = late_ref[...]
        at = place()[1]
        piece = outs[0].shape[0]
        for k, out_ref in enumerate(outs):
            first = pl.multiple_of(lax.bitwise_xor(at, k) * piece, piece)
            out_ref[:piece, :] = block_ref[pl.ds(first, piece), :]
        values = [value_ref[...], late_value_ref[...]]
        if final == 2:
            values = [refs[2][...]] + values
            groups = model_width // kv_width
            whole = jnp.concatenate(values, axis=0)
            values_ref[...] = whole
            share = 2 * BLOCK // groups
            for g in range(groups):
                outs[2][piece:, g * kv_width : (g + 1) * kv_width] = whole[
                    g * share : (g + 1) * share
                ]
        else:
            values_ref[...] = jnp.concatenate(values, axis=0)


def tick_step(tick, grads, block, turned, gain, kept=(), late=(), after=(), up=None):
    kv_width, model_width = turned.shape
    low = len(grads) == 2
    final = len(late) - 1 if late else 0
    arrays = [grad for grad, _ in grads]
    arrays += [block[1] if low else block[0], block[2], block[3], turned, gain]
    arrays += [array for pair in kept for array in pair]
    arrays += late
    operands = [near(array) for array in arrays]
    specs = [VMEM] * len(operands)
    if up is not None:
        operands.append(pltpu.with_memory_space_constraint(up, pltpu.HBM))
        specs.append(pl.BlockSpec(memory_space=pltpu.HBM))
    specs += [ANY] * len(after)
    bf16 = jnp.bfloat16
    scratch = [pltpu.VMEM((UNIT, model_width), jnp.float32)]
    if final:
        scratch += [pltpu.VMEM((BLOCK, model_width), bf16), pltpu.VMEM((UNIT, kv_width), bf16)]
        half = lax.axis_size("dp") // 2
        piece = BLOCK // half
        heights = [piece] * half
        if final == 2:
            heights[2] += 2 * BLOCK * kv_width // model_width
        outs = (jax.ShapeDtypeStruct((final * BLOCK, kv_width), bf16),)
        outs += tuple(jax.ShapeDtypeStruct((rows, model_width), bf16) for rows in heights)
    else:
        outs = (
            jax.ShapeDtypeStruct((UNIT, model_width), bf16),
            jax.ShapeDtypeStruct((UNIT, kv_width), bf16),
        )
        if up is not None:
            outs += (jax.ShapeDtypeStruct((UNIT, model_width), bf16),)
            scratch.append(pltpu.SemaphoreType.DMA)
    parts = [part for _, part in grads]
    return pl.pallas_call(
        functools.partial(
            tick_kernel, tick, EARLY if low else LATE, parts, len(kept), final, up is not None
        ),
        out_shape=outs,
        in_specs=specs,
        out_specs=(VMEM,) * len(outs),
        scratch_shapes=scratch,
        name="tick",
        **params(0.2),
    )(*operands, *after)


def pack_kernel(block, half, piece, query_ref, key_ref, hidden_ref, up_ref, seg_ref, *rest):
    late_ref, *early, seg_in_ref, sems = rest[-4 + block :]
    packed = rest[-4 + block - half : -4 + block]
    rest = rest[: -4 + block - half]
    side, at, _ = place()
    there = side if block == 0 else 1 - side
    copies = []

    def copy(source, target):
        made = pltpu.make_async_copy(source, target, sems.at[len(copies)])
        made.start()
        copies.append(made)

    copy(seg_ref, seg_in_ref)
    for k in range(half):
        replica = there * half + lax.bitwise_xor(at, k)
        rows = pl.ds(pl.multiple_of(replica * piece, piece), piece)
        first = 0
        for source in (query_ref, key_ref, hidden_ref):
            width = source.shape[1]
            copy(source.at[rows], packed[k].at[:, pl.ds(first, width)])
            first += width
    for first, target in [(UNIT, late_ref)] + [(0, ref) for ref in early]:
        rows = pl.ds(pl.multiple_of(there * BLOCK + first, UNIT), UNIT)
        copy(up_ref.at[rows], target.at[pl.ds(0, UNIT)])
    late_ref[UNIT:, :] = jnp.zeros((16, late_ref.shape[1]), jnp.bfloat16)
    copies[0].wait()
    ids = seg_in_ref[...].astype(jnp.float32)
    late_ref[UNIT:, : ids.shape[1]] = jnp.broadcast_to(ids, (16, ids.shape[1])).astype(
        jnp.bfloat16
    )
    if rest:
        turn_kernel(rest[0], rest[-1])
    for made in copies[1:]:
        made.wait()


def pack(block, half, piece, sources, weight=None):
    model_width = sources[0].shape[1]
    width = sum(source.shape[1] for source in sources[:3])
    bf16 = jnp.bfloat16
    operands = [pltpu.with_memory_space_constraint(array, pltpu.HBM) for array in sources]
    specs = [pl.BlockSpec(memory_space=pltpu.HBM)] * len(sources)
    outs = [jax.ShapeDtypeStruct((piece, width), bf16)] * half
    outs += [
        jax.ShapeDtypeStruct((rows, model_width), bf16) for rows in (UNIT + 16, UNIT)[: 2 - block]
    ]
    if weight is not None:
        operands.append(near(weight))
        specs.append(VMEM)
        outs = [jax.ShapeDtypeStruct(weight.shape[::-1], bf16)] + outs
    return pl.pallas_call(
        functools.partial(pack_kernel, block, half, piece),
        out_shape=tuple(outs),
        in_specs=specs,
        out_specs=(VMEM,) * len(outs),
        scratch_shapes=[
            pltpu.VMEM(sources[-1].shape, jnp.int32),
            pltpu.SemaphoreType.DMA((3 * half + 3 - block,)),
        ],
        name="pack",
        **params(1.2),
    )(*operands)


def columns_kernel(
    width, scale, first_ref, second_ref, weight_ref, gain_ref, after_ref, weight_out_ref,
    gain_out_ref, *outs
):
    me = place()[2]
    for k, out_ref in enumerate(outs):
        start = pl.multiple_of(lax.bitwise_xor(lax.div(me, 2), k) * width, width)
        out_ref[:BLOCK, :] = first_ref[:, pl.ds(start, width)]
        out_ref[BLOCK:, :] = second_ref[:, pl.ds(start, width)]
    shares = weight_out_ref.shape[0]
    first = pl.multiple_of(me * shares, shares)
    weight_out_ref[...] = weight_ref[pl.ds(first, shares), :].astype(jnp.float32) * scale
    gain = gain_ref[:, pl.ds(first, shares)]
    column = jnp.sum(jnp.where(diagonal(shares), gain, 0.0), axis=1, keepdims=True)
    gain_out_ref[...] = jnp.broadcast_to(column * scale, gain_out_ref.shape)


def partial_kernel(count, shares, piece, *refs):
    columns, values = refs[:count], refs[count : 2 * count]
    own_ref, other_ref = refs[-2:]
    kv_width = values[0].shape[1]
    parts = []
    for k, ref in enumerate(values):
        if k == 1:
            parts += [
                ref[piece:, first : first + kv_width] for first in range(0, ref.shape[1], kv_width)
            ]
        else:
            parts.append(ref[...])
    value = jnp.concatenate(parts, axis=0)
    mine = lax.rem(place()[2], 2)
    for ref, core in ((other_ref, 1 - mine), (own_ref, mine)):
        at = pl.ds(pl.multiple_of(core * shares, shares), shares)
        rows = jnp.concatenate([part[:, at] for part in columns], axis=0)
        ref[...] = lax.dot_general(
            rows, value, (((0,), (0,)), ((), ())), preferred_element_type=jnp.float32
        ).astype(ref.dtype)


def rows_kernel(half, *refs):
    pieces = refs[: 2 * half]
    rows_ref, sems = refs[-2:]
    side, at, _ = place()
    piece = pieces[0].shape[0]
    copies = []
    for block in range(2):
        for k in range(half):
            replica = (side if block == 0 else 1 - side) * half + lax.bitwise_xor(at, k)
            rows = pl.ds(pl.multiple_of(replica * piece, piece), piece)
            source = pieces[block * half + k].at[pl.ds(0, piece)]
            made = pltpu.make_async_copy(source, rows_ref.at[rows], sems.at[block * half + k])
            made.start()
            copies.append(made)
    for made in copies:
        made.wait()


def diagonal(size):
    return lax.broadcasted_iota(jnp.int32, (size, size), 0) == lax.broadcasted_iota(
        jnp.int32, (size, size), 1
    )


def finish_kernel(own_ref, other_ref, weight_ref, gain_ref, rows_ref, out_ref, gain_out_ref):
    total = own_ref[...] + other_ref[...].astype(jnp.float32)
    out_ref[...] = total * gain_ref[:, :1]
    sums = jnp.sum(total * weight_ref[...], axis=1, keepdims=True)
    gain_out_ref[...] = jnp.sum(
        jnp.where(diagonal(total.shape[0]), sums, 0.0), axis=0, keepdims=True
    )


def direct(hidden, query, key, segments, weight, norm_gain, upstream):
    tokens, model_width = hidden.shape
    kv_width = key.shape[1]
    replicas = lax.axis_size("dp")
    layers = lax.axis_size("section")
    half = replicas // 2
    piece = tokens // replicas
    shares = model_width // replicas

    def swap(array, k):
        return lax.ppermute(array, "dp", [(i, i ^ k) for i in range(replicas)])

    count = 2 * half
    bf16 = jnp.bfloat16
    sources = (query, key, hidden, upstream, segments)
    pieces, ups = [], []
    for b in range(2):
        if b:
            turned, *packed, late = pack(b, half, piece, sources, weight)
        else:
            *packed, late, early = pack(b, half, piece, sources)
        pieces.append([packed[0]] + [swap(packed[k], k) for k in range(1, half)])
        ups.append([swap(late, half)] if b else [late, early])
    whole = slice(0, UNIT)
    scale = float(tokens * replicas) ** (-0.5)
    blocks, kept, after = [], [], []
    for b in range(2):
        block = block_probs(pieces[b], ups[b][0], UNIT, model_width, kv_width, after)
        late, early = [(part, whole) for part in ups[b]]
        first = tick_step(0, [late], block, turned, norm_gain)
        up = None if b else upstream
        second = tick_step(0, [late, early], block, turned, norm_gain, after=[first[0]], up=up)
        if b == 0:
            *second, rows = second
            ups[1].append(swap(rows, half))
        blocks.append(block)
        kept += [[first], [second]]
        after = [second[0]]

    for tick in range(1, layers):
        hop = [(layers - tick, layers - 1 - tick)]
        grads = [(lax.ppermute(unit[-1][0], "section", hop), whole) for unit in kept]
        last = tick == layers - 1
        after, done = [], []
        if last:
            own_weight, own_gain, *columns = pl.pallas_call(
                functools.partial(columns_kernel, 2 * shares, scale),
                out_shape=(
                    jax.ShapeDtypeStruct((shares, kv_width), jnp.float32),
                    jax.ShapeDtypeStruct((shares, 128), jnp.float32),
                )
                + (jax.ShapeDtypeStruct((2 * BLOCK, 2 * shares), bf16),) * half,
                in_specs=[VMEM] * 4 + [ANY],
                out_specs=(VMEM,) * (2 + half),
                name="columns",
                **params(0.4),
            )(blocks[0][3], blocks[1][3], near(weight), norm_gain, kept[3][-1][0])
            columns = [columns[0]] + [swap(columns[k], 2 * k) for k in range(1, half)]
        for u in range(4):
            needs = grads[u - 1 : u + 1] if u % 2 else grads[u : u + 1]
            late = []
            if last and u % 2:
                late = list(done[u - 1]) + ([done[1][0]] if u == 3 else [])
            if last and u == 1:
                after = after + columns[1:]
            if last and u == 3:
                rows = [done[1][1]] + [swap(done[1][1 + k], k) for k in range(1, half)]
                after = after + rows[1:]
            done.append(
                tick_step(
                    tick, needs, blocks[u // 2], turned, norm_gain, kept[u] if last else (), late,
                    after,
                )
            )
            after = [done[u][0]]
            kept[u].append(done[u])
    values, *last_rows = done[3]
    last_rows = [last_rows[0]] + [swap(last_rows[k], k) for k in range(1, half)]
    gathered = [values, last_rows[2]] + [swap(values, 2 * k) for k in range(2, half)]
    own, other = pl.pallas_call(
        functools.partial(partial_kernel, half, shares, piece),
        out_shape=(
            jax.ShapeDtypeStruct((shares, kv_width), jnp.float32),
            jax.ShapeDtypeStruct((shares, kv_width), bf16),
        ),
        in_specs=[VMEM] * (2 * half) + [ANY] * 2,
        out_specs=(VMEM, VMEM),
        name="weight_partial",
        **params(0.5),
    )(*columns, *gathered, last_rows[1], last_rows[3])
    other = swap(other, 1)
    input_grad = pl.pallas_call(
        functools.partial(rows_kernel, half),
        out_shape=jax.ShapeDtypeStruct((tokens, model_width), bf16),
        in_specs=[VMEM] * count + [ANY],
        out_specs=ANY,
        scratch_shapes=[pltpu.SemaphoreType.DMA((count,))],
        name="rows",
        **params(1.2),
    )(*rows, *last_rows, own)
    weight_grad, gain_grad = pl.pallas_call(
        finish_kernel,
        out_shape=(
            jax.ShapeDtypeStruct((shares, kv_width), jnp.float32),
            jax.ShapeDtypeStruct((1, shares), jnp.float32),
        ),
        in_specs=[VMEM] * 4 + [ANY],
        out_specs=(VMEM, VMEM),
        name="finish",
        **params(1.0),
    )(own, other, own_weight, own_gain, input_grad)
    return input_grad[None], weight_grad[None], gain_grad


def weight_kernel(scale, columns_ref, value_ref, weight_ref, gain_ref, out_ref, gain_out_ref):
    total = lax.dot_general(
        columns_ref[...], value_ref[...], (((0,), (0,)), ((), ())),
        preferred_element_type=jnp.float32,
    ) * scale
    out_ref[...] = total * gain_ref[...]
    product = total * weight_ref[...].astype(jnp.float32)
    sums = lax.dot_general(
        jnp.ones((8, product.shape[1]), jnp.float32), product, (((1,), (1,)), ((), ())),
        preferred_element_type=jnp.float32, precision=lax.Precision.HIGHEST,
    )
    gain_out_ref[...] = sums[:1]


def grouped(hidden, query, key, segments, weight, norm_gain, upstream):
    tokens, model_width = hidden.shape
    kv_width = key.shape[1]
    replicas = lax.axis_size("dp")
    layers = lax.axis_size("section")
    half = replicas // 2
    me = lax.axis_index("dp")
    section = lax.axis_index("section")
    side = me // half
    groups = [list(range(half)), list(range(half, replicas))]
    across = [(i, (i + half) % replicas) for i in range(replicas)]
    shares = model_width // replicas

    def rows_of(array, which, axis=0):
        at = side if which == 0 else 1 - side
        return lax.dynamic_slice_in_dim(array, at * BLOCK, BLOCK, axis)

    def regroup(array):
        return lax.all_to_all(
            array, "dp", split_axis=0, concat_axis=0, axis_index_groups=groups, tiled=True
        )

    def spread(array):
        return lax.all_to_all(array, "dp", split_axis=0, concat_axis=0, tiled=True)

    turned = turn(weight)
    blocks, grads = [], []
    for which in range(2):
        up = rows_of(upstream, which)
        seg = jnp.broadcast_to(segments, (16, 2 * BLOCK)).astype(jnp.bfloat16)
        if which == 1:
            up = lax.ppermute(up, "dp", across)
            seg = lax.ppermute(seg, "dp", across)
        packed = jnp.concatenate(
            [rows_of(query, which), rows_of(key, which), rows_of(hidden, which)], axis=1
        )
        blocks.append(block_probs([regroup(packed)], seg, 0, model_width, kv_width))
        grads.append(up)

    def layer(tick, which, grad, kept):
        live = (section == layers - 1 - tick).astype(jnp.int32)[None]
        return layer_step(live, grad, blocks[which], turned, norm_gain, kept)

    held = [layer(0, which, grads[which], ()) for which in range(2)]
    hops = [(i, i - 1) for i in range(1, layers)]

    def step(tick, held):
        grads = [lax.ppermute(kept[0], "section", hops) for kept in held]
        return [layer(tick, which, grads[which], held[which]) for which in range(2)]

    held = lax.fori_loop(1, layers, step, held)

    columns, values, stored = [], [], []
    for which in range(2):
        block = blocks[which][3].reshape(BLOCK, replicas, shares).transpose(1, 0, 2)
        columns.append(spread(block.reshape(replicas * BLOCK, shares)))
        out, value = held[which]
        stored.append(regroup(out))
        values.append(spread(jnp.tile(value, (replicas, 1))))
    ordered = jnp.where(
        side == 0, jnp.concatenate(stored, axis=0), jnp.concatenate(stored[::-1], axis=0)
    )
    own_weight = lax.dynamic_slice_in_dim(weight, me * shares, shares, 0)
    own_gain = lax.dynamic_slice_in_dim(norm_gain[0], me * shares, shares, 0)
    scale = float(tokens * replicas) ** (-0.5)
    weight_grad, gain_grad = pl.pallas_call(
        functools.partial(weight_kernel, scale),
        out_shape=(
            jax.ShapeDtypeStruct((shares, kv_width), jnp.float32),
            jax.ShapeDtypeStruct((1, shares), jnp.float32),
        ),
        in_specs=[VMEM] * 4,
        out_specs=(VMEM, VMEM),
        name="weight_grad",
    )(
        jnp.concatenate(columns, axis=0),
        jnp.concatenate(values, axis=0),
        own_weight,
        own_gain[:, None],
    )
    return ordered[None], weight_grad[None], gain_grad


def on_device(hidden_in, queries, keys, segments, value_weight, norm_gain, upstream):
    replicas = lax.axis_size("dp")
    piece = hidden_in.shape[1] // replicas
    plan = direct if piece % 16 == 0 and replicas == 8 else grouped
    return plan(
        hidden_in[0], queries[0], keys[0], segments, value_weight[0], norm_gain, upstream
    )


def solution(mesh):
    in_specs = (
        P("section", "dp", None),
        P("section", "dp", None),
        P("section", "dp", None),
        P("dp", None),
        P("section", None, None),
        P("section", None),
        P("dp", None),
    )
    out_specs = (P("section", "dp", None), P("section", "dp", None), P("section", "dp"))
    return jax.shard_map(
        on_device, mesh=mesh, in_specs=in_specs, out_specs=out_specs, check_vma=False
    )
```

```python
import functools

import jax
import jax.numpy as jnp
from jax import lax
from jax.experimental import pallas as pl
from jax.experimental.pallas import tpu as pltpu
from jax.sharding import PartitionSpec as P

HEAD_FEATURES = 128
BLOCK = 64
UNIT = 32
EPSILON = 1e-06
MASKED = -1e30
UNITS = ("a_late", "a_early", "b_late", "b_early")
VMEM = pl.BlockSpec(memory_space=pltpu.VMEM)
SMEM = pl.BlockSpec(memory_space=pltpu.SMEM)


ANY = pl.BlockSpec(memory_space=pl.ANY)


LATE, EARLY = slice(UNIT, BLOCK), slice(0, UNIT)


def params(microseconds):
    flops = int(microseconds * 1.15e9)
    return dict(
        compiler_params=pltpu.CompilerParams(vmem_limit_bytes=16 << 20),
        cost_estimate=pl.CostEstimate(flops=flops, bytes_accessed=0, transcendentals=0),
    )


def near(array):
    return pltpu.with_memory_space_constraint(array, pltpu.VMEM)


def place():
    half = lax.axis_size("dp") // 2
    me = lax.axis_index("dp")
    return lax.div(me, half), lax.rem(me, half), me


def probs_kernel(count, seg_row, model_width, kv_width, *refs):
    pieces, seg_ref = refs[:count], refs[count]
    late_ref, early_ref, inv_ref, x_ref, rows_ref = refs[-5:]
    heads = model_width // kv_width
    rows = BLOCK // count
    side, at, _ = place()
    for k, piece in enumerate(pieces):
        if count == 1:
            rows_ref[...] = piece[...]
        else:
            first = pl.multiple_of(lax.bitwise_xor(at, k) * rows, rows)
            rows_ref[pl.ds(first, rows), :] = piece[...]

    def iota(shape, axis):
        return lax.broadcasted_iota(jnp.int32, shape, axis)

    seg = seg_ref[seg_row : seg_row + 16, : 2 * BLOCK].astype(jnp.float32)[:1]
    shape = (BLOCK, 2 * BLOCK)
    wanted = iota(shape, 1) == side * BLOCK + iota(shape, 0)
    ids = jnp.sum(jnp.where(wanted, seg, 0.0), axis=1, keepdims=True)
    key_code = ids * BLOCK + iota((BLOCK, 1), 0).astype(jnp.float32)
    list_start = ids * BLOCK
    shape = (BLOCK, heads * BLOCK)
    column = iota(shape, 1)
    query_at = lax.rem(column, UNIT) + jnp.where(column < heads * UNIT, UNIT, 0)
    same = iota(shape, 0) == query_at
    query_code = jnp.sum(jnp.where(same, key_code, 0.0), axis=0, keepdims=True)
    query_start = jnp.sum(jnp.where(same, list_start, 0.0), axis=0, keepdims=True)
    allowed = (key_code <= query_code) & (key_code >= query_start)
    for c in range(kv_width // HEAD_FEATURES):
        first = c * heads * HEAD_FEATURES
        query_stack = jnp.concatenate(
            [
                rows_ref[part, first + h * HEAD_FEATURES : first + (h + 1) * HEAD_FEATURES]
                for part in (LATE, EARLY)
                for h in range(heads)
            ],
            axis=0,
        )
        key_first = model_width + c * HEAD_FEATURES
        keys = rows_ref[:, key_first : key_first + HEAD_FEATURES]
        scores = lax.dot_general(
            keys, query_stack, (((1,), (1,)), ((), ())), preferred_element_type=jnp.float32
        ) * HEAD_FEATURES ** (-0.5)
        scores = jnp.where(allowed, scores, MASKED)
        exp_scores = jnp.exp(scores - jnp.max(scores, axis=0, keepdims=True))
        total = jnp.sum(exp_scores, axis=0, keepdims=True)
        probs = (exp_scores / total).astype(jnp.bfloat16)
        late_ref[c] = probs[LATE, : heads * UNIT]
        early_ref[c] = probs[EARLY]
    hidden = rows_ref[:, model_width + kv_width :]
    x_ref[...] = hidden
    x = hidden.astype(jnp.float32)
    mean_square = jnp.mean(x * x, axis=1, keepdims=True)
    inv_ref[...] = jnp.broadcast_to(lax.rsqrt(mean_square + EPSILON), inv_ref.shape)


def block_probs(pieces, seg, seg_row, model_width, kv_width, after=()):
    heads = model_width // kv_width
    key_heads = kv_width // HEAD_FEATURES
    operands = [near(piece) for piece in pieces] + [near(seg)]
    specs = [VMEM] * len(operands) + [ANY] * len(after)
    operands += after
    return pl.pallas_call(
        functools.partial(probs_kernel, len(pieces), seg_row, model_width, kv_width),
        out_shape=(
            jax.ShapeDtypeStruct((key_heads, UNIT, heads * UNIT), jnp.bfloat16),
            jax.ShapeDtypeStruct((key_heads, UNIT, heads * BLOCK), jnp.bfloat16),
            jax.ShapeDtypeStruct((BLOCK, 128), jnp.float32),
            jax.ShapeDtypeStruct((BLOCK, model_width), jnp.bfloat16),
        ),
        in_specs=specs,
        out_specs=(VMEM,) * 4,
        scratch_shapes=[pltpu.VMEM((BLOCK, 2 * model_width + kv_width), jnp.bfloat16)],
        name="probs",
        **params(0.35 if after else 2.0),
    )(*operands)


def unit_math(rows, grads, probs_ref, x_ref, inv_ref, turned_ref, gain_ref, scaled_ref, store, value_ref):
    kv_width, model_width = turned_ref.shape
    heads = model_width // kv_width
    chunk = min(512, model_width)
    inv = inv_ref[rows, :1]
    values = []
    for c in range(kv_width // HEAD_FEATURES):
        first = c * heads * HEAD_FEATURES
        grad_stack = jnp.concatenate(
            [
                grad_ref[part, first + h * HEAD_FEATURES : first + (h + 1) * HEAD_FEATURES]
                for grad_ref, part in grads
                for h in range(heads)
            ],
            axis=0,
        )
        values.append(
            jnp.dot(probs_ref[c], grad_stack, preferred_element_type=jnp.float32).astype(
                jnp.bfloat16
            )
        )
    value = jnp.concatenate(values, axis=1)
    value_ref[...] = (value.astype(jnp.float32) * inv).astype(jnp.bfloat16)
    inner = jnp.zeros((UNIT, 1), jnp.float32)
    for first in range(0, model_width, chunk):
        columns = slice(first, first + chunk)
        normed_grad = jnp.dot(value, turned_ref[:, columns], preferred_element_type=jnp.float32)
        scaled = normed_grad * gain_ref[:, columns]
        scaled_ref[:, columns] = scaled
        x = x_ref[rows, columns].astype(jnp.float32)
        inner = inner + jnp.sum(x * scaled, axis=1, keepdims=True)
    pull = inner * (inv * inv / model_width)
    grad_ref, part = grads[-1]
    for first in range(0, model_width, chunk):
        columns = slice(first, first + chunk)
        x = x_ref[rows, columns].astype(jnp.float32)
        change = inv * (scaled_ref[:, columns] - x * pull)
        grad = grad_ref[part, columns].astype(jnp.float32)
        store(columns, (grad + change).astype(jnp.bfloat16))


def turn_kernel(weight_ref, *refs):
    turned_ref = refs[-1]
    step = min(256, weight_ref.shape[0])
    for first in range(0, weight_ref.shape[0], step):
        turned_ref[:, first : first + step] = weight_ref[first : first + step, :].T


def turn(weight, after=()):
    return pl.pallas_call(
        turn_kernel,
        out_shape=jax.ShapeDtypeStruct(weight.shape[::-1], weight.dtype),
        in_specs=[VMEM] + [ANY] * len(after),
        out_specs=VMEM,
        name="turn",
        **params(1.5),
    )(near(weight), *after)


def layer_kernel(
    live_ref, grad_ref, late_ref, early_ref, inv_ref, x_ref, turned_ref, gain_ref, *rest
):
    out_ref, value_ref, scaled_ref = rest[-3:]
    if len(rest) == 5:

        @pl.when(live_ref[0] == 0)
        def _():
            out_ref[...] = rest[0][...]
            value_ref[...] = rest[1][...]

    @pl.when(live_ref[0] == 1)
    def _():
        for rows, parts, probs_ref in ((LATE, [LATE], late_ref), (EARLY, [LATE, EARLY], early_ref)):

            def store(columns, part, rows=rows):
                out_ref[rows, columns] = part

            grads = [(grad_ref, part) for part in parts]
            unit_math(
                rows, grads, probs_ref, x_ref, inv_ref, turned_ref, gain_ref, scaled_ref, store,
                value_ref.at[rows],
            )


def layer_step(live, grad, block, turned, gain, held=()):
    kv_width, model_width = turned.shape
    operands = [live, grad, *block, turned, gain, *held]
    return pl.pallas_call(
        layer_kernel,
        out_shape=(
            jax.ShapeDtypeStruct((BLOCK, model_width), jnp.bfloat16),
            jax.ShapeDtypeStruct((BLOCK, kv_width), jnp.bfloat16),
        ),
        in_specs=[SMEM] + [VMEM] * (len(operands) - 1),
        out_specs=(VMEM, VMEM),
        scratch_shapes=[pltpu.VMEM((UNIT, model_width), jnp.float32)],
        name="layer",
        **params(1.1),
    )(*operands)


def tick_kernel(tick, rows, parts, kept, final, *refs):
    grads = list(zip(refs, parts))
    probs_ref, inv_ref, x_ref, turned_ref, gain_ref = refs[len(parts) : len(parts) + 5]
    refs = refs[len(parts) + 5 :]
    earlier, refs = refs[: 2 * kept], refs[2 * kept :]
    kv_width, model_width = turned_ref.shape
    turn = lax.axis_size("section") - 1 - lax.axis_index("section")
    if final:
        late_ref, late_value_ref = refs[:2]
        values_ref, *outs = refs[-8:-3]
        scaled_ref, block_ref, value_ref = refs[-3:]

        def store(columns, part):
            block_ref[EARLY, columns] = part

    else:
        out_ref, value_ref, scaled_ref = refs[-3:]

        def store(columns, part):
            out_ref[:, columns] = part

    @pl.when(turn == tick)
    def _():
        unit_math(
            rows, grads, probs_ref, x_ref, inv_ref, turned_ref, gain_ref, scaled_ref, store,
            value_ref,
        )

    for at in range(kept):

        @pl.when(turn == at)
        def _(at=at):
            store(slice(None), earlier[2 * at][...])
            value_ref[...] = earlier[2 * at + 1][...]

    if final:
        block_ref[LATE, :] = late_ref[...]
        at = place()[1]
        piece = outs[0].shape[0]
        for k, out_ref in enumerate(outs):
            first = pl.multiple_of(lax.bitwise_xor(at, k) * piece, piece)
            out_ref[:piece, :] = block_ref[pl.ds(first, piece), :]
        values = [value_ref[...], late_value_ref[...]]
        if final == 2:
            values = [refs[2][...]] + values
            groups = model_width // kv_width
            whole = jnp.concatenate(values, axis=0)
            values_ref[...] = whole
            share = 2 * BLOCK // groups
            for g in range(groups):
                outs[2][piece:, g * kv_width : (g + 1) * kv_width] = whole[
                    g * share : (g + 1) * share
                ]
        else:
            values_ref[...] = jnp.concatenate(values, axis=0)


def tick_step(tick, grads, block, turned, gain, kept=(), late=(), after=(), name=""):
    kv_width, model_width = turned.shape
    low = len(grads) == 2
    final = len(late) - 1 if late else 0
    arrays = [grad for grad, _ in grads]
    arrays += [block[1] if low else block[0], block[2], block[3], turned, gain]
    arrays += [array for pair in kept for array in pair]
    arrays += late
    operands = [near(array) for array in arrays]
    specs = [VMEM] * len(operands) + [ANY] * len(after)
    bf16 = jnp.bfloat16
    scratch = [pltpu.VMEM((UNIT, model_width), jnp.float32)]
    if final:
        scratch += [pltpu.VMEM((BLOCK, model_width), bf16), pltpu.VMEM((UNIT, kv_width), bf16)]
        half = lax.axis_size("dp") // 2
        piece = BLOCK // half
        heights = [piece] * half
        if final == 2:
            heights[2] += 2 * BLOCK * kv_width // model_width
        outs = (jax.ShapeDtypeStruct((final * BLOCK, kv_width), bf16),)
        outs += tuple(jax.ShapeDtypeStruct((rows, model_width), bf16) for rows in heights)
    else:
        outs = (
            jax.ShapeDtypeStruct((UNIT, model_width), bf16),
            jax.ShapeDtypeStruct((UNIT, kv_width), bf16),
        )
    return pl.pallas_call(
        functools.partial(
            tick_kernel, tick, EARLY if low else LATE, [part for _, part in grads], len(kept), final
        ),
        out_shape=outs,
        in_specs=specs,
        out_specs=(VMEM,) * len(outs),
        scratch_shapes=scratch,
        name=f"tick{tick}_{name}",
        **params(0.0),
    )(*operands, *after)


def pack_kernel(block, half, piece, query_ref, key_ref, hidden_ref, up_ref, seg_ref, *rest):
    up_out_ref, seg_in_ref, sems = rest[-3:]
    packed = rest[-3 - half : -3]
    rest = rest[: -3 - half]
    side, at, _ = place()
    there = side if block == 0 else 1 - side
    copies = []

    def copy(source, target):
        made = pltpu.make_async_copy(source, target, sems.at[len(copies)])
        made.start()
        copies.append(made)

    copy(seg_ref, seg_in_ref)
    for k in range(half):
        replica = there * half + lax.bitwise_xor(at, k)
        rows = pl.ds(pl.multiple_of(replica * piece, piece), piece)
        first = 0
        for source in (query_ref, key_ref, hidden_ref):
            width = source.shape[1]
            copy(source.at[rows], packed[k].at[:, pl.ds(first, width)])
            first += width
    rows = pl.ds(pl.multiple_of(there * BLOCK, BLOCK), BLOCK)
    copy(up_ref.at[rows], up_out_ref.at[pl.ds(0, BLOCK)])
    up_out_ref[BLOCK:, :] = jnp.zeros((16, up_out_ref.shape[1]), jnp.bfloat16)
    copies[0].wait()
    ids = seg_in_ref[...].astype(jnp.float32)
    up_out_ref[BLOCK:, : ids.shape[1]] = jnp.broadcast_to(ids, (16, ids.shape[1])).astype(
        jnp.bfloat16
    )
    if block == 1:
        turn_kernel(rest[0], rest[-1])
    for made in copies[1:]:
        made.wait()


def pack(block, half, piece, sources, weight=None):
    model_width = sources[0].shape[1]
    width = sum(source.shape[1] for source in sources[:3])
    bf16 = jnp.bfloat16
    operands = [pltpu.with_memory_space_constraint(array, pltpu.HBM) for array in sources]
    specs = [pl.BlockSpec(memory_space=pltpu.HBM)] * len(sources)
    outs = [jax.ShapeDtypeStruct((piece, width), bf16)] * half
    outs.append(jax.ShapeDtypeStruct((BLOCK + 16, model_width), bf16))
    if weight is not None:
        operands.append(near(weight))
        specs.append(VMEM)
        outs = [jax.ShapeDtypeStruct(weight.shape[::-1], bf16)] + outs
    return pl.pallas_call(
        functools.partial(pack_kernel, block, half, piece),
        out_shape=tuple(outs),
        in_specs=specs,
        out_specs=(VMEM,) * len(outs),
        scratch_shapes=[
            pltpu.VMEM(sources[-1].shape, jnp.int32),
            pltpu.SemaphoreType.DMA((3 * half + 2,)),
        ],
        name="pack",
        **params(1.2),
    )(*operands)


def columns_kernel(
    width, scale, first_ref, second_ref, weight_ref, gain_ref, after_ref, weight_out_ref,
    gain_out_ref, out_ref
):
    me = place()[2]
    for block, block_ref in enumerate((first_ref, second_ref)):
        for pair in range(out_ref.shape[0] // (2 * BLOCK)):
            row = (2 * pair + block) * BLOCK
            out_ref[row : row + BLOCK, :] = block_ref[:, pair * width : (pair + 1) * width]
    shares = weight_out_ref.shape[0]
    first = pl.multiple_of(me * shares, shares)
    weight_out_ref[...] = weight_ref[pl.ds(first, shares), :].astype(jnp.float32) * scale
    gain = gain_ref[:, pl.ds(first, shares)]
    column = jnp.sum(jnp.where(diagonal(shares), gain, 0.0), axis=1, keepdims=True)
    gain_out_ref[...] = jnp.broadcast_to(column * scale, gain_out_ref.shape)


def partial_kernel(count, shares, piece, *refs):
    columns_ref, values = refs[0], refs[1 : 1 + count]
    own_ref, other_ref = refs[-2:]
    kv_width = values[0].shape[1]
    parts = []
    for k, ref in enumerate(values):
        if k == 1:
            parts += [
                ref[piece:, first : first + kv_width] for first in range(0, ref.shape[1], kv_width)
            ]
        else:
            parts.append(ref[...])
    value = jnp.concatenate(parts, axis=0)
    me = place()[2]
    pair, mine = lax.div(me, 2), lax.rem(me, 2)
    tokens = 2 * BLOCK
    for ref, core in ((other_ref, 1 - mine), (own_ref, mine)):
        at = pl.ds(pl.multiple_of(core * shares, shares), shares)
        rows = jnp.concatenate(
            [
                columns_ref[
                    pl.ds(pl.multiple_of(lax.bitwise_xor(pair, k) * tokens, tokens), tokens), at
                ]
                for k in range(count)
            ],
            axis=0,
        )
        ref[...] = lax.dot_general(
            rows, value, (((0,), (0,)), ((), ())), preferred_element_type=jnp.float32
        ).astype(ref.dtype)


def rows_kernel(half, *refs):
    pieces = refs[: 2 * half]
    rows_ref, token_ref, sems = refs[-3:]
    token_ref[...] = jnp.zeros_like(token_ref)
    side, at, _ = place()
    piece = pieces[0].shape[0]
    copies = []
    for block in range(2):
        for k in range(half):
            replica = (side if block == 0 else 1 - side) * half + lax.bitwise_xor(at, k)
            rows = pl.ds(pl.multiple_of(replica * piece, piece), piece)
            source = pieces[block * half + k].at[pl.ds(0, piece)]
            made = pltpu.make_async_copy(source, rows_ref.at[rows], sems.at[block * half + k])
            made.start()
            copies.append(made)
    for made in copies:
        made.wait()


def diagonal(size):
    return lax.broadcasted_iota(jnp.int32, (size, size), 0) == lax.broadcasted_iota(
        jnp.int32, (size, size), 1
    )


def finish_kernel(own_ref, other_ref, weight_ref, gain_ref, after_ref, out_ref, gain_out_ref):
    total = own_ref[...] + other_ref[...].astype(jnp.float32)
    out_ref[...] = total * gain_ref[:, :1]
    sums = jnp.sum(total * weight_ref[...], axis=1, keepdims=True)
    gain_out_ref[...] = jnp.sum(
        jnp.where(diagonal(total.shape[0]), sums, 0.0), axis=0, keepdims=True
    )


def direct(hidden, query, key, segments, weight, norm_gain, upstream):
    tokens, model_width = hidden.shape
    kv_width = key.shape[1]
    replicas = lax.axis_size("dp")
    layers = lax.axis_size("section")
    half = replicas // 2
    piece = tokens // replicas
    shares = model_width // replicas

    def swap(array, k):
        return lax.ppermute(array, "dp", [(i, i ^ k) for i in range(replicas)])

    count = 2 * half
    bf16 = jnp.bfloat16
    sources = (query, key, hidden, upstream, segments)
    pieces, ups = [], []
    for b in range(2):
        *packed, up = pack(b, half, piece, sources, weight if b else None)
        if b:
            turned, *packed = packed
        pieces.append([packed[0]] + [swap(packed[k], k) for k in range(1, half)])
        ups.append(swap(up, half) if b else up)
    whole = slice(0, UNIT)
    scale = float(tokens * replicas) ** (-0.5)
    blocks, kept, after = [], [], []
    for b in range(2):
        block = block_probs(pieces[b], ups[b], BLOCK, model_width, kv_width, after)
        late, early = (ups[b], LATE), (ups[b], EARLY)
        first = tick_step(0, [late], block, turned, norm_gain, name=UNITS[2 * b])
        second = tick_step(
            0, [late, early], block, turned, norm_gain, after=[first[0]], name=UNITS[2 * b + 1]
        )
        blocks.append(block)
        kept += [[first], [second]]
        after = [second[0]]

    for tick in range(1, layers):
        hop = [(layers - tick, layers - 1 - tick)]
        grads = [(lax.ppermute(unit[-1][0], "section", hop), whole) for unit in kept]
        last = tick == layers - 1
        after, done = [kept[3][-1][0]], []
        if last:
            own_weight, own_gain, columns = pl.pallas_call(
                functools.partial(columns_kernel, 2 * shares, scale),
                out_shape=(
                    jax.ShapeDtypeStruct((shares, kv_width), jnp.float32),
                    jax.ShapeDtypeStruct((shares, 128), jnp.float32),
                )
                + (jax.ShapeDtypeStruct((half * 2 * BLOCK, 2 * shares), bf16),),
                in_specs=[VMEM] * 4 + [ANY],
                out_specs=(VMEM,) * 3,
                name="columns",
                **params(0.4),
            )(blocks[0][3], blocks[1][3], near(weight), norm_gain, kept[3][-1][0])
            parities = [list(range(parity, replicas, 2)) for parity in range(2)]
            columns = lax.all_to_all(
                columns, "dp", split_axis=0, concat_axis=0, axis_index_groups=parities, tiled=True
            )
        for u in range(4):
            needs = grads[u - 1 : u + 1] if u % 2 else grads[u : u + 1]
            late = []
            if last and u % 2:
                late = list(done[u - 1]) + ([done[1][0]] if u == 3 else [])
            if last and u == 0:
                after = after + [columns]
            if last and u == 3:
                rows = [done[1][1]] + [swap(done[1][1 + k], k) for k in range(1, half)]
                after = after + rows[1:]
            done.append(
                tick_step(
                    tick, needs, blocks[u // 2], turned, norm_gain, kept[u] if last else (), late,
                    after, name=UNITS[u],
                )
            )
            after = [done[u][0]]
            kept[u].append(done[u])
    values, *last_rows = done[3]
    last_rows = [last_rows[0]] + [swap(last_rows[k], k) for k in range(1, half)]
    gathered = [values, last_rows[2]] + [swap(values, 2 * k) for k in range(2, half)]
    own, other = pl.pallas_call(
        functools.partial(partial_kernel, half, shares, piece),
        out_shape=(
            jax.ShapeDtypeStruct((shares, kv_width), jnp.float32),
            jax.ShapeDtypeStruct((shares, kv_width), bf16),
        ),
        in_specs=[VMEM] * (1 + half) + [ANY] * 2,
        out_specs=(VMEM, VMEM),
        name="weight_partial",
        **params(0.5),
    )(columns, *gathered, last_rows[1], last_rows[3])
    other = swap(other, 1)
    input_grad, token = pl.pallas_call(
        functools.partial(rows_kernel, half),
        out_shape=(
            jax.ShapeDtypeStruct((tokens, model_width), bf16),
            jax.ShapeDtypeStruct((8, 128), jnp.float32),
        ),
        in_specs=[VMEM] * count + [ANY],
        out_specs=(ANY, VMEM),
        scratch_shapes=[pltpu.SemaphoreType.DMA((count,))],
        name="rows",
        **params(1.2),
    )(*rows, *last_rows, own)
    weight_grad, gain_grad = pl.pallas_call(
        finish_kernel,
        out_shape=(
            jax.ShapeDtypeStruct((shares, kv_width), jnp.float32),
            jax.ShapeDtypeStruct((1, shares), jnp.float32),
        ),
        in_specs=[VMEM] * 4 + [ANY],
        out_specs=(VMEM, VMEM),
        name="finish",
        **params(1.0),
    )(own, other, own_weight, own_gain, token)
    return input_grad[None], weight_grad[None], gain_grad


def weight_kernel(scale, columns_ref, value_ref, weight_ref, gain_ref, out_ref, gain_out_ref):
    total = lax.dot_general(
        columns_ref[...], value_ref[...], (((0,), (0,)), ((), ())),
        preferred_element_type=jnp.float32,
    ) * scale
    out_ref[...] = total * gain_ref[...]
    product = total * weight_ref[...].astype(jnp.float32)
    sums = lax.dot_general(
        jnp.ones((8, product.shape[1]), jnp.float32), product, (((1,), (1,)), ((), ())),
        preferred_element_type=jnp.float32, precision=lax.Precision.HIGHEST,
    )
    gain_out_ref[...] = sums[:1]


def grouped(hidden, query, key, segments, weight, norm_gain, upstream):
    tokens, model_width = hidden.shape
    kv_width = key.shape[1]
    replicas = lax.axis_size("dp")
    layers = lax.axis_size("section")
    half = replicas // 2
    me = lax.axis_index("dp")
    section = lax.axis_index("section")
    side = me // half
    groups = [list(range(half)), list(range(half, replicas))]
    across = [(i, (i + half) % replicas) for i in range(replicas)]
    shares = model_width // replicas

    def rows_of(array, which, axis=0):
        at = side if which == 0 else 1 - side
        return lax.dynamic_slice_in_dim(array, at * BLOCK, BLOCK, axis)

    def regroup(array):
        return lax.all_to_all(
            array, "dp", split_axis=0, concat_axis=0, axis_index_groups=groups, tiled=True
        )

    def spread(array):
        return lax.all_to_all(array, "dp", split_axis=0, concat_axis=0, tiled=True)

    turned = turn(weight)
    blocks, grads = [], []
    for which in range(2):
        up = rows_of(upstream, which)
        seg = jnp.broadcast_to(segments, (16, 2 * BLOCK)).astype(jnp.bfloat16)
        if which == 1:
            up = lax.ppermute(up, "dp", across)
            seg = lax.ppermute(seg, "dp", across)
        packed = jnp.concatenate(
            [rows_of(query, which), rows_of(key, which), rows_of(hidden, which)], axis=1
        )
        blocks.append(block_probs([regroup(packed)], seg, 0, model_width, kv_width))
        grads.append(up)

    def layer(tick, which, grad, kept):
        live = (section == layers - 1 - tick).astype(jnp.int32)[None]
        return layer_step(live, grad, blocks[which], turned, norm_gain, kept)

    held = [layer(0, which, grads[which], ()) for which in range(2)]
    hops = [(i, i - 1) for i in range(1, layers)]

    def step(tick, held):
        grads = [lax.ppermute(kept[0], "section", hops) for kept in held]
        return [layer(tick, which, grads[which], held[which]) for which in range(2)]

    held = lax.fori_loop(1, layers, step, held)

    columns, values, stored = [], [], []
    for which in range(2):
        block = blocks[which][3].reshape(BLOCK, replicas, shares).transpose(1, 0, 2)
        columns.append(spread(block.reshape(replicas * BLOCK, shares)))
        out, value = held[which]
        stored.append(regroup(out))
        values.append(spread(jnp.tile(value, (replicas, 1))))
    ordered = jnp.where(
        side == 0, jnp.concatenate(stored, axis=0), jnp.concatenate(stored[::-1], axis=0)
    )
    own_weight = lax.dynamic_slice_in_dim(weight, me * shares, shares, 0)
    own_gain = lax.dynamic_slice_in_dim(norm_gain[0], me * shares, shares, 0)
    scale = float(tokens * replicas) ** (-0.5)
    weight_grad, gain_grad = pl.pallas_call(
        functools.partial(weight_kernel, scale),
        out_shape=(
            jax.ShapeDtypeStruct((shares, kv_width), jnp.float32),
            jax.ShapeDtypeStruct((1, shares), jnp.float32),
        ),
        in_specs=[VMEM] * 4,
        out_specs=(VMEM, VMEM),
        name="weight_grad",
    )(
        jnp.concatenate(columns, axis=0),
        jnp.concatenate(values, axis=0),
        own_weight,
        own_gain[:, None],
    )
    return ordered[None], weight_grad[None], gain_grad


def on_device(hidden_in, queries, keys, segments, value_weight, norm_gain, upstream):
    replicas = lax.axis_size("dp")
    piece = hidden_in.shape[1] // replicas
    plan = direct if piece % 16 == 0 and replicas == 8 else grouped
    return plan(
        hidden_in[0], queries[0], keys[0], segments, value_weight[0], norm_gain, upstream
    )


def solution(mesh):
    in_specs = (
        P("section", "dp", None),
        P("section", "dp", None),
        P("section", "dp", None),
        P("dp", None),
        P("section", None, None),
        P("section", None),
        P("dp", None),
    )
    out_specs = (P("section", "dp", None), P("section", "dp", None), P("section", "dp"))
    return jax.shard_map(
        on_device, mesh=mesh, in_specs=in_specs, out_specs=out_specs, check_vma=False
    )
```

```python
import functools

import jax
import jax.numpy as jnp
from jax import lax
from jax.experimental import pallas as pl
from jax.experimental.pallas import tpu as pltpu
from jax.sharding import PartitionSpec as P

HEAD_FEATURES = 128
BLOCK = 64
UNIT = 32
EPSILON = 1e-06
MASKED = -1e30
OUTS = {1: 2, 5: 6}
UNITS = ("a_late", "a_early", "b_late", "b_early")
VMEM = pl.BlockSpec(memory_space=pltpu.VMEM)
SMEM = pl.BlockSpec(memory_space=pltpu.SMEM)


ANY = pl.BlockSpec(memory_space=pl.ANY)


LATE, EARLY = slice(UNIT, BLOCK), slice(0, UNIT)


def params(microseconds):
    flops = int(microseconds * 1.15e9)
    return dict(
        compiler_params=pltpu.CompilerParams(vmem_limit_bytes=16 << 20),
        cost_estimate=pl.CostEstimate(flops=flops, bytes_accessed=0, transcendentals=0),
    )


def near(array):
    return pltpu.with_memory_space_constraint(array, pltpu.VMEM)


def place():
    half = lax.axis_size("dp") // 2
    me = lax.axis_index("dp")
    return lax.div(me, half), lax.rem(me, half), me


def probs_kernel(count, seg_row, model_width, kv_width, *refs):
    pieces, seg_ref = refs[:count], refs[count]
    late_ref, early_ref, inv_ref, x_ref, rows_ref = refs[-5:]
    heads = model_width // kv_width
    rows = BLOCK // count
    side, at, _ = place()
    for k, piece in enumerate(pieces):
        if count == 1:
            rows_ref[...] = piece[...]
        else:
            first = pl.multiple_of(lax.bitwise_xor(at, k) * rows, rows)
            rows_ref[pl.ds(first, rows), :] = piece[...]

    def iota(shape, axis):
        return lax.broadcasted_iota(jnp.int32, shape, axis)

    seg = seg_ref[seg_row : seg_row + 16, : 2 * BLOCK].astype(jnp.float32)[:1]
    shape = (BLOCK, 2 * BLOCK)
    wanted = iota(shape, 1) == side * BLOCK + iota(shape, 0)
    ids = jnp.sum(jnp.where(wanted, seg, 0.0), axis=1, keepdims=True)
    key_code = ids * BLOCK + iota((BLOCK, 1), 0).astype(jnp.float32)
    list_start = ids * BLOCK
    shape = (BLOCK, heads * BLOCK)
    column = iota(shape, 1)
    query_at = lax.rem(column, UNIT) + jnp.where(column < heads * UNIT, UNIT, 0)
    same = iota(shape, 0) == query_at
    query_code = jnp.sum(jnp.where(same, key_code, 0.0), axis=0, keepdims=True)
    query_start = jnp.sum(jnp.where(same, list_start, 0.0), axis=0, keepdims=True)
    allowed = (key_code <= query_code) & (key_code >= query_start)
    for c in range(kv_width // HEAD_FEATURES):
        first = c * heads * HEAD_FEATURES
        query_stack = jnp.concatenate(
            [
                rows_ref[part, first + h * HEAD_FEATURES : first + (h + 1) * HEAD_FEATURES]
                for part in (LATE, EARLY)
                for h in range(heads)
            ],
            axis=0,
        )
        key_first = model_width + c * HEAD_FEATURES
        keys = rows_ref[:, key_first : key_first + HEAD_FEATURES]
        scores = lax.dot_general(
            keys, query_stack, (((1,), (1,)), ((), ())), preferred_element_type=jnp.float32
        ) * HEAD_FEATURES ** (-0.5)
        scores = jnp.where(allowed, scores, MASKED)
        exp_scores = jnp.exp(scores - jnp.max(scores, axis=0, keepdims=True))
        total = jnp.sum(exp_scores, axis=0, keepdims=True)
        probs = (exp_scores / total).astype(jnp.bfloat16)
        late_ref[c] = probs[LATE, : heads * UNIT]
        early_ref[c] = probs[EARLY]
    hidden = rows_ref[:, model_width + kv_width :]
    x_ref[...] = hidden
    x = hidden.astype(jnp.float32)
    mean_square = jnp.mean(x * x, axis=1, keepdims=True)
    inv_ref[...] = jnp.broadcast_to(lax.rsqrt(mean_square + EPSILON), inv_ref.shape)


def block_probs(pieces, seg, seg_row, model_width, kv_width, after=()):
    heads = model_width // kv_width
    key_heads = kv_width // HEAD_FEATURES
    operands = [near(piece) for piece in pieces] + [near(seg)]
    specs = [VMEM] * len(operands) + [ANY] * len(after)
    operands += after
    return pl.pallas_call(
        functools.partial(probs_kernel, len(pieces), seg_row, model_width, kv_width),
        out_shape=(
            jax.ShapeDtypeStruct((key_heads, UNIT, heads * UNIT), jnp.bfloat16),
            jax.ShapeDtypeStruct((key_heads, UNIT, heads * BLOCK), jnp.bfloat16),
            jax.ShapeDtypeStruct((BLOCK, 128), jnp.float32),
            jax.ShapeDtypeStruct((BLOCK, model_width), jnp.bfloat16),
        ),
        in_specs=specs,
        out_specs=(VMEM,) * 4,
        scratch_shapes=[pltpu.VMEM((BLOCK, 2 * model_width + kv_width), jnp.bfloat16)],
        name="probs",
        **params(0.35 if after else 2.0),
    )(*operands)


def unit_math(rows, grads, probs_ref, x_ref, inv_ref, turned_ref, gain_ref, scaled_ref, store, value_ref):
    kv_width, model_width = turned_ref.shape
    heads = model_width // kv_width
    chunk = min(512, model_width)
    inv = inv_ref[rows, :1]
    values = []
    for c in range(kv_width // HEAD_FEATURES):
        first = c * heads * HEAD_FEATURES
        grad_stack = jnp.concatenate(
            [
                grad_ref[part, first + h * HEAD_FEATURES : first + (h + 1) * HEAD_FEATURES]
                for grad_ref, part in grads
                for h in range(heads)
            ],
            axis=0,
        )
        values.append(
            jnp.dot(probs_ref[c], grad_stack, preferred_element_type=jnp.float32).astype(
                jnp.bfloat16
            )
        )
    value = jnp.concatenate(values, axis=1)
    value_ref[...] = (value.astype(jnp.float32) * inv).astype(jnp.bfloat16)
    inner = jnp.zeros((UNIT, 1), jnp.float32)
    for first in range(0, model_width, chunk):
        columns = slice(first, first + chunk)
        normed_grad = jnp.dot(value, turned_ref[:, columns], preferred_element_type=jnp.float32)
        scaled = normed_grad * gain_ref[:, columns]
        scaled_ref[:, columns] = scaled
        x = x_ref[rows, columns].astype(jnp.float32)
        inner = inner + jnp.sum(x * scaled, axis=1, keepdims=True)
    pull = inner * (inv * inv / model_width)
    grad_ref, part = grads[-1]
    for first in range(0, model_width, chunk):
        columns = slice(first, first + chunk)
        x = x_ref[rows, columns].astype(jnp.float32)
        change = inv * (scaled_ref[:, columns] - x * pull)
        grad = grad_ref[part, columns].astype(jnp.float32)
        store(columns, (grad + change).astype(jnp.bfloat16))


def turn_kernel(weight_ref, *refs):
    turned_ref = refs[-1]
    step = min(256, weight_ref.shape[0])
    for first in range(0, weight_ref.shape[0], step):
        turned_ref[:, first : first + step] = weight_ref[first : first + step, :].T


def turn(weight, after=()):
    return pl.pallas_call(
        turn_kernel,
        out_shape=jax.ShapeDtypeStruct(weight.shape[::-1], weight.dtype),
        in_specs=[VMEM] + [ANY] * len(after),
        out_specs=VMEM,
        name="turn",
        **params(1.5),
    )(near(weight), *after)


def layer_kernel(
    live_ref, grad_ref, late_ref, early_ref, inv_ref, x_ref, turned_ref, gain_ref, *rest
):
    out_ref, value_ref, scaled_ref = rest[-3:]
    if len(rest) == 5:

        @pl.when(live_ref[0] == 0)
        def _():
            out_ref[...] = rest[0][...]
            value_ref[...] = rest[1][...]

    @pl.when(live_ref[0] == 1)
    def _():
        for rows, parts, probs_ref in ((LATE, [LATE], late_ref), (EARLY, [LATE, EARLY], early_ref)):

            def store(columns, part, rows=rows):
                out_ref[rows, columns] = part

            grads = [(grad_ref, part) for part in parts]
            unit_math(
                rows, grads, probs_ref, x_ref, inv_ref, turned_ref, gain_ref, scaled_ref, store,
                value_ref.at[rows],
            )


def layer_step(live, grad, block, turned, gain, held=()):
    kv_width, model_width = turned.shape
    operands = [live, grad, *block, turned, gain, *held]
    return pl.pallas_call(
        layer_kernel,
        out_shape=(
            jax.ShapeDtypeStruct((BLOCK, model_width), jnp.bfloat16),
            jax.ShapeDtypeStruct((BLOCK, kv_width), jnp.bfloat16),
        ),
        in_specs=[SMEM] + [VMEM] * (len(operands) - 1),
        out_specs=(VMEM, VMEM),
        scratch_shapes=[pltpu.VMEM((UNIT, model_width), jnp.float32)],
        name="layer",
        **params(1.1),
    )(*operands)


def tick_kernel(tick, rows, parts, kept, late, *refs):
    grads = list(zip(refs, parts))
    probs_ref, inv_ref, x_ref, turned_ref, gain_ref = refs[len(parts) : len(parts) + 5]
    refs = refs[len(parts) + 5 :]
    earlier, refs = refs[: 2 * kept], refs[2 * kept :]
    late_refs = refs[:late]
    kv_width, model_width = turned_ref.shape
    turn = lax.axis_size("section") - 1 - lax.axis_index("section")
    if late:
        outs, (scaled_ref, blocks_ref, value_ref) = refs[-3 - OUTS[late] : -3], refs[-3:]
    else:
        outs, scaled_ref = refs[-3:-1], refs[-1]
        value_ref = outs[1]
    if late > 1:

        def store(columns, part):
            blocks_ref[BLOCK : BLOCK + UNIT, columns] = part

    else:

        def store(columns, part):
            outs[0][:, columns] = part

    @pl.when(turn == tick)
    def _():
        unit_math(
            rows, grads, probs_ref, x_ref, inv_ref, turned_ref, gain_ref, scaled_ref, store,
            value_ref,
        )

    for at in range(kept):

        @pl.when(turn == at)
        def _(at=at):
            store(slice(None), earlier[2 * at][...])
            value_ref[...] = earlier[2 * at + 1][...]

    if late:
        values = jnp.concatenate([value_ref[...], late_refs[0][...]], axis=0)
        outs[1][...] = values
    if late > 1:
        late_a_ref, early_a_ref, late_b_ref, value_a_ref = late_refs[1:]
        outs[0][:BLOCK, :] = value_a_ref[...]
        outs[0][BLOCK:, :] = values
        blocks_ref[EARLY, :] = early_a_ref[...]
        blocks_ref[LATE, :] = late_a_ref[...]
        blocks_ref[BLOCK + UNIT :, :] = late_b_ref[...]
        at = place()[1]
        half = len(outs) - 2
        piece = BLOCK // half
        for k, out_ref in enumerate(outs[2:]):
            first = pl.multiple_of(lax.bitwise_xor(at, k) * piece, piece)
            out_ref[:piece, :] = blocks_ref[pl.ds(first, piece), :]
            out_ref[piece : 2 * piece, :] = blocks_ref[pl.ds(BLOCK + first, piece), :]
        groups = model_width // kv_width
        share = BLOCK // groups
        for g in range(groups):
            outs[4][2 * piece :, g * kv_width : (g + 1) * kv_width] = values[
                g * share : (g + 1) * share
            ]


def tick_step(tick, grads, block, turned, gain, kept=(), late=(), after=(), name=""):
    kv_width, model_width = turned.shape
    low = len(grads) == 2
    arrays = [grad for grad, _ in grads]
    arrays += [block[1] if low else block[0], block[2], block[3], turned, gain]
    arrays += [array for pair in kept for array in pair]
    arrays += late
    operands = [near(array) for array in arrays]
    specs = [VMEM] * len(operands) + [ANY] * len(after)
    bf16 = jnp.bfloat16
    scratch = [pltpu.VMEM((UNIT, model_width), jnp.float32)]
    rows, value = (UNIT, model_width), (UNIT, kv_width)
    shapes = [rows, value]
    if late:
        scratch += [pltpu.VMEM((2 * BLOCK, model_width), bf16), pltpu.VMEM(value, bf16)]
        shapes = [rows, (BLOCK, kv_width)]
    if len(late) > 1:
        half = lax.axis_size("dp") // 2
        shapes = [(2 * BLOCK // half, model_width)] * half
        shapes[2] = (2 * BLOCK // half + BLOCK * kv_width // model_width, model_width)
        shapes = [(2 * BLOCK, kv_width), (BLOCK, kv_width)] + shapes
    parts = [part for _, part in grads]
    return pl.pallas_call(
        functools.partial(
            tick_kernel, tick, EARLY if low else LATE, parts, len(kept), len(late)
        ),
        out_shape=tuple(jax.ShapeDtypeStruct(shape, bf16) for shape in shapes),
        in_specs=specs,
        out_specs=(VMEM,) * len(shapes),
        scratch_shapes=scratch,
        name=f"tick{tick}_{name}",
        **params(1.0 if kept else 0.0),
    )(*operands, *after)


def pack_kernel(block, half, piece, query_ref, key_ref, hidden_ref, up_ref, seg_ref, *rest):
    up_out_ref, seg_in_ref, sems = rest[-3:]
    packed = rest[-3 - half : -3]
    rest = rest[: -3 - half]
    side, at, _ = place()
    there = side if block == 0 else 1 - side
    copies = []

    def copy(source, target):
        made = pltpu.make_async_copy(source, target, sems.at[len(copies)])
        made.start()
        copies.append(made)

    copy(seg_ref, seg_in_ref)
    for k in range(half):
        replica = there * half + lax.bitwise_xor(at, k)
        rows = pl.ds(pl.multiple_of(replica * piece, piece), piece)
        first = 0
        for source in (query_ref, key_ref, hidden_ref):
            width = source.shape[1]
            copy(source.at[rows], packed[k].at[:, pl.ds(first, width)])
            first += width
    rows = pl.ds(pl.multiple_of(there * BLOCK, BLOCK), BLOCK)
    copy(up_ref.at[rows], up_out_ref.at[pl.ds(0, BLOCK)])
    up_out_ref[BLOCK:, :] = jnp.zeros((16, up_out_ref.shape[1]), jnp.bfloat16)
    copies[0].wait()
    ids = seg_in_ref[...].astype(jnp.float32)
    up_out_ref[BLOCK:, : ids.shape[1]] = jnp.broadcast_to(ids, (16, ids.shape[1])).astype(
        jnp.bfloat16
    )
    if block == 1:
        turn_kernel(rest[0], rest[-1])
    for made in copies[1:]:
        made.wait()


def pack(block, half, piece, sources, weight=None):
    model_width = sources[0].shape[1]
    width = sum(source.shape[1] for source in sources[:3])
    bf16 = jnp.bfloat16
    operands = [pltpu.with_memory_space_constraint(array, pltpu.HBM) for array in sources]
    specs = [pl.BlockSpec(memory_space=pltpu.HBM)] * len(sources)
    outs = [jax.ShapeDtypeStruct((piece, width), bf16)] * half
    outs.append(jax.ShapeDtypeStruct((BLOCK + 16, model_width), bf16))
    if weight is not None:
        operands.append(near(weight))
        specs.append(VMEM)
        outs = [jax.ShapeDtypeStruct(weight.shape[::-1], bf16)] + outs
    return pl.pallas_call(
        functools.partial(pack_kernel, block, half, piece),
        out_shape=tuple(outs),
        in_specs=specs,
        out_specs=(VMEM,) * len(outs),
        scratch_shapes=[
            pltpu.VMEM(sources[-1].shape, jnp.int32),
            pltpu.SemaphoreType.DMA((3 * half + 2,)),
        ],
        name="pack",
        **params(1.2),
    )(*operands)


def columns_kernel(width, distance, first_ref, second_ref, *refs):
    out_ref = refs[-1]
    there = lax.div(lax.bitwise_xor(place()[2], distance), 2)
    out_ref[:BLOCK, :] = first_ref[:, columns_of(there, width)]
    out_ref[BLOCK:, :] = second_ref[:, columns_of(there, width)]


def columns_for(distance, blocks, after):
    model_width = blocks[0][3].shape[1]
    width = 2 * model_width // lax.axis_size("dp")
    return pl.pallas_call(
        functools.partial(columns_kernel, width, distance),
        out_shape=jax.ShapeDtypeStruct((2 * BLOCK, width), jnp.bfloat16),
        in_specs=[VMEM] * 2 + [ANY] * len(after),
        out_specs=VMEM,
        name=f"columns{distance}",
        **params(0.0),
    )(blocks[0][3], blocks[1][3], *after)


def own_kernel(scale, weight_ref, gain_ref, after_ref, weight_out_ref, gain_out_ref):
    shares = weight_out_ref.shape[0]
    first = pl.multiple_of(place()[2] * shares, shares)
    weight_out_ref[...] = weight_ref[pl.ds(first, shares), :].astype(jnp.float32) * scale
    gain = gain_ref[:, pl.ds(first, shares)]
    column = jnp.sum(jnp.where(diagonal(shares), gain, 0.0), axis=1, keepdims=True)
    gain_out_ref[...] = jnp.broadcast_to(column * scale, gain_out_ref.shape)


def columns_of(pair, width):
    return pl.ds(pl.multiple_of(pair * width, width), width)


def partial_kernel(shares, first, *refs):
    columns, refs = refs[:4], refs[4:]
    own_out_ref, *other_refs = refs[6:]
    kv_width = own_out_ref.shape[1]
    parts = [ref[...] for ref in refs[:6]]
    packed = refs[2]
    parts[2:3] = [packed[first:, at : at + kv_width] for at in range(0, packed.shape[1], kv_width)]
    value = jnp.concatenate(parts, axis=0)
    mine = lax.rem(place()[2], 2)

    def share(core):
        at = pl.ds(pl.multiple_of(core * shares, shares), shares)
        rows = jnp.concatenate([ref[:, at] for ref in columns], axis=0)
        return lax.dot_general(
            rows, value, (((0,), (0,)), ((), ())), preferred_element_type=jnp.float32
        )

    other = share(1 - mine).astype(jnp.bfloat16)
    for part, ref in enumerate(other_refs):
        ref[...] = other[part * (shares // 2) : (part + 1) * (shares // 2)]
    own_out_ref[...] = share(mine)


def rows_kernel(half, *refs):
    pieces = refs[:half]
    rows_ref, token_ref, sems = refs[-3:]
    token_ref[...] = jnp.zeros_like(token_ref)
    side, at, _ = place()
    piece = BLOCK // half
    copies = []
    for block in range(2):
        for k in range(half):
            replica = (side if block == 0 else 1 - side) * half + lax.bitwise_xor(at, k)
            rows = pl.ds(pl.multiple_of(replica * piece, piece), piece)
            source = pieces[k].at[pl.ds(block * piece, piece)]
            made = pltpu.make_async_copy(source, rows_ref.at[rows], sems.at[block * half + k])
            made.start()
            copies.append(made)
    for made in copies:
        made.wait()


def diagonal(size):
    return lax.broadcasted_iota(jnp.int32, (size, size), 0) == lax.broadcasted_iota(
        jnp.int32, (size, size), 1
    )


def finish_kernel(
    own_ref, first_ref, second_ref, weight_ref, gain_ref, after_ref, out_ref, gain_out_ref
):
    other = jnp.concatenate([first_ref[...], second_ref[...]], axis=0)
    total = own_ref[...] + other.astype(jnp.float32)
    out_ref[...] = total * gain_ref[:, :1]
    sums = jnp.sum(total * weight_ref[...], axis=1, keepdims=True)
    gain_out_ref[...] = jnp.sum(
        jnp.where(diagonal(total.shape[0]), sums, 0.0), axis=0, keepdims=True
    )


def direct(hidden, query, key, segments, weight, norm_gain, upstream):
    tokens, model_width = hidden.shape
    kv_width = key.shape[1]
    replicas = lax.axis_size("dp")
    layers = lax.axis_size("section")
    half = replicas // 2
    piece = tokens // replicas
    shares = model_width // replicas

    def swap(array, k):
        return lax.ppermute(array, "dp", [(i, i ^ k) for i in range(replicas)])

    count = 2 * half
    bf16 = jnp.bfloat16
    sources = (query, key, hidden, upstream, segments)
    pieces, ups = [], []
    for b in range(2):
        *packed, up = pack(b, half, piece, sources, weight if b else None)
        if b:
            turned, *packed = packed
        pieces.append([packed[0]] + [swap(packed[k], k) for k in range(1, half)])
        ups.append(swap(up, half) if b else up)
    whole = slice(0, UNIT)
    scale = float(tokens * replicas) ** (-0.5)
    blocks, kept, after = [], [], []
    for b in range(2):
        block = block_probs(pieces[b], ups[b], BLOCK, model_width, kv_width, after)
        late, early = (ups[b], LATE), (ups[b], EARLY)
        first = tick_step(0, [late], block, turned, norm_gain, name=UNITS[2 * b])
        second = tick_step(
            0, [late, early], block, turned, norm_gain, after=[first[0]], name=UNITS[2 * b + 1]
        )
        blocks.append(block)
        kept += [[first], [second]]
        after = [second[0]]

    for tick in range(1, layers):
        hop = [(layers - tick, layers - 1 - tick)]
        grads = [(lax.ppermute(unit[-1][0], "section", hop), whole) for unit in kept]
        last = tick == layers - 1
        after, done = [kept[3][-1][0]], []
        if tick == layers - 2:
            own_weight, own_gain = pl.pallas_call(
                functools.partial(own_kernel, scale),
                out_shape=(
                    jax.ShapeDtypeStruct((shares, kv_width), jnp.float32),
                    jax.ShapeDtypeStruct((shares, 128), jnp.float32),
                ),
                in_specs=[VMEM, VMEM, ANY],
                out_specs=(VMEM, VMEM),
                name="own",
                **params(0.0),
            )(near(weight), norm_gain, *after)
            columns = {6: swap(columns_for(6, blocks, after + [own_gain]), 6)}
        if last:
            columns[2] = swap(columns_for(2, blocks, after + [columns[6]]), 2)
        for u in range(4):
            needs = grads[u - 1 : u + 1] if u % 2 else grads[u : u + 1]
            late = []
            if last and u == 1:
                late = [done[0][1]]
            if last and u == 3:
                late = [done[2][1], done[0][0], done[1][0], done[2][0], done[1][1]]
                first_values = {k: swap(done[1][1], k) for k in (2, 6)}
                columns[0] = columns_for(0, blocks, after)
                columns[4] = swap(columns_for(4, blocks, [done[1][0], columns[2]]), 4)
                after = after + [columns[4], first_values[2], first_values[6]]
            done.append(
                tick_step(
                    tick, needs, blocks[u // 2], turned, norm_gain, kept[u] if last else (), late,
                    after, name=UNITS[u],
                )
            )
            after = [done[u][0]]
            kept[u].append(done[u])
    values, last_value, *rows = done[3]
    rows = [rows[0]] + [swap(rows[k], k) for k in range(1, half)]
    values = [values, first_values[2], rows[2], swap(values, 4)]
    values += [first_values[6], swap(last_value, 6)]
    own, *other = pl.pallas_call(
        functools.partial(partial_kernel, shares, 2 * piece),
        out_shape=(jax.ShapeDtypeStruct((shares, kv_width), jnp.float32),)
        + (jax.ShapeDtypeStruct((shares // 2, kv_width), bf16),) * 2,
        in_specs=[VMEM] * 10,
        out_specs=(VMEM,) * 3,
        name="weight_partial",
        **params(0.0),
    )(*[columns[k] for k in (0, 2, 4, 6)], *values)
    other = [swap(part, 1) for part in other]
    input_grad, token = pl.pallas_call(
        functools.partial(rows_kernel, half),
        out_shape=(
            jax.ShapeDtypeStruct((tokens, model_width), bf16),
            jax.ShapeDtypeStruct((8, 128), jnp.float32),
        ),
        in_specs=[VMEM] * half + [ANY],
        out_specs=(ANY, VMEM),
        scratch_shapes=[pltpu.SemaphoreType.DMA((count,))],
        name="rows",
        **params(0.0),
    )(*rows, own)
    weight_grad, gain_grad = pl.pallas_call(
        finish_kernel,
        out_shape=(
            jax.ShapeDtypeStruct((shares, kv_width), jnp.float32),
            jax.ShapeDtypeStruct((1, shares), jnp.float32),
        ),
        in_specs=[VMEM] * 5 + [ANY],
        out_specs=(VMEM, VMEM),
        name="finish",
        **params(0.0),
    )(own, *other, own_weight, own_gain, token)
    return input_grad[None], weight_grad[None], gain_grad


def weight_kernel(scale, columns_ref, value_ref, weight_ref, gain_ref, out_ref, gain_out_ref):
    total = lax.dot_general(
        columns_ref[...], value_ref[...], (((0,), (0,)), ((), ())),
        preferred_element_type=jnp.float32,
    ) * scale
    out_ref[...] = total * gain_ref[...]
    product = total * weight_ref[...].astype(jnp.float32)
    sums = lax.dot_general(
        jnp.ones((8, product.shape[1]), jnp.float32), product, (((1,), (1,)), ((), ())),
        preferred_element_type=jnp.float32, precision=lax.Precision.HIGHEST,
    )
    gain_out_ref[...] = sums[:1]


def grouped(hidden, query, key, segments, weight, norm_gain, upstream):
    tokens, model_width = hidden.shape
    kv_width = key.shape[1]
    replicas = lax.axis_size("dp")
    layers = lax.axis_size("section")
    half = replicas // 2
    me = lax.axis_index("dp")
    section = lax.axis_index("section")
    side = me // half
    groups = [list(range(half)), list(range(half, replicas))]
    across = [(i, (i + half) % replicas) for i in range(replicas)]
    shares = model_width // replicas

    def rows_of(array, which, axis=0):
        at = side if which == 0 else 1 - side
        return lax.dynamic_slice_in_dim(array, at * BLOCK, BLOCK, axis)

    def regroup(array):
        return lax.all_to_all(
            array, "dp", split_axis=0, concat_axis=0, axis_index_groups=groups, tiled=True
        )

    def spread(array):
        return lax.all_to_all(array, "dp", split_axis=0, concat_axis=0, tiled=True)

    turned = turn(weight)
    blocks, grads = [], []
    for which in range(2):
        up = rows_of(upstream, which)
        seg = jnp.broadcast_to(segments, (16, 2 * BLOCK)).astype(jnp.bfloat16)
        if which == 1:
            up = lax.ppermute(up, "dp", across)
            seg = lax.ppermute(seg, "dp", across)
        packed = jnp.concatenate(
            [rows_of(query, which), rows_of(key, which), rows_of(hidden, which)], axis=1
        )
        blocks.append(block_probs([regroup(packed)], seg, 0, model_width, kv_width))
        grads.append(up)

    def layer(tick, which, grad, kept):
        live = (section == layers - 1 - tick).astype(jnp.int32)[None]
        return layer_step(live, grad, blocks[which], turned, norm_gain, kept)

    held = [layer(0, which, grads[which], ()) for which in range(2)]
    hops = [(i, i - 1) for i in range(1, layers)]

    def step(tick, held):
        grads = [lax.ppermute(kept[0], "section", hops) for kept in held]
        return [layer(tick, which, grads[which], held[which]) for which in range(2)]

    held = lax.fori_loop(1, layers, step, held)

    columns, values, stored = [], [], []
    for which in range(2):
        block = blocks[which][3].reshape(BLOCK, replicas, shares).transpose(1, 0, 2)
        columns.append(spread(block.reshape(replicas * BLOCK, shares)))
        out, value = held[which]
        stored.append(regroup(out))
        values.append(spread(jnp.tile(value, (replicas, 1))))
    ordered = jnp.where(
        side == 0, jnp.concatenate(stored, axis=0), jnp.concatenate(stored[::-1], axis=0)
    )
    own_weight = lax.dynamic_slice_in_dim(weight, me * shares, shares, 0)
    own_gain = lax.dynamic_slice_in_dim(norm_gain[0], me * shares, shares, 0)
    scale = float(tokens * replicas) ** (-0.5)
    weight_grad, gain_grad = pl.pallas_call(
        functools.partial(weight_kernel, scale),
        out_shape=(
            jax.ShapeDtypeStruct((shares, kv_width), jnp.float32),
            jax.ShapeDtypeStruct((1, shares), jnp.float32),
        ),
        in_specs=[VMEM] * 4,
        out_specs=(VMEM, VMEM),
        name="weight_grad",
    )(
        jnp.concatenate(columns, axis=0),
        jnp.concatenate(values, axis=0),
        own_weight,
        own_gain[:, None],
    )
    return ordered[None], weight_grad[None], gain_grad


def on_device(hidden_in, queries, keys, segments, value_weight, norm_gain, upstream):
    replicas = lax.axis_size("dp")
    piece = hidden_in.shape[1] // replicas
    plan = direct if piece % 16 == 0 and replicas == 8 else grouped
    return plan(
        hidden_in[0], queries[0], keys[0], segments, value_weight[0], norm_gain, upstream
    )


def solution(mesh):
    in_specs = (
        P("section", "dp", None),
        P("section", "dp", None),
        P("section", "dp", None),
        P("dp", None),
        P("section", None, None),
        P("section", None),
        P("dp", None),
    )
    out_specs = (P("section", "dp", None), P("section", "dp", None), P("section", "dp"))
    return jax.shard_map(
        on_device, mesh=mesh, in_specs=in_specs, out_specs=out_specs, check_vma=False
    )
```

```python
import functools

import jax
import jax.numpy as jnp
from jax import lax
from jax.experimental import pallas as pl
from jax.experimental.pallas import tpu as pltpu
from jax.sharding import PartitionSpec as P

HEAD_FEATURES = 128
BLOCK = 64
UNIT = 32
EPSILON = 1e-06
MASKED = -1e30
OUTS = {1: 2, 5: 6}
UNITS = ("a_late", "a_early", "b_late", "b_early")
VMEM = pl.BlockSpec(memory_space=pltpu.VMEM)
SMEM = pl.BlockSpec(memory_space=pltpu.SMEM)


ANY = pl.BlockSpec(memory_space=pl.ANY)


LATE, EARLY = slice(UNIT, BLOCK), slice(0, UNIT)


def params(microseconds):
    flops = int(microseconds * 1.15e9)
    return dict(
        compiler_params=pltpu.CompilerParams(vmem_limit_bytes=16 << 20),
        cost_estimate=pl.CostEstimate(flops=flops, bytes_accessed=0, transcendentals=0),
    )


def near(array):
    return pltpu.with_memory_space_constraint(array, pltpu.VMEM)


def place():
    half = lax.axis_size("dp") // 2
    me = lax.axis_index("dp")
    return lax.div(me, half), lax.rem(me, half), me


def probs_kernel(count, seg_row, model_width, kv_width, *refs):
    pieces, seg_ref = refs[:count], refs[count]
    late_ref, early_ref, inv_ref, x_ref, rows_ref = refs[-5:]
    heads = model_width // kv_width
    rows = BLOCK // count
    side, at, _ = place()
    for k, piece in enumerate(pieces):
        if count == 1:
            rows_ref[...] = piece[...]
        else:
            first = pl.multiple_of(lax.bitwise_xor(at, k) * rows, rows)
            rows_ref[pl.ds(first, rows), :] = piece[...]

    def iota(shape, axis):
        return lax.broadcasted_iota(jnp.int32, shape, axis)

    seg = seg_ref[seg_row : seg_row + 16, : 2 * BLOCK].astype(jnp.float32)[:1]
    shape = (BLOCK, 2 * BLOCK)
    wanted = iota(shape, 1) == side * BLOCK + iota(shape, 0)
    ids = jnp.sum(jnp.where(wanted, seg, 0.0), axis=1, keepdims=True)
    key_code = ids * BLOCK + iota((BLOCK, 1), 0).astype(jnp.float32)
    list_start = ids * BLOCK
    shape = (BLOCK, heads * BLOCK)
    column = iota(shape, 1)
    query_at = lax.rem(column, UNIT) + jnp.where(column < heads * UNIT, UNIT, 0)
    same = iota(shape, 0) == query_at
    query_code = jnp.sum(jnp.where(same, key_code, 0.0), axis=0, keepdims=True)
    query_start = jnp.sum(jnp.where(same, list_start, 0.0), axis=0, keepdims=True)
    allowed = (key_code <= query_code) & (key_code >= query_start)
    for c in range(kv_width // HEAD_FEATURES):
        first = c * heads * HEAD_FEATURES
        query_stack = jnp.concatenate(
            [
                rows_ref[part, first + h * HEAD_FEATURES : first + (h + 1) * HEAD_FEATURES]
                for part in (LATE, EARLY)
                for h in range(heads)
            ],
            axis=0,
        )
        key_first = model_width + c * HEAD_FEATURES
        keys = rows_ref[:, key_first : key_first + HEAD_FEATURES]
        scores = lax.dot_general(
            keys, query_stack, (((1,), (1,)), ((), ())), preferred_element_type=jnp.float32
        ) * HEAD_FEATURES ** (-0.5)
        scores = jnp.where(allowed, scores, MASKED)
        exp_scores = jnp.exp(scores - jnp.max(scores, axis=0, keepdims=True))
        total = jnp.sum(exp_scores, axis=0, keepdims=True)
        probs = (exp_scores / total).astype(jnp.bfloat16)
        late_ref[c] = probs[LATE, : heads * UNIT]
        early_ref[c] = probs[EARLY]
    hidden = rows_ref[:, model_width + kv_width :]
    x_ref[...] = hidden
    x = hidden.astype(jnp.float32)
    mean_square = jnp.mean(x * x, axis=1, keepdims=True)
    inv_ref[...] = jnp.broadcast_to(lax.rsqrt(mean_square + EPSILON), inv_ref.shape)


def block_probs(pieces, seg, seg_row, model_width, kv_width, after=()):
    heads = model_width // kv_width
    key_heads = kv_width // HEAD_FEATURES
    operands = [near(piece) for piece in pieces] + [near(seg)]
    specs = [VMEM] * len(operands) + [ANY] * len(after)
    operands += after
    return pl.pallas_call(
        functools.partial(probs_kernel, len(pieces), seg_row, model_width, kv_width),
        out_shape=(
            jax.ShapeDtypeStruct((key_heads, UNIT, heads * UNIT), jnp.bfloat16),
            jax.ShapeDtypeStruct((key_heads, UNIT, heads * BLOCK), jnp.bfloat16),
            jax.ShapeDtypeStruct((BLOCK, 128), jnp.float32),
            jax.ShapeDtypeStruct((BLOCK, model_width), jnp.bfloat16),
        ),
        in_specs=specs,
        out_specs=(VMEM,) * 4,
        scratch_shapes=[pltpu.VMEM((BLOCK, 2 * model_width + kv_width), jnp.bfloat16)],
        name="probs",
        **params(0.35 if after else 2.0),
    )(*operands)


def unit_math(rows, grads, probs_ref, x_ref, inv_ref, turned_ref, gain_ref, scaled_ref, store, value_ref):
    kv_width, model_width = turned_ref.shape
    heads = model_width // kv_width
    chunk = min(512, model_width)
    inv = inv_ref[rows, :1]
    values = []
    for c in range(kv_width // HEAD_FEATURES):
        first = c * heads * HEAD_FEATURES
        grad_stack = jnp.concatenate(
            [
                grad_ref[part, first + h * HEAD_FEATURES : first + (h + 1) * HEAD_FEATURES]
                for grad_ref, part in grads
                for h in range(heads)
            ],
            axis=0,
        )
        values.append(
            jnp.dot(probs_ref[c], grad_stack, preferred_element_type=jnp.float32).astype(
                jnp.bfloat16
            )
        )
    value = jnp.concatenate(values, axis=1)
    value_ref[...] = (value.astype(jnp.float32) * inv).astype(jnp.bfloat16)
    inner = jnp.zeros((UNIT, 1), jnp.float32)
    for first in range(0, model_width, chunk):
        columns = slice(first, first + chunk)
        normed_grad = jnp.dot(value, turned_ref[:, columns], preferred_element_type=jnp.float32)
        scaled = normed_grad * gain_ref[:, columns]
        scaled_ref[:, columns] = scaled
        x = x_ref[rows, columns].astype(jnp.float32)
        inner = inner + jnp.sum(x * scaled, axis=1, keepdims=True)
    pull = inner * (inv * inv / model_width)
    grad_ref, part = grads[-1]
    for first in range(0, model_width, chunk):
        columns = slice(first, first + chunk)
        x = x_ref[rows, columns].astype(jnp.float32)
        change = inv * (scaled_ref[:, columns] - x * pull)
        grad = grad_ref[part, columns].astype(jnp.float32)
        store(columns, (grad + change).astype(jnp.bfloat16))


def turn_kernel(weight_ref, *refs):
    turned_ref = refs[-1]
    step = min(256, weight_ref.shape[0])
    for first in range(0, weight_ref.shape[0], step):
        turned_ref[:, first : first + step] = weight_ref[first : first + step, :].T


def turn(weight, after=()):
    return pl.pallas_call(
        turn_kernel,
        out_shape=jax.ShapeDtypeStruct(weight.shape[::-1], weight.dtype),
        in_specs=[VMEM] + [ANY] * len(after),
        out_specs=VMEM,
        name="turn",
        **params(1.5),
    )(near(weight), *after)


def layer_kernel(
    live_ref, grad_ref, late_ref, early_ref, inv_ref, x_ref, turned_ref, gain_ref, *rest
):
    out_ref, value_ref, scaled_ref = rest[-3:]
    if len(rest) == 5:

        @pl.when(live_ref[0] == 0)
        def _():
            out_ref[...] = rest[0][...]
            value_ref[...] = rest[1][...]

    @pl.when(live_ref[0] == 1)
    def _():
        for rows, parts, probs_ref in ((LATE, [LATE], late_ref), (EARLY, [LATE, EARLY], early_ref)):

            def store(columns, part, rows=rows):
                out_ref[rows, columns] = part

            grads = [(grad_ref, part) for part in parts]
            unit_math(
                rows, grads, probs_ref, x_ref, inv_ref, turned_ref, gain_ref, scaled_ref, store,
                value_ref.at[rows],
            )


def layer_step(live, grad, block, turned, gain, held=()):
    kv_width, model_width = turned.shape
    operands = [live, grad, *block, turned, gain, *held]
    return pl.pallas_call(
        layer_kernel,
        out_shape=(
            jax.ShapeDtypeStruct((BLOCK, model_width), jnp.bfloat16),
            jax.ShapeDtypeStruct((BLOCK, kv_width), jnp.bfloat16),
        ),
        in_specs=[SMEM] + [VMEM] * (len(operands) - 1),
        out_specs=(VMEM, VMEM),
        scratch_shapes=[pltpu.VMEM((UNIT, model_width), jnp.float32)],
        name="layer",
        **params(1.1),
    )(*operands)


def tick_kernel(tick, rows, parts, kept, late, *refs):
    grads = list(zip(refs, parts))
    probs_ref, inv_ref, x_ref, turned_ref, gain_ref = refs[len(parts) : len(parts) + 5]
    refs = refs[len(parts) + 5 :]
    earlier, refs = refs[: 2 * kept], refs[2 * kept :]
    late_refs = refs[:late]
    kv_width, model_width = turned_ref.shape
    turn = lax.axis_size("section") - 1 - lax.axis_index("section")
    if late:
        outs, (scaled_ref, blocks_ref, value_ref) = refs[-3 - OUTS[late] : -3], refs[-3:]
    else:
        outs, scaled_ref = refs[-3:-1], refs[-1]
        value_ref = outs[1]
    if late > 1:

        def store(columns, part):
            blocks_ref[BLOCK : BLOCK + UNIT, columns] = part

    else:

        def store(columns, part):
            outs[0][:, columns] = part

    @pl.when(turn == tick)
    def _():
        unit_math(
            rows, grads, probs_ref, x_ref, inv_ref, turned_ref, gain_ref, scaled_ref, store,
            value_ref,
        )

    for at in range(kept):

        @pl.when(turn == at)
        def _(at=at):
            store(slice(None), earlier[2 * at][...])
            value_ref[...] = earlier[2 * at + 1][...]

    if late:
        values = jnp.concatenate([value_ref[...], late_refs[0][...]], axis=0)
        outs[1][...] = values
    if late > 1:
        late_a_ref, early_a_ref, late_b_ref, value_a_ref = late_refs[1:]
        outs[0][:BLOCK, :] = value_a_ref[...]
        outs[0][BLOCK:, :] = values
        blocks_ref[EARLY, :] = early_a_ref[...]
        blocks_ref[LATE, :] = late_a_ref[...]
        blocks_ref[BLOCK + UNIT :, :] = late_b_ref[...]
        at = place()[1]
        half = len(outs) - 2
        piece = BLOCK // half
        for k, out_ref in enumerate(outs[2:]):
            first = pl.multiple_of(lax.bitwise_xor(at, k) * piece, piece)
            out_ref[:piece, :] = blocks_ref[pl.ds(first, piece), :]
            out_ref[piece : 2 * piece, :] = blocks_ref[pl.ds(BLOCK + first, piece), :]
        groups = model_width // kv_width
        share = BLOCK // groups
        for g in range(groups):
            outs[4][2 * piece :, g * kv_width : (g + 1) * kv_width] = values[
                g * share : (g + 1) * share
            ]


def tick_step(tick, grads, block, turned, gain, kept=(), late=(), after=(), name=""):
    kv_width, model_width = turned.shape
    low = len(grads) == 2
    arrays = [grad for grad, _ in grads]
    arrays += [block[1] if low else block[0], block[2], block[3], turned, gain]
    arrays += [array for pair in kept for array in pair]
    arrays += late
    operands = [near(array) for array in arrays]
    specs = [VMEM] * len(operands) + [ANY] * len(after)
    bf16 = jnp.bfloat16
    scratch = [pltpu.VMEM((UNIT, model_width), jnp.float32)]
    rows, value = (UNIT, model_width), (UNIT, kv_width)
    shapes = [rows, value]
    if late:
        scratch += [pltpu.VMEM((2 * BLOCK, model_width), bf16), pltpu.VMEM(value, bf16)]
        shapes = [rows, (BLOCK, kv_width)]
    if len(late) > 1:
        half = lax.axis_size("dp") // 2
        shapes = [(2 * BLOCK // half, model_width)] * half
        shapes[2] = (2 * BLOCK // half + BLOCK * kv_width // model_width, model_width)
        shapes = [(2 * BLOCK, kv_width), (BLOCK, kv_width)] + shapes
    parts = [part for _, part in grads]
    return pl.pallas_call(
        functools.partial(
            tick_kernel, tick, EARLY if low else LATE, parts, len(kept), len(late)
        ),
        out_shape=tuple(jax.ShapeDtypeStruct(shape, bf16) for shape in shapes),
        in_specs=specs,
        out_specs=(VMEM,) * len(shapes),
        scratch_shapes=scratch,
        name=f"tick{tick}_{name}",
        **params(1.0 if kept else 0.0),
    )(*operands, *after)


def pack_kernel(block, half, piece, query_ref, key_ref, hidden_ref, up_ref, seg_ref, *rest):
    up_out_ref, seg_in_ref, sems = rest[-3:]
    packed = rest[-3 - half : -3]
    rest = rest[: -3 - half]
    side, at, _ = place()
    there = side if block == 0 else 1 - side
    copies = []

    def copy(source, target):
        made = pltpu.make_async_copy(source, target, sems.at[len(copies)])
        made.start()
        copies.append(made)

    copy(seg_ref, seg_in_ref)
    for k in range(half):
        replica = there * half + lax.bitwise_xor(at, k)
        rows = pl.ds(pl.multiple_of(replica * piece, piece), piece)
        first = 0
        for source in (query_ref, key_ref, hidden_ref):
            width = source.shape[1]
            copy(source.at[rows], packed[k].at[:, pl.ds(first, width)])
            first += width
    rows = pl.ds(pl.multiple_of(there * BLOCK, BLOCK), BLOCK)
    copy(up_ref.at[rows], up_out_ref.at[pl.ds(0, BLOCK)])
    up_out_ref[BLOCK:, :] = jnp.zeros((16, up_out_ref.shape[1]), jnp.bfloat16)
    copies[0].wait()
    ids = seg_in_ref[...].astype(jnp.float32)
    up_out_ref[BLOCK:, : ids.shape[1]] = jnp.broadcast_to(ids, (16, ids.shape[1])).astype(
        jnp.bfloat16
    )
    if block == 1:
        turn_kernel(rest[0], rest[-1])
    for made in copies[1:]:
        made.wait()


def pack(block, half, piece, sources, weight=None):
    model_width = sources[0].shape[1]
    width = sum(source.shape[1] for source in sources[:3])
    bf16 = jnp.bfloat16
    operands = [pltpu.with_memory_space_constraint(array, pltpu.HBM) for array in sources]
    specs = [pl.BlockSpec(memory_space=pltpu.HBM)] * len(sources)
    outs = [jax.ShapeDtypeStruct((piece, width), bf16)] * half
    outs.append(jax.ShapeDtypeStruct((BLOCK + 16, model_width), bf16))
    if weight is not None:
        operands.append(near(weight))
        specs.append(VMEM)
        outs = [jax.ShapeDtypeStruct(weight.shape[::-1], bf16)] + outs
    return pl.pallas_call(
        functools.partial(pack_kernel, block, half, piece),
        out_shape=tuple(outs),
        in_specs=specs,
        out_specs=(VMEM,) * len(outs),
        scratch_shapes=[
            pltpu.VMEM(sources[-1].shape, jnp.int32),
            pltpu.SemaphoreType.DMA((3 * half + 2,)),
        ],
        name="pack",
        **params(1.2),
    )(*operands)


def columns_kernel(width, distance, first_ref, second_ref, *refs):
    out_ref = refs[-1]
    there = lax.div(lax.bitwise_xor(place()[2], distance), 2)
    out_ref[:BLOCK, :] = first_ref[:, columns_of(there, width)]
    out_ref[BLOCK:, :] = second_ref[:, columns_of(there, width)]


def columns_for(distance, blocks, after):
    model_width = blocks[0][3].shape[1]
    width = 2 * model_width // lax.axis_size("dp")
    return pl.pallas_call(
        functools.partial(columns_kernel, width, distance),
        out_shape=jax.ShapeDtypeStruct((2 * BLOCK, width), jnp.bfloat16),
        in_specs=[VMEM] * 2 + [ANY] * len(after),
        out_specs=VMEM,
        name=f"columns{distance}",
        **params(0.0),
    )(blocks[0][3], blocks[1][3], *after)


def own_kernel(scale, weight_ref, gain_ref, after_ref, weight_out_ref, gain_out_ref):
    shares = weight_out_ref.shape[0]
    first = pl.multiple_of(place()[2] * shares, shares)
    weight_out_ref[...] = weight_ref[pl.ds(first, shares), :].astype(jnp.float32) * scale
    gain = gain_ref[:, pl.ds(first, shares)]
    column = jnp.sum(jnp.where(diagonal(shares), gain, 0.0), axis=1, keepdims=True)
    gain_out_ref[...] = jnp.broadcast_to(column * scale, gain_out_ref.shape)


def columns_of(pair, width):
    return pl.ds(pl.multiple_of(pair * width, width), width)


def partial_kernel(shares, first, *refs):
    columns, refs = refs[:4], refs[4:]
    own_out_ref, *other_refs = refs[6:]
    kv_width = own_out_ref.shape[1]
    parts = [ref[...] for ref in refs[:6]]
    packed = refs[2]
    parts[2:3] = [packed[first:, at : at + kv_width] for at in range(0, packed.shape[1], kv_width)]
    value = jnp.concatenate(parts, axis=0)
    mine = lax.rem(place()[2], 2)

    def share(core):
        at = pl.ds(pl.multiple_of(core * shares, shares), shares)
        rows = jnp.concatenate([ref[:, at] for ref in columns], axis=0)
        return lax.dot_general(
            rows, value, (((0,), (0,)), ((), ())), preferred_element_type=jnp.float32
        )

    other = share(1 - mine).astype(jnp.bfloat16)
    for part, ref in enumerate(other_refs):
        ref[...] = other[part * (shares // 2) : (part + 1) * (shares // 2)]
    own_out_ref[...] = share(mine)


def diagonal(size):
    return lax.broadcasted_iota(jnp.int32, (size, size), 0) == lax.broadcasted_iota(
        jnp.int32, (size, size), 1
    )


def finish_kernel(half, own_ref, first_ref, second_ref, weight_ref, gain_ref, *refs):
    pieces = refs[:half]
    rows_ref, out_ref, gain_out_ref, sems = refs[half:]
    side, at, _ = place()
    piece = BLOCK // half
    copies = []
    for block in range(2):
        for k in range(half):
            replica = (side if block == 0 else 1 - side) * half + lax.bitwise_xor(at, k)
            rows = pl.ds(pl.multiple_of(replica * piece, piece), piece)
            source = pieces[k].at[pl.ds(block * piece, piece)]
            made = pltpu.make_async_copy(source, rows_ref.at[rows], sems.at[block * half + k])
            made.start()
            copies.append(made)
    other = jnp.concatenate([first_ref[...], second_ref[...]], axis=0)
    total = own_ref[...] + other.astype(jnp.float32)
    out_ref[...] = total * gain_ref[:, :1]
    sums = jnp.sum(total * weight_ref[...], axis=1, keepdims=True)
    gain_out_ref[...] = jnp.sum(
        jnp.where(diagonal(total.shape[0]), sums, 0.0), axis=0, keepdims=True
    )
    for made in copies:
        made.wait()


def direct(hidden, query, key, segments, weight, norm_gain, upstream):
    tokens, model_width = hidden.shape
    kv_width = key.shape[1]
    replicas = lax.axis_size("dp")
    layers = lax.axis_size("section")
    half = replicas // 2
    piece = tokens // replicas
    shares = model_width // replicas

    def swap(array, k):
        return lax.ppermute(array, "dp", [(i, i ^ k) for i in range(replicas)])

    count = 2 * half
    bf16 = jnp.bfloat16
    sources = (query, key, hidden, upstream, segments)
    pieces, ups = [], []
    for b in range(2):
        *packed, up = pack(b, half, piece, sources, weight if b else None)
        if b:
            turned, *packed = packed
        pieces.append([packed[0]] + [swap(packed[k], k) for k in range(1, half)])
        ups.append(swap(up, half) if b else up)
    whole = slice(0, UNIT)
    scale = float(tokens * replicas) ** (-0.5)
    blocks, kept, after = [], [], []
    for b in range(2):
        block = block_probs(pieces[b], ups[b], BLOCK, model_width, kv_width, after)
        late, early = (ups[b], LATE), (ups[b], EARLY)
        first = tick_step(0, [late], block, turned, norm_gain, name=UNITS[2 * b])
        second = tick_step(
            0, [late, early], block, turned, norm_gain, after=[first[0]], name=UNITS[2 * b + 1]
        )
        blocks.append(block)
        kept += [[first], [second]]
        after = [second[0]]

    for tick in range(1, layers):
        hop = [(layers - tick, layers - 1 - tick)]
        grads = [(lax.ppermute(unit[-1][0], "section", hop), whole) for unit in kept]
        last = tick == layers - 1
        after, done = [kept[3][-1][0]], []
        if tick == layers - 2:
            own_weight, own_gain = pl.pallas_call(
                functools.partial(own_kernel, scale),
                out_shape=(
                    jax.ShapeDtypeStruct((shares, kv_width), jnp.float32),
                    jax.ShapeDtypeStruct((shares, 128), jnp.float32),
                ),
                in_specs=[VMEM, VMEM, ANY],
                out_specs=(VMEM, VMEM),
                name="own",
                **params(0.0),
            )(near(weight), norm_gain, *after)
            columns = {6: swap(columns_for(6, blocks, after + [own_gain]), 6)}
        if last:
            waits = after + [columns[6]]
            columns.update({k: swap(columns_for(k, blocks, waits), k) for k in (2, 4)})
        for u in range(4):
            needs = grads[u - 1 : u + 1] if u % 2 else grads[u : u + 1]
            late = []
            if last and u == 1:
                late = [done[0][1]]
            if last and u == 3:
                late = [done[2][1], done[0][0], done[1][0], done[2][0], done[1][1]]
                first_values = {k: swap(done[1][1], k) for k in (2, 6)}
                columns[0] = columns_for(0, blocks, after)
                after = after + [columns[2], columns[4], first_values[2], first_values[6]]
            done.append(
                tick_step(
                    tick, needs, blocks[u // 2], turned, norm_gain, kept[u] if last else (), late,
                    after, name=UNITS[u],
                )
            )
            after = [done[u][0]]
            kept[u].append(done[u])
    values, last_value, *rows = done[3]
    rows = [rows[0]] + [swap(rows[k], k) for k in range(1, half)]
    values = [values, first_values[2], rows[2], swap(values, 4)]
    values += [first_values[6], swap(last_value, 6)]
    own, *other = pl.pallas_call(
        functools.partial(partial_kernel, shares, 2 * piece),
        out_shape=(jax.ShapeDtypeStruct((shares, kv_width), jnp.float32),)
        + (jax.ShapeDtypeStruct((shares // 2, kv_width), bf16),) * 2,
        in_specs=[VMEM] * 10,
        out_specs=(VMEM,) * 3,
        name="weight_partial",
        **params(0.0),
    )(*[columns[k] for k in (0, 2, 4, 6)], *values)
    other = [swap(part, 1) for part in other]
    input_grad, weight_grad, gain_grad = pl.pallas_call(
        functools.partial(finish_kernel, half),
        out_shape=(
            jax.ShapeDtypeStruct((tokens, model_width), bf16),
            jax.ShapeDtypeStruct((shares, kv_width), jnp.float32),
            jax.ShapeDtypeStruct((1, shares), jnp.float32),
        ),
        in_specs=[VMEM] * (5 + half),
        out_specs=(ANY, VMEM, VMEM),
        scratch_shapes=[pltpu.SemaphoreType.DMA((count,))],
        name="finish",
        **params(0.0),
    )(own, *other, own_weight, own_gain, *rows)
    return input_grad[None], weight_grad[None], gain_grad


def weight_kernel(scale, columns_ref, value_ref, weight_ref, gain_ref, out_ref, gain_out_ref):
    total = lax.dot_general(
        columns_ref[...], value_ref[...], (((0,), (0,)), ((), ())),
        preferred_element_type=jnp.float32,
    ) * scale
    out_ref[...] = total * gain_ref[...]
    product = total * weight_ref[...].astype(jnp.float32)
    sums = lax.dot_general(
        jnp.ones((8, product.shape[1]), jnp.float32), product, (((1,), (1,)), ((), ())),
        preferred_element_type=jnp.float32, precision=lax.Precision.HIGHEST,
    )
    gain_out_ref[...] = sums[:1]


def grouped(hidden, query, key, segments, weight, norm_gain, upstream):
    tokens, model_width = hidden.shape
    kv_width = key.shape[1]
    replicas = lax.axis_size("dp")
    layers = lax.axis_size("section")
    half = replicas // 2
    me = lax.axis_index("dp")
    section = lax.axis_index("section")
    side = me // half
    groups = [list(range(half)), list(range(half, replicas))]
    across = [(i, (i + half) % replicas) for i in range(replicas)]
    shares = model_width // replicas

    def rows_of(array, which, axis=0):
        at = side if which == 0 else 1 - side
        return lax.dynamic_slice_in_dim(array, at * BLOCK, BLOCK, axis)

    def regroup(array):
        return lax.all_to_all(
            array, "dp", split_axis=0, concat_axis=0, axis_index_groups=groups, tiled=True
        )

    def spread(array):
        return lax.all_to_all(array, "dp", split_axis=0, concat_axis=0, tiled=True)

    turned = turn(weight)
    blocks, grads = [], []
    for which in range(2):
        up = rows_of(upstream, which)
        seg = jnp.broadcast_to(segments, (16, 2 * BLOCK)).astype(jnp.bfloat16)
        if which == 1:
            up = lax.ppermute(up, "dp", across)
            seg = lax.ppermute(seg, "dp", across)
        packed = jnp.concatenate(
            [rows_of(query, which), rows_of(key, which), rows_of(hidden, which)], axis=1
        )
        blocks.append(block_probs([regroup(packed)], seg, 0, model_width, kv_width))
        grads.append(up)

    def layer(tick, which, grad, kept):
        live = (section == layers - 1 - tick).astype(jnp.int32)[None]
        return layer_step(live, grad, blocks[which], turned, norm_gain, kept)

    held = [layer(0, which, grads[which], ()) for which in range(2)]
    hops = [(i, i - 1) for i in range(1, layers)]

    def step(tick, held):
        grads = [lax.ppermute(kept[0], "section", hops) for kept in held]
        return [layer(tick, which, grads[which], held[which]) for which in range(2)]

    held = lax.fori_loop(1, layers, step, held)

    columns, values, stored = [], [], []
    for which in range(2):
        block = blocks[which][3].reshape(BLOCK, replicas, shares).transpose(1, 0, 2)
        columns.append(spread(block.reshape(replicas * BLOCK, shares)))
        out, value = held[which]
        stored.append(regroup(out))
        values.append(spread(jnp.tile(value, (replicas, 1))))
    ordered = jnp.where(
        side == 0, jnp.concatenate(stored, axis=0), jnp.concatenate(stored[::-1], axis=0)
    )
    own_weight = lax.dynamic_slice_in_dim(weight, me * shares, shares, 0)
    own_gain = lax.dynamic_slice_in_dim(norm_gain[0], me * shares, shares, 0)
    scale = float(tokens * replicas) ** (-0.5)
    weight_grad, gain_grad = pl.pallas_call(
        functools.partial(weight_kernel, scale),
        out_shape=(
            jax.ShapeDtypeStruct((shares, kv_width), jnp.float32),
            jax.ShapeDtypeStruct((1, shares), jnp.float32),
        ),
        in_specs=[VMEM] * 4,
        out_specs=(VMEM, VMEM),
        name="weight_grad",
    )(
        jnp.concatenate(columns, axis=0),
        jnp.concatenate(values, axis=0),
        own_weight,
        own_gain[:, None],
    )
    return ordered[None], weight_grad[None], gain_grad


def on_device(hidden_in, queries, keys, segments, value_weight, norm_gain, upstream):
    replicas = lax.axis_size("dp")
    piece = hidden_in.shape[1] // replicas
    plan = direct if piece % 16 == 0 and replicas == 8 else grouped
    return plan(
        hidden_in[0], queries[0], keys[0], segments, value_weight[0], norm_gain, upstream
    )


def solution(mesh):
    in_specs = (
        P("section", "dp", None),
        P("section", "dp", None),
        P("section", "dp", None),
        P("dp", None),
        P("section", None, None),
        P("section", None),
        P("dp", None),
    )
    out_specs = (P("section", "dp", None), P("section", "dp", None), P("section", "dp"))
    return jax.shard_map(
        on_device, mesh=mesh, in_specs=in_specs, out_specs=out_specs, check_vma=False
    )
```

```python
import functools

import jax
import jax.numpy as jnp
from jax import lax
from jax.experimental import pallas as pl
from jax.experimental.pallas import tpu as pltpu
from jax.sharding import PartitionSpec as P

HEAD_FEATURES = 128
BLOCK = 64
UNIT = 32
EPSILON = 1e-06
MASKED = -1e30
OUTS = {2: 3, 5: 6}
UNITS = ("a_late", "a_early", "b_late", "b_early")
VMEM = pl.BlockSpec(memory_space=pltpu.VMEM)
SMEM = pl.BlockSpec(memory_space=pltpu.SMEM)


ANY = pl.BlockSpec(memory_space=pl.ANY)


LATE, EARLY = slice(UNIT, BLOCK), slice(0, UNIT)


def params(microseconds):
    flops = int(microseconds * 1.15e9)
    return dict(
        compiler_params=pltpu.CompilerParams(vmem_limit_bytes=16 << 20),
        cost_estimate=pl.CostEstimate(flops=flops, bytes_accessed=0, transcendentals=0),
    )


def near(array):
    return pltpu.with_memory_space_constraint(array, pltpu.VMEM)


def place():
    half = lax.axis_size("dp") // 2
    me = lax.axis_index("dp")
    return lax.div(me, half), lax.rem(me, half), me


def probs_kernel(count, seg_row, model_width, kv_width, *refs):
    pieces, seg_ref = refs[:count], refs[count]
    late_ref, early_ref, inv_ref, x_ref, rows_ref = refs[-5:]
    heads = model_width // kv_width
    rows = BLOCK // count
    side, at, _ = place()
    for k, piece in enumerate(pieces):
        if count == 1:
            rows_ref[...] = piece[...]
        else:
            first = pl.multiple_of(lax.bitwise_xor(at, k) * rows, rows)
            rows_ref[pl.ds(first, rows), :] = piece[...]

    def iota(shape, axis):
        return lax.broadcasted_iota(jnp.int32, shape, axis)

    seg = seg_ref[seg_row : seg_row + 16, : 2 * BLOCK].astype(jnp.float32)[:1]
    shape = (BLOCK, 2 * BLOCK)
    wanted = iota(shape, 1) == side * BLOCK + iota(shape, 0)
    ids = jnp.sum(jnp.where(wanted, seg, 0.0), axis=1, keepdims=True)
    key_code = ids * BLOCK + iota((BLOCK, 1), 0).astype(jnp.float32)
    list_start = ids * BLOCK
    shape = (BLOCK, heads * BLOCK)
    column = iota(shape, 1)
    query_at = lax.rem(column, UNIT) + jnp.where(column < heads * UNIT, UNIT, 0)
    same = iota(shape, 0) == query_at
    query_code = jnp.sum(jnp.where(same, key_code, 0.0), axis=0, keepdims=True)
    query_start = jnp.sum(jnp.where(same, list_start, 0.0), axis=0, keepdims=True)
    allowed = (key_code <= query_code) & (key_code >= query_start)
    for c in range(kv_width // HEAD_FEATURES):
        first = c * heads * HEAD_FEATURES
        query_stack = jnp.concatenate(
            [
                rows_ref[part, first + h * HEAD_FEATURES : first + (h + 1) * HEAD_FEATURES]
                for part in (LATE, EARLY)
                for h in range(heads)
            ],
            axis=0,
        )
        key_first = model_width + c * HEAD_FEATURES
        keys = rows_ref[:, key_first : key_first + HEAD_FEATURES]
        scores = lax.dot_general(
            keys, query_stack, (((1,), (1,)), ((), ())), preferred_element_type=jnp.float32
        ) * HEAD_FEATURES ** (-0.5)
        scores = jnp.where(allowed, scores, MASKED)
        exp_scores = jnp.exp(scores - jnp.max(scores, axis=0, keepdims=True))
        total = jnp.sum(exp_scores, axis=0, keepdims=True)
        probs = (exp_scores / total).astype(jnp.bfloat16)
        late_ref[c] = probs[LATE, : heads * UNIT]
        early_ref[c] = probs[EARLY]
    hidden = rows_ref[:, model_width + kv_width :]
    x_ref[...] = hidden
    x = hidden.astype(jnp.float32)
    mean_square = jnp.mean(x * x, axis=1, keepdims=True)
    inv_ref[...] = jnp.broadcast_to(lax.rsqrt(mean_square + EPSILON), inv_ref.shape)


def block_probs(pieces, seg, seg_row, model_width, kv_width, after=()):
    heads = model_width // kv_width
    key_heads = kv_width // HEAD_FEATURES
    operands = [near(piece) for piece in pieces] + [near(seg)]
    specs = [VMEM] * len(operands) + [ANY] * len(after)
    operands += after
    return pl.pallas_call(
        functools.partial(probs_kernel, len(pieces), seg_row, model_width, kv_width),
        out_shape=(
            jax.ShapeDtypeStruct((key_heads, UNIT, heads * UNIT), jnp.bfloat16),
            jax.ShapeDtypeStruct((key_heads, UNIT, heads * BLOCK), jnp.bfloat16),
            jax.ShapeDtypeStruct((BLOCK, 128), jnp.float32),
            jax.ShapeDtypeStruct((BLOCK, model_width), jnp.bfloat16),
        ),
        in_specs=specs,
        out_specs=(VMEM,) * 4,
        scratch_shapes=[pltpu.VMEM((BLOCK, 2 * model_width + kv_width), jnp.bfloat16)],
        name="probs",
        **params(0.35 if after else 2.0),
    )(*operands)


def unit_math(rows, grads, probs_ref, x_ref, inv_ref, turned_ref, gain_ref, scaled_ref, store, value_ref):
    kv_width, model_width = turned_ref.shape
    heads = model_width // kv_width
    chunk = min(512, model_width)
    inv = inv_ref[rows, :1]
    values = []
    for c in range(kv_width // HEAD_FEATURES):
        first = c * heads * HEAD_FEATURES
        grad_stack = jnp.concatenate(
            [
                grad_ref[part, first + h * HEAD_FEATURES : first + (h + 1) * HEAD_FEATURES]
                for grad_ref, part in grads
                for h in range(heads)
            ],
            axis=0,
        )
        values.append(
            jnp.dot(probs_ref[c], grad_stack, preferred_element_type=jnp.float32).astype(
                jnp.bfloat16
            )
        )
    value = jnp.concatenate(values, axis=1)
    value_ref[...] = (value.astype(jnp.float32) * inv).astype(jnp.bfloat16)
    inner = jnp.zeros((UNIT, 1), jnp.float32)
    for first in range(0, model_width, chunk):
        columns = slice(first, first + chunk)
        normed_grad = jnp.dot(value, turned_ref[:, columns], preferred_element_type=jnp.float32)
        scaled = normed_grad * gain_ref[:, columns]
        scaled_ref[:, columns] = scaled
        x = x_ref[rows, columns].astype(jnp.float32)
        inner = inner + jnp.sum(x * scaled, axis=1, keepdims=True)
    pull = inner * (inv * inv / model_width)
    grad_ref, part = grads[-1]
    for first in range(0, model_width, chunk):
        columns = slice(first, first + chunk)
        x = x_ref[rows, columns].astype(jnp.float32)
        change = inv * (scaled_ref[:, columns] - x * pull)
        grad = grad_ref[part, columns].astype(jnp.float32)
        store(columns, (grad + change).astype(jnp.bfloat16))


def turn_kernel(weight_ref, *refs):
    turned_ref = refs[-1]
    step = min(256, weight_ref.shape[0])
    for first in range(0, weight_ref.shape[0], step):
        turned_ref[:, first : first + step] = weight_ref[first : first + step, :].T


def turn(weight, after=()):
    return pl.pallas_call(
        turn_kernel,
        out_shape=jax.ShapeDtypeStruct(weight.shape[::-1], weight.dtype),
        in_specs=[VMEM] + [ANY] * len(after),
        out_specs=VMEM,
        name="turn",
        **params(1.5),
    )(near(weight), *after)


def layer_kernel(
    live_ref, grad_ref, late_ref, early_ref, inv_ref, x_ref, turned_ref, gain_ref, *rest
):
    out_ref, value_ref, scaled_ref = rest[-3:]
    if len(rest) == 5:

        @pl.when(live_ref[0] == 0)
        def _():
            out_ref[...] = rest[0][...]
            value_ref[...] = rest[1][...]

    @pl.when(live_ref[0] == 1)
    def _():
        for rows, parts, probs_ref in ((LATE, [LATE], late_ref), (EARLY, [LATE, EARLY], early_ref)):

            def store(columns, part, rows=rows):
                out_ref[rows, columns] = part

            grads = [(grad_ref, part) for part in parts]
            unit_math(
                rows, grads, probs_ref, x_ref, inv_ref, turned_ref, gain_ref, scaled_ref, store,
                value_ref.at[rows],
            )


def layer_step(live, grad, block, turned, gain, held=()):
    kv_width, model_width = turned.shape
    operands = [live, grad, *block, turned, gain, *held]
    return pl.pallas_call(
        layer_kernel,
        out_shape=(
            jax.ShapeDtypeStruct((BLOCK, model_width), jnp.bfloat16),
            jax.ShapeDtypeStruct((BLOCK, kv_width), jnp.bfloat16),
        ),
        in_specs=[SMEM] + [VMEM] * (len(operands) - 1),
        out_specs=(VMEM, VMEM),
        scratch_shapes=[pltpu.VMEM((UNIT, model_width), jnp.float32)],
        name="layer",
        **params(1.1),
    )(*operands)


def tick_kernel(tick, rows, parts, kept, late, *refs):
    grads = list(zip(refs, parts))
    probs_ref, inv_ref, x_ref, turned_ref, gain_ref = refs[len(parts) : len(parts) + 5]
    refs = refs[len(parts) + 5 :]
    earlier, refs = refs[: 2 * kept], refs[2 * kept :]
    late_refs = refs[:late]
    kv_width, model_width = turned_ref.shape
    turn = lax.axis_size("section") - 1 - lax.axis_index("section")
    if late:
        outs, (scaled_ref, blocks_ref, value_ref) = refs[late : -3], refs[-3:]
        outs = outs[len(outs) - OUTS[late] :]
    else:
        outs, scaled_ref = refs[-3:-1], refs[-1]
        value_ref = outs[1]
    first_row = BLOCK if late > 2 else 0

    def store(columns, part):
        if late:
            blocks_ref[first_row : first_row + UNIT, columns] = part
        if late <= 2:
            outs[0][:, columns] = part

    @pl.when(turn == tick)
    def _():
        unit_math(
            rows, grads, probs_ref, x_ref, inv_ref, turned_ref, gain_ref, scaled_ref, store,
            value_ref,
        )

    for at in range(kept):

        @pl.when(turn == at)
        def _(at=at):
            store(slice(None), earlier[2 * at][...])
            value_ref[...] = earlier[2 * at + 1][...]

    if not late:
        return
    values = jnp.concatenate([value_ref[...], late_refs[0][...]], axis=0)
    blocks_ref[first_row + UNIT : first_row + BLOCK, :] = late_refs[1][...]
    outs[1][...] = values
    if late > 2:
        late_a_ref, early_a_ref, value_a_ref = late_refs[2:]
        blocks_ref[EARLY, :] = early_a_ref[...]
        blocks_ref[LATE, :] = late_a_ref[...]
        outs[0][:BLOCK, :] = value_a_ref[...]
        outs[0][BLOCK:, :] = values
    at = place()[1]
    pieces = {2: outs[2]} if late == 2 else dict(enumerate(outs[2:]))
    piece = BLOCK * kv_width // model_width
    for k, out_ref in pieces.items():
        first = pl.multiple_of(lax.bitwise_xor(at, k) * piece, piece)
        here = blocks_ref[pl.ds(first_row + first, piece), :]
        if k == 2:
            out_ref[:piece, :] = here
            for g in range(model_width // kv_width):
                out_ref[piece:, g * kv_width : (g + 1) * kv_width] = values[
                    g * piece : (g + 1) * piece
                ]
        else:
            out_ref[:piece, :] = blocks_ref[pl.ds(first, piece), :]
            out_ref[piece:, :] = here


def tick_step(tick, grads, block, turned, gain, kept=(), late=(), after=(), name=""):
    kv_width, model_width = turned.shape
    low = len(grads) == 2
    arrays = [grad for grad, _ in grads]
    arrays += [block[1] if low else block[0], block[2], block[3], turned, gain]
    arrays += [array for pair in kept for array in pair]
    arrays += late
    operands = [near(array) for array in arrays]
    specs = [VMEM] * len(operands) + [ANY] * len(after)
    bf16 = jnp.bfloat16
    scratch = [pltpu.VMEM((UNIT, model_width), jnp.float32)]
    rows, value = (UNIT, model_width), (UNIT, kv_width)
    shapes = [rows, value]
    if late:
        half = lax.axis_size("dp") // 2
        scratch += [pltpu.VMEM((2 * BLOCK, model_width), bf16), pltpu.VMEM(value, bf16)]
        pieces = (2 * BLOCK // half, model_width)
        shapes = [rows, (BLOCK, kv_width), pieces]
    if len(late) > 2:
        shapes = [(2 * BLOCK, kv_width), (BLOCK, kv_width)] + [pieces] * half
    parts = [part for _, part in grads]
    return pl.pallas_call(
        functools.partial(
            tick_kernel, tick, EARLY if low else LATE, parts, len(kept), len(late)
        ),
        out_shape=tuple(jax.ShapeDtypeStruct(shape, bf16) for shape in shapes),
        in_specs=specs,
        out_specs=(VMEM,) * len(shapes),
        scratch_shapes=scratch,
        name=f"tick{tick}_{name}",
        **params(1.0 if kept else 0.0),
    )(*operands, *after)


def pack_kernel(block, half, piece, query_ref, key_ref, hidden_ref, up_ref, seg_ref, *rest):
    up_out_ref, seg_in_ref, sems = rest[-3:]
    packed = rest[-3 - half : -3]
    rest = rest[: -3 - half]
    side, at, _ = place()
    there = side if block == 0 else 1 - side
    copies = []

    def copy(source, target):
        made = pltpu.make_async_copy(source, target, sems.at[len(copies)])
        made.start()
        copies.append(made)

    copy(seg_ref, seg_in_ref)
    for k in range(half):
        replica = there * half + lax.bitwise_xor(at, k)
        rows = pl.ds(pl.multiple_of(replica * piece, piece), piece)
        first = 0
        for source in (query_ref, key_ref, hidden_ref):
            width = source.shape[1]
            copy(source.at[rows], packed[k].at[:, pl.ds(first, width)])
            first += width
    rows = pl.ds(pl.multiple_of(there * BLOCK, BLOCK), BLOCK)
    copy(up_ref.at[rows], up_out_ref.at[pl.ds(0, BLOCK)])
    up_out_ref[BLOCK:, :] = jnp.zeros((16, up_out_ref.shape[1]), jnp.bfloat16)
    copies[0].wait()
    ids = seg_in_ref[...].astype(jnp.float32)
    up_out_ref[BLOCK:, : ids.shape[1]] = jnp.broadcast_to(ids, (16, ids.shape[1])).astype(
        jnp.bfloat16
    )
    if block == 1:
        turn_kernel(rest[0], rest[-1])
    for made in copies[1:]:
        made.wait()


def pack(block, half, piece, sources, weight=None):
    model_width = sources[0].shape[1]
    width = sum(source.shape[1] for source in sources[:3])
    bf16 = jnp.bfloat16
    operands = [pltpu.with_memory_space_constraint(array, pltpu.HBM) for array in sources]
    specs = [pl.BlockSpec(memory_space=pltpu.HBM)] * len(sources)
    outs = [jax.ShapeDtypeStruct((piece, width), bf16)] * half
    outs.append(jax.ShapeDtypeStruct((BLOCK + 16, model_width), bf16))
    if weight is not None:
        operands.append(near(weight))
        specs.append(VMEM)
        outs = [jax.ShapeDtypeStruct(weight.shape[::-1], bf16)] + outs
    return pl.pallas_call(
        functools.partial(pack_kernel, block, half, piece),
        out_shape=tuple(outs),
        in_specs=specs,
        out_specs=(VMEM,) * len(outs),
        scratch_shapes=[
            pltpu.VMEM(sources[-1].shape, jnp.int32),
            pltpu.SemaphoreType.DMA((3 * half + 2,)),
        ],
        name="pack",
        **params(1.2),
    )(*operands)


def columns_kernel(width, distance, first_ref, second_ref, *refs):
    out_ref = refs[-1]
    there = lax.div(lax.bitwise_xor(place()[2], distance), 2)
    out_ref[:BLOCK, :] = first_ref[:, columns_of(there, width)]
    out_ref[BLOCK:, :] = second_ref[:, columns_of(there, width)]


def columns_for(distance, blocks, after):
    model_width = blocks[0][3].shape[1]
    width = 2 * model_width // lax.axis_size("dp")
    return pl.pallas_call(
        functools.partial(columns_kernel, width, distance),
        out_shape=jax.ShapeDtypeStruct((2 * BLOCK, width), jnp.bfloat16),
        in_specs=[VMEM] * 2 + [ANY] * len(after),
        out_specs=VMEM,
        name=f"columns{distance}",
        **params(0.0),
    )(blocks[0][3], blocks[1][3], *after)


def own_kernel(scale, weight_ref, gain_ref, after_ref, weight_out_ref, gain_out_ref):
    shares = weight_out_ref.shape[0]
    first = pl.multiple_of(place()[2] * shares, shares)
    weight_out_ref[...] = weight_ref[pl.ds(first, shares), :].astype(jnp.float32) * scale
    gain = gain_ref[:, pl.ds(first, shares)]
    column = jnp.sum(jnp.where(diagonal(shares), gain, 0.0), axis=1, keepdims=True)
    gain_out_ref[...] = jnp.broadcast_to(column * scale, gain_out_ref.shape)


def columns_of(pair, width):
    return pl.ds(pl.multiple_of(pair * width, width), width)


def partial_kernel(shares, first, *refs):
    columns, refs = refs[:4], refs[4:]
    own_out_ref, *other_refs = refs[6:]
    kv_width = own_out_ref.shape[1]
    parts = []
    for ref in refs[:6]:
        for at in range(0, ref.shape[1], kv_width):
            parts.append(ref[first:, at : at + kv_width] if ref.shape[1] > kv_width else ref[...])
    value = jnp.concatenate(parts, axis=0)
    mine = lax.rem(place()[2], 2)

    def share(core):
        at = pl.ds(pl.multiple_of(core * shares, shares), shares)
        rows = jnp.concatenate([ref[:, at] for ref in columns], axis=0)
        return lax.dot_general(
            rows, value, (((0,), (0,)), ((), ())), preferred_element_type=jnp.float32
        )

    other = share(1 - mine).astype(jnp.bfloat16)
    for part, ref in enumerate(other_refs):
        ref[...] = other[part * (shares // 2) : (part + 1) * (shares // 2)]
    own_out_ref[...] = share(mine)


def diagonal(size):
    return lax.broadcasted_iota(jnp.int32, (size, size), 0) == lax.broadcasted_iota(
        jnp.int32, (size, size), 1
    )


def finish_kernel(half, own_ref, first_ref, second_ref, weight_ref, gain_ref, *refs):
    first_rows_ref, pieces = refs[0], refs[1 : 1 + half]
    rows_ref, out_ref, gain_out_ref, sums_ref, sems = refs[1 + half :]
    side, at, _ = place()
    piece = BLOCK // half
    copies = []

    def copy(source, target):
        made = pltpu.make_async_copy(source, target, sems.at[len(copies)])
        made.start()
        copies.append(made)

    for block in range(2):
        for k in range(half):
            replica = (side if block == 0 else 1 - side) * half + lax.bitwise_xor(at, k)
            rows = pl.ds(pl.multiple_of(replica * piece, piece), piece)
            source, first = pieces[k], block * piece
            if k == 2:
                source, first = (pieces[k] if block else first_rows_ref), 0
            copy(source.at[pl.ds(first, piece)], rows_ref.at[rows])
    shares = own_ref.shape[0]
    gain_sums = []
    for part, ref in enumerate((first_ref, second_ref)):
        rows = slice(part * (shares // 2), (part + 1) * (shares // 2))
        total = own_ref[rows, :] + ref[...].astype(jnp.float32)
        sums_ref[rows, :] = total * gain_ref[rows, :1]
        copy(sums_ref.at[rows], out_ref.at[rows])
        gain_sums.append(jnp.sum(total * weight_ref[rows, :], axis=1, keepdims=True))
    gain_out_ref[...] = jnp.sum(
        jnp.where(diagonal(shares), jnp.concatenate(gain_sums, axis=0), 0.0), axis=0, keepdims=True
    )
    for made in copies:
        made.wait()


def direct(hidden, query, key, segments, weight, norm_gain, upstream):
    tokens, model_width = hidden.shape
    kv_width = key.shape[1]
    replicas = lax.axis_size("dp")
    layers = lax.axis_size("section")
    half = replicas // 2
    piece = tokens // replicas
    shares = model_width // replicas

    def swap(array, k):
        return lax.ppermute(array, "dp", [(i, i ^ k) for i in range(replicas)])

    count = 2 * half
    bf16 = jnp.bfloat16
    sources = (query, key, hidden, upstream, segments)
    pieces, ups = [], []
    for b in range(2):
        *packed, up = pack(b, half, piece, sources, weight if b else None)
        if b:
            turned, *packed = packed
        pieces.append([packed[0]] + [swap(packed[k], k) for k in range(1, half)])
        ups.append(swap(up, half) if b else up)
    whole = slice(0, UNIT)
    scale = float(tokens * replicas) ** (-0.5)
    blocks, kept, after = [], [], []
    for b in range(2):
        block = block_probs(pieces[b], ups[b], BLOCK, model_width, kv_width, after)
        late, early = (ups[b], LATE), (ups[b], EARLY)
        first = tick_step(0, [late], block, turned, norm_gain, name=UNITS[2 * b])
        second = tick_step(
            0, [late, early], block, turned, norm_gain, after=[first[0]], name=UNITS[2 * b + 1]
        )
        blocks.append(block)
        kept += [[first], [second]]
        after = [second[0]]

    for tick in range(1, layers):
        hop = [(layers - tick, layers - 1 - tick)]
        grads = [(lax.ppermute(unit[-1][0], "section", hop), whole) for unit in kept]
        last = tick == layers - 1
        after, done = [kept[3][-1][0]], []
        if tick == layers - 2:
            own_weight, own_gain = pl.pallas_call(
                functools.partial(own_kernel, scale),
                out_shape=(
                    jax.ShapeDtypeStruct((shares, kv_width), jnp.float32),
                    jax.ShapeDtypeStruct((shares, 128), jnp.float32),
                ),
                in_specs=[VMEM, VMEM, ANY],
                out_specs=(VMEM, VMEM),
                name="own",
                **params(0.0),
            )(near(weight), norm_gain, *after)
            columns = {6: swap(columns_for(6, blocks, after + [own_gain]), 6)}
        if last:
            waits = after + [columns[6]]
            columns.update({k: swap(columns_for(k, blocks, waits), k) for k in (2, 4)})
        for u in range(4):
            needs = grads[u - 1 : u + 1] if u % 2 else grads[u : u + 1]
            late = []
            if last and u == 1:
                late = [done[0][1], done[0][0]]
            if last and u == 3:
                late = [done[2][1], done[2][0], done[0][0], done[1][0], done[1][1]]
                first_value, first_rows = swap(done[1][1], 6), swap(done[1][2], 2)
                after = after + [columns[2], columns[4], first_value]
            done.append(
                tick_step(
                    tick, needs, blocks[u // 2], turned, norm_gain, kept[u] if last else (), late,
                    after, name=UNITS[u],
                )
            )
            after = [done[u][0]]
            kept[u].append(done[u])
    values, last_value, *rows = done[3]
    rows = [rows[0]] + [swap(rows[k], k) for k in range(1, half)]
    columns[0] = columns_for(0, blocks, [values, first_rows])
    values = [values, first_rows, rows[2], swap(values, 4), first_value, swap(last_value, 6)]
    own, *other = pl.pallas_call(
        functools.partial(partial_kernel, shares, piece),
        out_shape=(jax.ShapeDtypeStruct((shares, kv_width), jnp.float32),)
        + (jax.ShapeDtypeStruct((shares // 2, kv_width), bf16),) * 2,
        in_specs=[VMEM] * 10,
        out_specs=(VMEM,) * 3,
        name="weight_partial",
        **params(0.0),
    )(*[columns[k] for k in (0, 2, 4, 6)], *values)
    other = [swap(part, 1) for part in other]
    input_grad, weight_grad, gain_grad = pl.pallas_call(
        functools.partial(finish_kernel, half),
        out_shape=(
            jax.ShapeDtypeStruct((tokens, model_width), bf16),
            jax.ShapeDtypeStruct((shares, kv_width), jnp.float32),
            jax.ShapeDtypeStruct((1, shares), jnp.float32),
        ),
        in_specs=[VMEM] * (6 + half),
        out_specs=(ANY, ANY, VMEM),
        scratch_shapes=[
            pltpu.VMEM((shares, kv_width), jnp.float32),
            pltpu.SemaphoreType.DMA((count + 2,)),
        ],
        name="finish",
        **params(0.0),
    )(own, *other, own_weight, own_gain, first_rows, *rows)
    return input_grad[None], weight_grad[None], gain_grad


def weight_kernel(scale, columns_ref, value_ref, weight_ref, gain_ref, out_ref, gain_out_ref):
    total = lax.dot_general(
        columns_ref[...], value_ref[...], (((0,), (0,)), ((), ())),
        preferred_element_type=jnp.float32,
    ) * scale
    out_ref[...] = total * gain_ref[...]
    product = total * weight_ref[...].astype(jnp.float32)
    sums = lax.dot_general(
        jnp.ones((8, product.shape[1]), jnp.float32), product, (((1,), (1,)), ((), ())),
        preferred_element_type=jnp.float32, precision=lax.Precision.HIGHEST,
    )
    gain_out_ref[...] = sums[:1]


def grouped(hidden, query, key, segments, weight, norm_gain, upstream):
    tokens, model_width = hidden.shape
    kv_width = key.shape[1]
    replicas = lax.axis_size("dp")
    layers = lax.axis_size("section")
    half = replicas // 2
    me = lax.axis_index("dp")
    section = lax.axis_index("section")
    side = me // half
    groups = [list(range(half)), list(range(half, replicas))]
    across = [(i, (i + half) % replicas) for i in range(replicas)]
    shares = model_width // replicas

    def rows_of(array, which, axis=0):
        at = side if which == 0 else 1 - side
        return lax.dynamic_slice_in_dim(array, at * BLOCK, BLOCK, axis)

    def regroup(array):
        return lax.all_to_all(
            array, "dp", split_axis=0, concat_axis=0, axis_index_groups=groups, tiled=True
        )

    def spread(array):
        return lax.all_to_all(array, "dp", split_axis=0, concat_axis=0, tiled=True)

    turned = turn(weight)
    blocks, grads = [], []
    for which in range(2):
        up = rows_of(upstream, which)
        seg = jnp.broadcast_to(segments, (16, 2 * BLOCK)).astype(jnp.bfloat16)
        if which == 1:
            up = lax.ppermute(up, "dp", across)
            seg = lax.ppermute(seg, "dp", across)
        packed = jnp.concatenate(
            [rows_of(query, which), rows_of(key, which), rows_of(hidden, which)], axis=1
        )
        blocks.append(block_probs([regroup(packed)], seg, 0, model_width, kv_width))
        grads.append(up)

    def layer(tick, which, grad, kept):
        live = (section == layers - 1 - tick).astype(jnp.int32)[None]
        return layer_step(live, grad, blocks[which], turned, norm_gain, kept)

    held = [layer(0, which, grads[which], ()) for which in range(2)]
    hops = [(i, i - 1) for i in range(1, layers)]

    def step(tick, held):
        grads = [lax.ppermute(kept[0], "section", hops) for kept in held]
        return [layer(tick, which, grads[which], held[which]) for which in range(2)]

    held = lax.fori_loop(1, layers, step, held)

    columns, values, stored = [], [], []
    for which in range(2):
        block = blocks[which][3].reshape(BLOCK, replicas, shares).transpose(1, 0, 2)
        columns.append(spread(block.reshape(replicas * BLOCK, shares)))
        out, value = held[which]
        stored.append(regroup(out))
        values.append(spread(jnp.tile(value, (replicas, 1))))
    ordered = jnp.where(
        side == 0, jnp.concatenate(stored, axis=0), jnp.concatenate(stored[::-1], axis=0)
    )
    own_weight = lax.dynamic_slice_in_dim(weight, me * shares, shares, 0)
    own_gain = lax.dynamic_slice_in_dim(norm_gain[0], me * shares, shares, 0)
    scale = float(tokens * replicas) ** (-0.5)
    weight_grad, gain_grad = pl.pallas_call(
        functools.partial(weight_kernel, scale),
        out_shape=(
            jax.ShapeDtypeStruct((shares, kv_width), jnp.float32),
            jax.ShapeDtypeStruct((1, shares), jnp.float32),
        ),
        in_specs=[VMEM] * 4,
        out_specs=(VMEM, VMEM),
        name="weight_grad",
    )(
        jnp.concatenate(columns, axis=0),
        jnp.concatenate(values, axis=0),
        own_weight,
        own_gain[:, None],
    )
    return ordered[None], weight_grad[None], gain_grad


def on_device(hidden_in, queries, keys, segments, value_weight, norm_gain, upstream):
    replicas = lax.axis_size("dp")
    piece = hidden_in.shape[1] // replicas
    plan = direct if piece % 16 == 0 and replicas == 8 else grouped
    return plan(
        hidden_in[0], queries[0], keys[0], segments, value_weight[0], norm_gain, upstream
    )


def solution(mesh):
    in_specs = (
        P("section", "dp", None),
        P("section", "dp", None),
        P("section", "dp", None),
        P("dp", None),
        P("section", None, None),
        P("section", None),
        P("dp", None),
    )
    out_specs = (P("section", "dp", None), P("section", "dp", None), P("section", "dp"))
    return jax.shard_map(
        on_device, mesh=mesh, in_specs=in_specs, out_specs=out_specs, check_vma=False
    )
```

```python
import functools

import jax
import jax.numpy as jnp
from jax import lax
from jax.experimental import pallas as pl
from jax.experimental.pallas import tpu as pltpu
from jax.sharding import PartitionSpec as P

HEAD_FEATURES = 128
BLOCK = 64
UNIT = 32
EPSILON = 1e-06
MASKED = -1e30
OUTS = {2: 3, 5: 6}
UNITS = ("a_late", "a_early", "b_late", "b_early")
VMEM = pl.BlockSpec(memory_space=pltpu.VMEM)
SMEM = pl.BlockSpec(memory_space=pltpu.SMEM)


ANY = pl.BlockSpec(memory_space=pl.ANY)


LATE, EARLY = slice(UNIT, BLOCK), slice(0, UNIT)


def params(microseconds):
    flops = int(microseconds * 1.15e9)
    return dict(
        compiler_params=pltpu.CompilerParams(vmem_limit_bytes=16 << 20),
        cost_estimate=pl.CostEstimate(flops=flops, bytes_accessed=0, transcendentals=0),
    )


def near(array):
    return pltpu.with_memory_space_constraint(array, pltpu.VMEM)


def place():
    half = lax.axis_size("dp") // 2
    me = lax.axis_index("dp")
    return lax.div(me, half), lax.rem(me, half), me


def probs_kernel(count, seg_row, model_width, kv_width, *refs):
    pieces, seg_ref = refs[:count], refs[count]
    late_ref, early_ref, inv_ref, x_ref, rows_ref = refs[-5:]
    heads = model_width // kv_width
    rows = BLOCK // count
    side, at, _ = place()
    for k, piece in enumerate(pieces):
        if count == 1:
            rows_ref[...] = piece[...]
        else:
            first = pl.multiple_of(lax.bitwise_xor(at, k) * rows, rows)
            rows_ref[pl.ds(first, rows), :] = piece[...]

    def iota(shape, axis):
        return lax.broadcasted_iota(jnp.int32, shape, axis)

    seg = seg_ref[seg_row : seg_row + 16, : 2 * BLOCK].astype(jnp.float32)[:1]
    shape = (BLOCK, 2 * BLOCK)
    wanted = iota(shape, 1) == side * BLOCK + iota(shape, 0)
    ids = jnp.sum(jnp.where(wanted, seg, 0.0), axis=1, keepdims=True)
    key_code = ids * BLOCK + iota((BLOCK, 1), 0).astype(jnp.float32)
    list_start = ids * BLOCK
    shape = (BLOCK, heads * BLOCK)
    column = iota(shape, 1)
    query_at = lax.rem(column, UNIT) + jnp.where(column < heads * UNIT, UNIT, 0)
    same = iota(shape, 0) == query_at
    query_code = jnp.sum(jnp.where(same, key_code, 0.0), axis=0, keepdims=True)
    query_start = jnp.sum(jnp.where(same, list_start, 0.0), axis=0, keepdims=True)
    allowed = (key_code <= query_code) & (key_code >= query_start)
    for c in range(kv_width // HEAD_FEATURES):
        first = c * heads * HEAD_FEATURES
        query_stack = jnp.concatenate(
            [
                rows_ref[part, first + h * HEAD_FEATURES : first + (h + 1) * HEAD_FEATURES]
                for part in (LATE, EARLY)
                for h in range(heads)
            ],
            axis=0,
        )
        key_first = model_width + c * HEAD_FEATURES
        keys = rows_ref[:, key_first : key_first + HEAD_FEATURES]
        scores = lax.dot_general(
            keys, query_stack, (((1,), (1,)), ((), ())), preferred_element_type=jnp.float32
        ) * HEAD_FEATURES ** (-0.5)
        scores = jnp.where(allowed, scores, MASKED)
        exp_scores = jnp.exp(scores - jnp.max(scores, axis=0, keepdims=True))
        total = jnp.sum(exp_scores, axis=0, keepdims=True)
        probs = (exp_scores / total).astype(jnp.bfloat16)
        late_ref[c] = probs[LATE, : heads * UNIT]
        early_ref[c] = probs[EARLY]
    hidden = rows_ref[:, model_width + kv_width :]
    x_ref[...] = hidden
    x = hidden.astype(jnp.float32)
    mean_square = jnp.mean(x * x, axis=1, keepdims=True)
    inv_ref[...] = jnp.broadcast_to(lax.rsqrt(mean_square + EPSILON), inv_ref.shape)


def block_probs(pieces, seg, seg_row, model_width, kv_width, after=()):
    heads = model_width // kv_width
    key_heads = kv_width // HEAD_FEATURES
    operands = [near(piece) for piece in pieces] + [near(seg)]
    specs = [VMEM] * len(operands) + [ANY] * len(after)
    operands += after
    return pl.pallas_call(
        functools.partial(probs_kernel, len(pieces), seg_row, model_width, kv_width),
        out_shape=(
            jax.ShapeDtypeStruct((key_heads, UNIT, heads * UNIT), jnp.bfloat16),
            jax.ShapeDtypeStruct((key_heads, UNIT, heads * BLOCK), jnp.bfloat16),
            jax.ShapeDtypeStruct((BLOCK, 128), jnp.float32),
            jax.ShapeDtypeStruct((BLOCK, model_width), jnp.bfloat16),
        ),
        in_specs=specs,
        out_specs=(VMEM,) * 4,
        scratch_shapes=[pltpu.VMEM((BLOCK, 2 * model_width + kv_width), jnp.bfloat16)],
        name="probs",
        **params(0.35 if after else 2.0),
    )(*operands)


def unit_math(rows, grads, probs_ref, x_ref, inv_ref, turned_ref, gain_ref, scaled_ref, store, value_ref):
    kv_width, model_width = turned_ref.shape
    heads = model_width // kv_width
    chunk = min(512, model_width)
    inv = inv_ref[rows, :1]
    values = []
    for c in range(kv_width // HEAD_FEATURES):
        first = c * heads * HEAD_FEATURES
        grad_stack = jnp.concatenate(
            [
                grad_ref[part, first + h * HEAD_FEATURES : first + (h + 1) * HEAD_FEATURES]
                for grad_ref, part in grads
                for h in range(heads)
            ],
            axis=0,
        )
        values.append(
            jnp.dot(probs_ref[c], grad_stack, preferred_element_type=jnp.float32).astype(
                jnp.bfloat16
            )
        )
    value = jnp.concatenate(values, axis=1)
    value_ref[...] = (value.astype(jnp.float32) * inv).astype(jnp.bfloat16)
    inner = jnp.zeros((UNIT, 1), jnp.float32)
    for first in range(0, model_width, chunk):
        columns = slice(first, first + chunk)
        normed_grad = jnp.dot(value, turned_ref[:, columns], preferred_element_type=jnp.float32)
        scaled = normed_grad * gain_ref[:, columns]
        scaled_ref[:, columns] = scaled
        x = x_ref[rows, columns].astype(jnp.float32)
        inner = inner + jnp.sum(x * scaled, axis=1, keepdims=True)
    pull = inner * (inv * inv / model_width)
    grad_ref, part = grads[-1]
    for first in range(0, model_width, chunk):
        columns = slice(first, first + chunk)
        x = x_ref[rows, columns].astype(jnp.float32)
        change = inv * (scaled_ref[:, columns] - x * pull)
        grad = grad_ref[part, columns].astype(jnp.float32)
        store(columns, (grad + change).astype(jnp.bfloat16))


def turn_kernel(weight_ref, *refs):
    turned_ref = refs[-1]
    step = min(256, weight_ref.shape[0])
    for first in range(0, weight_ref.shape[0], step):
        turned_ref[:, first : first + step] = weight_ref[first : first + step, :].T


def turn(weight, after=()):
    return pl.pallas_call(
        turn_kernel,
        out_shape=jax.ShapeDtypeStruct(weight.shape[::-1], weight.dtype),
        in_specs=[VMEM] + [ANY] * len(after),
        out_specs=VMEM,
        name="turn",
        **params(1.5),
    )(near(weight), *after)


def layer_kernel(
    live_ref, grad_ref, late_ref, early_ref, inv_ref, x_ref, turned_ref, gain_ref, *rest
):
    out_ref, value_ref, scaled_ref = rest[-3:]
    if len(rest) == 5:

        @pl.when(live_ref[0] == 0)
        def _():
            out_ref[...] = rest[0][...]
            value_ref[...] = rest[1][...]

    @pl.when(live_ref[0] == 1)
    def _():
        for rows, parts, probs_ref in ((LATE, [LATE], late_ref), (EARLY, [LATE, EARLY], early_ref)):

            def store(columns, part, rows=rows):
                out_ref[rows, columns] = part

            grads = [(grad_ref, part) for part in parts]
            unit_math(
                rows, grads, probs_ref, x_ref, inv_ref, turned_ref, gain_ref, scaled_ref, store,
                value_ref.at[rows],
            )


def layer_step(live, grad, block, turned, gain, held=()):
    kv_width, model_width = turned.shape
    operands = [live, grad, *block, turned, gain, *held]
    return pl.pallas_call(
        layer_kernel,
        out_shape=(
            jax.ShapeDtypeStruct((BLOCK, model_width), jnp.bfloat16),
            jax.ShapeDtypeStruct((BLOCK, kv_width), jnp.bfloat16),
        ),
        in_specs=[SMEM] + [VMEM] * (len(operands) - 1),
        out_specs=(VMEM, VMEM),
        scratch_shapes=[pltpu.VMEM((UNIT, model_width), jnp.float32)],
        name="layer",
        **params(1.1),
    )(*operands)


def tick_kernel(tick, rows, parts, kept, late, *refs):
    grads = list(zip(refs, parts))
    probs_ref, inv_ref, x_ref, turned_ref, gain_ref = refs[len(parts) : len(parts) + 5]
    refs = refs[len(parts) + 5 :]
    earlier, refs = refs[: 2 * kept], refs[2 * kept :]
    late_refs = refs[:late]
    kv_width, model_width = turned_ref.shape
    turn = lax.axis_size("section") - 1 - lax.axis_index("section")
    if late:
        outs, (scaled_ref, blocks_ref, value_ref) = refs[late : -3], refs[-3:]
        outs = outs[len(outs) - OUTS[late] :]
    else:
        outs, scaled_ref = refs[-3:-1], refs[-1]
        value_ref = outs[1]
    first_row = BLOCK if late > 2 else 0

    def store(columns, part):
        if late:
            blocks_ref[first_row : first_row + UNIT, columns] = part
        if late <= 2:
            outs[0][:, columns] = part

    @pl.when(turn == tick)
    def _():
        unit_math(
            rows, grads, probs_ref, x_ref, inv_ref, turned_ref, gain_ref, scaled_ref, store,
            value_ref,
        )

    for at in range(kept):

        @pl.when(turn == at)
        def _(at=at):
            store(slice(None), earlier[2 * at][...])
            value_ref[...] = earlier[2 * at + 1][...]

    if not late:
        return
    values = jnp.concatenate([value_ref[...], late_refs[0][...]], axis=0)
    blocks_ref[first_row + UNIT : first_row + BLOCK, :] = late_refs[1][...]
    outs[1][...] = values
    if late > 2:
        late_a_ref, early_a_ref, value_a_ref = late_refs[2:]
        blocks_ref[EARLY, :] = early_a_ref[...]
        blocks_ref[LATE, :] = late_a_ref[...]
        outs[0][:BLOCK, :] = value_a_ref[...]
        outs[0][BLOCK:, :] = values
    at = place()[1]
    pieces = {2: outs[2]} if late == 2 else dict(enumerate(outs[2:]))
    piece = BLOCK * kv_width // model_width
    for k, out_ref in pieces.items():
        first = pl.multiple_of(lax.bitwise_xor(at, k) * piece, piece)
        here = blocks_ref[pl.ds(first_row + first, piece), :]
        if k == 2:
            out_ref[:piece, :] = here
            for g in range(model_width // kv_width):
                out_ref[piece:, g * kv_width : (g + 1) * kv_width] = values[
                    g * piece : (g + 1) * piece
                ]
        else:
            out_ref[:piece, :] = blocks_ref[pl.ds(first, piece), :]
            out_ref[piece:, :] = here


def tick_step(tick, grads, block, turned, gain, kept=(), late=(), after=(), name=""):
    kv_width, model_width = turned.shape
    low = len(grads) == 2
    arrays = [grad for grad, _ in grads]
    arrays += [block[1] if low else block[0], block[2], block[3], turned, gain]
    arrays += [array for pair in kept for array in pair]
    arrays += late
    operands = [near(array) for array in arrays]
    specs = [VMEM] * len(operands) + [ANY] * len(after)
    bf16 = jnp.bfloat16
    scratch = [pltpu.VMEM((UNIT, model_width), jnp.float32)]
    rows, value = (UNIT, model_width), (UNIT, kv_width)
    shapes = [rows, value]
    if late:
        half = lax.axis_size("dp") // 2
        scratch += [pltpu.VMEM((2 * BLOCK, model_width), bf16), pltpu.VMEM(value, bf16)]
        pieces = (2 * BLOCK // half, model_width)
        shapes = [rows, (BLOCK, kv_width), pieces]
    if len(late) > 2:
        shapes = [(2 * BLOCK, kv_width), (BLOCK, kv_width)] + [pieces] * half
    parts = [part for _, part in grads]
    return pl.pallas_call(
        functools.partial(
            tick_kernel, tick, EARLY if low else LATE, parts, len(kept), len(late)
        ),
        out_shape=tuple(jax.ShapeDtypeStruct(shape, bf16) for shape in shapes),
        in_specs=specs,
        out_specs=(VMEM,) * len(shapes),
        scratch_shapes=scratch,
        name=f"tick{tick}_{name}",
        **params(1.0 if kept else 0.0),
    )(*operands, *after)


def pack_kernel(block, half, piece, query_ref, key_ref, hidden_ref, up_ref, seg_ref, *rest):
    up_out_ref, seg_in_ref, rows_ref, sems = rest[-4:]
    packed = rest[-4 - half : -4]
    side, at, _ = place()
    there = side if block == 0 else 1 - side
    rows = pl.ds(pl.multiple_of(there * BLOCK, BLOCK), BLOCK)
    copies = []

    def copy(source, target):
        made = pltpu.make_async_copy(source, target, sems.at[len(copies)])
        made.start()
        copies.append(made)

    first = 0
    for source in (query_ref, key_ref, hidden_ref):
        width = source.shape[1]
        copy(source.at[rows], rows_ref.at[:, pl.ds(first, width)])
        first += width
    copy(seg_ref, seg_in_ref)
    copy(up_ref.at[rows], up_out_ref.at[pl.ds(0, BLOCK)])
    up_out_ref[BLOCK:, :] = jnp.zeros((16, up_out_ref.shape[1]), jnp.bfloat16)
    if block == 1:
        turn_kernel(rest[0], rest[-5 - half])
    for made in copies[:4]:
        made.wait()
    ids = seg_in_ref[...].astype(jnp.float32)
    up_out_ref[BLOCK:, : ids.shape[1]] = jnp.broadcast_to(ids, (16, ids.shape[1])).astype(
        jnp.bfloat16
    )
    for k in range(half):
        first = pl.multiple_of(lax.bitwise_xor(at, k) * piece, piece)
        packed[k][...] = rows_ref[pl.ds(first, piece), :]
    copies[4].wait()


def pack(block, half, piece, sources, weight=None):
    model_width = sources[0].shape[1]
    width = sum(source.shape[1] for source in sources[:3])
    bf16 = jnp.bfloat16
    operands = [pltpu.with_memory_space_constraint(array, pltpu.HBM) for array in sources]
    specs = [pl.BlockSpec(memory_space=pltpu.HBM)] * len(sources)
    outs = [jax.ShapeDtypeStruct((piece, width), bf16)] * half
    outs.append(jax.ShapeDtypeStruct((BLOCK + 16, model_width), bf16))
    if weight is not None:
        operands.append(near(weight))
        specs.append(VMEM)
        outs = [jax.ShapeDtypeStruct(weight.shape[::-1], bf16)] + outs
    return pl.pallas_call(
        functools.partial(pack_kernel, block, half, piece),
        out_shape=tuple(outs),
        in_specs=specs,
        out_specs=(VMEM,) * len(outs),
        scratch_shapes=[
            pltpu.VMEM(sources[-1].shape, jnp.int32),
            pltpu.VMEM((BLOCK, width), bf16),
            pltpu.SemaphoreType.DMA((5,)),
        ],
        name="pack",
        **params(1.2),
    )(*operands)


def columns_kernel(width, distance, first_ref, second_ref, *refs):
    out_ref = refs[-1]
    there = lax.div(lax.bitwise_xor(place()[2], distance), 2)
    out_ref[:BLOCK, :] = first_ref[:, columns_of(there, width)]
    out_ref[BLOCK:, :] = second_ref[:, columns_of(there, width)]


def columns_for(distance, blocks, after):
    model_width = blocks[0][3].shape[1]
    width = 2 * model_width // lax.axis_size("dp")
    return pl.pallas_call(
        functools.partial(columns_kernel, width, distance),
        out_shape=jax.ShapeDtypeStruct((2 * BLOCK, width), jnp.bfloat16),
        in_specs=[VMEM] * 2 + [ANY] * len(after),
        out_specs=VMEM,
        name=f"columns{distance}",
        **params(0.0 if distance else 1.0),
    )(blocks[0][3], blocks[1][3], *after)


def own_kernel(scale, weight_ref, gain_ref, after_ref, weight_out_ref, gain_out_ref):
    shares = weight_out_ref.shape[0]
    first = pl.multiple_of(place()[2] * shares, shares)
    weight_out_ref[...] = weight_ref[pl.ds(first, shares), :].astype(jnp.float32) * scale
    gain = gain_ref[:, pl.ds(first, shares)]
    column = jnp.sum(jnp.where(diagonal(shares), gain, 0.0), axis=1, keepdims=True)
    gain_out_ref[...] = jnp.broadcast_to(column * scale, gain_out_ref.shape)


def columns_of(pair, width):
    return pl.ds(pl.multiple_of(pair * width, width), width)


def partial_kernel(shares, first, *refs):
    columns, refs = refs[:4], refs[4:]
    own_out_ref, *other_refs = refs[6:]
    kv_width = own_out_ref.shape[1]
    parts = []
    for ref in refs[:6]:
        for at in range(0, ref.shape[1], kv_width):
            parts.append(ref[first:, at : at + kv_width] if ref.shape[1] > kv_width else ref[...])
    value = jnp.concatenate(parts, axis=0)
    mine = lax.rem(place()[2], 2)

    def share(core):
        at = pl.ds(pl.multiple_of(core * shares, shares), shares)
        rows = jnp.concatenate([ref[:, at] for ref in columns], axis=0)
        return lax.dot_general(
            rows, value, (((0,), (0,)), ((), ())), preferred_element_type=jnp.float32
        )

    other = share(1 - mine).astype(jnp.bfloat16)
    for part, ref in enumerate(other_refs):
        ref[...] = other[part * (shares // 2) : (part + 1) * (shares // 2)]
    own_out_ref[...] = share(mine)


def diagonal(size):
    return lax.broadcasted_iota(jnp.int32, (size, size), 0) == lax.broadcasted_iota(
        jnp.int32, (size, size), 1
    )


def finish_kernel(half, own_ref, first_ref, second_ref, weight_ref, gain_ref, *refs):
    first_rows_ref, pieces = refs[0], refs[1 : 1 + half]
    rows_ref, out_ref, gain_out_ref = refs[1 + half :]
    side, at, _ = place()
    piece = BLOCK // half
    for block in range(2):
        for k in range(half):
            replica = (side if block == 0 else 1 - side) * half + lax.bitwise_xor(at, k)
            rows = pl.ds(pl.multiple_of(replica * piece, piece), piece)
            source, first = pieces[k], block * piece
            if k == 2:
                source, first = (pieces[k] if block else first_rows_ref), 0
            rows_ref[rows, :] = source[first : first + piece, :]
    other = jnp.concatenate([first_ref[...], second_ref[...]], axis=0)
    total = own_ref[...] + other.astype(jnp.float32)
    out_ref[...] = total * gain_ref[:, :1]
    sums = jnp.sum(total * weight_ref[...], axis=1, keepdims=True)
    gain_out_ref[...] = jnp.sum(
        jnp.where(diagonal(total.shape[0]), sums, 0.0), axis=0, keepdims=True
    )


def direct(hidden, query, key, segments, weight, norm_gain, upstream):
    tokens, model_width = hidden.shape
    kv_width = key.shape[1]
    replicas = lax.axis_size("dp")
    layers = lax.axis_size("section")
    half = replicas // 2
    piece = tokens // replicas
    shares = model_width // replicas

    def swap(array, k):
        return lax.ppermute(array, "dp", [(i, i ^ k) for i in range(replicas)])

    count = 2 * half
    bf16 = jnp.bfloat16
    sources = (query, key, hidden, upstream, segments)
    pieces, ups = [], []
    for b in range(2):
        *packed, up = pack(b, half, piece, sources, weight if b else None)
        if b:
            turned, *packed = packed
        pieces.append([packed[0]] + [swap(packed[k], k) for k in range(1, half)])
        ups.append(swap(up, half) if b else up)
    whole = slice(0, UNIT)
    scale = float(tokens * replicas) ** (-0.5)
    blocks, kept, after = [], [], []
    for b in range(2):
        block = block_probs(pieces[b], ups[b], BLOCK, model_width, kv_width, after)
        late, early = (ups[b], LATE), (ups[b], EARLY)
        first = tick_step(0, [late], block, turned, norm_gain, name=UNITS[2 * b])
        second = tick_step(
            0, [late, early], block, turned, norm_gain, after=[first[0]], name=UNITS[2 * b + 1]
        )
        blocks.append(block)
        kept += [[first], [second]]
        after = [second[0]]

    for tick in range(1, layers):
        hop = [(layers - tick, layers - 1 - tick)]
        grads = [(lax.ppermute(unit[-1][0], "section", hop), whole) for unit in kept]
        last = tick == layers - 1
        after, done = [kept[3][-1][0]], []
        if tick == layers - 2:
            own_weight, own_gain = pl.pallas_call(
                functools.partial(own_kernel, scale),
                out_shape=(
                    jax.ShapeDtypeStruct((shares, kv_width), jnp.float32),
                    jax.ShapeDtypeStruct((shares, 128), jnp.float32),
                ),
                in_specs=[VMEM, VMEM, ANY],
                out_specs=(VMEM, VMEM),
                name="own",
                **params(0.0),
            )(near(weight), norm_gain, *after)
            columns = {6: swap(columns_for(6, blocks, after + [own_gain]), 6)}
        if last:
            waits = after + [columns[6]]
            columns.update({k: swap(columns_for(k, blocks, waits), k) for k in (2, 4)})
        for u in range(4):
            needs = grads[u - 1 : u + 1] if u % 2 else grads[u : u + 1]
            late = []
            if last and u == 1:
                late = [done[0][1], done[0][0]]
            if last and u == 3:
                late = [done[2][1], done[2][0], done[0][0], done[1][0], done[1][1]]
                first_value, first_rows = swap(done[1][1], 6), swap(done[1][2], 2)
                after = after + [columns[2], columns[4], first_value]
            done.append(
                tick_step(
                    tick, needs, blocks[u // 2], turned, norm_gain, kept[u] if last else (), late,
                    after, name=UNITS[u],
                )
            )
            after = [done[u][0]]
            kept[u].append(done[u])
    values, last_value, *rows = done[3]
    rows = [rows[0]] + [swap(rows[k], k) for k in range(1, half)]
    last_value = swap(last_value, 6)
    columns[0] = columns_for(0, blocks, [values, first_rows, last_value])
    values = [values, first_rows, rows[2], swap(values, 4), first_value, last_value]
    own, *other = pl.pallas_call(
        functools.partial(partial_kernel, shares, piece),
        out_shape=(jax.ShapeDtypeStruct((shares, kv_width), jnp.float32),)
        + (jax.ShapeDtypeStruct((shares // 2, kv_width), bf16),) * 2,
        in_specs=[VMEM] * 10,
        out_specs=(VMEM,) * 3,
        name="weight_partial",
        **params(0.0),
    )(*[columns[k] for k in (0, 2, 4, 6)], *values)
    other = [swap(part, 1) for part in other]
    input_grad, weight_grad, gain_grad = pl.pallas_call(
        functools.partial(finish_kernel, half),
        out_shape=(
            jax.ShapeDtypeStruct((tokens, model_width), bf16),
            jax.ShapeDtypeStruct((shares, kv_width), jnp.float32),
            jax.ShapeDtypeStruct((1, shares), jnp.float32),
        ),
        in_specs=[VMEM] * (6 + half),
        out_specs=(VMEM,) * 3,
        name="finish",
        **params(0.0),
    )(own, *other, own_weight, own_gain, first_rows, *rows)
    return input_grad[None], weight_grad[None], gain_grad


def weight_kernel(scale, columns_ref, value_ref, weight_ref, gain_ref, out_ref, gain_out_ref):
    total = lax.dot_general(
        columns_ref[...], value_ref[...], (((0,), (0,)), ((), ())),
        preferred_element_type=jnp.float32,
    ) * scale
    out_ref[...] = total * gain_ref[...]
    product = total * weight_ref[...].astype(jnp.float32)
    sums = lax.dot_general(
        jnp.ones((8, product.shape[1]), jnp.float32), product, (((1,), (1,)), ((), ())),
        preferred_element_type=jnp.float32, precision=lax.Precision.HIGHEST,
    )
    gain_out_ref[...] = sums[:1]


def grouped(hidden, query, key, segments, weight, norm_gain, upstream):
    tokens, model_width = hidden.shape
    kv_width = key.shape[1]
    replicas = lax.axis_size("dp")
    layers = lax.axis_size("section")
    half = replicas // 2
    me = lax.axis_index("dp")
    section = lax.axis_index("section")
    side = me // half
    groups = [list(range(half)), list(range(half, replicas))]
    across = [(i, (i + half) % replicas) for i in range(replicas)]
    shares = model_width // replicas

    def rows_of(array, which, axis=0):
        at = side if which == 0 else 1 - side
        return lax.dynamic_slice_in_dim(array, at * BLOCK, BLOCK, axis)

    def regroup(array):
        return lax.all_to_all(
            array, "dp", split_axis=0, concat_axis=0, axis_index_groups=groups, tiled=True
        )

    def spread(array):
        return lax.all_to_all(array, "dp", split_axis=0, concat_axis=0, tiled=True)

    turned = turn(weight)
    blocks, grads = [], []
    for which in range(2):
        up = rows_of(upstream, which)
        seg = jnp.broadcast_to(segments, (16, 2 * BLOCK)).astype(jnp.bfloat16)
        if which == 1:
            up = lax.ppermute(up, "dp", across)
            seg = lax.ppermute(seg, "dp", across)
        packed = jnp.concatenate(
            [rows_of(query, which), rows_of(key, which), rows_of(hidden, which)], axis=1
        )
        blocks.append(block_probs([regroup(packed)], seg, 0, model_width, kv_width))
        grads.append(up)

    def layer(tick, which, grad, kept):
        live = (section == layers - 1 - tick).astype(jnp.int32)[None]
        return layer_step(live, grad, blocks[which], turned, norm_gain, kept)

    held = [layer(0, which, grads[which], ()) for which in range(2)]
    hops = [(i, i - 1) for i in range(1, layers)]

    def step(tick, held):
        grads = [lax.ppermute(kept[0], "section", hops) for kept in held]
        return [layer(tick, which, grads[which], held[which]) for which in range(2)]

    held = lax.fori_loop(1, layers, step, held)

    columns, values, stored = [], [], []
    for which in range(2):
        block = blocks[which][3].reshape(BLOCK, replicas, shares).transpose(1, 0, 2)
        columns.append(spread(block.reshape(replicas * BLOCK, shares)))
        out, value = held[which]
        stored.append(regroup(out))
        values.append(spread(jnp.tile(value, (replicas, 1))))
    ordered = jnp.where(
        side == 0, jnp.concatenate(stored, axis=0), jnp.concatenate(stored[::-1], axis=0)
    )
    own_weight = lax.dynamic_slice_in_dim(weight, me * shares, shares, 0)
    own_gain = lax.dynamic_slice_in_dim(norm_gain[0], me * shares, shares, 0)
    scale = float(tokens * replicas) ** (-0.5)
    weight_grad, gain_grad = pl.pallas_call(
        functools.partial(weight_kernel, scale),
        out_shape=(
            jax.ShapeDtypeStruct((shares, kv_width), jnp.float32),
            jax.ShapeDtypeStruct((1, shares), jnp.float32),
        ),
        in_specs=[VMEM] * 4,
        out_specs=(VMEM, VMEM),
        name="weight_grad",
    )(
        jnp.concatenate(columns, axis=0),
        jnp.concatenate(values, axis=0),
        own_weight,
        own_gain[:, None],
    )
    return ordered[None], weight_grad[None], gain_grad


def on_device(hidden_in, queries, keys, segments, value_weight, norm_gain, upstream):
    replicas = lax.axis_size("dp")
    piece = hidden_in.shape[1] // replicas
    plan = direct if piece % 16 == 0 and replicas == 8 else grouped
    return plan(
        hidden_in[0], queries[0], keys[0], segments, value_weight[0], norm_gain, upstream
    )


def solution(mesh):
    in_specs = (
        P("section", "dp", None),
        P("section", "dp", None),
        P("section", "dp", None),
        P("dp", None),
        P("section", None, None),
        P("section", None),
        P("dp", None),
    )
    out_specs = (P("section", "dp", None), P("section", "dp", None), P("section", "dp"))
    return jax.shard_map(
        on_device, mesh=mesh, in_specs=in_specs, out_specs=out_specs, check_vma=False
    )
```

```python
import functools

import jax
import jax.numpy as jnp
from jax import lax
from jax.experimental import pallas as pl
from jax.experimental.pallas import tpu as pltpu
from jax.sharding import PartitionSpec as P

HEAD_FEATURES = 128
BLOCK = 64
UNIT = 32
EPSILON = 1e-06
MASKED = -1e30
OUTS = {2: 3, 5: 6}
UNITS = ("a_late", "a_early", "b_late", "b_early")
VMEM = pl.BlockSpec(memory_space=pltpu.VMEM)
SMEM = pl.BlockSpec(memory_space=pltpu.SMEM)


ANY = pl.BlockSpec(memory_space=pl.ANY)


LATE, EARLY = slice(UNIT, BLOCK), slice(0, UNIT)


def params(microseconds):
    flops = int(microseconds * 1.15e9)
    return dict(
        compiler_params=pltpu.CompilerParams(vmem_limit_bytes=16 << 20),
        cost_estimate=pl.CostEstimate(flops=flops, bytes_accessed=0, transcendentals=0),
    )


def near(array):
    return pltpu.with_memory_space_constraint(array, pltpu.VMEM)


def place():
    half = lax.axis_size("dp") // 2
    me = lax.axis_index("dp")
    return lax.div(me, half), lax.rem(me, half), me


def probs_kernel(count, seg_row, model_width, kv_width, *refs):
    pieces, seg_ref = refs[:count], refs[count]
    late_ref, early_ref, inv_ref, x_ref, rows_ref = refs[-5:]
    heads = model_width // kv_width
    rows = BLOCK // count
    side, at, _ = place()
    for k, piece in enumerate(pieces):
        if count == 1:
            rows_ref[...] = piece[...]
        else:
            first = pl.multiple_of(lax.bitwise_xor(at, k) * rows, rows)
            rows_ref[pl.ds(first, rows), :] = piece[...]

    def iota(shape, axis):
        return lax.broadcasted_iota(jnp.int32, shape, axis)

    seg = seg_ref[seg_row : seg_row + 16, : 2 * BLOCK].astype(jnp.float32)[:1]
    shape = (BLOCK, 2 * BLOCK)
    wanted = iota(shape, 1) == side * BLOCK + iota(shape, 0)
    ids = jnp.sum(jnp.where(wanted, seg, 0.0), axis=1, keepdims=True)
    key_code = ids * BLOCK + iota((BLOCK, 1), 0).astype(jnp.float32)
    list_start = ids * BLOCK
    shape = (BLOCK, heads * BLOCK)
    column = iota(shape, 1)
    query_at = lax.rem(column, UNIT) + jnp.where(column < heads * UNIT, UNIT, 0)
    same = iota(shape, 0) == query_at
    query_code = jnp.sum(jnp.where(same, key_code, 0.0), axis=0, keepdims=True)
    query_start = jnp.sum(jnp.where(same, list_start, 0.0), axis=0, keepdims=True)
    allowed = (key_code <= query_code) & (key_code >= query_start)
    for c in range(kv_width // HEAD_FEATURES):
        first = c * heads * HEAD_FEATURES
        query_stack = jnp.concatenate(
            [
                rows_ref[part, first + h * HEAD_FEATURES : first + (h + 1) * HEAD_FEATURES]
                for part in (LATE, EARLY)
                for h in range(heads)
            ],
            axis=0,
        )
        key_first = model_width + c * HEAD_FEATURES
        keys = rows_ref[:, key_first : key_first + HEAD_FEATURES]
        scores = lax.dot_general(
            keys, query_stack, (((1,), (1,)), ((), ())), preferred_element_type=jnp.float32
        ) * HEAD_FEATURES ** (-0.5)
        scores = jnp.where(allowed, scores, MASKED)
        exp_scores = jnp.exp(scores - jnp.max(scores, axis=0, keepdims=True))
        total = jnp.sum(exp_scores, axis=0, keepdims=True)
        probs = (exp_scores / total).astype(jnp.bfloat16)
        late_ref[c] = probs[LATE, : heads * UNIT]
        early_ref[c] = probs[EARLY]
    hidden = rows_ref[:, model_width + kv_width :]
    x_ref[...] = hidden
    x = hidden.astype(jnp.float32)
    mean_square = jnp.mean(x * x, axis=1, keepdims=True)
    inv_ref[...] = jnp.broadcast_to(lax.rsqrt(mean_square + EPSILON), inv_ref.shape)


def block_probs(pieces, seg, seg_row, model_width, kv_width, after=()):
    heads = model_width // kv_width
    key_heads = kv_width // HEAD_FEATURES
    operands = [near(piece) for piece in pieces] + [near(seg)]
    specs = [VMEM] * len(operands) + [ANY] * len(after)
    operands += after
    return pl.pallas_call(
        functools.partial(probs_kernel, len(pieces), seg_row, model_width, kv_width),
        out_shape=(
            jax.ShapeDtypeStruct((key_heads, UNIT, heads * UNIT), jnp.bfloat16),
            jax.ShapeDtypeStruct((key_heads, UNIT, heads * BLOCK), jnp.bfloat16),
            jax.ShapeDtypeStruct((BLOCK, 128), jnp.float32),
            jax.ShapeDtypeStruct((BLOCK, model_width), jnp.bfloat16),
        ),
        in_specs=specs,
        out_specs=(VMEM,) * 4,
        scratch_shapes=[pltpu.VMEM((BLOCK, 2 * model_width + kv_width), jnp.bfloat16)],
        name="probs",
        **params(0.35 if after else 2.0),
    )(*operands)


def unit_math(rows, grads, probs_ref, x_ref, inv_ref, turned_ref, gain_ref, scaled_ref, store, value_ref):
    kv_width, model_width = turned_ref.shape
    heads = model_width // kv_width
    chunk = min(512, model_width)
    inv = inv_ref[rows, :1]
    values = []
    for c in range(kv_width // HEAD_FEATURES):
        first = c * heads * HEAD_FEATURES
        grad_stack = jnp.concatenate(
            [
                grad_ref[part, first + h * HEAD_FEATURES : first + (h + 1) * HEAD_FEATURES]
                for grad_ref, part in grads
                for h in range(heads)
            ],
            axis=0,
        )
        values.append(
            jnp.dot(probs_ref[c], grad_stack, preferred_element_type=jnp.float32).astype(
                jnp.bfloat16
            )
        )
    value = jnp.concatenate(values, axis=1)
    value_ref[...] = (value.astype(jnp.float32) * inv).astype(jnp.bfloat16)
    inner = jnp.zeros((UNIT, 1), jnp.float32)
    for first in range(0, model_width, chunk):
        columns = slice(first, first + chunk)
        normed_grad = jnp.dot(value, turned_ref[:, columns], preferred_element_type=jnp.float32)
        scaled = normed_grad * gain_ref[:, columns]
        scaled_ref[:, columns] = scaled
        x = x_ref[rows, columns].astype(jnp.float32)
        inner = inner + jnp.sum(x * scaled, axis=1, keepdims=True)
    pull = inner * (inv * inv / model_width)
    grad_ref, part = grads[-1]
    for first in range(0, model_width, chunk):
        columns = slice(first, first + chunk)
        x = x_ref[rows, columns].astype(jnp.float32)
        change = inv * (scaled_ref[:, columns] - x * pull)
        grad = grad_ref[part, columns].astype(jnp.float32)
        store(columns, (grad + change).astype(jnp.bfloat16))


def turn_kernel(weight_ref, *refs):
    turned_ref = refs[-1]
    step = min(256, weight_ref.shape[0])
    for first in range(0, weight_ref.shape[0], step):
        turned_ref[:, first : first + step] = weight_ref[first : first + step, :].T


def turn(weight, after=()):
    return pl.pallas_call(
        turn_kernel,
        out_shape=jax.ShapeDtypeStruct(weight.shape[::-1], weight.dtype),
        in_specs=[VMEM] + [ANY] * len(after),
        out_specs=VMEM,
        name="turn",
        **params(1.5),
    )(near(weight), *after)


def layer_kernel(
    live_ref, grad_ref, late_ref, early_ref, inv_ref, x_ref, turned_ref, gain_ref, *rest
):
    out_ref, value_ref, scaled_ref = rest[-3:]
    if len(rest) == 5:

        @pl.when(live_ref[0] == 0)
        def _():
            out_ref[...] = rest[0][...]
            value_ref[...] = rest[1][...]

    @pl.when(live_ref[0] == 1)
    def _():
        for rows, parts, probs_ref in ((LATE, [LATE], late_ref), (EARLY, [LATE, EARLY], early_ref)):

            def store(columns, part, rows=rows):
                out_ref[rows, columns] = part

            grads = [(grad_ref, part) for part in parts]
            unit_math(
                rows, grads, probs_ref, x_ref, inv_ref, turned_ref, gain_ref, scaled_ref, store,
                value_ref.at[rows],
            )


def layer_step(live, grad, block, turned, gain, held=()):
    kv_width, model_width = turned.shape
    operands = [live, grad, *block, turned, gain, *held]
    return pl.pallas_call(
        layer_kernel,
        out_shape=(
            jax.ShapeDtypeStruct((BLOCK, model_width), jnp.bfloat16),
            jax.ShapeDtypeStruct((BLOCK, kv_width), jnp.bfloat16),
        ),
        in_specs=[SMEM] + [VMEM] * (len(operands) - 1),
        out_specs=(VMEM, VMEM),
        scratch_shapes=[pltpu.VMEM((UNIT, model_width), jnp.float32)],
        name="layer",
        **params(1.1),
    )(*operands)


def tick_kernel(tick, rows, parts, kept, late, *refs):
    grads = list(zip(refs, parts))
    probs_ref, inv_ref, x_ref, turned_ref, gain_ref = refs[len(parts) : len(parts) + 5]
    refs = refs[len(parts) + 5 :]
    earlier, refs = refs[: 2 * kept], refs[2 * kept :]
    late_refs = refs[:late]
    kv_width, model_width = turned_ref.shape
    turn = lax.axis_size("section") - 1 - lax.axis_index("section")
    if late:
        outs, (scaled_ref, blocks_ref, value_ref) = refs[late : -3], refs[-3:]
        outs = outs[len(outs) - OUTS[late] :]
    else:
        outs, scaled_ref = refs[-3:-1], refs[-1]
        value_ref = outs[1]
    first_row = BLOCK if late > 2 else 0

    def store(columns, part):
        if late:
            blocks_ref[first_row : first_row + UNIT, columns] = part
        if late <= 2:
            outs[0][:, columns] = part

    @pl.when(turn == tick)
    def _():
        unit_math(
            rows, grads, probs_ref, x_ref, inv_ref, turned_ref, gain_ref, scaled_ref, store,
            value_ref,
        )

    for at in range(kept):

        @pl.when(turn == at)
        def _(at=at):
            store(slice(None), earlier[2 * at][...])
            value_ref[...] = earlier[2 * at + 1][...]

    if not late:
        return
    values = jnp.concatenate([value_ref[...], late_refs[0][...]], axis=0)
    blocks_ref[first_row + UNIT : first_row + BLOCK, :] = late_refs[1][...]
    outs[1][...] = values
    if late > 2:
        late_a_ref, early_a_ref, value_a_ref = late_refs[2:]
        blocks_ref[EARLY, :] = early_a_ref[...]
        blocks_ref[LATE, :] = late_a_ref[...]
        outs[0][:BLOCK, :] = value_a_ref[...]
        outs[0][BLOCK:, :] = values
    at = place()[1]
    pieces = {2: outs[2]} if late == 2 else dict(enumerate(outs[2:]))
    piece = BLOCK * kv_width // model_width

    def rows_for(k, block):
        first = pl.multiple_of(lax.bitwise_xor(at, k) * piece, piece)
        return blocks_ref[pl.ds(block * BLOCK + first, piece), :]

    block = 0 if late == 2 else 1
    for k, out_ref in pieces.items():
        if k == 2:
            out_ref[:piece, :] = rows_for(2, block)
            for g in range(model_width // kv_width):
                out_ref[piece : 2 * piece, g * kv_width : (g + 1) * kv_width] = values[
                    g * piece : (g + 1) * piece
                ]
            if block == 0:
                out_ref[2 * piece :, :] = rows_for(3, 0)
        elif k == 3:
            out_ref[...] = rows_for(3, 1)
        else:
            out_ref[:piece, :] = rows_for(k, 0)
            out_ref[piece:, :] = rows_for(k, 1)


def tick_step(tick, grads, block, turned, gain, kept=(), late=(), after=(), name=""):
    kv_width, model_width = turned.shape
    low = len(grads) == 2
    arrays = [grad for grad, _ in grads]
    arrays += [block[1] if low else block[0], block[2], block[3], turned, gain]
    arrays += [array for pair in kept for array in pair]
    arrays += late
    operands = [near(array) for array in arrays]
    specs = [VMEM] * len(operands) + [ANY] * len(after)
    bf16 = jnp.bfloat16
    scratch = [pltpu.VMEM((UNIT, model_width), jnp.float32)]
    rows, value = (UNIT, model_width), (UNIT, kv_width)
    shapes = [rows, value]
    if late:
        half = lax.axis_size("dp") // 2
        scratch += [pltpu.VMEM((2 * BLOCK, model_width), bf16), pltpu.VMEM(value, bf16)]
        piece = BLOCK // half
        shapes = [rows, (BLOCK, kv_width), (3 * piece, model_width)]
    if len(late) > 2:
        shapes = [(2 * BLOCK, kv_width), (BLOCK, kv_width)]
        shapes += [(2 * piece, model_width)] * 3 + [(piece, model_width)]
    parts = [part for _, part in grads]
    return pl.pallas_call(
        functools.partial(
            tick_kernel, tick, EARLY if low else LATE, parts, len(kept), len(late)
        ),
        out_shape=tuple(jax.ShapeDtypeStruct(shape, bf16) for shape in shapes),
        in_specs=specs,
        out_specs=(VMEM,) * len(shapes),
        scratch_shapes=scratch,
        name=f"tick{tick}_{name}",
        **params(1.0 if kept else 0.0),
    )(*operands, *after)


def pack_kernel(block, half, piece, query_ref, key_ref, hidden_ref, up_ref, seg_ref, *rest):
    up_out_ref, seg_in_ref, rows_ref, sems = rest[-4:]
    packed = rest[-4 - half : -4]
    side, at, _ = place()
    there = side if block == 0 else 1 - side
    rows = pl.ds(pl.multiple_of(there * BLOCK, BLOCK), BLOCK)
    copies = []

    def copy(source, target):
        made = pltpu.make_async_copy(source, target, sems.at[len(copies)])
        made.start()
        copies.append(made)

    first = 0
    for source in (query_ref, key_ref, hidden_ref):
        width = source.shape[1]
        copy(source.at[rows], rows_ref.at[:, pl.ds(first, width)])
        first += width
    copy(seg_ref, seg_in_ref)
    copy(up_ref.at[rows], up_out_ref.at[pl.ds(0, BLOCK)])
    up_out_ref[BLOCK:, :] = jnp.zeros((16, up_out_ref.shape[1]), jnp.bfloat16)
    if block == 1:
        rest[2][...] = rest[1][...]
        turn_kernel(rest[0], rest[3])
    for made in copies[:4]:
        made.wait()
    ids = seg_in_ref[...].astype(jnp.float32)
    up_out_ref[BLOCK:, : ids.shape[1]] = jnp.broadcast_to(ids, (16, ids.shape[1])).astype(
        jnp.bfloat16
    )
    for k in range(half):
        first = pl.multiple_of(lax.bitwise_xor(at, k) * piece, piece)
        packed[k][...] = rows_ref[pl.ds(first, piece), :]
    copies[4].wait()


def pack(block, half, piece, sources, weight=None, gain=None):
    model_width = sources[0].shape[1]
    width = sum(source.shape[1] for source in sources[:3])
    bf16 = jnp.bfloat16
    operands = [pltpu.with_memory_space_constraint(array, pltpu.HBM) for array in sources]
    specs = [pl.BlockSpec(memory_space=pltpu.HBM)] * len(sources)
    outs = [jax.ShapeDtypeStruct((piece, width), bf16)] * half
    outs.append(jax.ShapeDtypeStruct((BLOCK + 16, model_width), bf16))
    if weight is not None:
        operands += [near(weight), gain]
        specs += [VMEM, VMEM]
        outs = [
            jax.ShapeDtypeStruct(gain.shape, gain.dtype),
            jax.ShapeDtypeStruct(weight.shape[::-1], bf16),
        ] + outs
    return pl.pallas_call(
        functools.partial(pack_kernel, block, half, piece),
        out_shape=tuple(outs),
        in_specs=specs,
        out_specs=(VMEM,) * len(outs),
        scratch_shapes=[
            pltpu.VMEM(sources[-1].shape, jnp.int32),
            pltpu.VMEM((BLOCK, width), bf16),
            pltpu.SemaphoreType.DMA((5,)),
        ],
        name="pack",
        **params(1.2),
    )(*operands)


def columns_kernel(width, distance, first_ref, second_ref, *refs):
    out_ref = refs[-1]
    if distance == 0:
        came_ref, out_ref, handed_ref = refs[0], refs[-2], refs[-1]
        handed_ref[...] = came_ref[came_ref.shape[0] - handed_ref.shape[0] :, :]
    there = lax.div(lax.bitwise_xor(place()[2], distance), 2)
    out_ref[:BLOCK, :] = first_ref[:, columns_of(there, width)]
    out_ref[BLOCK:, :] = second_ref[:, columns_of(there, width)]


def columns_for(distance, blocks, after, came=()):
    model_width = blocks[0][3].shape[1]
    width = 2 * model_width // lax.axis_size("dp")
    shapes = [(2 * BLOCK, width)] + [(array.shape[0] // 3, model_width) for array in came]
    outs = [jax.ShapeDtypeStruct(shape, jnp.bfloat16) for shape in shapes]
    results = pl.pallas_call(
        functools.partial(columns_kernel, width, distance),
        out_shape=tuple(outs),
        in_specs=[VMEM] * (2 + len(came)) + [ANY] * len(after),
        out_specs=(VMEM,) * len(outs),
        name=f"columns{distance}",
        **params(0.0 if distance else 1.0),
    )(blocks[0][3], blocks[1][3], *came, *after)
    return results if came else results[0]


def own_kernel(scale, weight_ref, gain_ref, after_ref, weight_out_ref, gain_out_ref):
    shares = weight_out_ref.shape[0]
    first = pl.multiple_of(place()[2] * shares, shares)
    weight_out_ref[...] = weight_ref[pl.ds(first, shares), :].astype(jnp.float32) * scale
    gain = gain_ref[:, pl.ds(first, shares)]
    column = jnp.sum(jnp.where(diagonal(shares), gain, 0.0), axis=1, keepdims=True)
    gain_out_ref[...] = jnp.broadcast_to(column * scale, gain_out_ref.shape)


def columns_of(pair, width):
    return pl.ds(pl.multiple_of(pair * width, width), width)


def partial_kernel(shares, first, *refs):
    columns, refs = refs[:4], refs[4:]
    own_out_ref, *other_refs = refs[6:]
    kv_width = own_out_ref.shape[1]
    parts = []
    for ref in refs[:6]:
        beside = ref.shape[1] > kv_width
        rows = slice(first, 2 * first) if beside else slice(0, ref.shape[0])
        parts += [ref[rows, at : at + kv_width] for at in range(0, ref.shape[1], kv_width)]
    value = jnp.concatenate(parts, axis=0)
    mine = lax.rem(place()[2], 2)

    def share(core):
        at = pl.ds(pl.multiple_of(core * shares, shares), shares)
        rows = jnp.concatenate([ref[:, at] for ref in columns], axis=0)
        return lax.dot_general(
            rows, value, (((0,), (0,)), ((), ())), preferred_element_type=jnp.float32
        )

    other = share(1 - mine).astype(jnp.bfloat16)
    for part, ref in enumerate(other_refs):
        ref[...] = other[part * (shares // 2) : (part + 1) * (shares // 2)]
    own_out_ref[...] = share(mine)


def diagonal(size):
    return lax.broadcasted_iota(jnp.int32, (size, size), 0) == lax.broadcasted_iota(
        jnp.int32, (size, size), 1
    )


def rows_kernel(half, first_rows_ref, handed_ref, *refs):
    pieces = refs[:half]
    rows_ref, token_ref = refs[half:]
    side, at, _ = place()
    piece = BLOCK // half
    for block in range(2):
        for k in range(half):
            replica = (side if block == 0 else 1 - side) * half + lax.bitwise_xor(at, k)
            rows = pl.ds(pl.multiple_of(replica * piece, piece), piece)
            source, first = pieces[k], block * piece
            if k == 2:
                source, first = (pieces[k] if block else first_rows_ref), 0
            if k == 3:
                source, first = (pieces[k] if block else handed_ref), 0
            rows_ref[rows, :] = source[first : first + piece, :]
    token_ref[...] = jnp.zeros_like(token_ref)


def finish_kernel(
    own_ref, first_ref, second_ref, weight_ref, gain_ref, after_ref, out_ref, gain_out_ref
):
    other = jnp.concatenate([first_ref[...], second_ref[...]], axis=0)
    total = own_ref[...] + other.astype(jnp.float32)
    out_ref[...] = total * gain_ref[:, :1]
    sums = jnp.sum(total * weight_ref[...], axis=1, keepdims=True)
    gain_out_ref[...] = jnp.sum(
        jnp.where(diagonal(total.shape[0]), sums, 0.0), axis=0, keepdims=True
    )


def direct(hidden, query, key, segments, weight, norm_gain, upstream):
    tokens, model_width = hidden.shape
    kv_width = key.shape[1]
    replicas = lax.axis_size("dp")
    layers = lax.axis_size("section")
    half = replicas // 2
    piece = tokens // replicas
    shares = model_width // replicas

    def swap(array, k):
        return lax.ppermute(array, "dp", [(i, i ^ k) for i in range(replicas)])

    count = 2 * half
    bf16 = jnp.bfloat16
    sources = (query, key, hidden, upstream, segments)
    pieces, ups = [], []
    for b in range(2):
        extra = (weight, norm_gain) if b else ()
        *packed, up = pack(b, half, piece, sources, *extra)
        if b:
            gain, turned, *packed = packed
        pieces.append([packed[0]] + [swap(packed[k], k) for k in range(1, half)])
        ups.append(swap(up, half) if b else up)
    whole = slice(0, UNIT)
    scale = float(tokens * replicas) ** (-0.5)
    blocks, kept, after = [], [], []
    for b in range(2):
        block = block_probs(pieces[b], ups[b], BLOCK, model_width, kv_width, after)
        late, early = (ups[b], LATE), (ups[b], EARLY)
        first = tick_step(0, [late], block, turned, gain, name=UNITS[2 * b])
        second = tick_step(
            0, [late, early], block, turned, gain, after=[first[0]], name=UNITS[2 * b + 1]
        )
        blocks.append(block)
        kept += [[first], [second]]
        after = [second[0]]

    for tick in range(1, layers):
        hop = [(layers - tick, layers - 1 - tick)]
        grads = [(lax.ppermute(unit[-1][0], "section", hop), whole) for unit in kept]
        last = tick == layers - 1
        after, done = [kept[3][-1][0]], []
        if tick == layers - 2:
            own_weight, own_gain = pl.pallas_call(
                functools.partial(own_kernel, scale),
                out_shape=(
                    jax.ShapeDtypeStruct((shares, kv_width), jnp.float32),
                    jax.ShapeDtypeStruct((shares, 128), jnp.float32),
                ),
                in_specs=[VMEM, VMEM, ANY],
                out_specs=(VMEM, VMEM),
                name="own",
                **params(0.0),
            )(near(weight), near(gain), *after)
            columns = {6: swap(columns_for(6, blocks, after + [own_gain]), 6)}
        if last:
            waits = after + [columns[6]]
            columns.update({k: swap(columns_for(k, blocks, waits), k) for k in (2, 4)})
        for u in range(4):
            needs = grads[u - 1 : u + 1] if u % 2 else grads[u : u + 1]
            late = []
            if last and u == 1:
                late = [done[0][1], done[0][0]]
            if last and u == 3:
                late = [done[2][1], done[2][0], done[0][0], done[1][0], done[1][1]]
                first_value, first_rows = swap(done[1][1], 6), swap(done[1][2], 2)
                after = after + [columns[2], columns[4], first_value]
            done.append(
                tick_step(
                    tick, needs, blocks[u // 2], turned, gain, kept[u] if last else (), late,
                    after, name=UNITS[u],
                )
            )
            after = [done[u][0]]
            kept[u].append(done[u])
    values, last_value, *rows = done[3]
    rows = [rows[0]] + [swap(rows[k], k) for k in range(1, half)]
    last_value = swap(last_value, 6)
    columns[0], handed = columns_for(0, blocks, [values, last_value], [first_rows])
    handed = swap(handed, 1)
    values = [values, first_rows, rows[2], swap(values, 4), first_value, last_value]
    own, *other = pl.pallas_call(
        functools.partial(partial_kernel, shares, piece),
        out_shape=(jax.ShapeDtypeStruct((shares, kv_width), jnp.float32),)
        + (jax.ShapeDtypeStruct((shares // 2, kv_width), bf16),) * 2,
        in_specs=[VMEM] * 10,
        out_specs=(VMEM,) * 3,
        name="weight_partial",
        **params(0.0),
    )(*[columns[k] for k in (0, 2, 4, 6)], *values)
    other = [swap(part, 1) for part in other]
    input_grad, token = pl.pallas_call(
        functools.partial(rows_kernel, half),
        out_shape=(
            jax.ShapeDtypeStruct((tokens, model_width), bf16),
            jax.ShapeDtypeStruct((8, 128), jnp.float32),
        ),
        in_specs=[VMEM] * (2 + half),
        out_specs=(VMEM, VMEM),
        name="rows",
        **params(0.8),
    )(first_rows, handed, *rows)
    weight_grad, gain_grad = pl.pallas_call(
        finish_kernel,
        out_shape=(
            jax.ShapeDtypeStruct((shares, kv_width), jnp.float32),
            jax.ShapeDtypeStruct((1, shares), jnp.float32),
        ),
        in_specs=[VMEM] * 5 + [ANY],
        out_specs=(VMEM, VMEM),
        name="finish",
        **params(0.0),
    )(own, *other, own_weight, own_gain, token)
    return input_grad[None], weight_grad[None], gain_grad


def weight_kernel(scale, columns_ref, value_ref, weight_ref, gain_ref, out_ref, gain_out_ref):
    total = lax.dot_general(
        columns_ref[...], value_ref[...], (((0,), (0,)), ((), ())),
        preferred_element_type=jnp.float32,
    ) * scale
    out_ref[...] = total * gain_ref[...]
    product = total * weight_ref[...].astype(jnp.float32)
    sums = lax.dot_general(
        jnp.ones((8, product.shape[1]), jnp.float32), product, (((1,), (1,)), ((), ())),
        preferred_element_type=jnp.float32, precision=lax.Precision.HIGHEST,
    )
    gain_out_ref[...] = sums[:1]


def grouped(hidden, query, key, segments, weight, norm_gain, upstream):
    tokens, model_width = hidden.shape
    kv_width = key.shape[1]
    replicas = lax.axis_size("dp")
    layers = lax.axis_size("section")
    half = replicas // 2
    me = lax.axis_index("dp")
    section = lax.axis_index("section")
    side = me // half
    groups = [list(range(half)), list(range(half, replicas))]
    across = [(i, (i + half) % replicas) for i in range(replicas)]
    shares = model_width // replicas

    def rows_of(array, which, axis=0):
        at = side if which == 0 else 1 - side
        return lax.dynamic_slice_in_dim(array, at * BLOCK, BLOCK, axis)

    def regroup(array):
        return lax.all_to_all(
            array, "dp", split_axis=0, concat_axis=0, axis_index_groups=groups, tiled=True
        )

    def spread(array):
        return lax.all_to_all(array, "dp", split_axis=0, concat_axis=0, tiled=True)

    turned = turn(weight)
    blocks, grads = [], []
    for which in range(2):
        up = rows_of(upstream, which)
        seg = jnp.broadcast_to(segments, (16, 2 * BLOCK)).astype(jnp.bfloat16)
        if which == 1:
            up = lax.ppermute(up, "dp", across)
            seg = lax.ppermute(seg, "dp", across)
        packed = jnp.concatenate(
            [rows_of(query, which), rows_of(key, which), rows_of(hidden, which)], axis=1
        )
        blocks.append(block_probs([regroup(packed)], seg, 0, model_width, kv_width))
        grads.append(up)

    def layer(tick, which, grad, kept):
        live = (section == layers - 1 - tick).astype(jnp.int32)[None]
        return layer_step(live, grad, blocks[which], turned, norm_gain, kept)

    held = [layer(0, which, grads[which], ()) for which in range(2)]
    hops = [(i, i - 1) for i in range(1, layers)]

    def step(tick, held):
        grads = [lax.ppermute(kept[0], "section", hops) for kept in held]
        return [layer(tick, which, grads[which], held[which]) for which in range(2)]

    held = lax.fori_loop(1, layers, step, held)

    columns, values, stored = [], [], []
    for which in range(2):
        block = blocks[which][3].reshape(BLOCK, replicas, shares).transpose(1, 0, 2)
        columns.append(spread(block.reshape(replicas * BLOCK, shares)))
        out, value = held[which]
        stored.append(regroup(out))
        values.append(spread(jnp.tile(value, (replicas, 1))))
    ordered = jnp.where(
        side == 0, jnp.concatenate(stored, axis=0), jnp.concatenate(stored[::-1], axis=0)
    )
    own_weight = lax.dynamic_slice_in_dim(weight, me * shares, shares, 0)
    own_gain = lax.dynamic_slice_in_dim(norm_gain[0], me * shares, shares, 0)
    scale = float(tokens * replicas) ** (-0.5)
    weight_grad, gain_grad = pl.pallas_call(
        functools.partial(weight_kernel, scale),
        out_shape=(
            jax.ShapeDtypeStruct((shares, kv_width), jnp.float32),
            jax.ShapeDtypeStruct((1, shares), jnp.float32),
        ),
        in_specs=[VMEM] * 4,
        out_specs=(VMEM, VMEM),
        name="weight_grad",
    )(
        jnp.concatenate(columns, axis=0),
        jnp.concatenate(values, axis=0),
        own_weight,
        own_gain[:, None],
    )
    return ordered[None], weight_grad[None], gain_grad


def on_device(hidden_in, queries, keys, segments, value_weight, norm_gain, upstream):
    replicas = lax.axis_size("dp")
    piece = hidden_in.shape[1] // replicas
    plan = direct if piece % 16 == 0 and replicas == 8 else grouped
    return plan(
        hidden_in[0], queries[0], keys[0], segments, value_weight[0], norm_gain, upstream
    )


def solution(mesh):
    in_specs = (
        P("section", "dp", None),
        P("section", "dp", None),
        P("section", "dp", None),
        P("dp", None),
        P("section", None, None),
        P("section", None),
        P("dp", None),
    )
    out_specs = (P("section", "dp", None), P("section", "dp", None), P("section", "dp"))
    return jax.shard_map(
        on_device, mesh=mesh, in_specs=in_specs, out_specs=out_specs, check_vma=False
    )
```

```python
import functools

import jax
import jax.numpy as jnp
from jax import lax
from jax.experimental import pallas as pl
from jax.experimental.pallas import tpu as pltpu
from jax.sharding import PartitionSpec as P

HEAD_FEATURES = 128
BLOCK = 64
UNIT = 32
EPSILON = 1e-06
MASKED = -1e30
OUTS = {2: 3, 4: 5}
UNITS = ("a_late", "a_early", "b_late", "b_early")
VMEM = pl.BlockSpec(memory_space=pltpu.VMEM)
SMEM = pl.BlockSpec(memory_space=pltpu.SMEM)


ANY = pl.BlockSpec(memory_space=pl.ANY)


LATE, EARLY = slice(UNIT, BLOCK), slice(0, UNIT)


def params(microseconds):
    flops = int(microseconds * 1.15e9)
    return dict(
        compiler_params=pltpu.CompilerParams(vmem_limit_bytes=16 << 20),
        cost_estimate=pl.CostEstimate(flops=flops, bytes_accessed=0, transcendentals=0),
    )


def near(array):
    return pltpu.with_memory_space_constraint(array, pltpu.VMEM)


def place():
    half = lax.axis_size("dp") // 2
    me = lax.axis_index("dp")
    return lax.div(me, half), lax.rem(me, half), me


def probs_kernel(count, seg_row, model_width, kv_width, *refs):
    pieces, seg_ref = refs[:count], refs[count]
    late_ref, early_ref, inv_ref, x_ref, rows_ref = refs[-5:]
    heads = model_width // kv_width
    rows = BLOCK // count
    side, at, _ = place()
    for k, piece in enumerate(pieces):
        if count == 1:
            rows_ref[...] = piece[...]
        else:
            first = pl.multiple_of(lax.bitwise_xor(at, k) * rows, rows)
            rows_ref[pl.ds(first, rows), :] = piece[...]

    def iota(shape, axis):
        return lax.broadcasted_iota(jnp.int32, shape, axis)

    seg = seg_ref[seg_row : seg_row + 16, : 2 * BLOCK].astype(jnp.float32)[:1]
    shape = (BLOCK, 2 * BLOCK)
    wanted = iota(shape, 1) == side * BLOCK + iota(shape, 0)
    ids = jnp.sum(jnp.where(wanted, seg, 0.0), axis=1, keepdims=True)
    key_code = ids * BLOCK + iota((BLOCK, 1), 0).astype(jnp.float32)
    list_start = ids * BLOCK
    shape = (BLOCK, heads * BLOCK)
    column = iota(shape, 1)
    query_at = lax.rem(column, UNIT) + jnp.where(column < heads * UNIT, UNIT, 0)
    same = iota(shape, 0) == query_at
    query_code = jnp.sum(jnp.where(same, key_code, 0.0), axis=0, keepdims=True)
    query_start = jnp.sum(jnp.where(same, list_start, 0.0), axis=0, keepdims=True)
    allowed = (key_code <= query_code) & (key_code >= query_start)
    for c in range(kv_width // HEAD_FEATURES):
        first = c * heads * HEAD_FEATURES
        query_stack = jnp.concatenate(
            [
                rows_ref[part, first + h * HEAD_FEATURES : first + (h + 1) * HEAD_FEATURES]
                for part in (LATE, EARLY)
                for h in range(heads)
            ],
            axis=0,
        )
        key_first = model_width + c * HEAD_FEATURES
        keys = rows_ref[:, key_first : key_first + HEAD_FEATURES]
        scores = lax.dot_general(
            keys, query_stack, (((1,), (1,)), ((), ())), preferred_element_type=jnp.float32
        ) * HEAD_FEATURES ** (-0.5)
        scores = jnp.where(allowed, scores, MASKED)
        exp_scores = jnp.exp(scores - jnp.max(scores, axis=0, keepdims=True))
        total = jnp.sum(exp_scores, axis=0, keepdims=True)
        probs = (exp_scores / total).astype(jnp.bfloat16)
        late_ref[c] = probs[LATE, : heads * UNIT]
        early_ref[c] = probs[EARLY]
    hidden = rows_ref[:, model_width + kv_width :]
    x_ref[...] = hidden
    x = hidden.astype(jnp.float32)
    mean_square = jnp.mean(x * x, axis=1, keepdims=True)
    inv_ref[...] = jnp.broadcast_to(lax.rsqrt(mean_square + EPSILON), inv_ref.shape)


def block_probs(pieces, seg, seg_row, model_width, kv_width, after=()):
    heads = model_width // kv_width
    key_heads = kv_width // HEAD_FEATURES
    operands = [near(piece) for piece in pieces] + [near(seg)]
    specs = [VMEM] * len(operands) + [ANY] * len(after)
    operands += after
    return pl.pallas_call(
        functools.partial(probs_kernel, len(pieces), seg_row, model_width, kv_width),
        out_shape=(
            jax.ShapeDtypeStruct((key_heads, UNIT, heads * UNIT), jnp.bfloat16),
            jax.ShapeDtypeStruct((key_heads, UNIT, heads * BLOCK), jnp.bfloat16),
            jax.ShapeDtypeStruct((BLOCK, 128), jnp.float32),
            jax.ShapeDtypeStruct((BLOCK, model_width), jnp.bfloat16),
        ),
        in_specs=specs,
        out_specs=(VMEM,) * 4,
        scratch_shapes=[pltpu.VMEM((BLOCK, 2 * model_width + kv_width), jnp.bfloat16)],
        name="probs",
        **params(0.35 if after else 2.0),
    )(*operands)


def unit_math(rows, grads, probs_ref, x_ref, inv_ref, turned_ref, gain_ref, scaled_ref, store, value_ref):
    kv_width, model_width = turned_ref.shape
    heads = model_width // kv_width
    chunk = min(512, model_width)
    inv = inv_ref[rows, :1]
    values = []
    for c in range(kv_width // HEAD_FEATURES):
        first = c * heads * HEAD_FEATURES
        grad_stack = jnp.concatenate(
            [
                grad_ref[part, first + h * HEAD_FEATURES : first + (h + 1) * HEAD_FEATURES]
                for grad_ref, part in grads
                for h in range(heads)
            ],
            axis=0,
        )
        values.append(
            jnp.dot(probs_ref[c], grad_stack, preferred_element_type=jnp.float32).astype(
                jnp.bfloat16
            )
        )
    value = jnp.concatenate(values, axis=1)
    value_ref[...] = (value.astype(jnp.float32) * inv).astype(jnp.bfloat16)
    inner = jnp.zeros((UNIT, 1), jnp.float32)
    for first in range(0, model_width, chunk):
        columns = slice(first, first + chunk)
        normed_grad = jnp.dot(value, turned_ref[:, columns], preferred_element_type=jnp.float32)
        scaled = normed_grad * gain_ref[:, columns]
        scaled_ref[:, columns] = scaled
        x = x_ref[rows, columns].astype(jnp.float32)
        inner = inner + jnp.sum(x * scaled, axis=1, keepdims=True)
    pull = inner * (inv * inv / model_width)
    grad_ref, part = grads[-1]
    for first in range(0, model_width, chunk):
        columns = slice(first, first + chunk)
        x = x_ref[rows, columns].astype(jnp.float32)
        change = inv * (scaled_ref[:, columns] - x * pull)
        grad = grad_ref[part, columns].astype(jnp.float32)
        store(columns, (grad + change).astype(jnp.bfloat16))


def turn_kernel(weight_ref, *refs):
    turned_ref = refs[-1]
    step = min(256, weight_ref.shape[0])
    for first in range(0, weight_ref.shape[0], step):
        turned_ref[:, first : first + step] = weight_ref[first : first + step, :].T


def turn(weight, after=()):
    return pl.pallas_call(
        turn_kernel,
        out_shape=jax.ShapeDtypeStruct(weight.shape[::-1], weight.dtype),
        in_specs=[VMEM] + [ANY] * len(after),
        out_specs=VMEM,
        name="turn",
        **params(1.5),
    )(near(weight), *after)


def layer_kernel(
    live_ref, grad_ref, late_ref, early_ref, inv_ref, x_ref, turned_ref, gain_ref, *rest
):
    out_ref, value_ref, scaled_ref = rest[-3:]
    if len(rest) == 5:

        @pl.when(live_ref[0] == 0)
        def _():
            out_ref[...] = rest[0][...]
            value_ref[...] = rest[1][...]

    @pl.when(live_ref[0] == 1)
    def _():
        for rows, parts, probs_ref in ((LATE, [LATE], late_ref), (EARLY, [LATE, EARLY], early_ref)):

            def store(columns, part, rows=rows):
                out_ref[rows, columns] = part

            grads = [(grad_ref, part) for part in parts]
            unit_math(
                rows, grads, probs_ref, x_ref, inv_ref, turned_ref, gain_ref, scaled_ref, store,
                value_ref.at[rows],
            )


def layer_step(live, grad, block, turned, gain, held=()):
    kv_width, model_width = turned.shape
    operands = [live, grad, *block, turned, gain, *held]
    return pl.pallas_call(
        layer_kernel,
        out_shape=(
            jax.ShapeDtypeStruct((BLOCK, model_width), jnp.bfloat16),
            jax.ShapeDtypeStruct((BLOCK, kv_width), jnp.bfloat16),
        ),
        in_specs=[SMEM] + [VMEM] * (len(operands) - 1),
        out_specs=(VMEM, VMEM),
        scratch_shapes=[pltpu.VMEM((UNIT, model_width), jnp.float32)],
        name="layer",
        **params(1.1),
    )(*operands)


def tick_kernel(tick, rows, parts, kept, late, *refs):
    grads = list(zip(refs, parts))
    probs_ref, inv_ref, x_ref, turned_ref, gain_ref = refs[len(parts) : len(parts) + 5]
    refs = refs[len(parts) + 5 :]
    earlier, refs = refs[: 2 * kept], refs[2 * kept :]
    late_refs = refs[:late]
    kv_width, model_width = turned_ref.shape
    turn = lax.axis_size("section") - 1 - lax.axis_index("section")
    if late:
        outs, (scaled_ref, blocks_ref, value_ref) = refs[late : -3], refs[-3:]
        outs = outs[len(outs) - OUTS[late] :]
    else:
        outs, scaled_ref = refs[-3:-1], refs[-1]
        value_ref = outs[1]
    first_row = BLOCK if late > 2 else 0

    def store(columns, part):
        if late:
            blocks_ref[first_row : first_row + UNIT, columns] = part
        if late <= 2:
            outs[0][:, columns] = part

    @pl.when(turn == tick)
    def _():
        unit_math(
            rows, grads, probs_ref, x_ref, inv_ref, turned_ref, gain_ref, scaled_ref, store,
            value_ref,
        )

    for at in range(kept):

        @pl.when(turn == at)
        def _(at=at):
            store(slice(None), earlier[2 * at][...])
            value_ref[...] = earlier[2 * at + 1][...]

    if not late:
        return
    values = jnp.concatenate([value_ref[...], late_refs[0][...]], axis=0)
    blocks_ref[first_row + UNIT : first_row + BLOCK, :] = late_refs[1][...]
    outs[1 if late == 2 else 0][...] = values
    if late > 2:
        late_a_ref, early_a_ref = late_refs[2:]
        blocks_ref[EARLY, :] = early_a_ref[...]
        blocks_ref[LATE, :] = late_a_ref[...]
    at = place()[1]
    pieces = {2: outs[2]} if late == 2 else dict(enumerate(outs[1:]))
    piece = BLOCK * kv_width // model_width

    def rows_for(k, block):
        first = pl.multiple_of(lax.bitwise_xor(at, k) * piece, piece)
        return blocks_ref[pl.ds(block * BLOCK + first, piece), :]

    block = 0 if late == 2 else 1
    for k, out_ref in pieces.items():
        if k == 2:
            out_ref[:piece, :] = rows_for(2, block)
            for g in range(model_width // kv_width):
                out_ref[piece : 2 * piece, g * kv_width : (g + 1) * kv_width] = values[
                    g * piece : (g + 1) * piece
                ]
            if block == 0:
                out_ref[2 * piece :, :] = rows_for(3, 0)
        elif k == 3:
            out_ref[...] = rows_for(3, 1)
        else:
            out_ref[:piece, :] = rows_for(k, 0)
            out_ref[piece:, :] = rows_for(k, 1)


def tick_step(tick, grads, block, turned, gain, kept=(), late=(), after=(), name=""):
    kv_width, model_width = turned.shape
    low = len(grads) == 2
    arrays = [grad for grad, _ in grads]
    arrays += [block[1] if low else block[0], block[2], block[3], turned, gain]
    arrays += [array for pair in kept for array in pair]
    arrays += late
    operands = [near(array) for array in arrays]
    specs = [VMEM] * len(operands) + [ANY] * len(after)
    bf16 = jnp.bfloat16
    scratch = [pltpu.VMEM((UNIT, model_width), jnp.float32)]
    rows, value = (UNIT, model_width), (UNIT, kv_width)
    shapes = [rows, value]
    if late:
        half = lax.axis_size("dp") // 2
        scratch += [pltpu.VMEM((2 * BLOCK, model_width), bf16), pltpu.VMEM(value, bf16)]
        piece = BLOCK // half
        shapes = [rows, (BLOCK, kv_width), (3 * piece, model_width)]
    if len(late) > 2:
        shapes = [(BLOCK, kv_width)]
        shapes += [(2 * piece, model_width)] * 3 + [(piece, model_width)]
    parts = [part for _, part in grads]
    return pl.pallas_call(
        functools.partial(
            tick_kernel, tick, EARLY if low else LATE, parts, len(kept), len(late)
        ),
        out_shape=tuple(jax.ShapeDtypeStruct(shape, bf16) for shape in shapes),
        in_specs=specs,
        out_specs=(VMEM,) * len(shapes),
        scratch_shapes=scratch,
        name=f"tick{tick}_{name}",
        **params(1.0 if kept else 0.0),
    )(*operands, *after)


def pack_kernel(block, half, piece, query_ref, key_ref, hidden_ref, up_ref, seg_ref, *rest):
    up_out_ref, seg_in_ref, rows_ref, sems = rest[-4:]
    packed = rest[-4 - half : -4]
    side, at, _ = place()
    there = side if block == 0 else 1 - side
    rows = pl.ds(pl.multiple_of(there * BLOCK, BLOCK), BLOCK)
    copies = []

    def copy(source, target):
        made = pltpu.make_async_copy(source, target, sems.at[len(copies)])
        made.start()
        copies.append(made)

    first = 0
    for source in (query_ref, key_ref, hidden_ref):
        width = source.shape[1]
        copy(source.at[rows], rows_ref.at[:, pl.ds(first, width)])
        first += width
    copy(seg_ref, seg_in_ref)
    copy(up_ref.at[rows], up_out_ref.at[pl.ds(0, BLOCK)])
    up_out_ref[BLOCK:, :] = jnp.zeros((16, up_out_ref.shape[1]), jnp.bfloat16)
    if block == 1:
        rest[2][...] = rest[1][...]
        turn_kernel(rest[0], rest[3])
    for made in copies[:4]:
        made.wait()
    ids = seg_in_ref[...].astype(jnp.float32)
    up_out_ref[BLOCK:, : ids.shape[1]] = jnp.broadcast_to(ids, (16, ids.shape[1])).astype(
        jnp.bfloat16
    )
    for k in range(half):
        first = pl.multiple_of(lax.bitwise_xor(at, k) * piece, piece)
        packed[k][...] = rows_ref[pl.ds(first, piece), :]
    copies[4].wait()


def pack(block, half, piece, sources, weight=None, gain=None):
    model_width = sources[0].shape[1]
    width = sum(source.shape[1] for source in sources[:3])
    bf16 = jnp.bfloat16
    operands = [pltpu.with_memory_space_constraint(array, pltpu.HBM) for array in sources]
    specs = [pl.BlockSpec(memory_space=pltpu.HBM)] * len(sources)
    outs = [jax.ShapeDtypeStruct((piece, width), bf16)] * half
    outs.append(jax.ShapeDtypeStruct((BLOCK + 16, model_width), bf16))
    if weight is not None:
        operands += [near(weight), gain]
        specs += [VMEM, VMEM]
        outs = [
            jax.ShapeDtypeStruct(gain.shape, gain.dtype),
            jax.ShapeDtypeStruct(weight.shape[::-1], bf16),
        ] + outs
    return pl.pallas_call(
        functools.partial(pack_kernel, block, half, piece),
        out_shape=tuple(outs),
        in_specs=specs,
        out_specs=(VMEM,) * len(outs),
        scratch_shapes=[
            pltpu.VMEM(sources[-1].shape, jnp.int32),
            pltpu.VMEM((BLOCK, width), bf16),
            pltpu.SemaphoreType.DMA((5,)),
        ],
        name="pack",
        **params(1.2),
    )(*operands)


def columns_kernel(width, distance, first_ref, second_ref, *refs):
    out_ref = refs[-1]
    if distance == 0:
        came_ref, out_ref, handed_ref = refs[0], refs[-2], refs[-1]
        handed_ref[...] = came_ref[came_ref.shape[0] - handed_ref.shape[0] :, :]
    if distance == 4:
        out_ref[2 * BLOCK :, :] = refs[0][...]
    there = lax.div(lax.bitwise_xor(place()[2], distance), 2)
    out_ref[:BLOCK, :] = first_ref[:, columns_of(there, width)]
    out_ref[BLOCK : 2 * BLOCK, :] = second_ref[:, columns_of(there, width)]


def columns_for(distance, blocks, after, came=()):
    model_width = blocks[0][3].shape[1]
    width = 2 * model_width // lax.axis_size("dp")
    shapes = [(2 * BLOCK, width)]
    if distance == 0:
        shapes.append((came[0].shape[0] // 3, model_width))
    if distance == 4:
        shapes = [(3 * BLOCK, width)]
    outs = [jax.ShapeDtypeStruct(shape, jnp.bfloat16) for shape in shapes]
    results = pl.pallas_call(
        functools.partial(columns_kernel, width, distance),
        out_shape=tuple(outs),
        in_specs=[VMEM] * (2 + len(came)) + [ANY] * len(after),
        out_specs=(VMEM,) * len(outs),
        name=f"columns{distance}",
        **params(0.0 if distance else 1.0),
    )(blocks[0][3], blocks[1][3], *came, *after)
    return results if distance == 0 else results[0]


def own_kernel(scale, weight_ref, gain_ref, after_ref, weight_out_ref, gain_out_ref):
    shares = weight_out_ref.shape[0]
    first = pl.multiple_of(place()[2] * shares, shares)
    weight_out_ref[...] = weight_ref[pl.ds(first, shares), :].astype(jnp.float32) * scale
    gain = gain_ref[:, pl.ds(first, shares)]
    column = jnp.sum(jnp.where(diagonal(shares), gain, 0.0), axis=1, keepdims=True)
    gain_out_ref[...] = jnp.broadcast_to(column * scale, gain_out_ref.shape)


def columns_of(pair, width):
    return pl.ds(pl.multiple_of(pair * width, width), width)


def partial_kernel(shares, first, *refs):
    columns, values, (own_out_ref, *other_refs) = refs[:4], refs[4:-3], refs[-3:]
    kv_width = own_out_ref.shape[1]
    parts = []
    for ref in values:
        beside = ref.shape[1] > kv_width
        rows = slice(first, 2 * first) if beside else slice(0, ref.shape[0])
        parts += [ref[rows, at : at + kv_width] for at in range(0, ref.shape[1], kv_width)]
    parts.insert(len(parts) - 3, columns[2][2 * BLOCK :, :])
    value = jnp.concatenate(parts, axis=0)
    mine = lax.rem(place()[2], 2)

    def share(core):
        at = pl.ds(pl.multiple_of(core * shares, shares), shares)
        rows = jnp.concatenate([ref[: 2 * BLOCK, at] for ref in columns], axis=0)
        return lax.dot_general(
            rows, value, (((0,), (0,)), ((), ())), preferred_element_type=jnp.float32
        )

    other = share(1 - mine).astype(jnp.bfloat16)
    for part, ref in enumerate(other_refs):
        ref[...] = other[part * (shares // 2) : (part + 1) * (shares // 2)]
    own_out_ref[...] = share(mine)


def diagonal(size):
    return lax.broadcasted_iota(jnp.int32, (size, size), 0) == lax.broadcasted_iota(
        jnp.int32, (size, size), 1
    )


def rows_kernel(half, first_rows_ref, handed_ref, *refs):
    pieces = refs[:half]
    rows_ref, token_ref = refs[half:]
    side, at, _ = place()
    piece = BLOCK // half
    for block in range(2):
        for k in range(half):
            replica = (side if block == 0 else 1 - side) * half + lax.bitwise_xor(at, k)
            rows = pl.ds(pl.multiple_of(replica * piece, piece), piece)
            source, first = pieces[k], block * piece
            if k == 2:
                source, first = (pieces[k] if block else first_rows_ref), 0
            if k == 3:
                source, first = (pieces[k] if block else handed_ref), 0
            rows_ref[rows, :] = source[first : first + piece, :]
    token_ref[...] = jnp.zeros_like(token_ref)


def finish_kernel(
    own_ref, first_ref, second_ref, weight_ref, gain_ref, after_ref, out_ref, gain_out_ref
):
    other = jnp.concatenate([first_ref[...], second_ref[...]], axis=0)
    total = own_ref[...] + other.astype(jnp.float32)
    out_ref[...] = total * gain_ref[:, :1]
    sums = jnp.sum(total * weight_ref[...], axis=1, keepdims=True)
    gain_out_ref[...] = jnp.sum(
        jnp.where(diagonal(total.shape[0]), sums, 0.0), axis=0, keepdims=True
    )


def direct(hidden, query, key, segments, weight, norm_gain, upstream):
    tokens, model_width = hidden.shape
    kv_width = key.shape[1]
    replicas = lax.axis_size("dp")
    layers = lax.axis_size("section")
    half = replicas // 2
    piece = tokens // replicas
    shares = model_width // replicas

    def swap(array, k):
        return lax.ppermute(array, "dp", [(i, i ^ k) for i in range(replicas)])

    count = 2 * half
    bf16 = jnp.bfloat16
    sources = (query, key, hidden, upstream, segments)
    pieces, ups = [], []
    for b in range(2):
        extra = (weight, norm_gain) if b else ()
        *packed, up = pack(b, half, piece, sources, *extra)
        if b:
            gain, turned, *packed = packed
        pieces.append([packed[0]] + [swap(packed[k], k) for k in range(1, half)])
        ups.append(swap(up, half) if b else up)
    whole = slice(0, UNIT)
    scale = float(tokens * replicas) ** (-0.5)
    blocks, kept, after = [], [], []
    for b in range(2):
        block = block_probs(pieces[b], ups[b], BLOCK, model_width, kv_width, after)
        late, early = (ups[b], LATE), (ups[b], EARLY)
        first = tick_step(0, [late], block, turned, gain, name=UNITS[2 * b])
        second = tick_step(
            0, [late, early], block, turned, gain, after=[first[0]], name=UNITS[2 * b + 1]
        )
        blocks.append(block)
        kept += [[first], [second]]
        after = [second[0]]

    for tick in range(1, layers):
        hop = [(layers - tick, layers - 1 - tick)]
        grads = [(lax.ppermute(unit[-1][0], "section", hop), whole) for unit in kept]
        last = tick == layers - 1
        after, done = [kept[3][-1][0]], []
        if tick == layers - 2:
            own_weight, own_gain = pl.pallas_call(
                functools.partial(own_kernel, scale),
                out_shape=(
                    jax.ShapeDtypeStruct((shares, kv_width), jnp.float32),
                    jax.ShapeDtypeStruct((shares, 128), jnp.float32),
                ),
                in_specs=[VMEM, VMEM, ANY],
                out_specs=(VMEM, VMEM),
                name="own",
                **params(0.0),
            )(near(weight), near(gain), *after)
            columns = {6: swap(columns_for(6, blocks, after + [own_gain]), 6)}
        if last:
            columns[2] = swap(columns_for(2, blocks, after + [columns[6]]), 2)
        for u in range(4):
            needs = grads[u - 1 : u + 1] if u % 2 else grads[u : u + 1]
            late = []
            if last and u == 1:
                late = [done[0][1], done[0][0]]
            if last and u == 3:
                late = [done[2][1], done[2][0], done[0][0], done[1][0]]
                first_value, first_rows = swap(done[1][1], 6), swap(done[1][2], 2)
                columns[4] = swap(columns_for(4, blocks, [], [done[1][1]]), 4)
                after = after + [columns[2], first_value]
            done.append(
                tick_step(
                    tick, needs, blocks[u // 2], turned, gain, kept[u] if last else (), late,
                    after, name=UNITS[u],
                )
            )
            after = [done[u][0]]
            kept[u].append(done[u])
    own_value, *rows = done[3]
    own_first = done[1][1]
    rows = [rows[0]] + [swap(rows[k], k) for k in range(1, half)]
    last_value = swap(own_value, 6)
    columns[0], handed = columns_for(0, blocks, [own_value, columns[4]], [first_rows])
    handed = swap(handed, 1)
    values = [own_first, own_value, first_rows, rows[2], swap(own_value, 4), first_value, last_value]
    own, *other = pl.pallas_call(
        functools.partial(partial_kernel, shares, piece),
        out_shape=(jax.ShapeDtypeStruct((shares, kv_width), jnp.float32),)
        + (jax.ShapeDtypeStruct((shares // 2, kv_width), bf16),) * 2,
        in_specs=[VMEM] * 11,
        out_specs=(VMEM,) * 3,
        name="weight_partial",
        **params(0.0),
    )(*[columns[k] for k in (0, 2, 4, 6)], *values)
    other = [swap(part, 1) for part in other]
    input_grad, token = pl.pallas_call(
        functools.partial(rows_kernel, half),
        out_shape=(
            jax.ShapeDtypeStruct((tokens, model_width), bf16),
            jax.ShapeDtypeStruct((8, 128), jnp.float32),
        ),
        in_specs=[VMEM] * (2 + half),
        out_specs=(VMEM, VMEM),
        name="rows",
        **params(0.8),
    )(first_rows, handed, *rows)
    weight_grad, gain_grad = pl.pallas_call(
        finish_kernel,
        out_shape=(
            jax.ShapeDtypeStruct((shares, kv_width), jnp.float32),
            jax.ShapeDtypeStruct((1, shares), jnp.float32),
        ),
        in_specs=[VMEM] * 5 + [ANY],
        out_specs=(VMEM, VMEM),
        name="finish",
        **params(0.0),
    )(own, *other, own_weight, own_gain, token)
    return input_grad[None], weight_grad[None], gain_grad


def weight_kernel(scale, columns_ref, value_ref, weight_ref, gain_ref, out_ref, gain_out_ref):
    total = lax.dot_general(
        columns_ref[...], value_ref[...], (((0,), (0,)), ((), ())),
        preferred_element_type=jnp.float32,
    ) * scale
    out_ref[...] = total * gain_ref[...]
    product = total * weight_ref[...].astype(jnp.float32)
    sums = lax.dot_general(
        jnp.ones((8, product.shape[1]), jnp.float32), product, (((1,), (1,)), ((), ())),
        preferred_element_type=jnp.float32, precision=lax.Precision.HIGHEST,
    )
    gain_out_ref[...] = sums[:1]


def grouped(hidden, query, key, segments, weight, norm_gain, upstream):
    tokens, model_width = hidden.shape
    kv_width = key.shape[1]
    replicas = lax.axis_size("dp")
    layers = lax.axis_size("section")
    half = replicas // 2
    me = lax.axis_index("dp")
    section = lax.axis_index("section")
    side = me // half
    groups = [list(range(half)), list(range(half, replicas))]
    across = [(i, (i + half) % replicas) for i in range(replicas)]
    shares = model_width // replicas

    def rows_of(array, which, axis=0):
        at = side if which == 0 else 1 - side
        return lax.dynamic_slice_in_dim(array, at * BLOCK, BLOCK, axis)

    def regroup(array):
        return lax.all_to_all(
            array, "dp", split_axis=0, concat_axis=0, axis_index_groups=groups, tiled=True
        )

    def spread(array):
        return lax.all_to_all(array, "dp", split_axis=0, concat_axis=0, tiled=True)

    turned = turn(weight)
    blocks, grads = [], []
    for which in range(2):
        up = rows_of(upstream, which)
        seg = jnp.broadcast_to(segments, (16, 2 * BLOCK)).astype(jnp.bfloat16)
        if which == 1:
            up = lax.ppermute(up, "dp", across)
            seg = lax.ppermute(seg, "dp", across)
        packed = jnp.concatenate(
            [rows_of(query, which), rows_of(key, which), rows_of(hidden, which)], axis=1
        )
        blocks.append(block_probs([regroup(packed)], seg, 0, model_width, kv_width))
        grads.append(up)

    def layer(tick, which, grad, kept):
        live = (section == layers - 1 - tick).astype(jnp.int32)[None]
        return layer_step(live, grad, blocks[which], turned, norm_gain, kept)

    held = [layer(0, which, grads[which], ()) for which in range(2)]
    hops = [(i, i - 1) for i in range(1, layers)]

    def step(tick, held):
        grads = [lax.ppermute(kept[0], "section", hops) for kept in held]
        return [layer(tick, which, grads[which], held[which]) for which in range(2)]

    held = lax.fori_loop(1, layers, step, held)

    columns, values, stored = [], [], []
    for which in range(2):
        block = blocks[which][3].reshape(BLOCK, replicas, shares).transpose(1, 0, 2)
        columns.append(spread(block.reshape(replicas * BLOCK, shares)))
        out, value = held[which]
        stored.append(regroup(out))
        values.append(spread(jnp.tile(value, (replicas, 1))))
    ordered = jnp.where(
        side == 0, jnp.concatenate(stored, axis=0), jnp.concatenate(stored[::-1], axis=0)
    )
    own_weight = lax.dynamic_slice_in_dim(weight, me * shares, shares, 0)
    own_gain = lax.dynamic_slice_in_dim(norm_gain[0], me * shares, shares, 0)
    scale = float(tokens * replicas) ** (-0.5)
    weight_grad, gain_grad = pl.pallas_call(
        functools.partial(weight_kernel, scale),
        out_shape=(
            jax.ShapeDtypeStruct((shares, kv_width), jnp.float32),
            jax.ShapeDtypeStruct((1, shares), jnp.float32),
        ),
        in_specs=[VMEM] * 4,
        out_specs=(VMEM, VMEM),
        name="weight_grad",
    )(
        jnp.concatenate(columns, axis=0),
        jnp.concatenate(values, axis=0),
        own_weight,
        own_gain[:, None],
    )
    return ordered[None], weight_grad[None], gain_grad


def on_device(hidden_in, queries, keys, segments, value_weight, norm_gain, upstream):
    replicas = lax.axis_size("dp")
    piece = hidden_in.shape[1] // replicas
    plan = direct if piece % 16 == 0 and replicas == 8 else grouped
    return plan(
        hidden_in[0], queries[0], keys[0], segments, value_weight[0], norm_gain, upstream
    )


def solution(mesh):
    in_specs = (
        P("section", "dp", None),
        P("section", "dp", None),
        P("section", "dp", None),
        P("dp", None),
        P("section", None, None),
        P("section", None),
        P("dp", None),
    )
    out_specs = (P("section", "dp", None), P("section", "dp", None), P("section", "dp"))
    return jax.shard_map(
        on_device, mesh=mesh, in_specs=in_specs, out_specs=out_specs, check_vma=False
    )
```

```python
import functools

import jax
import jax.numpy as jnp
from jax import lax
from jax.experimental import pallas as pl
from jax.experimental.pallas import tpu as pltpu
from jax.sharding import PartitionSpec as P

HEAD_FEATURES = 128
BLOCK = 64
UNIT = 32
EPSILON = 1e-06
MASKED = -1e30
OUTS = {2: 3, 5: 6}
UNITS = ("a_late", "a_early", "b_late", "b_early")
VMEM = pl.BlockSpec(memory_space=pltpu.VMEM)
SMEM = pl.BlockSpec(memory_space=pltpu.SMEM)


ANY = pl.BlockSpec(memory_space=pl.ANY)


LATE, EARLY = slice(UNIT, BLOCK), slice(0, UNIT)


def params(microseconds):
    flops = int(microseconds * 1.15e9)
    return dict(
        compiler_params=pltpu.CompilerParams(vmem_limit_bytes=16 << 20),
        cost_estimate=pl.CostEstimate(flops=flops, bytes_accessed=0, transcendentals=0),
    )


def near(array):
    return pltpu.with_memory_space_constraint(array, pltpu.VMEM)


def place():
    half = lax.axis_size("dp") // 2
    me = lax.axis_index("dp")
    return lax.div(me, half), lax.rem(me, half), me


def probs_kernel(count, seg_row, model_width, kv_width, *refs):
    pieces, seg_ref = refs[:count], refs[count]
    late_ref, early_ref, inv_ref, x_ref, rows_ref = refs[-5:]
    heads = model_width // kv_width
    rows = BLOCK // count
    side, at, _ = place()
    for k, piece in enumerate(pieces):
        if count == 1:
            rows_ref[...] = piece[...]
        else:
            first = pl.multiple_of(lax.bitwise_xor(at, k) * rows, rows)
            rows_ref[pl.ds(first, rows), :] = piece[...]

    def iota(shape, axis):
        return lax.broadcasted_iota(jnp.int32, shape, axis)

    seg = seg_ref[seg_row : seg_row + 16, : 2 * BLOCK].astype(jnp.float32)[:1]
    shape = (BLOCK, 2 * BLOCK)
    wanted = iota(shape, 1) == side * BLOCK + iota(shape, 0)
    ids = jnp.sum(jnp.where(wanted, seg, 0.0), axis=1, keepdims=True)
    key_code = ids * BLOCK + iota((BLOCK, 1), 0).astype(jnp.float32)
    list_start = ids * BLOCK
    shape = (BLOCK, heads * BLOCK)
    column = iota(shape, 1)
    query_at = lax.rem(column, UNIT) + jnp.where(column < heads * UNIT, UNIT, 0)
    same = iota(shape, 0) == query_at
    query_code = jnp.sum(jnp.where(same, key_code, 0.0), axis=0, keepdims=True)
    query_start = jnp.sum(jnp.where(same, list_start, 0.0), axis=0, keepdims=True)
    allowed = (key_code <= query_code) & (key_code >= query_start)
    for c in range(kv_width // HEAD_FEATURES):
        first = c * heads * HEAD_FEATURES
        query_stack = jnp.concatenate(
            [
                rows_ref[part, first + h * HEAD_FEATURES : first + (h + 1) * HEAD_FEATURES]
                for part in (LATE, EARLY)
                for h in range(heads)
            ],
            axis=0,
        )
        key_first = model_width + c * HEAD_FEATURES
        keys = rows_ref[:, key_first : key_first + HEAD_FEATURES]
        scores = lax.dot_general(
            keys, query_stack, (((1,), (1,)), ((), ())), preferred_element_type=jnp.float32
        ) * HEAD_FEATURES ** (-0.5)
        scores = jnp.where(allowed, scores, MASKED)
        exp_scores = jnp.exp(scores - jnp.max(scores, axis=0, keepdims=True))
        total = jnp.sum(exp_scores, axis=0, keepdims=True)
        probs = (exp_scores / total).astype(jnp.bfloat16)
        late_ref[c] = probs[LATE, : heads * UNIT]
        early_ref[c] = probs[EARLY]
    hidden = rows_ref[:, model_width + kv_width :]
    x_ref[...] = hidden
    x = hidden.astype(jnp.float32)
    mean_square = jnp.mean(x * x, axis=1, keepdims=True)
    inv_ref[...] = jnp.broadcast_to(lax.rsqrt(mean_square + EPSILON), inv_ref.shape)


def block_probs(pieces, seg, seg_row, model_width, kv_width, after=()):
    heads = model_width // kv_width
    key_heads = kv_width // HEAD_FEATURES
    operands = [near(piece) for piece in pieces] + [near(seg)]
    specs = [VMEM] * len(operands) + [ANY] * len(after)
    operands += after
    return pl.pallas_call(
        functools.partial(probs_kernel, len(pieces), seg_row, model_width, kv_width),
        out_shape=(
            jax.ShapeDtypeStruct((key_heads, UNIT, heads * UNIT), jnp.bfloat16),
            jax.ShapeDtypeStruct((key_heads, UNIT, heads * BLOCK), jnp.bfloat16),
            jax.ShapeDtypeStruct((BLOCK, 128), jnp.float32),
            jax.ShapeDtypeStruct((BLOCK, model_width), jnp.bfloat16),
        ),
        in_specs=specs,
        out_specs=(VMEM,) * 4,
        scratch_shapes=[pltpu.VMEM((BLOCK, 2 * model_width + kv_width), jnp.bfloat16)],
        name="probs",
        **params(0.35 if after else 2.0),
    )(*operands)


def unit_math(rows, grads, probs_ref, x_ref, inv_ref, turned_ref, gain_ref, scaled_ref, store, value_ref):
    kv_width, model_width = turned_ref.shape
    heads = model_width // kv_width
    chunk = min(1024, model_width)
    inv = inv_ref[rows, :1]
    values = []
    for c in range(kv_width // HEAD_FEATURES):
        first = c * heads * HEAD_FEATURES
        grad_stack = jnp.concatenate(
            [
                grad_ref[part, first + h * HEAD_FEATURES : first + (h + 1) * HEAD_FEATURES]
                for grad_ref, part in grads
                for h in range(heads)
            ],
            axis=0,
        )
        values.append(
            jnp.dot(probs_ref[c], grad_stack, preferred_element_type=jnp.float32).astype(
                jnp.bfloat16
            )
        )
    value = jnp.concatenate(values, axis=1)
    value_ref[...] = (value.astype(jnp.float32) * inv).astype(jnp.bfloat16)
    inner = jnp.zeros((UNIT, 1), jnp.float32)
    for first in range(0, model_width, chunk):
        columns = slice(first, first + chunk)
        normed_grad = jnp.dot(value, turned_ref[:, columns], preferred_element_type=jnp.float32)
        scaled = normed_grad * gain_ref[:, columns]
        scaled_ref[:, columns] = scaled
        x = x_ref[rows, columns].astype(jnp.float32)
        inner = inner + jnp.sum(x * scaled, axis=1, keepdims=True)
    pull = inner * (inv * inv / model_width)
    grad_ref, part = grads[-1]
    for first in range(0, model_width, chunk):
        columns = slice(first, first + chunk)
        x = x_ref[rows, columns].astype(jnp.float32)
        change = inv * (scaled_ref[:, columns] - x * pull)
        grad = grad_ref[part, columns].astype(jnp.float32)
        store(columns, (grad + change).astype(jnp.bfloat16))


def turn_kernel(weight_ref, *refs):
    turned_ref = refs[-1]
    step = min(256, weight_ref.shape[0])
    for first in range(0, weight_ref.shape[0], step):
        turned_ref[:, first : first + step] = weight_ref[first : first + step, :].T


def turn(weight, after=()):
    return pl.pallas_call(
        turn_kernel,
        out_shape=jax.ShapeDtypeStruct(weight.shape[::-1], weight.dtype),
        in_specs=[VMEM] + [ANY] * len(after),
        out_specs=VMEM,
        name="turn",
        **params(1.5),
    )(near(weight), *after)


def layer_kernel(
    live_ref, grad_ref, late_ref, early_ref, inv_ref, x_ref, turned_ref, gain_ref, *rest
):
    out_ref, value_ref, scaled_ref = rest[-3:]
    if len(rest) == 5:

        @pl.when(live_ref[0] == 0)
        def _():
            out_ref[...] = rest[0][...]
            value_ref[...] = rest[1][...]

    @pl.when(live_ref[0] == 1)
    def _():
        for rows, parts, probs_ref in ((LATE, [LATE], late_ref), (EARLY, [LATE, EARLY], early_ref)):

            def store(columns, part, rows=rows):
                out_ref[rows, columns] = part

            grads = [(grad_ref, part) for part in parts]
            unit_math(
                rows, grads, probs_ref, x_ref, inv_ref, turned_ref, gain_ref, scaled_ref, store,
                value_ref.at[rows],
            )


def layer_step(live, grad, block, turned, gain, held=()):
    kv_width, model_width = turned.shape
    operands = [live, grad, *block, turned, gain, *held]
    return pl.pallas_call(
        layer_kernel,
        out_shape=(
            jax.ShapeDtypeStruct((BLOCK, model_width), jnp.bfloat16),
            jax.ShapeDtypeStruct((BLOCK, kv_width), jnp.bfloat16),
        ),
        in_specs=[SMEM] + [VMEM] * (len(operands) - 1),
        out_specs=(VMEM, VMEM),
        scratch_shapes=[pltpu.VMEM((UNIT, model_width), jnp.float32)],
        name="layer",
        **params(1.1),
    )(*operands)


def tick_kernel(tick, rows, parts, kept, late, *refs):
    grads = list(zip(refs, parts))
    probs_ref, inv_ref, x_ref, turned_ref, gain_ref = refs[len(parts) : len(parts) + 5]
    refs = refs[len(parts) + 5 :]
    earlier, refs = refs[: 2 * kept], refs[2 * kept :]
    late_refs = refs[:late]
    kv_width, model_width = turned_ref.shape
    turn = lax.axis_size("section") - 1 - lax.axis_index("section")
    if late:
        outs, (scaled_ref, blocks_ref, value_ref) = refs[late : -3], refs[-3:]
        outs = outs[len(outs) - OUTS[late] :]
    else:
        outs, scaled_ref = refs[-3:-1], refs[-1]
        value_ref = outs[1]
    first_row = BLOCK if late > 2 else 0

    def store(columns, part):
        if late:
            blocks_ref[first_row : first_row + UNIT, columns] = part
        if late <= 2:
            outs[0][:, columns] = part

    @pl.when(turn == tick)
    def _():
        unit_math(
            rows, grads, probs_ref, x_ref, inv_ref, turned_ref, gain_ref, scaled_ref, store,
            value_ref,
        )

    for at in range(kept):

        @pl.when(turn == at)
        def _(at=at):
            store(slice(None), earlier[2 * at][...])
            value_ref[...] = earlier[2 * at + 1][...]

    if not late:
        return
    values = jnp.concatenate([value_ref[...], late_refs[0][...]], axis=0)
    blocks_ref[first_row + UNIT : first_row + BLOCK, :] = late_refs[1][...]
    outs[1 if late == 2 else 0][...] = values
    if late > 2:
        late_a_ref, early_a_ref, value_a_ref = late_refs[2:]
        outs[1][:BLOCK, :] = value_a_ref[...]
        outs[1][BLOCK:, :] = values
        blocks_ref[EARLY, :] = early_a_ref[...]
        blocks_ref[LATE, :] = late_a_ref[...]
    at = place()[1]
    pieces = {2: outs[2]} if late == 2 else dict(enumerate(outs[2:]))
    piece = BLOCK * kv_width // model_width

    def rows_for(k, block):
        first = pl.multiple_of(lax.bitwise_xor(at, k) * piece, piece)
        return blocks_ref[pl.ds(block * BLOCK + first, piece), :]

    block = 0 if late == 2 else 1
    for k, out_ref in pieces.items():
        if k == 2:
            out_ref[:piece, :] = rows_for(2, block)
            for g in range(model_width // kv_width):
                out_ref[piece : 2 * piece, g * kv_width : (g + 1) * kv_width] = values[
                    g * piece : (g + 1) * piece
                ]
            if block == 0:
                out_ref[2 * piece :, :] = rows_for(3, 0)
        elif k == 3:
            out_ref[...] = rows_for(3, 1)
        else:
            out_ref[:piece, :] = rows_for(k, 0)
            out_ref[piece:, :] = rows_for(k, 1)


def tick_step(tick, grads, block, turned, gain, kept=(), late=(), after=(), name=""):
    kv_width, model_width = turned.shape
    low = len(grads) == 2
    arrays = [grad for grad, _ in grads]
    arrays += [block[1] if low else block[0], block[2], block[3], turned, gain]
    arrays += [array for pair in kept for array in pair]
    arrays += late
    operands = [near(array) for array in arrays]
    specs = [VMEM] * len(operands) + [ANY] * len(after)
    bf16 = jnp.bfloat16
    scratch = [pltpu.VMEM((UNIT, model_width), jnp.float32)]
    rows, value = (UNIT, model_width), (UNIT, kv_width)
    shapes = [rows, value]
    if late:
        half = lax.axis_size("dp") // 2
        scratch += [pltpu.VMEM((2 * BLOCK, model_width), bf16), pltpu.VMEM(value, bf16)]
        piece = BLOCK // half
        shapes = [rows, (BLOCK, kv_width), (3 * piece, model_width)]
    if len(late) > 2:
        shapes = [(BLOCK, kv_width), (2 * BLOCK, kv_width)]
        shapes += [(2 * piece, model_width)] * 3 + [(piece, model_width)]
    parts = [part for _, part in grads]
    return pl.pallas_call(
        functools.partial(
            tick_kernel, tick, EARLY if low else LATE, parts, len(kept), len(late)
        ),
        out_shape=tuple(jax.ShapeDtypeStruct(shape, bf16) for shape in shapes),
        in_specs=specs,
        out_specs=(VMEM,) * len(shapes),
        scratch_shapes=scratch,
        name=f"tick{tick}_{name}",
        **params(1.0 if kept else 0.0),
    )(*operands, *after)


def pack_kernel(block, half, piece, query_ref, key_ref, hidden_ref, up_ref, seg_ref, *rest):
    up_out_ref, seg_in_ref, rows_ref, sems = rest[-4:]
    packed = rest[-4 - half : -4]
    side, at, _ = place()
    there = side if block == 0 else 1 - side
    rows = pl.ds(pl.multiple_of(there * BLOCK, BLOCK), BLOCK)
    copies = []

    def copy(source, target):
        made = pltpu.make_async_copy(source, target, sems.at[len(copies)])
        made.start()
        copies.append(made)

    first = 0
    for source in (query_ref, key_ref, hidden_ref):
        width = source.shape[1]
        copy(source.at[rows], rows_ref.at[:, pl.ds(first, width)])
        first += width
    copy(seg_ref, seg_in_ref)
    copy(up_ref.at[rows], up_out_ref.at[pl.ds(0, BLOCK)])
    up_out_ref[BLOCK:, :] = jnp.zeros((16, up_out_ref.shape[1]), jnp.bfloat16)
    if block == 1:
        rest[2][...] = rest[1][...]
        turn_kernel(rest[0], rest[3])
    for made in copies[:4]:
        made.wait()
    ids = seg_in_ref[...].astype(jnp.float32)
    up_out_ref[BLOCK:, : ids.shape[1]] = jnp.broadcast_to(ids, (16, ids.shape[1])).astype(
        jnp.bfloat16
    )
    for k in range(half):
        first = pl.multiple_of(lax.bitwise_xor(at, k) * piece, piece)
        packed[k][...] = rows_ref[pl.ds(first, piece), :]
    copies[4].wait()


def pack(block, half, piece, sources, weight=None, gain=None):
    model_width = sources[0].shape[1]
    width = sum(source.shape[1] for source in sources[:3])
    bf16 = jnp.bfloat16
    operands = [pltpu.with_memory_space_constraint(array, pltpu.HBM) for array in sources]
    specs = [pl.BlockSpec(memory_space=pltpu.HBM)] * len(sources)
    outs = [jax.ShapeDtypeStruct((piece, width), bf16)] * half
    outs.append(jax.ShapeDtypeStruct((BLOCK + 16, model_width), bf16))
    if weight is not None:
        operands += [near(weight), gain]
        specs += [VMEM, VMEM]
        outs = [
            jax.ShapeDtypeStruct(gain.shape, gain.dtype),
            jax.ShapeDtypeStruct(weight.shape[::-1], bf16),
        ] + outs
    return pl.pallas_call(
        functools.partial(pack_kernel, block, half, piece),
        out_shape=tuple(outs),
        in_specs=specs,
        out_specs=(VMEM,) * len(outs),
        scratch_shapes=[
            pltpu.VMEM(sources[-1].shape, jnp.int32),
            pltpu.VMEM((BLOCK, width), bf16),
            pltpu.SemaphoreType.DMA((5,)),
        ],
        name="pack",
        **params(1.2),
    )(*operands)


def columns_kernel(width, distance, first_ref, second_ref, *refs):
    out_ref = refs[-1]
    if distance == 0:
        came_ref, out_ref, handed_ref = refs[0], refs[-2], refs[-1]
        handed_ref[...] = came_ref[came_ref.shape[0] - handed_ref.shape[0] :, :]
    if distance == 4:
        out_ref[2 * BLOCK :, :] = refs[0][...]
    there = lax.div(lax.bitwise_xor(place()[2], distance), 2)
    out_ref[:BLOCK, :] = first_ref[:, columns_of(there, width)]
    out_ref[BLOCK : 2 * BLOCK, :] = second_ref[:, columns_of(there, width)]


def columns_for(distance, blocks, after, came=()):
    model_width = blocks[0][3].shape[1]
    width = 2 * model_width // lax.axis_size("dp")
    shapes = [(2 * BLOCK, width)]
    if distance == 0:
        shapes.append((came[0].shape[0] // 3, model_width))
    if distance == 4:
        shapes = [(3 * BLOCK, width)]
    outs = [jax.ShapeDtypeStruct(shape, jnp.bfloat16) for shape in shapes]
    results = pl.pallas_call(
        functools.partial(columns_kernel, width, distance),
        out_shape=tuple(outs),
        in_specs=[VMEM] * (2 + len(came)) + [ANY] * len(after),
        out_specs=(VMEM,) * len(outs),
        name=f"columns{distance}",
        **params(0.0 if distance else 1.0),
    )(blocks[0][3], blocks[1][3], *came, *after)
    return results if distance == 0 else results[0]


def own_kernel(scale, weight_ref, gain_ref, after_ref, weight_out_ref, gain_out_ref):
    shares = weight_out_ref.shape[0]
    first = pl.multiple_of(place()[2] * shares, shares)
    weight_out_ref[...] = weight_ref[pl.ds(first, shares), :].astype(jnp.float32) * scale
    gain = gain_ref[:, pl.ds(first, shares)]
    column = jnp.sum(jnp.where(diagonal(shares), gain, 0.0), axis=1, keepdims=True)
    gain_out_ref[...] = jnp.broadcast_to(column * scale, gain_out_ref.shape)


def columns_of(pair, width):
    return pl.ds(pl.multiple_of(pair * width, width), width)


def partial_kernel(shares, first, *refs):
    columns, values, (own_out_ref, *other_refs) = refs[:4], refs[4:-3], refs[-3:]
    kv_width = own_out_ref.shape[1]
    parts = []
    for ref in values:
        beside = ref.shape[1] > kv_width
        rows = slice(first, 2 * first) if beside else slice(0, ref.shape[0])
        parts += [ref[rows, at : at + kv_width] for at in range(0, ref.shape[1], kv_width)]
    parts.insert(len(parts) - 2, columns[2][2 * BLOCK :, :])
    value = jnp.concatenate(parts, axis=0)
    mine = lax.rem(place()[2], 2)

    def share(core):
        at = pl.ds(pl.multiple_of(core * shares, shares), shares)
        rows = jnp.concatenate([ref[: 2 * BLOCK, at] for ref in columns], axis=0)
        return lax.dot_general(
            rows, value, (((0,), (0,)), ((), ())), preferred_element_type=jnp.float32
        )

    other = share(1 - mine).astype(jnp.bfloat16)
    for part, ref in enumerate(other_refs):
        ref[...] = other[part * (shares // 2) : (part + 1) * (shares // 2)]
    own_out_ref[...] = share(mine)


def diagonal(size):
    return lax.broadcasted_iota(jnp.int32, (size, size), 0) == lax.broadcasted_iota(
        jnp.int32, (size, size), 1
    )


def rows_kernel(half, first_rows_ref, handed_ref, *refs):
    pieces = refs[:half]
    rows_ref, token_ref = refs[half:]
    side, at, _ = place()
    piece = BLOCK // half
    for block in range(2):
        for k in range(half):
            replica = (side if block == 0 else 1 - side) * half + lax.bitwise_xor(at, k)
            rows = pl.ds(pl.multiple_of(replica * piece, piece), piece)
            source, first = pieces[k], block * piece
            if k == 2:
                source, first = (pieces[k] if block else first_rows_ref), 0
            if k == 3:
                source, first = (pieces[k] if block else handed_ref), 0
            rows_ref[rows, :] = source[first : first + piece, :]
    token_ref[...] = jnp.zeros_like(token_ref)


def finish_kernel(
    own_ref, first_ref, second_ref, weight_ref, gain_ref, after_ref, out_ref, gain_out_ref
):
    other = jnp.concatenate([first_ref[...], second_ref[...]], axis=0)
    total = own_ref[...] + other.astype(jnp.float32)
    out_ref[...] = total * gain_ref[:, :1]
    sums = jnp.sum(total * weight_ref[...], axis=1, keepdims=True)
    gain_out_ref[...] = jnp.sum(
        jnp.where(diagonal(total.shape[0]), sums, 0.0), axis=0, keepdims=True
    )


def direct(hidden, query, key, segments, weight, norm_gain, upstream):
    tokens, model_width = hidden.shape
    kv_width = key.shape[1]
    replicas = lax.axis_size("dp")
    layers = lax.axis_size("section")
    half = replicas // 2
    piece = tokens // replicas
    shares = model_width // replicas

    def swap(array, k):
        return lax.ppermute(array, "dp", [(i, i ^ k) for i in range(replicas)])

    count = 2 * half
    bf16 = jnp.bfloat16
    sources = (query, key, hidden, upstream, segments)
    pieces, ups = [], []
    for b in range(2):
        extra = (weight, norm_gain) if b else ()
        *packed, up = pack(b, half, piece, sources, *extra)
        if b:
            gain, turned, *packed = packed
        pieces.append([packed[0]] + [swap(packed[k], k) for k in range(1, half)])
        ups.append(swap(up, half) if b else up)
    whole = slice(0, UNIT)
    scale = float(tokens * replicas) ** (-0.5)
    blocks, kept, after = [], [], []
    for b in range(2):
        block = block_probs(pieces[b], ups[b], BLOCK, model_width, kv_width, after)
        late, early = (ups[b], LATE), (ups[b], EARLY)
        first = tick_step(0, [late], block, turned, gain, name=UNITS[2 * b])
        second = tick_step(
            0, [late, early], block, turned, gain, after=[first[0]], name=UNITS[2 * b + 1]
        )
        blocks.append(block)
        kept += [[first], [second]]
        after = [second[0]]

    for tick in range(1, layers):
        hop = [(layers - tick, layers - 1 - tick)]
        grads = [(lax.ppermute(unit[-1][0], "section", hop), whole) for unit in kept]
        last = tick == layers - 1
        after, done = [kept[3][-1][0]], []
        if tick == layers - 2:
            own_weight, own_gain = pl.pallas_call(
                functools.partial(own_kernel, scale),
                out_shape=(
                    jax.ShapeDtypeStruct((shares, kv_width), jnp.float32),
                    jax.ShapeDtypeStruct((shares, 128), jnp.float32),
                ),
                in_specs=[VMEM, VMEM, ANY],
                out_specs=(VMEM, VMEM),
                name="own",
                **params(0.0),
            )(near(weight), near(gain), *after)
            columns = {6: swap(columns_for(6, blocks, after + [own_gain]), 6)}
        if last:
            columns[2] = swap(columns_for(2, blocks, after + [columns[6]]), 2)
        for u in range(4):
            needs = grads[u - 1 : u + 1] if u % 2 else grads[u : u + 1]
            late = []
            if last and u == 1:
                late = [done[0][1], done[0][0]]
            if last and u == 3:
                late = [done[2][1], done[2][0], done[0][0], done[1][0], done[1][1]]
                first_rows = swap(done[1][2], 2)
                columns[4] = swap(columns_for(4, blocks, [], [done[1][1]]), 4)
                after = after + [columns[2]]
            done.append(
                tick_step(
                    tick, needs, blocks[u // 2], turned, gain, kept[u] if last else (), late,
                    after, name=UNITS[u],
                )
            )
            after = [done[u][0]]
            kept[u].append(done[u])
    own_value, own_values, *rows = done[3]
    rows = [rows[0]] + [swap(rows[k], k) for k in range(1, half)]
    far_values, across_value = swap(own_values, 6), swap(own_value, 4)
    columns[0], handed = columns_for(0, blocks, [own_value, columns[4], far_values, across_value], [first_rows])
    handed = swap(handed, 1)
    values = [own_values, first_rows, rows[2], across_value, far_values]
    own, *other = pl.pallas_call(
        functools.partial(partial_kernel, shares, piece),
        out_shape=(jax.ShapeDtypeStruct((shares, kv_width), jnp.float32),)
        + (jax.ShapeDtypeStruct((shares // 2, kv_width), bf16),) * 2,
        in_specs=[VMEM] * 9,
        out_specs=(VMEM,) * 3,
        name="weight_partial",
        **params(0.0),
    )(*[columns[k] for k in (0, 2, 4, 6)], *values)
    other = [swap(part, 1) for part in other]
    input_grad, token = pl.pallas_call(
        functools.partial(rows_kernel, half),
        out_shape=(
            jax.ShapeDtypeStruct((tokens, model_width), bf16),
            jax.ShapeDtypeStruct((8, 128), jnp.float32),
        ),
        in_specs=[VMEM] * (2 + half),
        out_specs=(VMEM, VMEM),
        name="rows",
        **params(0.8),
    )(first_rows, handed, *rows)
    weight_grad, gain_grad = pl.pallas_call(
        finish_kernel,
        out_shape=(
            jax.ShapeDtypeStruct((shares, kv_width), jnp.float32),
            jax.ShapeDtypeStruct((1, shares), jnp.float32),
        ),
        in_specs=[VMEM] * 5 + [ANY],
        out_specs=(VMEM, VMEM),
        name="finish",
        **params(0.0),
    )(own, *other, own_weight, own_gain, token)
    return input_grad[None], weight_grad[None], gain_grad


def weight_kernel(scale, columns_ref, value_ref, weight_ref, gain_ref, out_ref, gain_out_ref):
    total = lax.dot_general(
        columns_ref[...], value_ref[...], (((0,), (0,)), ((), ())),
        preferred_element_type=jnp.float32,
    ) * scale
    out_ref[...] = total * gain_ref[...]
    product = total * weight_ref[...].astype(jnp.float32)
    sums = lax.dot_general(
        jnp.ones((8, product.shape[1]), jnp.float32), product, (((1,), (1,)), ((), ())),
        preferred_element_type=jnp.float32, precision=lax.Precision.HIGHEST,
    )
    gain_out_ref[...] = sums[:1]


def grouped(hidden, query, key, segments, weight, norm_gain, upstream):
    tokens, model_width = hidden.shape
    kv_width = key.shape[1]
    replicas = lax.axis_size("dp")
    layers = lax.axis_size("section")
    half = replicas // 2
    me = lax.axis_index("dp")
    section = lax.axis_index("section")
    side = me // half
    groups = [list(range(half)), list(range(half, replicas))]
    across = [(i, (i + half) % replicas) for i in range(replicas)]
    shares = model_width // replicas

    def rows_of(array, which, axis=0):
        at = side if which == 0 else 1 - side
        return lax.dynamic_slice_in_dim(array, at * BLOCK, BLOCK, axis)

    def regroup(array):
        return lax.all_to_all(
            array, "dp", split_axis=0, concat_axis=0, axis_index_groups=groups, tiled=True
        )

    def spread(array):
        return lax.all_to_all(array, "dp", split_axis=0, concat_axis=0, tiled=True)

    turned = turn(weight)
    blocks, grads = [], []
    for which in range(2):
        up = rows_of(upstream, which)
        seg = jnp.broadcast_to(segments, (16, 2 * BLOCK)).astype(jnp.bfloat16)
        if which == 1:
            up = lax.ppermute(up, "dp", across)
            seg = lax.ppermute(seg, "dp", across)
        packed = jnp.concatenate(
            [rows_of(query, which), rows_of(key, which), rows_of(hidden, which)], axis=1
        )
        blocks.append(block_probs([regroup(packed)], seg, 0, model_width, kv_width))
        grads.append(up)

    def layer(tick, which, grad, kept):
        live = (section == layers - 1 - tick).astype(jnp.int32)[None]
        return layer_step(live, grad, blocks[which], turned, norm_gain, kept)

    held = [layer(0, which, grads[which], ()) for which in range(2)]
    hops = [(i, i - 1) for i in range(1, layers)]

    def step(tick, held):
        grads = [lax.ppermute(kept[0], "section", hops) for kept in held]
        return [layer(tick, which, grads[which], held[which]) for which in range(2)]

    held = lax.fori_loop(1, layers, step, held)

    columns, values, stored = [], [], []
    for which in range(2):
        block = blocks[which][3].reshape(BLOCK, replicas, shares).transpose(1, 0, 2)
        columns.append(spread(block.reshape(replicas * BLOCK, shares)))
        out, value = held[which]
        stored.append(regroup(out))
        values.append(spread(jnp.tile(value, (replicas, 1))))
    ordered = jnp.where(
        side == 0, jnp.concatenate(stored, axis=0), jnp.concatenate(stored[::-1], axis=0)
    )
    own_weight = lax.dynamic_slice_in_dim(weight, me * shares, shares, 0)
    own_gain = lax.dynamic_slice_in_dim(norm_gain[0], me * shares, shares, 0)
    scale = float(tokens * replicas) ** (-0.5)
    weight_grad, gain_grad = pl.pallas_call(
        functools.partial(weight_kernel, scale),
        out_shape=(
            jax.ShapeDtypeStruct((shares, kv_width), jnp.float32),
            jax.ShapeDtypeStruct((1, shares), jnp.float32),
        ),
        in_specs=[VMEM] * 4,
        out_specs=(VMEM, VMEM),
        name="weight_grad",
    )(
        jnp.concatenate(columns, axis=0),
        jnp.concatenate(values, axis=0),
        own_weight,
        own_gain[:, None],
    )
    return ordered[None], weight_grad[None], gain_grad


def on_device(hidden_in, queries, keys, segments, value_weight, norm_gain, upstream):
    replicas = lax.axis_size("dp")
    piece = hidden_in.shape[1] // replicas
    plan = direct if piece % 16 == 0 and replicas == 8 else grouped
    return plan(
        hidden_in[0], queries[0], keys[0], segments, value_weight[0], norm_gain, upstream
    )


def solution(mesh):
    in_specs = (
        P("section", "dp", None),
        P("section", "dp", None),
        P("section", "dp", None),
        P("dp", None),
        P("section", None, None),
        P("section", None),
        P("dp", None),
    )
    out_specs = (P("section", "dp", None), P("section", "dp", None), P("section", "dp"))
    return jax.shard_map(
        on_device, mesh=mesh, in_specs=in_specs, out_specs=out_specs, check_vma=False
    )
```

```python
import functools

import jax
import jax.numpy as jnp
from jax import lax
from jax.experimental import pallas as pl
from jax.experimental.pallas import tpu as pltpu
from jax.sharding import PartitionSpec as P

HEAD_FEATURES = 128
BLOCK = 64
UNIT = 32
EPSILON = 1e-06
MASKED = -1e30
OUTS = {2: 3, 5: 6}
UNITS = ("a_late", "a_early", "b_late", "b_early")
VMEM = pl.BlockSpec(memory_space=pltpu.VMEM)
SMEM = pl.BlockSpec(memory_space=pltpu.SMEM)


ANY = pl.BlockSpec(memory_space=pl.ANY)


LATE, EARLY = slice(UNIT, BLOCK), slice(0, UNIT)


def params(microseconds):
    flops = int(microseconds * 1.15e9)
    return dict(
        compiler_params=pltpu.CompilerParams(vmem_limit_bytes=16 << 20),
        cost_estimate=pl.CostEstimate(flops=flops, bytes_accessed=0, transcendentals=0),
    )


def near(array):
    return pltpu.with_memory_space_constraint(array, pltpu.VMEM)


def place():
    half = lax.axis_size("dp") // 2
    me = lax.axis_index("dp")
    return lax.div(me, half), lax.rem(me, half), me


def probs_kernel(count, seg_row, model_width, kv_width, *refs):
    pieces, seg_ref = refs[:count], refs[count]
    late_ref, early_ref, inv_ref, x_ref, rows_ref = refs[-5:]
    heads = model_width // kv_width
    rows = BLOCK // count
    side, at, _ = place()
    for k, piece in enumerate(pieces):
        if count == 1:
            rows_ref[...] = piece[...]
        else:
            first = pl.multiple_of(lax.bitwise_xor(at, k) * rows, rows)
            rows_ref[pl.ds(first, rows), :] = piece[...]

    def iota(shape, axis):
        return lax.broadcasted_iota(jnp.int32, shape, axis)

    seg = seg_ref[seg_row : seg_row + 16, : 2 * BLOCK].astype(jnp.float32)[:1]
    shape = (BLOCK, 2 * BLOCK)
    wanted = iota(shape, 1) == side * BLOCK + iota(shape, 0)
    ids = jnp.sum(jnp.where(wanted, seg, 0.0), axis=1, keepdims=True)
    key_code = ids * BLOCK + iota((BLOCK, 1), 0).astype(jnp.float32)
    list_start = ids * BLOCK
    shape = (BLOCK, heads * BLOCK)
    column = iota(shape, 1)
    query_at = lax.rem(column, UNIT) + jnp.where(column < heads * UNIT, UNIT, 0)
    same = iota(shape, 0) == query_at
    query_code = jnp.sum(jnp.where(same, key_code, 0.0), axis=0, keepdims=True)
    query_start = jnp.sum(jnp.where(same, list_start, 0.0), axis=0, keepdims=True)
    allowed = (key_code <= query_code) & (key_code >= query_start)
    for c in range(kv_width // HEAD_FEATURES):
        first = c * heads * HEAD_FEATURES
        query_stack = jnp.concatenate(
            [
                rows_ref[part, first + h * HEAD_FEATURES : first + (h + 1) * HEAD_FEATURES]
                for part in (LATE, EARLY)
                for h in range(heads)
            ],
            axis=0,
        )
        key_first = model_width + c * HEAD_FEATURES
        keys = rows_ref[:, key_first : key_first + HEAD_FEATURES]
        scores = lax.dot_general(
            keys, query_stack, (((1,), (1,)), ((), ())), preferred_element_type=jnp.float32
        ) * HEAD_FEATURES ** (-0.5)
        scores = jnp.where(allowed, scores, MASKED)
        exp_scores = jnp.exp(scores - jnp.max(scores, axis=0, keepdims=True))
        total = jnp.sum(exp_scores, axis=0, keepdims=True)
        probs = (exp_scores / total).astype(jnp.bfloat16)
        late_ref[c] = probs[LATE, : heads * UNIT]
        early_ref[c] = probs[EARLY]
    hidden = rows_ref[:, model_width + kv_width :]
    x_ref[...] = hidden
    x = hidden.astype(jnp.float32)
    mean_square = jnp.mean(x * x, axis=1, keepdims=True)
    inv_ref[...] = jnp.broadcast_to(lax.rsqrt(mean_square + EPSILON), inv_ref.shape)


def block_probs(pieces, seg, seg_row, model_width, kv_width, after=()):
    heads = model_width // kv_width
    key_heads = kv_width // HEAD_FEATURES
    operands = [near(piece) for piece in pieces] + [near(seg)]
    specs = [VMEM] * len(operands) + [ANY] * len(after)
    operands += after
    return pl.pallas_call(
        functools.partial(probs_kernel, len(pieces), seg_row, model_width, kv_width),
        out_shape=(
            jax.ShapeDtypeStruct((key_heads, UNIT, heads * UNIT), jnp.bfloat16),
            jax.ShapeDtypeStruct((key_heads, UNIT, heads * BLOCK), jnp.bfloat16),
            jax.ShapeDtypeStruct((BLOCK, 128), jnp.float32),
            jax.ShapeDtypeStruct((BLOCK, model_width), jnp.bfloat16),
        ),
        in_specs=specs,
        out_specs=(VMEM,) * 4,
        scratch_shapes=[pltpu.VMEM((BLOCK, 2 * model_width + kv_width), jnp.bfloat16)],
        name="probs",
        **params(0.35 if after else 2.0),
    )(*operands)


def unit_math(rows, grads, probs_ref, x_ref, inv_ref, turned_ref, gain_ref, scaled_ref, store, value_ref):
    kv_width, model_width = turned_ref.shape
    heads = model_width // kv_width
    chunk = min(512, model_width)
    inv = inv_ref[rows, :1]
    values = []
    for c in range(kv_width // HEAD_FEATURES):
        first = c * heads * HEAD_FEATURES
        grad_stack = jnp.concatenate(
            [
                grad_ref[part, first + h * HEAD_FEATURES : first + (h + 1) * HEAD_FEATURES]
                for grad_ref, part in grads
                for h in range(heads)
            ],
            axis=0,
        )
        values.append(
            jnp.dot(probs_ref[c], grad_stack, preferred_element_type=jnp.float32).astype(
                jnp.bfloat16
            )
        )
    value = jnp.concatenate(values, axis=1)
    value_ref[...] = (value.astype(jnp.float32) * inv).astype(jnp.bfloat16)
    inner = jnp.zeros((UNIT, 1), jnp.float32)
    for first in range(0, model_width, chunk):
        columns = slice(first, first + chunk)
        normed_grad = jnp.dot(value, turned_ref[:, columns], preferred_element_type=jnp.float32)
        scaled = normed_grad * gain_ref[:, columns]
        scaled_ref[:, columns] = scaled
        x = x_ref[rows, columns].astype(jnp.float32)
        inner = inner + jnp.sum(x * scaled, axis=1, keepdims=True)
    pull = inner * (inv * inv / model_width)
    grad_ref, part = grads[-1]
    for first in range(0, model_width, chunk):
        columns = slice(first, first + chunk)
        x = x_ref[rows, columns].astype(jnp.float32)
        change = inv * (scaled_ref[:, columns] - x * pull)
        grad = grad_ref[part, columns].astype(jnp.float32)
        store(columns, (grad + change).astype(jnp.bfloat16))


def turn_kernel(weight_ref, *refs):
    turned_ref = refs[-1]
    step = min(256, weight_ref.shape[0])
    for first in range(0, weight_ref.shape[0], step):
        turned_ref[:, first : first + step] = weight_ref[first : first + step, :].T


def turn(weight, after=()):
    return pl.pallas_call(
        turn_kernel,
        out_shape=jax.ShapeDtypeStruct(weight.shape[::-1], weight.dtype),
        in_specs=[VMEM] + [ANY] * len(after),
        out_specs=VMEM,
        name="turn",
        **params(1.5),
    )(near(weight), *after)


def layer_kernel(
    live_ref, grad_ref, late_ref, early_ref, inv_ref, x_ref, turned_ref, gain_ref, *rest
):
    out_ref, value_ref, scaled_ref = rest[-3:]
    if len(rest) == 5:

        @pl.when(live_ref[0] == 0)
        def _():
            out_ref[...] = rest[0][...]
            value_ref[...] = rest[1][...]

    @pl.when(live_ref[0] == 1)
    def _():
        for rows, parts, probs_ref in ((LATE, [LATE], late_ref), (EARLY, [LATE, EARLY], early_ref)):

            def store(columns, part, rows=rows):
                out_ref[rows, columns] = part

            grads = [(grad_ref, part) for part in parts]
            unit_math(
                rows, grads, probs_ref, x_ref, inv_ref, turned_ref, gain_ref, scaled_ref, store,
                value_ref.at[rows],
            )


def layer_step(live, grad, block, turned, gain, held=()):
    kv_width, model_width = turned.shape
    operands = [live, grad, *block, turned, gain, *held]
    return pl.pallas_call(
        layer_kernel,
        out_shape=(
            jax.ShapeDtypeStruct((BLOCK, model_width), jnp.bfloat16),
            jax.ShapeDtypeStruct((BLOCK, kv_width), jnp.bfloat16),
        ),
        in_specs=[SMEM] + [VMEM] * (len(operands) - 1),
        out_specs=(VMEM, VMEM),
        scratch_shapes=[pltpu.VMEM((UNIT, model_width), jnp.float32)],
        name="layer",
        **params(1.1),
    )(*operands)


def tick_kernel(tick, rows, parts, kept, late, *refs):
    grads = list(zip(refs, parts))
    probs_ref, inv_ref, x_ref, turned_ref, gain_ref = refs[len(parts) : len(parts) + 5]
    refs = refs[len(parts) + 5 :]
    earlier, refs = refs[: 2 * kept], refs[2 * kept :]
    late_refs = refs[:late]
    kv_width, model_width = turned_ref.shape
    turn = lax.axis_size("section") - 1 - lax.axis_index("section")
    if late:
        outs, (scaled_ref, blocks_ref, value_ref) = refs[late : -3], refs[-3:]
        outs = outs[len(outs) - OUTS[late] :]
    else:
        outs, scaled_ref = refs[-3:-1], refs[-1]
        value_ref = outs[1]
    first_row = BLOCK if late > 2 else 0

    def store(columns, part):
        if late:
            blocks_ref[first_row : first_row + UNIT, columns] = part
        if late <= 2:
            outs[0][:, columns] = part

    @pl.when(turn == tick)
    def _():
        unit_math(
            rows, grads, probs_ref, x_ref, inv_ref, turned_ref, gain_ref, scaled_ref, store,
            value_ref,
        )

    for at in range(kept):

        @pl.when(turn == at)
        def _(at=at):
            store(slice(None), earlier[2 * at][...])
            value_ref[...] = earlier[2 * at + 1][...]

    if not late:
        return
    values = jnp.concatenate([value_ref[...], late_refs[0][...]], axis=0)
    blocks_ref[first_row + UNIT : first_row + BLOCK, :] = late_refs[1][...]
    outs[1 if late == 2 else 0][...] = values
    if late > 2:
        late_a_ref, early_a_ref, value_a_ref = late_refs[2:]
        outs[1][:BLOCK, :] = value_a_ref[...]
        outs[1][BLOCK:, :] = values
        blocks_ref[EARLY, :] = early_a_ref[...]
        blocks_ref[LATE, :] = late_a_ref[...]
    at = place()[1]
    pieces = {2: outs[2]} if late == 2 else dict(enumerate(outs[2:]))
    piece = BLOCK * kv_width // model_width

    def rows_for(k, block):
        first = pl.multiple_of(lax.bitwise_xor(at, k) * piece, piece)
        return blocks_ref[pl.ds(block * BLOCK + first, piece), :]

    block = 0 if late == 2 else 1
    for k, out_ref in pieces.items():
        if k == 2:
            out_ref[:piece, :] = rows_for(2, block)
            for g in range(model_width // kv_width):
                out_ref[piece : 2 * piece, g * kv_width : (g + 1) * kv_width] = values[
                    g * piece : (g + 1) * piece
                ]
            if block == 0:
                out_ref[2 * piece :, :] = rows_for(3, 0)
        elif k == 3:
            out_ref[...] = rows_for(3, 1)
        else:
            out_ref[:piece, :] = rows_for(k, 0)
            out_ref[piece:, :] = rows_for(k, 1)


def tick_step(tick, grads, block, turned, gain, kept=(), late=(), after=(), name=""):
    kv_width, model_width = turned.shape
    low = len(grads) == 2
    arrays = [grad for grad, _ in grads]
    arrays += [block[1] if low else block[0], block[2], block[3], turned, gain]
    arrays += [array for pair in kept for array in pair]
    arrays += late
    operands = [near(array) for array in arrays]
    specs = [VMEM] * len(operands) + [ANY] * len(after)
    bf16 = jnp.bfloat16
    scratch = [pltpu.VMEM((UNIT, model_width), jnp.float32)]
    rows, value = (UNIT, model_width), (UNIT, kv_width)
    shapes = [rows, value]
    if late:
        half = lax.axis_size("dp") // 2
        scratch += [pltpu.VMEM((2 * BLOCK, model_width), bf16), pltpu.VMEM(value, bf16)]
        piece = BLOCK // half
        shapes = [rows, (BLOCK, kv_width), (3 * piece, model_width)]
    if len(late) > 2:
        shapes = [(BLOCK, kv_width), (2 * BLOCK, kv_width)]
        shapes += [(2 * piece, model_width)] * 3 + [(piece, model_width)]
    parts = [part for _, part in grads]
    return pl.pallas_call(
        functools.partial(
            tick_kernel, tick, EARLY if low else LATE, parts, len(kept), len(late)
        ),
        out_shape=tuple(jax.ShapeDtypeStruct(shape, bf16) for shape in shapes),
        in_specs=specs,
        out_specs=(VMEM,) * len(shapes),
        scratch_shapes=scratch,
        name=f"tick{tick}_{name}",
        **params(1.0 if kept else 0.0),
    )(*operands, *after)


def pack_kernel(block, half, piece, query_ref, key_ref, hidden_ref, up_ref, seg_ref, *rest):
    up_out_ref, seg_in_ref, rows_ref, sems = rest[-4:]
    packed = rest[-4 - half : -4]
    side, at, _ = place()
    there = side if block == 0 else 1 - side
    rows = pl.ds(pl.multiple_of(there * BLOCK, BLOCK), BLOCK)
    copies = []

    def copy(source, target):
        made = pltpu.make_async_copy(source, target, sems.at[len(copies)])
        made.start()
        copies.append(made)

    first = 0
    for source in (query_ref, key_ref, hidden_ref):
        width = source.shape[1]
        copy(source.at[rows], rows_ref.at[:, pl.ds(first, width)])
        first += width
    copy(seg_ref, seg_in_ref)
    copy(up_ref.at[rows], up_out_ref.at[pl.ds(0, BLOCK)])
    up_out_ref[BLOCK:, :] = jnp.zeros((16, up_out_ref.shape[1]), jnp.bfloat16)
    if block == 1:
        rest[2][...] = rest[1][...]
        turn_kernel(rest[0], rest[3])
    for made in copies[:4]:
        made.wait()
    ids = seg_in_ref[...].astype(jnp.float32)
    up_out_ref[BLOCK:, : ids.shape[1]] = jnp.broadcast_to(ids, (16, ids.shape[1])).astype(
        jnp.bfloat16
    )
    for k in range(half):
        first = pl.multiple_of(lax.bitwise_xor(at, k) * piece, piece)
        packed[k][...] = rows_ref[pl.ds(first, piece), :]
    copies[4].wait()


def pack(block, half, piece, sources, weight=None, gain=None):
    model_width = sources[0].shape[1]
    width = sum(source.shape[1] for source in sources[:3])
    bf16 = jnp.bfloat16
    operands = [pltpu.with_memory_space_constraint(array, pltpu.HBM) for array in sources]
    specs = [pl.BlockSpec(memory_space=pltpu.HBM)] * len(sources)
    outs = [jax.ShapeDtypeStruct((piece, width), bf16)] * half
    outs.append(jax.ShapeDtypeStruct((BLOCK + 16, model_width), bf16))
    if weight is not None:
        operands += [near(weight), gain]
        specs += [VMEM, VMEM]
        outs = [
            jax.ShapeDtypeStruct(gain.shape, gain.dtype),
            jax.ShapeDtypeStruct(weight.shape[::-1], bf16),
        ] + outs
    return pl.pallas_call(
        functools.partial(pack_kernel, block, half, piece),
        out_shape=tuple(outs),
        in_specs=specs,
        out_specs=(VMEM,) * len(outs),
        scratch_shapes=[
            pltpu.VMEM(sources[-1].shape, jnp.int32),
            pltpu.VMEM((BLOCK, width), bf16),
            pltpu.SemaphoreType.DMA((5,)),
        ],
        name="pack",
        **params(1.2),
    )(*operands)


def columns_kernel(width, distance, first_ref, second_ref, *refs):
    out_ref = refs[-1]
    if distance == 0:
        came_ref, out_ref, handed_ref = refs[0], refs[-2], refs[-1]
        handed_ref[...] = came_ref[came_ref.shape[0] - handed_ref.shape[0] :, :]
    if distance == 4:
        out_ref[2 * BLOCK :, :] = refs[0][...]
    there = lax.div(lax.bitwise_xor(place()[2], distance), 2)
    out_ref[:BLOCK, :] = first_ref[:, columns_of(there, width)]
    out_ref[BLOCK : 2 * BLOCK, :] = second_ref[:, columns_of(there, width)]


def columns_for(distance, blocks, after, came=()):
    model_width = blocks[0][3].shape[1]
    width = 2 * model_width // lax.axis_size("dp")
    shapes = [(2 * BLOCK, width)]
    if distance == 0:
        shapes.append((came[0].shape[0] // 3, model_width))
    if distance == 4:
        shapes = [(3 * BLOCK, width)]
    outs = [jax.ShapeDtypeStruct(shape, jnp.bfloat16) for shape in shapes]
    results = pl.pallas_call(
        functools.partial(columns_kernel, width, distance),
        out_shape=tuple(outs),
        in_specs=[VMEM] * (2 + len(came)) + [ANY] * len(after),
        out_specs=(VMEM,) * len(outs),
        name=f"columns{distance}",
        **params(0.0 if distance else 1.0),
    )(blocks[0][3], blocks[1][3], *came, *after)
    return results if distance == 0 else results[0]


def own_kernel(scale, weight_ref, gain_ref, after_ref, weight_out_ref, gain_out_ref):
    shares = weight_out_ref.shape[0]
    first = pl.multiple_of(place()[2] * shares, shares)
    weight_out_ref[...] = weight_ref[pl.ds(first, shares), :].astype(jnp.float32) * scale
    gain = gain_ref[:, pl.ds(first, shares)]
    column = jnp.sum(jnp.where(diagonal(shares), gain, 0.0), axis=1, keepdims=True)
    gain_out_ref[...] = jnp.broadcast_to(column * scale, gain_out_ref.shape)


def columns_of(pair, width):
    return pl.ds(pl.multiple_of(pair * width, width), width)


def partial_kernel(shares, first, for_other, *refs):
    columns, values, out_ref = refs[:4], refs[4:9], refs[-1]
    kv_width = out_ref.shape[1]
    parts = []
    for ref in values:
        beside = ref.shape[1] > kv_width
        rows = slice(first, 2 * first) if beside else slice(0, ref.shape[0])
        parts += [ref[rows, at : at + kv_width] for at in range(0, ref.shape[1], kv_width)]
    parts.insert(len(parts) - 2, columns[2][2 * BLOCK :, :])
    value = jnp.concatenate(parts, axis=0)
    mine = lax.rem(place()[2], 2)
    core = 1 - mine if for_other else mine
    at = pl.ds(pl.multiple_of(core * shares, shares), shares)
    rows = jnp.concatenate([ref[: 2 * BLOCK, at] for ref in columns], axis=0)
    out_ref[...] = lax.dot_general(
        rows, value, (((0,), (0,)), ((), ())), preferred_element_type=jnp.float32
    ).astype(out_ref.dtype)


def partial_sums(shares, piece, for_other, columns, values, after=()):
    kv_width = values[0].shape[1]
    return pl.pallas_call(
        functools.partial(partial_kernel, shares, piece, for_other),
        out_shape=jax.ShapeDtypeStruct(
            (shares, kv_width), jnp.bfloat16 if for_other else jnp.float32
        ),
        in_specs=[VMEM] * 9 + [ANY] * len(after),
        out_specs=VMEM,
        name="partial_other" if for_other else "partial_own",
        **params(0.0 if for_other else 0.5),
    )(*[columns[k] for k in (0, 2, 4, 6)], *values, *after)


def diagonal(size):
    return lax.broadcasted_iota(jnp.int32, (size, size), 0) == lax.broadcasted_iota(
        jnp.int32, (size, size), 1
    )


def rows_kernel(half, first_rows_ref, handed_ref, *refs):
    pieces = refs[:half]
    rows_ref, token_ref = refs[half:]
    side, at, _ = place()
    piece = BLOCK // half
    for block in range(2):
        for k in range(half):
            replica = (side if block == 0 else 1 - side) * half + lax.bitwise_xor(at, k)
            rows = pl.ds(pl.multiple_of(replica * piece, piece), piece)
            source, first = pieces[k], block * piece
            if k == 2:
                source, first = (pieces[k] if block else first_rows_ref), 0
            if k == 3:
                source, first = (pieces[k] if block else handed_ref), 0
            rows_ref[rows, :] = source[first : first + piece, :]
    token_ref[...] = jnp.zeros_like(token_ref)


def finish_kernel(
    own_ref, other_ref, weight_ref, gain_ref, after_ref, out_ref, gain_out_ref
):
    total = own_ref[...] + other_ref[...].astype(jnp.float32)
    out_ref[...] = total * gain_ref[:, :1]
    sums = jnp.sum(total * weight_ref[...], axis=1, keepdims=True)
    gain_out_ref[...] = jnp.sum(
        jnp.where(diagonal(total.shape[0]), sums, 0.0), axis=0, keepdims=True
    )


def direct(hidden, query, key, segments, weight, norm_gain, upstream):
    tokens, model_width = hidden.shape
    kv_width = key.shape[1]
    replicas = lax.axis_size("dp")
    layers = lax.axis_size("section")
    half = replicas // 2
    piece = tokens // replicas
    shares = model_width // replicas

    def swap(array, k):
        return lax.ppermute(array, "dp", [(i, i ^ k) for i in range(replicas)])

    count = 2 * half
    bf16 = jnp.bfloat16
    sources = (query, key, hidden, upstream, segments)
    pieces, ups = [], []
    for b in range(2):
        extra = (weight, norm_gain) if b else ()
        *packed, up = pack(b, half, piece, sources, *extra)
        if b:
            gain, turned, *packed = packed
        pieces.append([packed[0]] + [swap(packed[k], k) for k in range(1, half)])
        ups.append(swap(up, half) if b else up)
    whole = slice(0, UNIT)
    scale = float(tokens * replicas) ** (-0.5)
    blocks, kept, after = [], [], []
    for b in range(2):
        block = block_probs(pieces[b], ups[b], BLOCK, model_width, kv_width, after)
        late, early = (ups[b], LATE), (ups[b], EARLY)
        first = tick_step(0, [late], block, turned, gain, name=UNITS[2 * b])
        second = tick_step(
            0, [late, early], block, turned, gain, after=[first[0]], name=UNITS[2 * b + 1]
        )
        blocks.append(block)
        kept += [[first], [second]]
        after = [second[0]]

    for tick in range(1, layers):
        hop = [(layers - tick, layers - 1 - tick)]
        grads = [(lax.ppermute(unit[-1][0], "section", hop), whole) for unit in kept]
        last = tick == layers - 1
        after, done = [kept[3][-1][0]], []
        if tick == layers - 2:
            own_weight, own_gain = pl.pallas_call(
                functools.partial(own_kernel, scale),
                out_shape=(
                    jax.ShapeDtypeStruct((shares, kv_width), jnp.float32),
                    jax.ShapeDtypeStruct((shares, 128), jnp.float32),
                ),
                in_specs=[VMEM, VMEM, ANY],
                out_specs=(VMEM, VMEM),
                name="own",
                **params(0.0),
            )(near(weight), near(gain), *after)
            columns = {6: swap(columns_for(6, blocks, after + [own_gain]), 6)}
        if last:
            columns[2] = swap(columns_for(2, blocks, after + [columns[6]]), 2)
        for u in range(4):
            needs = grads[u - 1 : u + 1] if u % 2 else grads[u : u + 1]
            late = []
            if last and u == 1:
                late = [done[0][1], done[0][0]]
            if last and u == 3:
                late = [done[2][1], done[2][0], done[0][0], done[1][0], done[1][1]]
                first_rows = swap(done[1][2], 2)
                columns[4] = swap(columns_for(4, blocks, [], [done[1][1]]), 4)
                after = after + [columns[2]]
            done.append(
                tick_step(
                    tick, needs, blocks[u // 2], turned, gain, kept[u] if last else (), late,
                    after, name=UNITS[u],
                )
            )
            after = [done[u][0]]
            kept[u].append(done[u])
    own_value, own_values, *rows = done[3]
    rows = [rows[0]] + [swap(rows[k], k) for k in range(1, half)]
    far_values, across_value = swap(own_values, 6), swap(own_value, 4)
    columns[0], handed = columns_for(0, blocks, [own_value, columns[4], across_value], [first_rows])
    handed = swap(handed, 1)
    values = [own_values, first_rows, rows[2], across_value, far_values]
    other = partial_sums(shares, piece, True, columns, values)
    own = partial_sums(shares, piece, False, columns, values, [other])
    other = swap(other, 1)
    input_grad, token = pl.pallas_call(
        functools.partial(rows_kernel, half),
        out_shape=(
            jax.ShapeDtypeStruct((tokens, model_width), bf16),
            jax.ShapeDtypeStruct((8, 128), jnp.float32),
        ),
        in_specs=[VMEM] * (2 + half),
        out_specs=(VMEM, VMEM),
        name="rows",
        **params(3.0),
    )(first_rows, handed, *rows)
    weight_grad, gain_grad = pl.pallas_call(
        finish_kernel,
        out_shape=(
            jax.ShapeDtypeStruct((shares, kv_width), jnp.float32),
            jax.ShapeDtypeStruct((1, shares), jnp.float32),
        ),
        in_specs=[VMEM] * 4 + [ANY],
        out_specs=(VMEM, VMEM),
        name="finish",
        **params(0.0),
    )(own, other, own_weight, own_gain, token)
    return input_grad[None], weight_grad[None], gain_grad


def weight_kernel(scale, columns_ref, value_ref, weight_ref, gain_ref, out_ref, gain_out_ref):
    total = lax.dot_general(
        columns_ref[...], value_ref[...], (((0,), (0,)), ((), ())),
        preferred_element_type=jnp.float32,
    ) * scale
    out_ref[...] = total * gain_ref[...]
    product = total * weight_ref[...].astype(jnp.float32)
    sums = lax.dot_general(
        jnp.ones((8, product.shape[1]), jnp.float32), product, (((1,), (1,)), ((), ())),
        preferred_element_type=jnp.float32, precision=lax.Precision.HIGHEST,
    )
    gain_out_ref[...] = sums[:1]


def grouped(hidden, query, key, segments, weight, norm_gain, upstream):
    tokens, model_width = hidden.shape
    kv_width = key.shape[1]
    replicas = lax.axis_size("dp")
    layers = lax.axis_size("section")
    half = replicas // 2
    me = lax.axis_index("dp")
    section = lax.axis_index("section")
    side = me // half
    groups = [list(range(half)), list(range(half, replicas))]
    across = [(i, (i + half) % replicas) for i in range(replicas)]
    shares = model_width // replicas

    def rows_of(array, which, axis=0):
        at = side if which == 0 else 1 - side
        return lax.dynamic_slice_in_dim(array, at * BLOCK, BLOCK, axis)

    def regroup(array):
        return lax.all_to_all(
            array, "dp", split_axis=0, concat_axis=0, axis_index_groups=groups, tiled=True
        )

    def spread(array):
        return lax.all_to_all(array, "dp", split_axis=0, concat_axis=0, tiled=True)

    turned = turn(weight)
    blocks, grads = [], []
    for which in range(2):
        up = rows_of(upstream, which)
        seg = jnp.broadcast_to(segments, (16, 2 * BLOCK)).astype(jnp.bfloat16)
        if which == 1:
            up = lax.ppermute(up, "dp", across)
            seg = lax.ppermute(seg, "dp", across)
        packed = jnp.concatenate(
            [rows_of(query, which), rows_of(key, which), rows_of(hidden, which)], axis=1
        )
        blocks.append(block_probs([regroup(packed)], seg, 0, model_width, kv_width))
        grads.append(up)

    def layer(tick, which, grad, kept):
        live = (section == layers - 1 - tick).astype(jnp.int32)[None]
        return layer_step(live, grad, blocks[which], turned, norm_gain, kept)

    held = [layer(0, which, grads[which], ()) for which in range(2)]
    hops = [(i, i - 1) for i in range(1, layers)]

    def step(tick, held):
        grads = [lax.ppermute(kept[0], "section", hops) for kept in held]
        return [layer(tick, which, grads[which], held[which]) for which in range(2)]

    held = lax.fori_loop(1, layers, step, held)

    columns, values, stored = [], [], []
    for which in range(2):
        block = blocks[which][3].reshape(BLOCK, replicas, shares).transpose(1, 0, 2)
        columns.append(spread(block.reshape(replicas * BLOCK, shares)))
        out, value = held[which]
        stored.append(regroup(out))
        values.append(spread(jnp.tile(value, (replicas, 1))))
    ordered = jnp.where(
        side == 0, jnp.concatenate(stored, axis=0), jnp.concatenate(stored[::-1], axis=0)
    )
    own_weight = lax.dynamic_slice_in_dim(weight, me * shares, shares, 0)
    own_gain = lax.dynamic_slice_in_dim(norm_gain[0], me * shares, shares, 0)
    scale = float(tokens * replicas) ** (-0.5)
    weight_grad, gain_grad = pl.pallas_call(
        functools.partial(weight_kernel, scale),
        out_shape=(
            jax.ShapeDtypeStruct((shares, kv_width), jnp.float32),
            jax.ShapeDtypeStruct((1, shares), jnp.float32),
        ),
        in_specs=[VMEM] * 4,
        out_specs=(VMEM, VMEM),
        name="weight_grad",
    )(
        jnp.concatenate(columns, axis=0),
        jnp.concatenate(values, axis=0),
        own_weight,
        own_gain[:, None],
    )
    return ordered[None], weight_grad[None], gain_grad


def on_device(hidden_in, queries, keys, segments, value_weight, norm_gain, upstream):
    replicas = lax.axis_size("dp")
    piece = hidden_in.shape[1] // replicas
    plan = direct if piece % 16 == 0 and replicas == 8 else grouped
    return plan(
        hidden_in[0], queries[0], keys[0], segments, value_weight[0], norm_gain, upstream
    )


def solution(mesh):
    in_specs = (
        P("section", "dp", None),
        P("section", "dp", None),
        P("section", "dp", None),
        P("dp", None),
        P("section", None, None),
        P("section", None),
        P("dp", None),
    )
    out_specs = (P("section", "dp", None), P("section", "dp", None), P("section", "dp"))
    return jax.shard_map(
        on_device, mesh=mesh, in_specs=in_specs, out_specs=out_specs, check_vma=False
    )
```

```python
import functools

import jax
import jax.numpy as jnp
from jax import lax
from jax.experimental import pallas as pl
from jax.experimental.pallas import tpu as pltpu
from jax.sharding import PartitionSpec as P

HEAD_FEATURES = 128
BLOCK = 64
UNIT = 32
EPSILON = 1e-06
MASKED = -1e30
OUTS = {2: 3, 5: 6}
UNITS = ("a_late", "a_early", "b_late", "b_early")
VMEM = pl.BlockSpec(memory_space=pltpu.VMEM)
SMEM = pl.BlockSpec(memory_space=pltpu.SMEM)


ANY = pl.BlockSpec(memory_space=pl.ANY)


LATE, EARLY = slice(UNIT, BLOCK), slice(0, UNIT)


def params(microseconds):
    flops = int(microseconds * 1.15e9)
    return dict(
        compiler_params=pltpu.CompilerParams(vmem_limit_bytes=16 << 20),
        cost_estimate=pl.CostEstimate(flops=flops, bytes_accessed=0, transcendentals=0),
    )


def near(array):
    return pltpu.with_memory_space_constraint(array, pltpu.VMEM)


def place():
    half = lax.axis_size("dp") // 2
    me = lax.axis_index("dp")
    return lax.div(me, half), lax.rem(me, half), me


def probs_kernel(count, seg_row, model_width, kv_width, *refs):
    pieces, seg_ref = refs[:count], refs[count]
    late_ref, early_ref, inv_ref, x_ref, rows_ref = refs[-5:]
    heads = model_width // kv_width
    rows = BLOCK // count
    side, at, _ = place()
    for k, piece in enumerate(pieces):
        if count == 1:
            rows_ref[...] = piece[...]
        else:
            first = pl.multiple_of(lax.bitwise_xor(at, k) * rows, rows)
            rows_ref[pl.ds(first, rows), :] = piece[...]

    def iota(shape, axis):
        return lax.broadcasted_iota(jnp.int32, shape, axis)

    seg = seg_ref[seg_row : seg_row + 16, : 2 * BLOCK].astype(jnp.float32)[:1]
    shape = (BLOCK, 2 * BLOCK)
    wanted = iota(shape, 1) == side * BLOCK + iota(shape, 0)
    ids = jnp.sum(jnp.where(wanted, seg, 0.0), axis=1, keepdims=True)
    key_code = ids * BLOCK + iota((BLOCK, 1), 0).astype(jnp.float32)
    list_start = ids * BLOCK
    shape = (BLOCK, heads * BLOCK)
    column = iota(shape, 1)
    query_at = lax.rem(column, UNIT) + jnp.where(column < heads * UNIT, UNIT, 0)
    same = iota(shape, 0) == query_at
    query_code = jnp.sum(jnp.where(same, key_code, 0.0), axis=0, keepdims=True)
    query_start = jnp.sum(jnp.where(same, list_start, 0.0), axis=0, keepdims=True)
    allowed = (key_code <= query_code) & (key_code >= query_start)
    for c in range(kv_width // HEAD_FEATURES):
        first = c * heads * HEAD_FEATURES
        query_stack = jnp.concatenate(
            [
                rows_ref[part, first + h * HEAD_FEATURES : first + (h + 1) * HEAD_FEATURES]
                for part in (LATE, EARLY)
                for h in range(heads)
            ],
            axis=0,
        )
        key_first = model_width + c * HEAD_FEATURES
        keys = rows_ref[:, key_first : key_first + HEAD_FEATURES]
        scores = lax.dot_general(
            keys, query_stack, (((1,), (1,)), ((), ())), preferred_element_type=jnp.float32
        ) * HEAD_FEATURES ** (-0.5)
        scores = jnp.where(allowed, scores, MASKED)
        exp_scores = jnp.exp(scores - jnp.max(scores, axis=0, keepdims=True))
        total = jnp.sum(exp_scores, axis=0, keepdims=True)
        probs = (exp_scores / total).astype(jnp.bfloat16)
        late_ref[c] = probs[LATE, : heads * UNIT]
        early_ref[c] = probs[EARLY]
    hidden = rows_ref[:, model_width + kv_width :]
    x_ref[...] = hidden
    x = hidden.astype(jnp.float32)
    mean_square = jnp.mean(x * x, axis=1, keepdims=True)
    inv_ref[...] = jnp.broadcast_to(lax.rsqrt(mean_square + EPSILON), inv_ref.shape)


def block_probs(pieces, seg, seg_row, model_width, kv_width, after=()):
    heads = model_width // kv_width
    key_heads = kv_width // HEAD_FEATURES
    operands = [near(piece) for piece in pieces] + [near(seg)]
    specs = [VMEM] * len(operands) + [ANY] * len(after)
    operands += after
    return pl.pallas_call(
        functools.partial(probs_kernel, len(pieces), seg_row, model_width, kv_width),
        out_shape=(
            jax.ShapeDtypeStruct((key_heads, UNIT, heads * UNIT), jnp.bfloat16),
            jax.ShapeDtypeStruct((key_heads, UNIT, heads * BLOCK), jnp.bfloat16),
            jax.ShapeDtypeStruct((BLOCK, 128), jnp.float32),
            jax.ShapeDtypeStruct((BLOCK, model_width), jnp.bfloat16),
        ),
        in_specs=specs,
        out_specs=(VMEM,) * 4,
        scratch_shapes=[pltpu.VMEM((BLOCK, 2 * model_width + kv_width), jnp.bfloat16)],
        name="probs",
        **params(0.35 if after else 2.0),
    )(*operands)


def unit_math(rows, grads, probs_ref, x_ref, inv_ref, turned_ref, gain_ref, scaled_ref, store, value_ref):
    kv_width, model_width = turned_ref.shape
    heads = model_width // kv_width
    chunk = min(512, model_width)
    inv = inv_ref[rows, :1]
    values = []
    for c in range(kv_width // HEAD_FEATURES):
        first = c * heads * HEAD_FEATURES
        grad_stack = jnp.concatenate(
            [
                grad_ref[part, first + h * HEAD_FEATURES : first + (h + 1) * HEAD_FEATURES]
                for grad_ref, part in grads
                for h in range(heads)
            ],
            axis=0,
        )
        values.append(
            jnp.dot(probs_ref[c], grad_stack, preferred_element_type=jnp.float32).astype(
                jnp.bfloat16
            )
        )
    value = jnp.concatenate(values, axis=1)
    value_ref[...] = (value.astype(jnp.float32) * inv).astype(jnp.bfloat16)
    inner = jnp.zeros((UNIT, 1), jnp.float32)
    for first in range(0, model_width, chunk):
        columns = slice(first, first + chunk)
        normed_grad = jnp.dot(value, turned_ref[:, columns], preferred_element_type=jnp.float32)
        scaled = normed_grad * gain_ref[:, columns]
        scaled_ref[:, columns] = scaled
        x = x_ref[rows, columns].astype(jnp.float32)
        inner = inner + jnp.sum(x * scaled, axis=1, keepdims=True)
    pull = inner * (inv * inv / model_width)
    grad_ref, part = grads[-1]
    for first in range(0, model_width, chunk):
        columns = slice(first, first + chunk)
        x = x_ref[rows, columns].astype(jnp.float32)
        change = inv * (scaled_ref[:, columns] - x * pull)
        grad = grad_ref[part, columns].astype(jnp.float32)
        store(columns, (grad + change).astype(jnp.bfloat16))


def turn_kernel(weight_ref, *refs):
    turned_ref = refs[-1]
    step = min(256, weight_ref.shape[0])
    for first in range(0, weight_ref.shape[0], step):
        turned_ref[:, first : first + step] = weight_ref[first : first + step, :].T


def turn(weight, after=()):
    return pl.pallas_call(
        turn_kernel,
        out_shape=jax.ShapeDtypeStruct(weight.shape[::-1], weight.dtype),
        in_specs=[VMEM] + [ANY] * len(after),
        out_specs=VMEM,
        name="turn",
        **params(1.5),
    )(near(weight), *after)


def layer_kernel(
    live_ref, grad_ref, late_ref, early_ref, inv_ref, x_ref, turned_ref, gain_ref, *rest
):
    out_ref, value_ref, scaled_ref = rest[-3:]
    if len(rest) == 5:

        @pl.when(live_ref[0] == 0)
        def _():
            out_ref[...] = rest[0][...]
            value_ref[...] = rest[1][...]

    @pl.when(live_ref[0] == 1)
    def _():
        for rows, parts, probs_ref in ((LATE, [LATE], late_ref), (EARLY, [LATE, EARLY], early_ref)):

            def store(columns, part, rows=rows):
                out_ref[rows, columns] = part

            grads = [(grad_ref, part) for part in parts]
            unit_math(
                rows, grads, probs_ref, x_ref, inv_ref, turned_ref, gain_ref, scaled_ref, store,
                value_ref.at[rows],
            )


def layer_step(live, grad, block, turned, gain, held=()):
    kv_width, model_width = turned.shape
    operands = [live, grad, *block, turned, gain, *held]
    return pl.pallas_call(
        layer_kernel,
        out_shape=(
            jax.ShapeDtypeStruct((BLOCK, model_width), jnp.bfloat16),
            jax.ShapeDtypeStruct((BLOCK, kv_width), jnp.bfloat16),
        ),
        in_specs=[SMEM] + [VMEM] * (len(operands) - 1),
        out_specs=(VMEM, VMEM),
        scratch_shapes=[pltpu.VMEM((UNIT, model_width), jnp.float32)],
        name="layer",
        **params(1.1),
    )(*operands)


def tick_kernel(tick, rows, parts, kept, late, *refs):
    grads = list(zip(refs, parts))
    probs_ref, inv_ref, x_ref, turned_ref, gain_ref = refs[len(parts) : len(parts) + 5]
    refs = refs[len(parts) + 5 :]
    earlier, refs = refs[: 2 * kept], refs[2 * kept :]
    late_refs = refs[:late]
    kv_width, model_width = turned_ref.shape
    turn = lax.axis_size("section") - 1 - lax.axis_index("section")
    if late:
        outs, (scaled_ref, blocks_ref, value_ref) = refs[late : -3], refs[-3:]
        outs = outs[len(outs) - OUTS[late] :]
    else:
        outs, scaled_ref = refs[-3:-1], refs[-1]
        value_ref = outs[1]
    first_row = BLOCK if late > 2 else 0

    def store(columns, part):
        if late:
            blocks_ref[first_row : first_row + UNIT, columns] = part
        if late <= 2:
            outs[0][:, columns] = part

    @pl.when(turn == tick)
    def _():
        unit_math(
            rows, grads, probs_ref, x_ref, inv_ref, turned_ref, gain_ref, scaled_ref, store,
            value_ref,
        )

    for at in range(kept):

        @pl.when(turn == at)
        def _(at=at):
            store(slice(None), earlier[2 * at][...])
            value_ref[...] = earlier[2 * at + 1][...]

    if not late:
        return
    values = jnp.concatenate([value_ref[...], late_refs[0][...]], axis=0)
    blocks_ref[first_row + UNIT : first_row + BLOCK, :] = late_refs[1][...]
    outs[1 if late == 2 else 0][...] = values
    if late > 2:
        late_a_ref, early_a_ref, value_a_ref = late_refs[2:]
        outs[1][:BLOCK, :] = value_a_ref[...]
        outs[1][BLOCK:, :] = values
        blocks_ref[EARLY, :] = early_a_ref[...]
        blocks_ref[LATE, :] = late_a_ref[...]
    at = place()[1]
    pieces = {2: outs[2]} if late == 2 else dict(enumerate(outs[2:]))
    piece = BLOCK * kv_width // model_width

    def rows_for(k, block):
        first = pl.multiple_of(lax.bitwise_xor(at, k) * piece, piece)
        return blocks_ref[pl.ds(block * BLOCK + first, piece), :]

    block = 0 if late == 2 else 1
    for k, out_ref in pieces.items():
        if k == 2:
            out_ref[:piece, :] = rows_for(2, block)
            for g in range(model_width // kv_width):
                out_ref[piece : 2 * piece, g * kv_width : (g + 1) * kv_width] = values[
                    g * piece : (g + 1) * piece
                ]
            if block == 0:
                out_ref[2 * piece :, :] = rows_for(3, 0)
        elif k == 3:
            out_ref[...] = rows_for(3, 1)
        else:
            out_ref[:piece, :] = rows_for(k, 0)
            out_ref[piece:, :] = rows_for(k, 1)


def tick_step(tick, grads, block, turned, gain, kept=(), late=(), after=(), name=""):
    kv_width, model_width = turned.shape
    low = len(grads) == 2
    arrays = [grad for grad, _ in grads]
    arrays += [block[1] if low else block[0], block[2], block[3], turned, gain]
    arrays += [array for pair in kept for array in pair]
    arrays += late
    operands = [near(array) for array in arrays]
    specs = [VMEM] * len(operands) + [ANY] * len(after)
    bf16 = jnp.bfloat16
    scratch = [pltpu.VMEM((UNIT, model_width), jnp.float32)]
    rows, value = (UNIT, model_width), (UNIT, kv_width)
    shapes = [rows, value]
    if late:
        half = lax.axis_size("dp") // 2
        scratch += [pltpu.VMEM((2 * BLOCK, model_width), bf16), pltpu.VMEM(value, bf16)]
        piece = BLOCK // half
        shapes = [rows, (BLOCK, kv_width), (3 * piece, model_width)]
    if len(late) > 2:
        shapes = [(BLOCK, kv_width), (2 * BLOCK, kv_width)]
        shapes += [(2 * piece, model_width)] * 3 + [(piece, model_width)]
    parts = [part for _, part in grads]
    return pl.pallas_call(
        functools.partial(
            tick_kernel, tick, EARLY if low else LATE, parts, len(kept), len(late)
        ),
        out_shape=tuple(jax.ShapeDtypeStruct(shape, bf16) for shape in shapes),
        in_specs=specs,
        out_specs=(VMEM,) * len(shapes),
        scratch_shapes=scratch,
        name=f"tick{tick}_{name}",
        **params(1.0 if kept else 0.0),
    )(*operands, *after)


def pack_kernel(block, half, piece, query_ref, key_ref, hidden_ref, up_ref, seg_ref, *rest):
    up_out_ref, seg_in_ref, rows_ref, sems = rest[-4:]
    packed = rest[-4 - half : -4]
    side, at, _ = place()
    there = side if block == 0 else 1 - side
    rows = pl.ds(pl.multiple_of(there * BLOCK, BLOCK), BLOCK)
    copies = []

    def copy(source, target):
        made = pltpu.make_async_copy(source, target, sems.at[len(copies)])
        made.start()
        copies.append(made)

    first = 0
    for source in (query_ref, key_ref, hidden_ref):
        width = source.shape[1]
        copy(source.at[rows], rows_ref.at[:, pl.ds(first, width)])
        first += width
    copy(seg_ref, seg_in_ref)
    copy(up_ref.at[rows], up_out_ref.at[pl.ds(0, BLOCK)])
    up_out_ref[BLOCK:, :] = jnp.zeros((16, up_out_ref.shape[1]), jnp.bfloat16)
    if block == 1:
        rest[2][...] = rest[1][...]
        turn_kernel(rest[0], rest[3])
    for made in copies[:4]:
        made.wait()
    ids = seg_in_ref[...].astype(jnp.float32)
    up_out_ref[BLOCK:, : ids.shape[1]] = jnp.broadcast_to(ids, (16, ids.shape[1])).astype(
        jnp.bfloat16
    )
    for k in range(half):
        first = pl.multiple_of(lax.bitwise_xor(at, k) * piece, piece)
        packed[k][...] = rows_ref[pl.ds(first, piece), :]
    copies[4].wait()


def pack(block, half, piece, sources, weight=None, gain=None):
    model_width = sources[0].shape[1]
    width = sum(source.shape[1] for source in sources[:3])
    bf16 = jnp.bfloat16
    operands = [pltpu.with_memory_space_constraint(array, pltpu.HBM) for array in sources]
    specs = [pl.BlockSpec(memory_space=pltpu.HBM)] * len(sources)
    outs = [jax.ShapeDtypeStruct((piece, width), bf16)] * half
    outs.append(jax.ShapeDtypeStruct((BLOCK + 16, model_width), bf16))
    if weight is not None:
        operands += [near(weight), gain]
        specs += [VMEM, VMEM]
        outs = [
            jax.ShapeDtypeStruct(gain.shape, gain.dtype),
            jax.ShapeDtypeStruct(weight.shape[::-1], bf16),
        ] + outs
    return pl.pallas_call(
        functools.partial(pack_kernel, block, half, piece),
        out_shape=tuple(outs),
        in_specs=specs,
        out_specs=(VMEM,) * len(outs),
        scratch_shapes=[
            pltpu.VMEM(sources[-1].shape, jnp.int32),
            pltpu.VMEM((BLOCK, width), bf16),
            pltpu.SemaphoreType.DMA((5,)),
        ],
        name="pack",
        **params(1.2),
    )(*operands)


def columns_kernel(width, distance, first_ref, second_ref, *refs):
    out_ref = refs[-1]
    if distance == 0:
        came_ref, out_ref, handed_ref = refs[0], refs[-2], refs[-1]
        handed_ref[...] = came_ref[came_ref.shape[0] - handed_ref.shape[0] :, :]
    if distance == 4:
        out_ref[2 * BLOCK :, :] = refs[0][...]
    there = lax.div(lax.bitwise_xor(place()[2], distance), 2)
    out_ref[:BLOCK, :] = first_ref[:, columns_of(there, width)]
    out_ref[BLOCK : 2 * BLOCK, :] = second_ref[:, columns_of(there, width)]


def columns_for(distance, blocks, after, came=()):
    model_width = blocks[0][3].shape[1]
    width = 2 * model_width // lax.axis_size("dp")
    shapes = [(2 * BLOCK, width)]
    if distance == 0:
        shapes.append((came[0].shape[0] // 3, model_width))
    if distance == 4:
        shapes = [(3 * BLOCK, width)]
    outs = [jax.ShapeDtypeStruct(shape, jnp.bfloat16) for shape in shapes]
    results = pl.pallas_call(
        functools.partial(columns_kernel, width, distance),
        out_shape=tuple(outs),
        in_specs=[VMEM] * (2 + len(came)) + [ANY] * len(after),
        out_specs=(VMEM,) * len(outs),
        name=f"columns{distance}",
        **params(0.0 if distance else 2.5),
    )(blocks[0][3], blocks[1][3], *came, *after)
    return results if distance == 0 else results[0]


def own_kernel(scale, weight_ref, gain_ref, after_ref, weight_out_ref, gain_out_ref):
    shares = weight_out_ref.shape[0]
    first = pl.multiple_of(place()[2] * shares, shares)
    weight_out_ref[...] = weight_ref[pl.ds(first, shares), :].astype(jnp.float32) * scale
    gain = gain_ref[:, pl.ds(first, shares)]
    column = jnp.sum(jnp.where(diagonal(shares), gain, 0.0), axis=1, keepdims=True)
    gain_out_ref[...] = jnp.broadcast_to(column * scale, gain_out_ref.shape)


def columns_of(pair, width):
    return pl.ds(pl.multiple_of(pair * width, width), width)


def partial_kernel(shares, first, for_other, *refs):
    columns, values, out_ref = refs[:4], refs[4:10], refs[-1]
    kv_width = out_ref.shape[1]
    parts = []
    for ref in values:
        beside = ref.shape[1] > kv_width
        rows = slice(first, 2 * first) if beside else slice(0, ref.shape[0])
        parts += [ref[rows, at : at + kv_width] for at in range(0, ref.shape[1], kv_width)]
    parts.insert(len(parts) - 3, columns[2][2 * BLOCK :, :])
    value = jnp.concatenate(parts, axis=0)
    mine = lax.rem(place()[2], 2)
    core = 1 - mine if for_other else mine
    at = pl.ds(pl.multiple_of(core * shares, shares), shares)
    rows = jnp.concatenate([ref[: 2 * BLOCK, at] for ref in columns], axis=0)
    out_ref[...] = lax.dot_general(
        rows, value, (((0,), (0,)), ((), ())), preferred_element_type=jnp.float32
    ).astype(out_ref.dtype)


def partial_sums(shares, piece, for_other, columns, values, after=()):
    kv_width = values[0].shape[1]
    return pl.pallas_call(
        functools.partial(partial_kernel, shares, piece, for_other),
        out_shape=jax.ShapeDtypeStruct(
            (shares, kv_width), jnp.bfloat16 if for_other else jnp.float32
        ),
        in_specs=[VMEM] * 10 + [ANY] * len(after),
        out_specs=VMEM,
        name="partial_other" if for_other else "partial_own",
        **params(0.0 if for_other else 0.5),
    )(*[columns[k] for k in (0, 2, 4, 6)], *values, *after)


def diagonal(size):
    return lax.broadcasted_iota(jnp.int32, (size, size), 0) == lax.broadcasted_iota(
        jnp.int32, (size, size), 1
    )


def rows_kernel(half, first_rows_ref, handed_ref, *refs):
    pieces = refs[:half]
    rows_ref, token_ref = refs[half:]
    side, at, _ = place()
    piece = BLOCK // half
    for block in range(2):
        for k in range(half):
            replica = (side if block == 0 else 1 - side) * half + lax.bitwise_xor(at, k)
            rows = pl.ds(pl.multiple_of(replica * piece, piece), piece)
            source, first = pieces[k], block * piece
            if k == 2:
                source, first = (pieces[k] if block else first_rows_ref), 0
            if k == 3:
                source, first = (pieces[k] if block else handed_ref), 0
            rows_ref[rows, :] = source[first : first + piece, :]
    token_ref[...] = jnp.zeros_like(token_ref)


def finish_kernel(
    own_ref, other_ref, weight_ref, gain_ref, after_ref, out_ref, gain_out_ref
):
    total = own_ref[...] + other_ref[...].astype(jnp.float32)
    out_ref[...] = total * gain_ref[:, :1]
    sums = jnp.sum(total * weight_ref[...], axis=1, keepdims=True)
    gain_out_ref[...] = jnp.sum(
        jnp.where(diagonal(total.shape[0]), sums, 0.0), axis=0, keepdims=True
    )


def direct(hidden, query, key, segments, weight, norm_gain, upstream):
    tokens, model_width = hidden.shape
    kv_width = key.shape[1]
    replicas = lax.axis_size("dp")
    layers = lax.axis_size("section")
    half = replicas // 2
    piece = tokens // replicas
    shares = model_width // replicas

    def swap(array, k):
        return lax.ppermute(array, "dp", [(i, i ^ k) for i in range(replicas)])

    count = 2 * half
    bf16 = jnp.bfloat16
    sources = (query, key, hidden, upstream, segments)
    pieces, ups = [], []
    for b in range(2):
        extra = (weight, norm_gain) if b else ()
        *packed, up = pack(b, half, piece, sources, *extra)
        if b:
            gain, turned, *packed = packed
        pieces.append([packed[0]] + [swap(packed[k], k) for k in range(1, half)])
        ups.append(swap(up, half) if b else up)
    whole = slice(0, UNIT)
    scale = float(tokens * replicas) ** (-0.5)
    blocks, kept, after = [], [], []
    for b in range(2):
        block = block_probs(pieces[b], ups[b], BLOCK, model_width, kv_width, after)
        late, early = (ups[b], LATE), (ups[b], EARLY)
        first = tick_step(0, [late], block, turned, gain, name=UNITS[2 * b])
        second = tick_step(
            0, [late, early], block, turned, gain, after=[first[0]], name=UNITS[2 * b + 1]
        )
        blocks.append(block)
        kept += [[first], [second]]
        after = [second[0]]

    for tick in range(1, layers):
        hop = [(layers - tick, layers - 1 - tick)]
        grads = [(lax.ppermute(unit[-1][0], "section", hop), whole) for unit in kept]
        last = tick == layers - 1
        after, done = [kept[3][-1][0]], []
        if tick == layers - 2:
            own_weight, own_gain = pl.pallas_call(
                functools.partial(own_kernel, scale),
                out_shape=(
                    jax.ShapeDtypeStruct((shares, kv_width), jnp.float32),
                    jax.ShapeDtypeStruct((shares, 128), jnp.float32),
                ),
                in_specs=[VMEM, VMEM, ANY],
                out_specs=(VMEM, VMEM),
                name="own",
                **params(0.0),
            )(near(weight), near(gain), *after)
            columns = {6: swap(columns_for(6, blocks, after + [own_gain]), 6)}
        if last:
            columns[2] = swap(columns_for(2, blocks, after + [columns[6]]), 2)
        for u in range(4):
            needs = grads[u - 1 : u + 1] if u % 2 else grads[u : u + 1]
            late = []
            if last and u == 1:
                late = [done[0][1], done[0][0]]
            if last and u == 3:
                late = [done[2][1], done[2][0], done[0][0], done[1][0], done[1][1]]
                first_rows, far_first = swap(done[1][2], 2), swap(done[1][1], 6)
                columns[4] = swap(columns_for(4, blocks, [], [done[1][1]]), 4)
                after = after + [columns[2]]
            done.append(
                tick_step(
                    tick, needs, blocks[u // 2], turned, gain, kept[u] if last else (), late,
                    after, name=UNITS[u],
                )
            )
            after = [done[u][0]]
            kept[u].append(done[u])
    own_value, own_values, *rows = done[3]
    rows = [rows[0]] + [swap(rows[k], k) for k in range(1, half)]
    far_value, across_value = swap(own_value, 6), swap(own_value, 4)
    columns[0], handed = columns_for(0, blocks, [own_value, columns[4], far_first, far_value], [first_rows])
    handed = swap(handed, 1)
    values = [own_values, first_rows, rows[2], across_value, far_first, far_value]
    other = partial_sums(shares, piece, True, columns, values)
    own = partial_sums(shares, piece, False, columns, values, [other])
    other = swap(other, 1)
    input_grad, token = pl.pallas_call(
        functools.partial(rows_kernel, half),
        out_shape=(
            jax.ShapeDtypeStruct((tokens, model_width), bf16),
            jax.ShapeDtypeStruct((8, 128), jnp.float32),
        ),
        in_specs=[VMEM] * (2 + half),
        out_specs=(VMEM, VMEM),
        name="rows",
        **params(2.5),
    )(first_rows, handed, *rows)
    weight_grad, gain_grad = pl.pallas_call(
        finish_kernel,
        out_shape=(
            jax.ShapeDtypeStruct((shares, kv_width), jnp.float32),
            jax.ShapeDtypeStruct((1, shares), jnp.float32),
        ),
        in_specs=[VMEM] * 4 + [ANY],
        out_specs=(VMEM, VMEM),
        name="finish",
        **params(0.0),
    )(own, other, own_weight, own_gain, token)
    return input_grad[None], weight_grad[None], gain_grad


def weight_kernel(scale, columns_ref, value_ref, weight_ref, gain_ref, out_ref, gain_out_ref):
    total = lax.dot_general(
        columns_ref[...], value_ref[...], (((0,), (0,)), ((), ())),
        preferred_element_type=jnp.float32,
    ) * scale
    out_ref[...] = total * gain_ref[...]
    product = total * weight_ref[...].astype(jnp.float32)
    sums = lax.dot_general(
        jnp.ones((8, product.shape[1]), jnp.float32), product, (((1,), (1,)), ((), ())),
        preferred_element_type=jnp.float32, precision=lax.Precision.HIGHEST,
    )
    gain_out_ref[...] = sums[:1]


def grouped(hidden, query, key, segments, weight, norm_gain, upstream):
    tokens, model_width = hidden.shape
    kv_width = key.shape[1]
    replicas = lax.axis_size("dp")
    layers = lax.axis_size("section")
    half = replicas // 2
    me = lax.axis_index("dp")
    section = lax.axis_index("section")
    side = me // half
    groups = [list(range(half)), list(range(half, replicas))]
    across = [(i, (i + half) % replicas) for i in range(replicas)]
    shares = model_width // replicas

    def rows_of(array, which, axis=0):
        at = side if which == 0 else 1 - side
        return lax.dynamic_slice_in_dim(array, at * BLOCK, BLOCK, axis)

    def regroup(array):
        return lax.all_to_all(
            array, "dp", split_axis=0, concat_axis=0, axis_index_groups=groups, tiled=True
        )

    def spread(array):
        return lax.all_to_all(array, "dp", split_axis=0, concat_axis=0, tiled=True)

    turned = turn(weight)
    blocks, grads = [], []
    for which in range(2):
        up = rows_of(upstream, which)
        seg = jnp.broadcast_to(segments, (16, 2 * BLOCK)).astype(jnp.bfloat16)
        if which == 1:
            up = lax.ppermute(up, "dp", across)
            seg = lax.ppermute(seg, "dp", across)
        packed = jnp.concatenate(
            [rows_of(query, which), rows_of(key, which), rows_of(hidden, which)], axis=1
        )
        blocks.append(block_probs([regroup(packed)], seg, 0, model_width, kv_width))
        grads.append(up)

    def layer(tick, which, grad, kept):
        live = (section == layers - 1 - tick).astype(jnp.int32)[None]
        return layer_step(live, grad, blocks[which], turned, norm_gain, kept)

    held = [layer(0, which, grads[which], ()) for which in range(2)]
    hops = [(i, i - 1) for i in range(1, layers)]

    def step(tick, held):
        grads = [lax.ppermute(kept[0], "section", hops) for kept in held]
        return [layer(tick, which, grads[which], held[which]) for which in range(2)]

    held = lax.fori_loop(1, layers, step, held)

    columns, values, stored = [], [], []
    for which in range(2):
        block = blocks[which][3].reshape(BLOCK, replicas, shares).transpose(1, 0, 2)
        columns.append(spread(block.reshape(replicas * BLOCK, shares)))
        out, value = held[which]
        stored.append(regroup(out))
        values.append(spread(jnp.tile(value, (replicas, 1))))
    ordered = jnp.where(
        side == 0, jnp.concatenate(stored, axis=0), jnp.concatenate(stored[::-1], axis=0)
    )
    own_weight = lax.dynamic_slice_in_dim(weight, me * shares, shares, 0)
    own_gain = lax.dynamic_slice_in_dim(norm_gain[0], me * shares, shares, 0)
    scale = float(tokens * replicas) ** (-0.5)
    weight_grad, gain_grad = pl.pallas_call(
        functools.partial(weight_kernel, scale),
        out_shape=(
            jax.ShapeDtypeStruct((shares, kv_width), jnp.float32),
            jax.ShapeDtypeStruct((1, shares), jnp.float32),
        ),
        in_specs=[VMEM] * 4,
        out_specs=(VMEM, VMEM),
        name="weight_grad",
    )(
        jnp.concatenate(columns, axis=0),
        jnp.concatenate(values, axis=0),
        own_weight,
        own_gain[:, None],
    )
    return ordered[None], weight_grad[None], gain_grad


def on_device(hidden_in, queries, keys, segments, value_weight, norm_gain, upstream):
    replicas = lax.axis_size("dp")
    piece = hidden_in.shape[1] // replicas
    plan = direct if piece % 16 == 0 and replicas == 8 else grouped
    return plan(
        hidden_in[0], queries[0], keys[0], segments, value_weight[0], norm_gain, upstream
    )


def solution(mesh):
    in_specs = (
        P("section", "dp", None),
        P("section", "dp", None),
        P("section", "dp", None),
        P("dp", None),
        P("section", None, None),
        P("section", None),
        P("dp", None),
    )
    out_specs = (P("section", "dp", None), P("section", "dp", None), P("section", "dp"))
    return jax.shard_map(
        on_device, mesh=mesh, in_specs=in_specs, out_specs=out_specs, check_vma=False
    )
```

```python
import functools

import jax
import jax.numpy as jnp
from jax import lax
from jax.experimental import pallas as pl
from jax.experimental.pallas import tpu as pltpu
from jax.sharding import PartitionSpec as P

HEAD_FEATURES = 128
BLOCK = 64
UNIT = 32
EPSILON = 1e-06
MASKED = -1e30
OUTS = {2: 3, 5: 6}
UNITS = ("a_late", "a_early", "b_late", "b_early")
VMEM = pl.BlockSpec(memory_space=pltpu.VMEM)
SMEM = pl.BlockSpec(memory_space=pltpu.SMEM)


ANY = pl.BlockSpec(memory_space=pl.ANY)


LATE, EARLY = slice(UNIT, BLOCK), slice(0, UNIT)


def params(microseconds):
    flops = int(microseconds * 1.15e9)
    return dict(
        compiler_params=pltpu.CompilerParams(vmem_limit_bytes=16 << 20),
        cost_estimate=pl.CostEstimate(flops=flops, bytes_accessed=0, transcendentals=0),
    )


def near(array):
    return pltpu.with_memory_space_constraint(array, pltpu.VMEM)


def place():
    half = lax.axis_size("dp") // 2
    me = lax.axis_index("dp")
    return lax.div(me, half), lax.rem(me, half), me


def probs_kernel(count, seg_row, model_width, kv_width, *refs):
    pieces, seg_ref = refs[:count], refs[count]
    late_ref, early_ref, inv_ref, x_ref, rows_ref = refs[-5:]
    heads = model_width // kv_width
    rows = BLOCK // count
    side, at, _ = place()
    for k, piece in enumerate(pieces):
        if count == 1:
            rows_ref[...] = piece[...]
        else:
            first = pl.multiple_of(lax.bitwise_xor(at, k) * rows, rows)
            rows_ref[pl.ds(first, rows), :] = piece[...]

    def iota(shape, axis):
        return lax.broadcasted_iota(jnp.int32, shape, axis)

    seg = seg_ref[seg_row : seg_row + 16, : 2 * BLOCK].astype(jnp.float32)[:1]
    shape = (BLOCK, 2 * BLOCK)
    wanted = iota(shape, 1) == side * BLOCK + iota(shape, 0)
    ids = jnp.sum(jnp.where(wanted, seg, 0.0), axis=1, keepdims=True)
    key_code = ids * BLOCK + iota((BLOCK, 1), 0).astype(jnp.float32)
    list_start = ids * BLOCK
    shape = (BLOCK, heads * BLOCK)
    column = iota(shape, 1)
    query_at = lax.rem(column, UNIT) + jnp.where(column < heads * UNIT, UNIT, 0)
    same = iota(shape, 0) == query_at
    query_code = jnp.sum(jnp.where(same, key_code, 0.0), axis=0, keepdims=True)
    query_start = jnp.sum(jnp.where(same, list_start, 0.0), axis=0, keepdims=True)
    allowed = (key_code <= query_code) & (key_code >= query_start)
    for c in range(kv_width // HEAD_FEATURES):
        first = c * heads * HEAD_FEATURES
        query_stack = jnp.concatenate(
            [
                rows_ref[part, first + h * HEAD_FEATURES : first + (h + 1) * HEAD_FEATURES]
                for part in (LATE, EARLY)
                for h in range(heads)
            ],
            axis=0,
        )
        key_first = model_width + c * HEAD_FEATURES
        keys = rows_ref[:, key_first : key_first + HEAD_FEATURES]
        scores = lax.dot_general(
            keys, query_stack, (((1,), (1,)), ((), ())), preferred_element_type=jnp.float32
        ) * HEAD_FEATURES ** (-0.5)
        scores = jnp.where(allowed, scores, MASKED)
        exp_scores = jnp.exp(scores - jnp.max(scores, axis=0, keepdims=True))
        total = jnp.sum(exp_scores, axis=0, keepdims=True)
        probs = (exp_scores / total).astype(jnp.bfloat16)
        late_ref[c] = probs[LATE, : heads * UNIT]
        early_ref[c] = probs[EARLY]
    hidden = rows_ref[:, model_width + kv_width :]
    x_ref[...] = hidden
    x = hidden.astype(jnp.float32)
    mean_square = jnp.mean(x * x, axis=1, keepdims=True)
    inv_ref[...] = jnp.broadcast_to(lax.rsqrt(mean_square + EPSILON), inv_ref.shape)


def block_probs(pieces, seg, seg_row, model_width, kv_width, after=()):
    heads = model_width // kv_width
    key_heads = kv_width // HEAD_FEATURES
    operands = [near(piece) for piece in pieces] + [near(seg)]
    specs = [VMEM] * len(operands) + [ANY] * len(after)
    operands += after
    return pl.pallas_call(
        functools.partial(probs_kernel, len(pieces), seg_row, model_width, kv_width),
        out_shape=(
            jax.ShapeDtypeStruct((key_heads, UNIT, heads * UNIT), jnp.bfloat16),
            jax.ShapeDtypeStruct((key_heads, UNIT, heads * BLOCK), jnp.bfloat16),
            jax.ShapeDtypeStruct((BLOCK, 128), jnp.float32),
            jax.ShapeDtypeStruct((BLOCK, model_width), jnp.bfloat16),
        ),
        in_specs=specs,
        out_specs=(VMEM,) * 4,
        scratch_shapes=[pltpu.VMEM((BLOCK, 2 * model_width + kv_width), jnp.bfloat16)],
        name="probs",
        **params(0.35 if after else 2.0),
    )(*operands)


def unit_math(rows, grads, probs_ref, x_ref, inv_ref, turned_ref, gain_ref, scaled_ref, store, value_ref):
    kv_width, model_width = turned_ref.shape
    heads = model_width // kv_width
    chunk = min(512, model_width)
    inv = inv_ref[rows, :1]
    values = []
    for c in range(kv_width // HEAD_FEATURES):
        first = c * heads * HEAD_FEATURES
        grad_stack = jnp.concatenate(
            [
                grad_ref[part, first + h * HEAD_FEATURES : first + (h + 1) * HEAD_FEATURES]
                for grad_ref, part in grads
                for h in range(heads)
            ],
            axis=0,
        )
        values.append(
            jnp.dot(probs_ref[c], grad_stack, preferred_element_type=jnp.float32).astype(
                jnp.bfloat16
            )
        )
    value = jnp.concatenate(values, axis=1)
    value_ref[...] = (value.astype(jnp.float32) * inv).astype(jnp.bfloat16)
    inner = jnp.zeros((UNIT, 1), jnp.float32)
    for first in range(0, model_width, chunk):
        columns = slice(first, first + chunk)
        normed_grad = jnp.dot(value, turned_ref[:, columns], preferred_element_type=jnp.float32)
        scaled = normed_grad * gain_ref[:, columns]
        scaled_ref[:, columns] = scaled
        x = x_ref[rows, columns].astype(jnp.float32)
        inner = inner + jnp.sum(x * scaled, axis=1, keepdims=True)
    pull = inner * (inv * inv / model_width)
    grad_ref, part = grads[-1]
    for first in range(0, model_width, chunk):
        columns = slice(first, first + chunk)
        x = x_ref[rows, columns].astype(jnp.float32)
        change = inv * (scaled_ref[:, columns] - x * pull)
        grad = grad_ref[part, columns].astype(jnp.float32)
        store(columns, (grad + change).astype(jnp.bfloat16))


def turn_kernel(weight_ref, *refs):
    turned_ref = refs[-1]
    step = min(256, weight_ref.shape[0])
    for first in range(0, weight_ref.shape[0], step):
        turned_ref[:, first : first + step] = weight_ref[first : first + step, :].T


def turn(weight, after=()):
    return pl.pallas_call(
        turn_kernel,
        out_shape=jax.ShapeDtypeStruct(weight.shape[::-1], weight.dtype),
        in_specs=[VMEM] + [ANY] * len(after),
        out_specs=VMEM,
        name="turn",
        **params(1.5),
    )(near(weight), *after)


def layer_kernel(
    live_ref, grad_ref, late_ref, early_ref, inv_ref, x_ref, turned_ref, gain_ref, *rest
):
    out_ref, value_ref, scaled_ref = rest[-3:]
    if len(rest) == 5:

        @pl.when(live_ref[0] == 0)
        def _():
            out_ref[...] = rest[0][...]
            value_ref[...] = rest[1][...]

    @pl.when(live_ref[0] == 1)
    def _():
        for rows, parts, probs_ref in ((LATE, [LATE], late_ref), (EARLY, [LATE, EARLY], early_ref)):

            def store(columns, part, rows=rows):
                out_ref[rows, columns] = part

            grads = [(grad_ref, part) for part in parts]
            unit_math(
                rows, grads, probs_ref, x_ref, inv_ref, turned_ref, gain_ref, scaled_ref, store,
                value_ref.at[rows],
            )


def layer_step(live, grad, block, turned, gain, held=()):
    kv_width, model_width = turned.shape
    operands = [live, grad, *block, turned, gain, *held]
    return pl.pallas_call(
        layer_kernel,
        out_shape=(
            jax.ShapeDtypeStruct((BLOCK, model_width), jnp.bfloat16),
            jax.ShapeDtypeStruct((BLOCK, kv_width), jnp.bfloat16),
        ),
        in_specs=[SMEM] + [VMEM] * (len(operands) - 1),
        out_specs=(VMEM, VMEM),
        scratch_shapes=[pltpu.VMEM((UNIT, model_width), jnp.float32)],
        name="layer",
        **params(1.1),
    )(*operands)


def tick_kernel(tick, rows, parts, kept, late, *refs):
    grads = list(zip(refs, parts))
    probs_ref, inv_ref, x_ref, turned_ref, gain_ref = refs[len(parts) : len(parts) + 5]
    refs = refs[len(parts) + 5 :]
    earlier, refs = refs[: 2 * kept], refs[2 * kept :]
    late_refs = refs[:late]
    kv_width, model_width = turned_ref.shape
    turn = lax.axis_size("section") - 1 - lax.axis_index("section")
    if late:
        outs, (scaled_ref, blocks_ref, value_ref) = refs[late : -3], refs[-3:]
        outs = outs[len(outs) - OUTS[late] :]
    else:
        outs, scaled_ref = refs[-3:-1], refs[-1]
        value_ref = outs[1]
    first_row = BLOCK if late > 2 else 0

    def store(columns, part):
        if late:
            blocks_ref[first_row : first_row + UNIT, columns] = part
        if late <= 2:
            outs[0][:, columns] = part

    @pl.when(turn == tick)
    def _():
        unit_math(
            rows, grads, probs_ref, x_ref, inv_ref, turned_ref, gain_ref, scaled_ref, store,
            value_ref,
        )

    for at in range(kept):

        @pl.when(turn == at)
        def _(at=at):
            store(slice(None), earlier[2 * at][...])
            value_ref[...] = earlier[2 * at + 1][...]

    if not late:
        return
    values = jnp.concatenate([value_ref[...], late_refs[0][...]], axis=0)
    blocks_ref[first_row + UNIT : first_row + BLOCK, :] = late_refs[1][...]
    outs[1 if late == 2 else 0][...] = values
    if late > 2:
        late_a_ref, early_a_ref, value_a_ref = late_refs[2:]
        outs[1][:BLOCK, :] = value_a_ref[...]
        outs[1][BLOCK:, :] = values
        blocks_ref[EARLY, :] = early_a_ref[...]
        blocks_ref[LATE, :] = late_a_ref[...]
    at = place()[1]
    pieces = {2: outs[2]} if late == 2 else dict(enumerate(outs[2:]))
    piece = BLOCK * kv_width // model_width

    def rows_for(k, block):
        first = pl.multiple_of(lax.bitwise_xor(at, k) * piece, piece)
        return blocks_ref[pl.ds(block * BLOCK + first, piece), :]

    block = 0 if late == 2 else 1
    for k, out_ref in pieces.items():
        if k == 2:
            out_ref[:piece, :] = rows_for(2, block)
            for g in range(model_width // kv_width):
                out_ref[piece : 2 * piece, g * kv_width : (g + 1) * kv_width] = values[
                    g * piece : (g + 1) * piece
                ]
            if block == 0:
                out_ref[2 * piece :, :] = rows_for(3, 0)
        elif k == 3:
            out_ref[...] = rows_for(3, 1)
        else:
            out_ref[:piece, :] = rows_for(k, 0)
            out_ref[piece:, :] = rows_for(k, 1)


def tick_step(tick, grads, block, turned, gain, kept=(), late=(), after=(), name=""):
    kv_width, model_width = turned.shape
    low = len(grads) == 2
    arrays = [grad for grad, _ in grads]
    arrays += [block[1] if low else block[0], block[2], block[3], turned, gain]
    arrays += [array for pair in kept for array in pair]
    arrays += late
    operands = [near(array) for array in arrays]
    specs = [VMEM] * len(operands) + [ANY] * len(after)
    bf16 = jnp.bfloat16
    scratch = [pltpu.VMEM((UNIT, model_width), jnp.float32)]
    rows, value = (UNIT, model_width), (UNIT, kv_width)
    shapes = [rows, value]
    if late:
        half = lax.axis_size("dp") // 2
        scratch += [pltpu.VMEM((2 * BLOCK, model_width), bf16), pltpu.VMEM(value, bf16)]
        piece = BLOCK // half
        shapes = [rows, (BLOCK, kv_width), (3 * piece, model_width)]
    if len(late) > 2:
        shapes = [(BLOCK, kv_width), (2 * BLOCK, kv_width)]
        shapes += [(2 * piece, model_width)] * 3 + [(piece, model_width)]
    parts = [part for _, part in grads]
    return pl.pallas_call(
        functools.partial(
            tick_kernel, tick, EARLY if low else LATE, parts, len(kept), len(late)
        ),
        out_shape=tuple(jax.ShapeDtypeStruct(shape, bf16) for shape in shapes),
        in_specs=specs,
        out_specs=(VMEM,) * len(shapes),
        scratch_shapes=scratch,
        name=f"tick{tick}_{name}",
        **params(1.0 if kept else 0.0),
    )(*operands, *after)


def pack_kernel(block, half, piece, query_ref, key_ref, hidden_ref, up_ref, seg_ref, *rest):
    up_out_ref, seg_in_ref, rows_ref, sems = rest[-4:]
    packed = rest[-4 - half : -4]
    side, at, _ = place()
    there = side if block == 0 else 1 - side
    rows = pl.ds(pl.multiple_of(there * BLOCK, BLOCK), BLOCK)
    copies = []

    def copy(source, target):
        made = pltpu.make_async_copy(source, target, sems.at[len(copies)])
        made.start()
        copies.append(made)

    first = 0
    for source in (query_ref, key_ref, hidden_ref):
        width = source.shape[1]
        copy(source.at[rows], rows_ref.at[:, pl.ds(first, width)])
        first += width
    copy(seg_ref, seg_in_ref)
    copy(up_ref.at[rows], up_out_ref.at[pl.ds(0, BLOCK)])
    up_out_ref[BLOCK:, :] = jnp.zeros((16, up_out_ref.shape[1]), jnp.bfloat16)
    if block == 1:
        rest[2][...] = rest[1][...]
        turn_kernel(rest[0], rest[3])
    for made in copies[:4]:
        made.wait()
    ids = seg_in_ref[...].astype(jnp.float32)
    up_out_ref[BLOCK:, : ids.shape[1]] = jnp.broadcast_to(ids, (16, ids.shape[1])).astype(
        jnp.bfloat16
    )
    for k in range(half):
        first = pl.multiple_of(lax.bitwise_xor(at, k) * piece, piece)
        packed[k][...] = rows_ref[pl.ds(first, piece), :]
    copies[4].wait()


def pack(block, half, piece, sources, weight=None, gain=None):
    model_width = sources[0].shape[1]
    width = sum(source.shape[1] for source in sources[:3])
    bf16 = jnp.bfloat16
    operands = [pltpu.with_memory_space_constraint(array, pltpu.HBM) for array in sources]
    specs = [pl.BlockSpec(memory_space=pltpu.HBM)] * len(sources)
    outs = [jax.ShapeDtypeStruct((piece, width), bf16)] * half
    outs.append(jax.ShapeDtypeStruct((BLOCK + 16, model_width), bf16))
    if weight is not None:
        operands += [near(weight), gain]
        specs += [VMEM, VMEM]
        outs = [
            jax.ShapeDtypeStruct(gain.shape, gain.dtype),
            jax.ShapeDtypeStruct(weight.shape[::-1], bf16),
        ] + outs
    return pl.pallas_call(
        functools.partial(pack_kernel, block, half, piece),
        out_shape=tuple(outs),
        in_specs=specs,
        out_specs=(VMEM,) * len(outs),
        scratch_shapes=[
            pltpu.VMEM(sources[-1].shape, jnp.int32),
            pltpu.VMEM((BLOCK, width), bf16),
            pltpu.SemaphoreType.DMA((5,)),
        ],
        name="pack",
        **params(1.2),
    )(*operands)


def columns_kernel(width, distance, first_ref, second_ref, *refs):
    out_ref = refs[-1]
    if distance == 0:
        came_ref, out_ref, handed_ref = refs[0], refs[-2], refs[-1]
        handed_ref[...] = came_ref[came_ref.shape[0] - handed_ref.shape[0] :, :]
    if distance == 4:
        out_ref[2 * BLOCK :, :] = refs[0][...]
    there = lax.div(lax.bitwise_xor(place()[2], distance), 2)
    out_ref[:BLOCK, :] = first_ref[:, columns_of(there, width)]
    out_ref[BLOCK : 2 * BLOCK, :] = second_ref[:, columns_of(there, width)]


def columns_for(distance, blocks, after, came=()):
    model_width = blocks[0][3].shape[1]
    width = 2 * model_width // lax.axis_size("dp")
    shapes = [(2 * BLOCK, width)]
    if distance == 0:
        shapes.append((came[0].shape[0] // 3, model_width))
    if distance == 4:
        shapes = [(3 * BLOCK, width)]
    outs = [jax.ShapeDtypeStruct(shape, jnp.bfloat16) for shape in shapes]
    results = pl.pallas_call(
        functools.partial(columns_kernel, width, distance),
        out_shape=tuple(outs),
        in_specs=[VMEM] * (2 + len(came)) + [ANY] * len(after),
        out_specs=(VMEM,) * len(outs),
        name=f"columns{distance}",
        **params(0.0 if distance else 1.0),
    )(blocks[0][3], blocks[1][3], *came, *after)
    return results if distance == 0 else results[0]


def own_kernel(scale, weight_ref, gain_ref, after_ref, weight_out_ref, gain_out_ref):
    shares = weight_out_ref.shape[0]
    first = pl.multiple_of(place()[2] * shares, shares)
    weight_out_ref[...] = weight_ref[pl.ds(first, shares), :].astype(jnp.float32) * scale
    gain = gain_ref[:, pl.ds(first, shares)]
    column = jnp.sum(jnp.where(diagonal(shares), gain, 0.0), axis=1, keepdims=True)
    gain_out_ref[...] = jnp.broadcast_to(column * scale, gain_out_ref.shape)


def columns_of(pair, width):
    return pl.ds(pl.multiple_of(pair * width, width), width)


def partial_kernel(shares, first, for_other, *refs):
    columns, values, out_ref = refs[:4], refs[4:10], refs[-1]
    kv_width = out_ref.shape[1]
    parts = []
    for ref in values:
        beside = ref.shape[1] > kv_width
        rows = slice(first, 2 * first) if beside else slice(0, ref.shape[0])
        parts += [ref[rows, at : at + kv_width] for at in range(0, ref.shape[1], kv_width)]
    parts.insert(len(parts) - 3, columns[2][2 * BLOCK :, :])
    value = jnp.concatenate(parts, axis=0)
    mine = lax.rem(place()[2], 2)
    core = 1 - mine if for_other else mine
    at = pl.ds(pl.multiple_of(core * shares, shares), shares)
    rows = jnp.concatenate([ref[: 2 * BLOCK, at] for ref in columns], axis=0)
    out_ref[...] = lax.dot_general(
        rows, value, (((0,), (0,)), ((), ())), preferred_element_type=jnp.float32
    ).astype(out_ref.dtype)


def partial_sums(shares, piece, for_other, columns, values, after=()):
    kv_width = values[0].shape[1]
    return pl.pallas_call(
        functools.partial(partial_kernel, shares, piece, for_other),
        out_shape=jax.ShapeDtypeStruct(
            (shares, kv_width), jnp.bfloat16 if for_other else jnp.float32
        ),
        in_specs=[VMEM] * 10 + [ANY] * len(after),
        out_specs=VMEM,
        name="partial_other" if for_other else "partial_own",
        **params(0.0 if for_other else 0.5),
    )(*[columns[k] for k in (0, 2, 4, 6)], *values, *after)


def diagonal(size):
    return lax.broadcasted_iota(jnp.int32, (size, size), 0) == lax.broadcasted_iota(
        jnp.int32, (size, size), 1
    )


def rows_kernel(half, first_rows_ref, handed_ref, *refs):
    pieces = refs[:half]
    rows_ref, token_ref = refs[half:]
    side, at, _ = place()
    piece = BLOCK // half
    for block in range(2):
        for k in range(half):
            replica = (side if block == 0 else 1 - side) * half + lax.bitwise_xor(at, k)
            rows = pl.ds(pl.multiple_of(replica * piece, piece), piece)
            source, first = pieces[k], block * piece
            if k == 2:
                source, first = (pieces[k] if block else first_rows_ref), 0
            if k == 3:
                source, first = (pieces[k] if block else handed_ref), 0
            rows_ref[rows, :] = source[first : first + piece, :]
    token_ref[...] = jnp.zeros_like(token_ref)


def finish_kernel(
    own_ref, other_ref, weight_ref, gain_ref, after_ref, out_ref, gain_out_ref
):
    total = own_ref[...] + other_ref[...].astype(jnp.float32)
    out_ref[...] = total * gain_ref[:, :1]
    sums = jnp.sum(total * weight_ref[...], axis=1, keepdims=True)
    gain_out_ref[...] = jnp.sum(
        jnp.where(diagonal(total.shape[0]), sums, 0.0), axis=0, keepdims=True
    )


def direct(hidden, query, key, segments, weight, norm_gain, upstream):
    tokens, model_width = hidden.shape
    kv_width = key.shape[1]
    replicas = lax.axis_size("dp")
    layers = lax.axis_size("section")
    half = replicas // 2
    piece = tokens // replicas
    shares = model_width // replicas

    def swap(array, k):
        return lax.ppermute(array, "dp", [(i, i ^ k) for i in range(replicas)])

    count = 2 * half
    bf16 = jnp.bfloat16
    sources = (query, key, hidden, upstream, segments)
    pieces, ups = [], []
    for b in range(2):
        extra = (weight, norm_gain) if b else ()
        *packed, up = pack(b, half, piece, sources, *extra)
        if b:
            gain, turned, *packed = packed
        pieces.append([packed[0]] + [swap(packed[k], k) for k in range(1, half)])
        ups.append(swap(up, half) if b else up)
    whole = slice(0, UNIT)
    scale = float(tokens * replicas) ** (-0.5)
    blocks, kept, after = [], [], []
    for b in range(2):
        block = block_probs(pieces[b], ups[b], BLOCK, model_width, kv_width, after)
        late, early = (ups[b], LATE), (ups[b], EARLY)
        first = tick_step(0, [late], block, turned, gain, name=UNITS[2 * b])
        second = tick_step(
            0, [late, early], block, turned, gain, after=[first[0]], name=UNITS[2 * b + 1]
        )
        blocks.append(block)
        kept += [[first], [second]]
        after = [second[0]]

    for tick in range(1, layers):
        hop = [(layers - tick, layers - 1 - tick)]
        grads = [(lax.ppermute(unit[-1][0], "section", hop), whole) for unit in kept]
        last = tick == layers - 1
        after, done = [kept[3][-1][0]], []
        if tick == layers - 2:
            own_weight, own_gain = pl.pallas_call(
                functools.partial(own_kernel, scale),
                out_shape=(
                    jax.ShapeDtypeStruct((shares, kv_width), jnp.float32),
                    jax.ShapeDtypeStruct((shares, 128), jnp.float32),
                ),
                in_specs=[VMEM, VMEM, ANY],
                out_specs=(VMEM, VMEM),
                name="own",
                **params(0.0),
            )(near(weight), near(gain), *after)
            columns = {6: swap(columns_for(6, blocks, after + [own_gain]), 6)}
        if last:
            columns[2] = swap(columns_for(2, blocks, after + [columns[6]]), 2)
        for u in range(4):
            needs = grads[u - 1 : u + 1] if u % 2 else grads[u : u + 1]
            late = []
            if last and u == 1:
                late = [done[0][1], done[0][0]]
            if last and u == 3:
                late = [done[2][1], done[2][0], done[0][0], done[1][0], done[1][1]]
                first_rows, far_first = swap(done[1][2], 2), swap(done[1][1], 6)
                columns[4] = swap(columns_for(4, blocks, [], [done[1][1]]), 4)
                after = after + [columns[2]]
            done.append(
                tick_step(
                    tick, needs, blocks[u // 2], turned, gain, kept[u] if last else (), late,
                    after, name=UNITS[u],
                )
            )
            after = [done[u][0]]
            kept[u].append(done[u])
    own_value, own_values, *rows = done[3]
    rows = [rows[0]] + [swap(rows[k], k) for k in range(1, half)]
    far_value, across_value = swap(own_value, 6), swap(own_value, 4)
    columns[0], handed = columns_for(0, blocks, [own_value, columns[4], far_first], [first_rows])
    handed = swap(handed, 1)
    values = [own_values, first_rows, rows[2], across_value, far_first, far_value]
    other = partial_sums(shares, piece, True, columns, values)
    own = partial_sums(shares, piece, False, columns, values, [other])
    other = swap(other, 1)
    input_grad, token = pl.pallas_call(
        functools.partial(rows_kernel, half),
        out_shape=(
            jax.ShapeDtypeStruct((tokens, model_width), bf16),
            jax.ShapeDtypeStruct((8, 128), jnp.float32),
        ),
        in_specs=[VMEM] * (2 + half),
        out_specs=(VMEM, VMEM),
        name="rows",
        **params(2.5),
    )(first_rows, handed, *rows)
    weight_grad, gain_grad = pl.pallas_call(
        finish_kernel,
        out_shape=(
            jax.ShapeDtypeStruct((shares, kv_width), jnp.float32),
            jax.ShapeDtypeStruct((1, shares), jnp.float32),
        ),
        in_specs=[VMEM] * 4 + [ANY],
        out_specs=(VMEM, VMEM),
        name="finish",
        **params(0.0),
    )(own, other, own_weight, own_gain, token)
    return input_grad[None], weight_grad[None], gain_grad


def weight_kernel(scale, columns_ref, value_ref, weight_ref, gain_ref, out_ref, gain_out_ref):
    total = lax.dot_general(
        columns_ref[...], value_ref[...], (((0,), (0,)), ((), ())),
        preferred_element_type=jnp.float32,
    ) * scale
    out_ref[...] = total * gain_ref[...]
    product = total * weight_ref[...].astype(jnp.float32)
    sums = lax.dot_general(
        jnp.ones((8, product.shape[1]), jnp.float32), product, (((1,), (1,)), ((), ())),
        preferred_element_type=jnp.float32, precision=lax.Precision.HIGHEST,
    )
    gain_out_ref[...] = sums[:1]


def grouped(hidden, query, key, segments, weight, norm_gain, upstream):
    tokens, model_width = hidden.shape
    kv_width = key.shape[1]
    replicas = lax.axis_size("dp")
    layers = lax.axis_size("section")
    half = replicas // 2
    me = lax.axis_index("dp")
    section = lax.axis_index("section")
    side = me // half
    groups = [list(range(half)), list(range(half, replicas))]
    across = [(i, (i + half) % replicas) for i in range(replicas)]
    shares = model_width // replicas

    def rows_of(array, which, axis=0):
        at = side if which == 0 else 1 - side
        return lax.dynamic_slice_in_dim(array, at * BLOCK, BLOCK, axis)

    def regroup(array):
        return lax.all_to_all(
            array, "dp", split_axis=0, concat_axis=0, axis_index_groups=groups, tiled=True
        )

    def spread(array):
        return lax.all_to_all(array, "dp", split_axis=0, concat_axis=0, tiled=True)

    turned = turn(weight)
    blocks, grads = [], []
    for which in range(2):
        up = rows_of(upstream, which)
        seg = jnp.broadcast_to(segments, (16, 2 * BLOCK)).astype(jnp.bfloat16)
        if which == 1:
            up = lax.ppermute(up, "dp", across)
            seg = lax.ppermute(seg, "dp", across)
        packed = jnp.concatenate(
            [rows_of(query, which), rows_of(key, which), rows_of(hidden, which)], axis=1
        )
        blocks.append(block_probs([regroup(packed)], seg, 0, model_width, kv_width))
        grads.append(up)

    def layer(tick, which, grad, kept):
        live = (section == layers - 1 - tick).astype(jnp.int32)[None]
        return layer_step(live, grad, blocks[which], turned, norm_gain, kept)

    held = [layer(0, which, grads[which], ()) for which in range(2)]
    hops = [(i, i - 1) for i in range(1, layers)]

    def step(tick, held):
        grads = [lax.ppermute(kept[0], "section", hops) for kept in held]
        return [layer(tick, which, grads[which], held[which]) for which in range(2)]

    held = lax.fori_loop(1, layers, step, held)

    columns, values, stored = [], [], []
    for which in range(2):
        block = blocks[which][3].reshape(BLOCK, replicas, shares).transpose(1, 0, 2)
        columns.append(spread(block.reshape(replicas * BLOCK, shares)))
        out, value = held[which]
        stored.append(regroup(out))
        values.append(spread(jnp.tile(value, (replicas, 1))))
    ordered = jnp.where(
        side == 0, jnp.concatenate(stored, axis=0), jnp.concatenate(stored[::-1], axis=0)
    )
    own_weight = lax.dynamic_slice_in_dim(weight, me * shares, shares, 0)
    own_gain = lax.dynamic_slice_in_dim(norm_gain[0], me * shares, shares, 0)
    scale = float(tokens * replicas) ** (-0.5)
    weight_grad, gain_grad = pl.pallas_call(
        functools.partial(weight_kernel, scale),
        out_shape=(
            jax.ShapeDtypeStruct((shares, kv_width), jnp.float32),
            jax.ShapeDtypeStruct((1, shares), jnp.float32),
        ),
        in_specs=[VMEM] * 4,
        out_specs=(VMEM, VMEM),
        name="weight_grad",
    )(
        jnp.concatenate(columns, axis=0),
        jnp.concatenate(values, axis=0),
        own_weight,
        own_gain[:, None],
    )
    return ordered[None], weight_grad[None], gain_grad


def on_device(hidden_in, queries, keys, segments, value_weight, norm_gain, upstream):
    replicas = lax.axis_size("dp")
    piece = hidden_in.shape[1] // replicas
    plan = direct if piece % 16 == 0 and replicas == 8 else grouped
    return plan(
        hidden_in[0], queries[0], keys[0], segments, value_weight[0], norm_gain, upstream
    )


def solution(mesh):
    in_specs = (
        P("section", "dp", None),
        P("section", "dp", None),
        P("section", "dp", None),
        P("dp", None),
        P("section", None, None),
        P("section", None),
        P("dp", None),
    )
    out_specs = (P("section", "dp", None), P("section", "dp", None), P("section", "dp"))
    return jax.shard_map(
        on_device, mesh=mesh, in_specs=in_specs, out_specs=out_specs, check_vma=False
    )
```

```python
import functools

import jax
import jax.numpy as jnp
from jax import lax
from jax.experimental import pallas as pl
from jax.experimental.pallas import tpu as pltpu
from jax.sharding import PartitionSpec as P

HEAD_FEATURES = 128
BLOCK = 64
UNIT = 32
EPSILON = 1e-06
MASKED = -1e30
OUTS = {2: 3, 5: 6}
UNITS = ("a_late", "a_early", "b_late", "b_early")
VMEM = pl.BlockSpec(memory_space=pltpu.VMEM)
SMEM = pl.BlockSpec(memory_space=pltpu.SMEM)


ANY = pl.BlockSpec(memory_space=pl.ANY)


LATE, EARLY = slice(UNIT, BLOCK), slice(0, UNIT)


def params(microseconds):
    flops = int(microseconds * 1.15e9)
    return dict(
        compiler_params=pltpu.CompilerParams(vmem_limit_bytes=16 << 20),
        cost_estimate=pl.CostEstimate(flops=flops, bytes_accessed=0, transcendentals=0),
    )


def near(array):
    return pltpu.with_memory_space_constraint(array, pltpu.VMEM)


def place():
    half = lax.axis_size("dp") // 2
    me = lax.axis_index("dp")
    return lax.div(me, half), lax.rem(me, half), me


def probs_kernel(count, seg_row, model_width, kv_width, *refs):
    pieces, seg_ref = refs[:count], refs[count]
    late_ref, early_ref, inv_ref, x_ref, rows_ref = refs[-5:]
    heads = model_width // kv_width
    rows = BLOCK // count
    side, at, _ = place()
    for k, piece in enumerate(pieces):
        if count == 1:
            rows_ref[...] = piece[...]
        else:
            first = pl.multiple_of(lax.bitwise_xor(at, k) * rows, rows)
            rows_ref[pl.ds(first, rows), :] = piece[...]

    def iota(shape, axis):
        return lax.broadcasted_iota(jnp.int32, shape, axis)

    seg = seg_ref[seg_row : seg_row + 16, : 2 * BLOCK].astype(jnp.float32)[:1]
    shape = (BLOCK, 2 * BLOCK)
    wanted = iota(shape, 1) == side * BLOCK + iota(shape, 0)
    ids = jnp.sum(jnp.where(wanted, seg, 0.0), axis=1, keepdims=True)
    key_code = ids * BLOCK + iota((BLOCK, 1), 0).astype(jnp.float32)
    list_start = ids * BLOCK
    shape = (BLOCK, heads * BLOCK)
    column = iota(shape, 1)
    query_at = lax.rem(column, UNIT) + jnp.where(column < heads * UNIT, UNIT, 0)
    same = iota(shape, 0) == query_at
    query_code = jnp.sum(jnp.where(same, key_code, 0.0), axis=0, keepdims=True)
    query_start = jnp.sum(jnp.where(same, list_start, 0.0), axis=0, keepdims=True)
    allowed = (key_code <= query_code) & (key_code >= query_start)
    for c in range(kv_width // HEAD_FEATURES):
        first = c * heads * HEAD_FEATURES
        query_stack = jnp.concatenate(
            [
                rows_ref[part, first + h * HEAD_FEATURES : first + (h + 1) * HEAD_FEATURES]
                for part in (LATE, EARLY)
                for h in range(heads)
            ],
            axis=0,
        )
        key_first = model_width + c * HEAD_FEATURES
        keys = rows_ref[:, key_first : key_first + HEAD_FEATURES]
        scores = lax.dot_general(
            keys, query_stack, (((1,), (1,)), ((), ())), preferred_element_type=jnp.float32
        ) * HEAD_FEATURES ** (-0.5)
        scores = jnp.where(allowed, scores, MASKED)
        exp_scores = jnp.exp(scores - jnp.max(scores, axis=0, keepdims=True))
        total = jnp.sum(exp_scores, axis=0, keepdims=True)
        probs = (exp_scores / total).astype(jnp.bfloat16)
        late_ref[c] = probs[LATE, : heads * UNIT]
        early_ref[c] = probs[EARLY]
    hidden = rows_ref[:, model_width + kv_width :]
    x_ref[...] = hidden
    x = hidden.astype(jnp.float32)
    mean_square = jnp.mean(x * x, axis=1, keepdims=True)
    inv_ref[...] = jnp.broadcast_to(lax.rsqrt(mean_square + EPSILON), inv_ref.shape)


def block_probs(pieces, seg, seg_row, model_width, kv_width, after=()):
    heads = model_width // kv_width
    key_heads = kv_width // HEAD_FEATURES
    operands = [near(piece) for piece in pieces] + [near(seg)]
    specs = [VMEM] * len(operands) + [ANY] * len(after)
    operands += after
    return pl.pallas_call(
        functools.partial(probs_kernel, len(pieces), seg_row, model_width, kv_width),
        out_shape=(
            jax.ShapeDtypeStruct((key_heads, UNIT, heads * UNIT), jnp.bfloat16),
            jax.ShapeDtypeStruct((key_heads, UNIT, heads * BLOCK), jnp.bfloat16),
            jax.ShapeDtypeStruct((BLOCK, 128), jnp.float32),
            jax.ShapeDtypeStruct((BLOCK, model_width), jnp.bfloat16),
        ),
        in_specs=specs,
        out_specs=(VMEM,) * 4,
        scratch_shapes=[pltpu.VMEM((BLOCK, 2 * model_width + kv_width), jnp.bfloat16)],
        name="probs",
        **params(0.35 if after else 2.0),
    )(*operands)


def unit_math(rows, grads, probs_ref, x_ref, inv_ref, turned_ref, gain_ref, scaled_ref, store, value_ref):
    kv_width, model_width = turned_ref.shape
    heads = model_width // kv_width
    chunk = min(512, model_width)
    inv = inv_ref[rows, :1]
    values = []
    for c in range(kv_width // HEAD_FEATURES):
        first = c * heads * HEAD_FEATURES
        grad_stack = jnp.concatenate(
            [
                grad_ref[part, first + h * HEAD_FEATURES : first + (h + 1) * HEAD_FEATURES]
                for grad_ref, part in grads
                for h in range(heads)
            ],
            axis=0,
        )
        values.append(
            jnp.dot(probs_ref[c], grad_stack, preferred_element_type=jnp.float32).astype(
                jnp.bfloat16
            )
        )
    value = jnp.concatenate(values, axis=1)
    value_ref[...] = (value.astype(jnp.float32) * inv).astype(jnp.bfloat16)
    inner = jnp.zeros((UNIT, 1), jnp.float32)
    for first in range(0, model_width, chunk):
        columns = slice(first, first + chunk)
        normed_grad = jnp.dot(value, turned_ref[:, columns], preferred_element_type=jnp.float32)
        scaled = normed_grad * gain_ref[:, columns]
        scaled_ref[:, columns] = scaled
        x = x_ref[rows, columns].astype(jnp.float32)
        inner = inner + jnp.sum(x * scaled, axis=1, keepdims=True)
    pull = inner * (inv * inv / model_width)
    grad_ref, part = grads[-1]
    for first in range(0, model_width, chunk):
        columns = slice(first, first + chunk)
        x = x_ref[rows, columns].astype(jnp.float32)
        change = inv * (scaled_ref[:, columns] - x * pull)
        grad = grad_ref[part, columns].astype(jnp.float32)
        store(columns, (grad + change).astype(jnp.bfloat16))


def turn_kernel(weight_ref, *refs):
    turned_ref = refs[-1]
    step = min(256, weight_ref.shape[0])
    for first in range(0, weight_ref.shape[0], step):
        turned_ref[:, first : first + step] = weight_ref[first : first + step, :].T


def turn(weight, after=()):
    return pl.pallas_call(
        turn_kernel,
        out_shape=jax.ShapeDtypeStruct(weight.shape[::-1], weight.dtype),
        in_specs=[VMEM] + [ANY] * len(after),
        out_specs=VMEM,
        name="turn",
        **params(1.5),
    )(near(weight), *after)


def layer_kernel(
    live_ref, grad_ref, late_ref, early_ref, inv_ref, x_ref, turned_ref, gain_ref, *rest
):
    out_ref, value_ref, scaled_ref = rest[-3:]
    if len(rest) == 5:

        @pl.when(live_ref[0] == 0)
        def _():
            out_ref[...] = rest[0][...]
            value_ref[...] = rest[1][...]

    @pl.when(live_ref[0] == 1)
    def _():
        for rows, parts, probs_ref in ((LATE, [LATE], late_ref), (EARLY, [LATE, EARLY], early_ref)):

            def store(columns, part, rows=rows):
                out_ref[rows, columns] = part

            grads = [(grad_ref, part) for part in parts]
            unit_math(
                rows, grads, probs_ref, x_ref, inv_ref, turned_ref, gain_ref, scaled_ref, store,
                value_ref.at[rows],
            )


def layer_step(live, grad, block, turned, gain, held=()):
    kv_width, model_width = turned.shape
    operands = [live, grad, *block, turned, gain, *held]
    return pl.pallas_call(
        layer_kernel,
        out_shape=(
            jax.ShapeDtypeStruct((BLOCK, model_width), jnp.bfloat16),
            jax.ShapeDtypeStruct((BLOCK, kv_width), jnp.bfloat16),
        ),
        in_specs=[SMEM] + [VMEM] * (len(operands) - 1),
        out_specs=(VMEM, VMEM),
        scratch_shapes=[pltpu.VMEM((UNIT, model_width), jnp.float32)],
        name="layer",
        **params(1.1),
    )(*operands)


def tick_kernel(tick, rows, parts, kept, late, *refs):
    grads = list(zip(refs, parts))
    probs_ref, inv_ref, x_ref, turned_ref, gain_ref = refs[len(parts) : len(parts) + 5]
    refs = refs[len(parts) + 5 :]
    earlier, refs = refs[: 2 * kept], refs[2 * kept :]
    late_refs = refs[:late]
    kv_width, model_width = turned_ref.shape
    turn = lax.axis_size("section") - 1 - lax.axis_index("section")
    if late:
        outs, (scaled_ref, blocks_ref, value_ref) = refs[late : -3], refs[-3:]
        outs = outs[len(outs) - OUTS[late] :]
    else:
        outs, scaled_ref = refs[-3:-1], refs[-1]
        value_ref = outs[1]
    first_row = BLOCK if late > 2 else 0

    def store(columns, part):
        if late:
            blocks_ref[first_row : first_row + UNIT, columns] = part
        if late <= 2:
            outs[0][:, columns] = part

    @pl.when(turn == tick)
    def _():
        unit_math(
            rows, grads, probs_ref, x_ref, inv_ref, turned_ref, gain_ref, scaled_ref, store,
            value_ref,
        )

    for at in range(kept):

        @pl.when(turn == at)
        def _(at=at):
            store(slice(None), earlier[2 * at][...])
            value_ref[...] = earlier[2 * at + 1][...]

    if not late:
        return
    values = jnp.concatenate([value_ref[...], late_refs[0][...]], axis=0)
    blocks_ref[first_row + UNIT : first_row + BLOCK, :] = late_refs[1][...]
    outs[1 if late == 2 else 0][...] = values
    if late > 2:
        late_a_ref, early_a_ref, value_a_ref = late_refs[2:]
        outs[1][:BLOCK, :] = value_a_ref[...]
        outs[1][BLOCK:, :] = values
        blocks_ref[EARLY, :] = early_a_ref[...]
        blocks_ref[LATE, :] = late_a_ref[...]
    at = place()[1]
    pieces = {2: outs[2]} if late == 2 else dict(enumerate(outs[2:]))
    piece = BLOCK * kv_width // model_width

    def rows_for(k, block):
        first = pl.multiple_of(lax.bitwise_xor(at, k) * piece, piece)
        return blocks_ref[pl.ds(block * BLOCK + first, piece), :]

    block = 0 if late == 2 else 1
    for k, out_ref in pieces.items():
        if k == 2:
            out_ref[:piece, :] = rows_for(2, block)
            for g in range(model_width // kv_width):
                out_ref[piece : 2 * piece, g * kv_width : (g + 1) * kv_width] = values[
                    g * piece : (g + 1) * piece
                ]
            if block == 0:
                out_ref[2 * piece :, :] = rows_for(3, 0)
        elif k == 3:
            out_ref[...] = rows_for(3, 1)
        else:
            out_ref[:piece, :] = rows_for(k, 0)
            out_ref[piece:, :] = rows_for(k, 1)


def tick_step(tick, grads, block, turned, gain, kept=(), late=(), after=(), name=""):
    kv_width, model_width = turned.shape
    low = len(grads) == 2
    arrays = [grad for grad, _ in grads]
    arrays += [block[1] if low else block[0], block[2], block[3], turned, gain]
    arrays += [array for pair in kept for array in pair]
    arrays += late
    operands = [near(array) for array in arrays]
    specs = [VMEM] * len(operands) + [ANY] * len(after)
    bf16 = jnp.bfloat16
    scratch = [pltpu.VMEM((UNIT, model_width), jnp.float32)]
    rows, value = (UNIT, model_width), (UNIT, kv_width)
    shapes = [rows, value]
    if late:
        half = lax.axis_size("dp") // 2
        scratch += [pltpu.VMEM((2 * BLOCK, model_width), bf16), pltpu.VMEM(value, bf16)]
        piece = BLOCK // half
        shapes = [rows, (BLOCK, kv_width), (3 * piece, model_width)]
    if len(late) > 2:
        shapes = [(BLOCK, kv_width), (2 * BLOCK, kv_width)]
        shapes += [(2 * piece, model_width)] * 3 + [(piece, model_width)]
    parts = [part for _, part in grads]
    return pl.pallas_call(
        functools.partial(
            tick_kernel, tick, EARLY if low else LATE, parts, len(kept), len(late)
        ),
        out_shape=tuple(jax.ShapeDtypeStruct(shape, bf16) for shape in shapes),
        in_specs=specs,
        out_specs=(VMEM,) * len(shapes),
        scratch_shapes=scratch,
        name=f"tick{tick}_{name}",
        **params(1.0 if kept else 0.0),
    )(*operands, *after)


def pack_kernel(block, half, piece, query_ref, key_ref, hidden_ref, up_ref, seg_ref, *rest):
    up_out_ref, seg_in_ref, rows_ref, sems = rest[-4:]
    packed = rest[-4 - half : -4]
    side, at, _ = place()
    there = side if block == 0 else 1 - side
    rows = pl.ds(pl.multiple_of(there * BLOCK, BLOCK), BLOCK)
    copies = []

    def copy(source, target):
        made = pltpu.make_async_copy(source, target, sems.at[len(copies)])
        made.start()
        copies.append(made)

    first = 0
    for source in (query_ref, key_ref, hidden_ref):
        width = source.shape[1]
        copy(source.at[rows], rows_ref.at[:, pl.ds(first, width)])
        first += width
    copy(seg_ref, seg_in_ref)
    copy(up_ref.at[rows], up_out_ref.at[pl.ds(0, BLOCK)])
    up_out_ref[BLOCK:, :] = jnp.zeros((16, up_out_ref.shape[1]), jnp.bfloat16)
    if block == 1:
        rest[2][...] = rest[1][...]
        turn_kernel(rest[0], rest[3])
    for made in copies[:4]:
        made.wait()
    ids = seg_in_ref[...].astype(jnp.float32)
    up_out_ref[BLOCK:, : ids.shape[1]] = jnp.broadcast_to(ids, (16, ids.shape[1])).astype(
        jnp.bfloat16
    )
    for k in range(half):
        first = pl.multiple_of(lax.bitwise_xor(at, k) * piece, piece)
        packed[k][...] = rows_ref[pl.ds(first, piece), :]
    copies[4].wait()


def pack(block, half, piece, sources, weight=None, gain=None):
    model_width = sources[0].shape[1]
    width = sum(source.shape[1] for source in sources[:3])
    bf16 = jnp.bfloat16
    operands = [pltpu.with_memory_space_constraint(array, pltpu.HBM) for array in sources]
    specs = [pl.BlockSpec(memory_space=pltpu.HBM)] * len(sources)
    outs = [jax.ShapeDtypeStruct((piece, width), bf16)] * half
    outs.append(jax.ShapeDtypeStruct((BLOCK + 16, model_width), bf16))
    if weight is not None:
        operands += [near(weight), gain]
        specs += [VMEM, VMEM]
        outs = [
            jax.ShapeDtypeStruct(gain.shape, gain.dtype),
            jax.ShapeDtypeStruct(weight.shape[::-1], bf16),
        ] + outs
    return pl.pallas_call(
        functools.partial(pack_kernel, block, half, piece),
        out_shape=tuple(outs),
        in_specs=specs,
        out_specs=(VMEM,) * len(outs),
        scratch_shapes=[
            pltpu.VMEM(sources[-1].shape, jnp.int32),
            pltpu.VMEM((BLOCK, width), bf16),
            pltpu.SemaphoreType.DMA((5,)),
        ],
        name="pack",
        **params(1.2),
    )(*operands)


def columns_kernel(width, distance, first_ref, second_ref, *refs):
    out_ref = refs[-1]
    if distance == 0:
        came_ref, out_ref, handed_ref = refs[0], refs[-2], refs[-1]
        handed_ref[...] = came_ref[came_ref.shape[0] - handed_ref.shape[0] :, :]
    if distance == 4:
        out_ref[2 * BLOCK :, :] = refs[0][...]
    there = lax.div(lax.bitwise_xor(place()[2], distance), 2)
    out_ref[:BLOCK, :] = first_ref[:, columns_of(there, width)]
    out_ref[BLOCK : 2 * BLOCK, :] = second_ref[:, columns_of(there, width)]


def columns_for(distance, blocks, after, came=()):
    model_width = blocks[0][3].shape[1]
    width = 2 * model_width // lax.axis_size("dp")
    shapes = [(2 * BLOCK, width)]
    if distance == 0:
        shapes.append((came[0].shape[0] // 3, model_width))
    if distance == 4:
        shapes = [(3 * BLOCK, width)]
    outs = [jax.ShapeDtypeStruct(shape, jnp.bfloat16) for shape in shapes]
    results = pl.pallas_call(
        functools.partial(columns_kernel, width, distance),
        out_shape=tuple(outs),
        in_specs=[VMEM] * (2 + len(came)) + [ANY] * len(after),
        out_specs=(VMEM,) * len(outs),
        name=f"columns{distance}",
        **params(0.0 if distance else 0.8),
    )(blocks[0][3], blocks[1][3], *came, *after)
    return results if distance == 0 else results[0]


def own_kernel(scale, weight_ref, gain_ref, after_ref, weight_out_ref, gain_out_ref):
    shares = weight_out_ref.shape[0]
    first = pl.multiple_of(place()[2] * shares, shares)
    weight_out_ref[...] = weight_ref[pl.ds(first, shares), :].astype(jnp.float32) * scale
    gain = gain_ref[:, pl.ds(first, shares)]
    column = jnp.sum(jnp.where(diagonal(shares), gain, 0.0), axis=1, keepdims=True)
    gain_out_ref[...] = jnp.broadcast_to(column * scale, gain_out_ref.shape)


def columns_of(pair, width):
    return pl.ds(pl.multiple_of(pair * width, width), width)


def partial_kernel(shares, first, for_other, *refs):
    columns, values, out_ref = refs[:4], refs[4:10], refs[-1]
    kv_width = out_ref.shape[1]
    parts = []
    for ref in values:
        beside = ref.shape[1] > kv_width
        rows = slice(first, 2 * first) if beside else slice(0, ref.shape[0])
        parts += [ref[rows, at : at + kv_width] for at in range(0, ref.shape[1], kv_width)]
    parts.insert(len(parts) - 3, columns[2][2 * BLOCK :, :])
    value = jnp.concatenate(parts, axis=0)
    mine = lax.rem(place()[2], 2)
    core = 1 - mine if for_other else mine
    at = pl.ds(pl.multiple_of(core * shares, shares), shares)
    rows = jnp.concatenate([ref[: 2 * BLOCK, at] for ref in columns], axis=0)
    out_ref[...] = lax.dot_general(
        rows, value, (((0,), (0,)), ((), ())), preferred_element_type=jnp.float32
    ).astype(out_ref.dtype)


def partial_sums(shares, piece, for_other, columns, values, after=()):
    kv_width = values[0].shape[1]
    return pl.pallas_call(
        functools.partial(partial_kernel, shares, piece, for_other),
        out_shape=jax.ShapeDtypeStruct(
            (shares, kv_width), jnp.bfloat16 if for_other else jnp.float32
        ),
        in_specs=[VMEM] * 10 + [ANY] * len(after),
        out_specs=VMEM,
        name="partial_other" if for_other else "partial_own",
        **params(0.0 if for_other else 0.5),
    )(*[columns[k] for k in (0, 2, 4, 6)], *values, *after)


def diagonal(size):
    return lax.broadcasted_iota(jnp.int32, (size, size), 0) == lax.broadcasted_iota(
        jnp.int32, (size, size), 1
    )


def rows_kernel(half, first_rows_ref, handed_ref, *refs):
    pieces = refs[:half]
    rows_ref, token_ref = refs[half:]
    side, at, _ = place()
    piece = BLOCK // half
    for block in range(2):
        for k in range(half):
            replica = (side if block == 0 else 1 - side) * half + lax.bitwise_xor(at, k)
            rows = pl.ds(pl.multiple_of(replica * piece, piece), piece)
            source, first = pieces[k], block * piece
            if k == 2:
                source, first = (pieces[k] if block else first_rows_ref), 0
            if k == 3:
                source, first = (pieces[k] if block else handed_ref), 0
            rows_ref[rows, :] = source[first : first + piece, :]
    token_ref[...] = jnp.zeros_like(token_ref)


def finish_kernel(
    own_ref, other_ref, weight_ref, gain_ref, after_ref, out_ref, gain_out_ref
):
    total = own_ref[...] + other_ref[...].astype(jnp.float32)
    out_ref[...] = total * gain_ref[:, :1]
    sums = jnp.sum(total * weight_ref[...], axis=1, keepdims=True)
    gain_out_ref[...] = jnp.sum(
        jnp.where(diagonal(total.shape[0]), sums, 0.0), axis=0, keepdims=True
    )


def direct(hidden, query, key, segments, weight, norm_gain, upstream):
    tokens, model_width = hidden.shape
    kv_width = key.shape[1]
    replicas = lax.axis_size("dp")
    layers = lax.axis_size("section")
    half = replicas // 2
    piece = tokens // replicas
    shares = model_width // replicas

    def swap(array, k):
        return lax.ppermute(array, "dp", [(i, i ^ k) for i in range(replicas)])

    count = 2 * half
    bf16 = jnp.bfloat16
    sources = (query, key, hidden, upstream, segments)
    pieces, ups = [], []
    for b in range(2):
        extra = (weight, norm_gain) if b else ()
        *packed, up = pack(b, half, piece, sources, *extra)
        if b:
            gain, turned, *packed = packed
        pieces.append([packed[0]] + [swap(packed[k], k) for k in range(1, half)])
        ups.append(swap(up, half) if b else up)
    whole = slice(0, UNIT)
    scale = float(tokens * replicas) ** (-0.5)
    blocks, kept, after = [], [], []
    for b in range(2):
        block = block_probs(pieces[b], ups[b], BLOCK, model_width, kv_width, after)
        late, early = (ups[b], LATE), (ups[b], EARLY)
        first = tick_step(0, [late], block, turned, gain, name=UNITS[2 * b])
        second = tick_step(
            0, [late, early], block, turned, gain, after=[first[0]], name=UNITS[2 * b + 1]
        )
        blocks.append(block)
        kept += [[first], [second]]
        after = [second[0]]

    for tick in range(1, layers):
        hop = [(layers - tick, layers - 1 - tick)]
        grads = [(lax.ppermute(unit[-1][0], "section", hop), whole) for unit in kept]
        last = tick == layers - 1
        after, done = [kept[3][-1][0]], []
        if tick == layers - 2:
            own_weight, own_gain = pl.pallas_call(
                functools.partial(own_kernel, scale),
                out_shape=(
                    jax.ShapeDtypeStruct((shares, kv_width), jnp.float32),
                    jax.ShapeDtypeStruct((shares, 128), jnp.float32),
                ),
                in_specs=[VMEM, VMEM, ANY],
                out_specs=(VMEM, VMEM),
                name="own",
                **params(0.0),
            )(near(weight), near(gain), *after)
            columns = {6: swap(columns_for(6, blocks, after + [own_gain]), 6)}
        if last:
            columns[2] = swap(columns_for(2, blocks, after + [columns[6]]), 2)
        for u in range(4):
            needs = grads[u - 1 : u + 1] if u % 2 else grads[u : u + 1]
            late = []
            if last and u == 1:
                late = [done[0][1], done[0][0]]
            if last and u == 3:
                late = [done[2][1], done[2][0], done[0][0], done[1][0], done[1][1]]
                first_rows, far_first = swap(done[1][2], 2), swap(done[1][1], 6)
                columns[4] = swap(columns_for(4, blocks, [], [done[1][1]]), 4)
                after = after + [columns[2]]
            done.append(
                tick_step(
                    tick, needs, blocks[u // 2], turned, gain, kept[u] if last else (), late,
                    after, name=UNITS[u],
                )
            )
            after = [done[u][0]]
            kept[u].append(done[u])
    own_value, own_values, *rows = done[3]
    rows = [rows[0]] + [swap(rows[k], k) for k in range(1, half)]
    far_value, across_value = swap(own_value, 6), swap(own_value, 4)
    columns[0], handed = columns_for(0, blocks, [own_value, columns[4], far_first, far_value], [first_rows])
    handed = swap(handed, 1)
    values = [own_values, first_rows, rows[2], across_value, far_first, far_value]
    other = partial_sums(shares, piece, True, columns, values)
    own = partial_sums(shares, piece, False, columns, values, [other])
    other = swap(other, 1)
    input_grad, token = pl.pallas_call(
        functools.partial(rows_kernel, half),
        out_shape=(
            jax.ShapeDtypeStruct((tokens, model_width), bf16),
            jax.ShapeDtypeStruct((8, 128), jnp.float32),
        ),
        in_specs=[VMEM] * (2 + half),
        out_specs=(VMEM, VMEM),
        name="rows",
        **params(2.5),
    )(first_rows, handed, *rows)
    weight_grad, gain_grad = pl.pallas_call(
        finish_kernel,
        out_shape=(
            jax.ShapeDtypeStruct((shares, kv_width), jnp.float32),
            jax.ShapeDtypeStruct((1, shares), jnp.float32),
        ),
        in_specs=[VMEM] * 4 + [ANY],
        out_specs=(VMEM, VMEM),
        name="finish",
        **params(0.0),
    )(own, other, own_weight, own_gain, token)
    return input_grad[None], weight_grad[None], gain_grad


def weight_kernel(scale, columns_ref, value_ref, weight_ref, gain_ref, out_ref, gain_out_ref):
    total = lax.dot_general(
        columns_ref[...], value_ref[...], (((0,), (0,)), ((), ())),
        preferred_element_type=jnp.float32,
    ) * scale
    out_ref[...] = total * gain_ref[...]
    product = total * weight_ref[...].astype(jnp.float32)
    sums = lax.dot_general(
        jnp.ones((8, product.shape[1]), jnp.float32), product, (((1,), (1,)), ((), ())),
        preferred_element_type=jnp.float32, precision=lax.Precision.HIGHEST,
    )
    gain_out_ref[...] = sums[:1]


def grouped(hidden, query, key, segments, weight, norm_gain, upstream):
    tokens, model_width = hidden.shape
    kv_width = key.shape[1]
    replicas = lax.axis_size("dp")
    layers = lax.axis_size("section")
    half = replicas // 2
    me = lax.axis_index("dp")
    section = lax.axis_index("section")
    side = me // half
    groups = [list(range(half)), list(range(half, replicas))]
    across = [(i, (i + half) % replicas) for i in range(replicas)]
    shares = model_width // replicas

    def rows_of(array, which, axis=0):
        at = side if which == 0 else 1 - side
        return lax.dynamic_slice_in_dim(array, at * BLOCK, BLOCK, axis)

    def regroup(array):
        return lax.all_to_all(
            array, "dp", split_axis=0, concat_axis=0, axis_index_groups=groups, tiled=True
        )

    def spread(array):
        return lax.all_to_all(array, "dp", split_axis=0, concat_axis=0, tiled=True)

    turned = turn(weight)
    blocks, grads = [], []
    for which in range(2):
        up = rows_of(upstream, which)
        seg = jnp.broadcast_to(segments, (16, 2 * BLOCK)).astype(jnp.bfloat16)
        if which == 1:
            up = lax.ppermute(up, "dp", across)
            seg = lax.ppermute(seg, "dp", across)
        packed = jnp.concatenate(
            [rows_of(query, which), rows_of(key, which), rows_of(hidden, which)], axis=1
        )
        blocks.append(block_probs([regroup(packed)], seg, 0, model_width, kv_width))
        grads.append(up)

    def layer(tick, which, grad, kept):
        live = (section == layers - 1 - tick).astype(jnp.int32)[None]
        return layer_step(live, grad, blocks[which], turned, norm_gain, kept)

    held = [layer(0, which, grads[which], ()) for which in range(2)]
    hops = [(i, i - 1) for i in range(1, layers)]

    def step(tick, held):
        grads = [lax.ppermute(kept[0], "section", hops) for kept in held]
        return [layer(tick, which, grads[which], held[which]) for which in range(2)]

    held = lax.fori_loop(1, layers, step, held)

    columns, values, stored = [], [], []
    for which in range(2):
        block = blocks[which][3].reshape(BLOCK, replicas, shares).transpose(1, 0, 2)
        columns.append(spread(block.reshape(replicas * BLOCK, shares)))
        out, value = held[which]
        stored.append(regroup(out))
        values.append(spread(jnp.tile(value, (replicas, 1))))
    ordered = jnp.where(
        side == 0, jnp.concatenate(stored, axis=0), jnp.concatenate(stored[::-1], axis=0)
    )
    own_weight = lax.dynamic_slice_in_dim(weight, me * shares, shares, 0)
    own_gain = lax.dynamic_slice_in_dim(norm_gain[0], me * shares, shares, 0)
    scale = float(tokens * replicas) ** (-0.5)
    weight_grad, gain_grad = pl.pallas_call(
        functools.partial(weight_kernel, scale),
        out_shape=(
            jax.ShapeDtypeStruct((shares, kv_width), jnp.float32),
            jax.ShapeDtypeStruct((1, shares), jnp.float32),
        ),
        in_specs=[VMEM] * 4,
        out_specs=(VMEM, VMEM),
        name="weight_grad",
    )(
        jnp.concatenate(columns, axis=0),
        jnp.concatenate(values, axis=0),
        own_weight,
        own_gain[:, None],
    )
    return ordered[None], weight_grad[None], gain_grad


def on_device(hidden_in, queries, keys, segments, value_weight, norm_gain, upstream):
    replicas = lax.axis_size("dp")
    piece = hidden_in.shape[1] // replicas
    plan = direct if piece % 16 == 0 and replicas == 8 else grouped
    return plan(
        hidden_in[0], queries[0], keys[0], segments, value_weight[0], norm_gain, upstream
    )


def solution(mesh):
    in_specs = (
        P("section", "dp", None),
        P("section", "dp", None),
        P("section", "dp", None),
        P("dp", None),
        P("section", None, None),
        P("section", None),
        P("dp", None),
    )
    out_specs = (P("section", "dp", None), P("section", "dp", None), P("section", "dp"))
    return jax.shard_map(
        on_device, mesh=mesh, in_specs=in_specs, out_specs=out_specs, check_vma=False
    )
```

```python
import functools

import jax
import jax.numpy as jnp
from jax import lax
from jax.experimental import pallas as pl
from jax.experimental.pallas import tpu as pltpu
from jax.sharding import PartitionSpec as P

HEAD_FEATURES = 128
BLOCK = 64
UNIT = 32
EPSILON = 1e-06
MASKED = -1e30
OUTS = {2: 3, 5: 6}
UNITS = ("a_late", "a_early", "b_late", "b_early")
VMEM = pl.BlockSpec(memory_space=pltpu.VMEM)
SMEM = pl.BlockSpec(memory_space=pltpu.SMEM)


ANY = pl.BlockSpec(memory_space=pl.ANY)


LATE, EARLY = slice(UNIT, BLOCK), slice(0, UNIT)


def params(microseconds):
    flops = int(microseconds * 1.15e9)
    return dict(
        compiler_params=pltpu.CompilerParams(vmem_limit_bytes=16 << 20),
        cost_estimate=pl.CostEstimate(flops=flops, bytes_accessed=0, transcendentals=0),
    )


def near(array):
    return pltpu.with_memory_space_constraint(array, pltpu.VMEM)


def place():
    half = lax.axis_size("dp") // 2
    me = lax.axis_index("dp")
    return lax.div(me, half), lax.rem(me, half), me


def probs_kernel(count, seg_row, model_width, kv_width, *refs):
    pieces, seg_ref = refs[:count], refs[count]
    late_ref, early_ref, inv_ref, x_ref, rows_ref = refs[-5:]
    heads = model_width // kv_width
    rows = BLOCK // count
    side, at, _ = place()
    for k, piece in enumerate(pieces):
        if count == 1:
            rows_ref[...] = piece[...]
        else:
            first = pl.multiple_of(lax.bitwise_xor(at, k) * rows, rows)
            rows_ref[pl.ds(first, rows), :] = piece[...]

    def iota(shape, axis):
        return lax.broadcasted_iota(jnp.int32, shape, axis)

    seg = seg_ref[seg_row : seg_row + 16, : 2 * BLOCK].astype(jnp.float32)[:1]
    shape = (BLOCK, 2 * BLOCK)
    wanted = iota(shape, 1) == side * BLOCK + iota(shape, 0)
    ids = jnp.sum(jnp.where(wanted, seg, 0.0), axis=1, keepdims=True)
    key_code = ids * BLOCK + iota((BLOCK, 1), 0).astype(jnp.float32)
    list_start = ids * BLOCK
    shape = (BLOCK, heads * BLOCK)
    column = iota(shape, 1)
    query_at = lax.rem(column, UNIT) + jnp.where(column < heads * UNIT, UNIT, 0)
    same = iota(shape, 0) == query_at
    query_code = jnp.sum(jnp.where(same, key_code, 0.0), axis=0, keepdims=True)
    query_start = jnp.sum(jnp.where(same, list_start, 0.0), axis=0, keepdims=True)
    allowed = (key_code <= query_code) & (key_code >= query_start)
    for c in range(kv_width // HEAD_FEATURES):
        first = c * heads * HEAD_FEATURES
        query_stack = jnp.concatenate(
            [
                rows_ref[part, first + h * HEAD_FEATURES : first + (h + 1) * HEAD_FEATURES]
                for part in (LATE, EARLY)
                for h in range(heads)
            ],
            axis=0,
        )
        key_first = model_width + c * HEAD_FEATURES
        keys = rows_ref[:, key_first : key_first + HEAD_FEATURES]
        scores = lax.dot_general(
            keys, query_stack, (((1,), (1,)), ((), ())), preferred_element_type=jnp.float32
        ) * HEAD_FEATURES ** (-0.5)
        scores = jnp.where(allowed, scores, MASKED)
        exp_scores = jnp.exp(scores - jnp.max(scores, axis=0, keepdims=True))
        total = jnp.sum(exp_scores, axis=0, keepdims=True)
        probs = (exp_scores / total).astype(jnp.bfloat16)
        late_ref[c] = probs[LATE, : heads * UNIT]
        early_ref[c] = probs[EARLY]
    hidden = rows_ref[:, model_width + kv_width :]
    x_ref[...] = hidden
    x = hidden.astype(jnp.float32)
    mean_square = jnp.mean(x * x, axis=1, keepdims=True)
    inv_ref[...] = jnp.broadcast_to(lax.rsqrt(mean_square + EPSILON), inv_ref.shape)


def block_probs(pieces, seg, seg_row, model_width, kv_width, after=()):
    heads = model_width // kv_width
    key_heads = kv_width // HEAD_FEATURES
    operands = [near(piece) for piece in pieces] + [near(seg)]
    specs = [VMEM] * len(operands) + [ANY] * len(after)
    operands += after
    return pl.pallas_call(
        functools.partial(probs_kernel, len(pieces), seg_row, model_width, kv_width),
        out_shape=(
            jax.ShapeDtypeStruct((key_heads, UNIT, heads * UNIT), jnp.bfloat16),
            jax.ShapeDtypeStruct((key_heads, UNIT, heads * BLOCK), jnp.bfloat16),
            jax.ShapeDtypeStruct((BLOCK, 128), jnp.float32),
            jax.ShapeDtypeStruct((BLOCK, model_width), jnp.bfloat16),
        ),
        in_specs=specs,
        out_specs=(VMEM,) * 4,
        scratch_shapes=[pltpu.VMEM((BLOCK, 2 * model_width + kv_width), jnp.bfloat16)],
        name="probs",
        **params(0.35 if after else 2.0),
    )(*operands)


def unit_math(rows, grads, probs_ref, x_ref, inv_ref, turned_ref, gain_ref, scaled_ref, store, value_ref):
    kv_width, model_width = turned_ref.shape
    heads = model_width // kv_width
    chunk = min(512, model_width)
    inv = inv_ref[rows, :1]
    values = []
    for c in range(kv_width // HEAD_FEATURES):
        first = c * heads * HEAD_FEATURES
        grad_stack = jnp.concatenate(
            [
                grad_ref[part, first + h * HEAD_FEATURES : first + (h + 1) * HEAD_FEATURES]
                for grad_ref, part in grads
                for h in range(heads)
            ],
            axis=0,
        )
        values.append(
            jnp.dot(probs_ref[c], grad_stack, preferred_element_type=jnp.float32).astype(
                jnp.bfloat16
            )
        )
    value = jnp.concatenate(values, axis=1)
    value_ref[...] = (value.astype(jnp.float32) * inv).astype(jnp.bfloat16)
    inner = jnp.zeros((UNIT, 1), jnp.float32)
    for first in range(0, model_width, chunk):
        columns = slice(first, first + chunk)
        normed_grad = jnp.dot(value, turned_ref[:, columns], preferred_element_type=jnp.float32)
        scaled = normed_grad * gain_ref[:, columns]
        scaled_ref[:, columns] = scaled
        x = x_ref[rows, columns].astype(jnp.float32)
        inner = inner + jnp.sum(x * scaled, axis=1, keepdims=True)
    pull = inner * (inv * inv / model_width)
    grad_ref, part = grads[-1]
    for first in range(0, model_width, chunk):
        columns = slice(first, first + chunk)
        x = x_ref[rows, columns].astype(jnp.float32)
        change = inv * (scaled_ref[:, columns] - x * pull)
        grad = grad_ref[part, columns].astype(jnp.float32)
        store(columns, (grad + change).astype(jnp.bfloat16))


def turn_kernel(weight_ref, *refs):
    turned_ref = refs[-1]
    step = min(256, weight_ref.shape[0])
    for first in range(0, weight_ref.shape[0], step):
        turned_ref[:, first : first + step] = weight_ref[first : first + step, :].T


def turn(weight, after=()):
    return pl.pallas_call(
        turn_kernel,
        out_shape=jax.ShapeDtypeStruct(weight.shape[::-1], weight.dtype),
        in_specs=[VMEM] + [ANY] * len(after),
        out_specs=VMEM,
        name="turn",
        **params(1.5),
    )(near(weight), *after)


def layer_kernel(
    live_ref, grad_ref, late_ref, early_ref, inv_ref, x_ref, turned_ref, gain_ref, *rest
):
    out_ref, value_ref, scaled_ref = rest[-3:]
    if len(rest) == 5:

        @pl.when(live_ref[0] == 0)
        def _():
            out_ref[...] = rest[0][...]
            value_ref[...] = rest[1][...]

    @pl.when(live_ref[0] == 1)
    def _():
        for rows, parts, probs_ref in ((LATE, [LATE], late_ref), (EARLY, [LATE, EARLY], early_ref)):

            def store(columns, part, rows=rows):
                out_ref[rows, columns] = part

            grads = [(grad_ref, part) for part in parts]
            unit_math(
                rows, grads, probs_ref, x_ref, inv_ref, turned_ref, gain_ref, scaled_ref, store,
                value_ref.at[rows],
            )


def layer_step(live, grad, block, turned, gain, held=()):
    kv_width, model_width = turned.shape
    operands = [live, grad, *block, turned, gain, *held]
    return pl.pallas_call(
        layer_kernel,
        out_shape=(
            jax.ShapeDtypeStruct((BLOCK, model_width), jnp.bfloat16),
            jax.ShapeDtypeStruct((BLOCK, kv_width), jnp.bfloat16),
        ),
        in_specs=[SMEM] + [VMEM] * (len(operands) - 1),
        out_specs=(VMEM, VMEM),
        scratch_shapes=[pltpu.VMEM((UNIT, model_width), jnp.float32)],
        name="layer",
        **params(1.1),
    )(*operands)


def tick_kernel(tick, rows, parts, kept, late, *refs):
    grads = list(zip(refs, parts))
    probs_ref, inv_ref, x_ref, turned_ref, gain_ref = refs[len(parts) : len(parts) + 5]
    refs = refs[len(parts) + 5 :]
    earlier, refs = refs[: 2 * kept], refs[2 * kept :]
    late_refs = refs[:late]
    kv_width, model_width = turned_ref.shape
    turn = lax.axis_size("section") - 1 - lax.axis_index("section")
    if late:
        outs, (scaled_ref, blocks_ref, value_ref) = refs[late : -3], refs[-3:]
        outs = outs[len(outs) - OUTS[late] :]
    else:
        outs, scaled_ref = refs[-3:-1], refs[-1]
        value_ref = outs[1]
    first_row = BLOCK if late > 2 else 0

    def store(columns, part):
        if late:
            blocks_ref[first_row : first_row + UNIT, columns] = part
        if late <= 2:
            outs[0][:, columns] = part

    @pl.when(turn == tick)
    def _():
        unit_math(
            rows, grads, probs_ref, x_ref, inv_ref, turned_ref, gain_ref, scaled_ref, store,
            value_ref,
        )

    for at in range(kept):

        @pl.when(turn == at)
        def _(at=at):
            store(slice(None), earlier[2 * at][...])
            value_ref[...] = earlier[2 * at + 1][...]

    if not late:
        return
    values = jnp.concatenate([value_ref[...], late_refs[0][...]], axis=0)
    blocks_ref[first_row + UNIT : first_row + BLOCK, :] = late_refs[1][...]
    outs[1 if late == 2 else 0][...] = values
    if late > 2:
        late_a_ref, early_a_ref, value_a_ref = late_refs[2:]
        outs[1][:BLOCK, :] = value_a_ref[...]
        outs[1][BLOCK:, :] = values
        blocks_ref[EARLY, :] = early_a_ref[...]
        blocks_ref[LATE, :] = late_a_ref[...]
    at = place()[1]
    pieces = {2: outs[2]} if late == 2 else dict(enumerate(outs[2:]))
    piece = BLOCK * kv_width // model_width

    def rows_for(k, block):
        first = pl.multiple_of(lax.bitwise_xor(at, k) * piece, piece)
        return blocks_ref[pl.ds(block * BLOCK + first, piece), :]

    block = 0 if late == 2 else 1
    for k, out_ref in pieces.items():
        if k == 2:
            out_ref[:piece, :] = rows_for(2, block)
            for g in range(model_width // kv_width):
                out_ref[piece : 2 * piece, g * kv_width : (g + 1) * kv_width] = values[
                    g * piece : (g + 1) * piece
                ]
            if block == 0:
                out_ref[2 * piece :, :] = rows_for(3, 0)
        elif k == 3:
            out_ref[...] = rows_for(3, 1)
        else:
            out_ref[:piece, :] = rows_for(k, 0)
            out_ref[piece:, :] = rows_for(k, 1)


def tick_step(tick, grads, block, turned, gain, kept=(), late=(), after=(), name=""):
    kv_width, model_width = turned.shape
    low = len(grads) == 2
    arrays = [grad for grad, _ in grads]
    arrays += [block[1] if low else block[0], block[2], block[3], turned, gain]
    arrays += [array for pair in kept for array in pair]
    arrays += late
    operands = [near(array) for array in arrays]
    specs = [VMEM] * len(operands) + [ANY] * len(after)
    bf16 = jnp.bfloat16
    scratch = [pltpu.VMEM((UNIT, model_width), jnp.float32)]
    rows, value = (UNIT, model_width), (UNIT, kv_width)
    shapes = [rows, value]
    if late:
        half = lax.axis_size("dp") // 2
        scratch += [pltpu.VMEM((2 * BLOCK, model_width), bf16), pltpu.VMEM(value, bf16)]
        piece = BLOCK // half
        shapes = [rows, (BLOCK, kv_width), (3 * piece, model_width)]
    if len(late) > 2:
        shapes = [(BLOCK, kv_width), (2 * BLOCK, kv_width)]
        shapes += [(2 * piece, model_width)] * 3 + [(piece, model_width)]
    parts = [part for _, part in grads]
    return pl.pallas_call(
        functools.partial(
            tick_kernel, tick, EARLY if low else LATE, parts, len(kept), len(late)
        ),
        out_shape=tuple(jax.ShapeDtypeStruct(shape, bf16) for shape in shapes),
        in_specs=specs,
        out_specs=(VMEM,) * len(shapes),
        scratch_shapes=scratch,
        name=f"tick{tick}_{name}",
        **params(1.0 if kept else 1.5 if tick == 1 and name in UNITS[2:] else 0.0),
    )(*operands, *after)


def pack_kernel(block, half, piece, query_ref, key_ref, hidden_ref, up_ref, seg_ref, *rest):
    up_out_ref, seg_in_ref, rows_ref, sems = rest[-4:]
    packed = rest[-4 - half : -4]
    side, at, _ = place()
    there = side if block == 0 else 1 - side
    rows = pl.ds(pl.multiple_of(there * BLOCK, BLOCK), BLOCK)
    copies = []

    def copy(source, target):
        made = pltpu.make_async_copy(source, target, sems.at[len(copies)])
        made.start()
        copies.append(made)

    first = 0
    for source in (query_ref, key_ref, hidden_ref):
        width = source.shape[1]
        copy(source.at[rows], rows_ref.at[:, pl.ds(first, width)])
        first += width
    copy(seg_ref, seg_in_ref)
    copy(up_ref.at[rows], up_out_ref.at[pl.ds(0, BLOCK)])
    up_out_ref[BLOCK:, :] = jnp.zeros((16, up_out_ref.shape[1]), jnp.bfloat16)
    if block == 1:
        rest[2][...] = rest[1][...]
        turn_kernel(rest[0], rest[3])
    for made in copies[:4]:
        made.wait()
    ids = seg_in_ref[...].astype(jnp.float32)
    up_out_ref[BLOCK:, : ids.shape[1]] = jnp.broadcast_to(ids, (16, ids.shape[1])).astype(
        jnp.bfloat16
    )
    for k in range(half):
        first = pl.multiple_of(lax.bitwise_xor(at, k) * piece, piece)
        packed[k][...] = rows_ref[pl.ds(first, piece), :]
    copies[4].wait()


def pack(block, half, piece, sources, weight=None, gain=None):
    model_width = sources[0].shape[1]
    width = sum(source.shape[1] for source in sources[:3])
    bf16 = jnp.bfloat16
    operands = [pltpu.with_memory_space_constraint(array, pltpu.HBM) for array in sources]
    specs = [pl.BlockSpec(memory_space=pltpu.HBM)] * len(sources)
    outs = [jax.ShapeDtypeStruct((piece, width), bf16)] * half
    outs.append(jax.ShapeDtypeStruct((BLOCK + 16, model_width), bf16))
    if weight is not None:
        operands += [near(weight), gain]
        specs += [VMEM, VMEM]
        outs = [
            jax.ShapeDtypeStruct(gain.shape, gain.dtype),
            jax.ShapeDtypeStruct(weight.shape[::-1], bf16),
        ] + outs
    return pl.pallas_call(
        functools.partial(pack_kernel, block, half, piece),
        out_shape=tuple(outs),
        in_specs=specs,
        out_specs=(VMEM,) * len(outs),
        scratch_shapes=[
            pltpu.VMEM(sources[-1].shape, jnp.int32),
            pltpu.VMEM((BLOCK, width), bf16),
            pltpu.SemaphoreType.DMA((5,)),
        ],
        name="pack",
        **params(1.2),
    )(*operands)


def columns_kernel(width, distance, first_ref, second_ref, *refs):
    out_ref = refs[-1]
    if distance == 0:
        came_ref, out_ref, handed_ref = refs[0], refs[-2], refs[-1]
        handed_ref[...] = came_ref[came_ref.shape[0] - handed_ref.shape[0] :, :]
    if distance == 4:
        out_ref[2 * BLOCK :, :] = refs[0][...]
    there = lax.div(lax.bitwise_xor(place()[2], distance), 2)
    out_ref[:BLOCK, :] = first_ref[:, columns_of(there, width)]
    out_ref[BLOCK : 2 * BLOCK, :] = second_ref[:, columns_of(there, width)]


def columns_for(distance, blocks, after, came=()):
    model_width = blocks[0][3].shape[1]
    width = 2 * model_width // lax.axis_size("dp")
    shapes = [(2 * BLOCK, width)]
    if distance == 0:
        shapes.append((came[0].shape[0] // 3, model_width))
    if distance == 4:
        shapes = [(3 * BLOCK, width)]
    outs = [jax.ShapeDtypeStruct(shape, jnp.bfloat16) for shape in shapes]
    results = pl.pallas_call(
        functools.partial(columns_kernel, width, distance),
        out_shape=tuple(outs),
        in_specs=[VMEM] * (2 + len(came)) + [ANY] * len(after),
        out_specs=(VMEM,) * len(outs),
        name=f"columns{distance}",
        **params(0.0 if distance else 0.8),
    )(blocks[0][3], blocks[1][3], *came, *after)
    return results if distance == 0 else results[0]


def own_kernel(scale, weight_ref, gain_ref, after_ref, weight_out_ref, gain_out_ref):
    shares = weight_out_ref.shape[0]
    first = pl.multiple_of(place()[2] * shares, shares)
    weight_out_ref[...] = weight_ref[pl.ds(first, shares), :].astype(jnp.float32) * scale
    gain = gain_ref[:, pl.ds(first, shares)]
    column = jnp.sum(jnp.where(diagonal(shares), gain, 0.0), axis=1, keepdims=True)
    gain_out_ref[...] = jnp.broadcast_to(column * scale, gain_out_ref.shape)


def columns_of(pair, width):
    return pl.ds(pl.multiple_of(pair * width, width), width)


def partial_kernel(shares, first, for_other, *refs):
    columns, values, out_ref = refs[:4], refs[4:10], refs[-1]
    kv_width = out_ref.shape[1]
    parts = []
    for ref in values:
        beside = ref.shape[1] > kv_width
        rows = slice(first, 2 * first) if beside else slice(0, ref.shape[0])
        parts += [ref[rows, at : at + kv_width] for at in range(0, ref.shape[1], kv_width)]
    parts.insert(len(parts) - 3, columns[2][2 * BLOCK :, :])
    value = jnp.concatenate(parts, axis=0)
    mine = lax.rem(place()[2], 2)
    core = 1 - mine if for_other else mine
    at = pl.ds(pl.multiple_of(core * shares, shares), shares)
    rows = jnp.concatenate([ref[: 2 * BLOCK, at] for ref in columns], axis=0)
    out_ref[...] = lax.dot_general(
        rows, value, (((0,), (0,)), ((), ())), preferred_element_type=jnp.float32
    ).astype(out_ref.dtype)


def partial_sums(shares, piece, for_other, columns, values, after=()):
    kv_width = values[0].shape[1]
    return pl.pallas_call(
        functools.partial(partial_kernel, shares, piece, for_other),
        out_shape=jax.ShapeDtypeStruct(
            (shares, kv_width), jnp.bfloat16 if for_other else jnp.float32
        ),
        in_specs=[VMEM] * 10 + [ANY] * len(after),
        out_specs=VMEM,
        name="partial_other" if for_other else "partial_own",
        **params(0.0 if for_other else 0.5),
    )(*[columns[k] for k in (0, 2, 4, 6)], *values, *after)


def diagonal(size):
    return lax.broadcasted_iota(jnp.int32, (size, size), 0) == lax.broadcasted_iota(
        jnp.int32, (size, size), 1
    )


def rows_kernel(half, first_rows_ref, handed_ref, *refs):
    pieces = refs[:half]
    rows_ref, token_ref = refs[half:]
    side, at, _ = place()
    piece = BLOCK // half
    for block in range(2):
        for k in range(half):
            replica = (side if block == 0 else 1 - side) * half + lax.bitwise_xor(at, k)
            rows = pl.ds(pl.multiple_of(replica * piece, piece), piece)
            source, first = pieces[k], block * piece
            if k == 2:
                source, first = (pieces[k] if block else first_rows_ref), 0
            if k == 3:
                source, first = (pieces[k] if block else handed_ref), 0
            rows_ref[rows, :] = source[first : first + piece, :]
    token_ref[...] = jnp.zeros_like(token_ref)


def finish_kernel(
    own_ref, other_ref, weight_ref, gain_ref, after_ref, out_ref, gain_out_ref
):
    total = own_ref[...] + other_ref[...].astype(jnp.float32)
    out_ref[...] = total * gain_ref[:, :1]
    sums = jnp.sum(total * weight_ref[...], axis=1, keepdims=True)
    gain_out_ref[...] = jnp.sum(
        jnp.where(diagonal(total.shape[0]), sums, 0.0), axis=0, keepdims=True
    )


def direct(hidden, query, key, segments, weight, norm_gain, upstream):
    tokens, model_width = hidden.shape
    kv_width = key.shape[1]
    replicas = lax.axis_size("dp")
    layers = lax.axis_size("section")
    half = replicas // 2
    piece = tokens // replicas
    shares = model_width // replicas

    def swap(array, k):
        return lax.ppermute(array, "dp", [(i, i ^ k) for i in range(replicas)])

    count = 2 * half
    bf16 = jnp.bfloat16
    sources = (query, key, hidden, upstream, segments)
    pieces, ups = [], []
    for b in range(2):
        extra = (weight, norm_gain) if b else ()
        *packed, up = pack(b, half, piece, sources, *extra)
        if b:
            gain, turned, *packed = packed
        pieces.append([packed[0]] + [swap(packed[k], k) for k in range(1, half)])
        ups.append(swap(up, half) if b else up)
    whole = slice(0, UNIT)
    scale = float(tokens * replicas) ** (-0.5)
    blocks, kept, after = [], [], []
    for b in range(2):
        block = block_probs(pieces[b], ups[b], BLOCK, model_width, kv_width, after)
        late, early = (ups[b], LATE), (ups[b], EARLY)
        first = tick_step(0, [late], block, turned, gain, name=UNITS[2 * b])
        second = tick_step(
            0, [late, early], block, turned, gain, after=[first[0]], name=UNITS[2 * b + 1]
        )
        blocks.append(block)
        kept += [[first], [second]]
        after = [second[0]]

    for tick in range(1, layers):
        hop = [(layers - tick, layers - 1 - tick)]
        grads = [(lax.ppermute(unit[-1][0], "section", hop), whole) for unit in kept]
        last = tick == layers - 1
        after, done = [kept[3][-1][0]], []
        if tick == layers - 2:
            own_weight, own_gain = pl.pallas_call(
                functools.partial(own_kernel, scale),
                out_shape=(
                    jax.ShapeDtypeStruct((shares, kv_width), jnp.float32),
                    jax.ShapeDtypeStruct((shares, 128), jnp.float32),
                ),
                in_specs=[VMEM, VMEM, ANY],
                out_specs=(VMEM, VMEM),
                name="own",
                **params(0.0),
            )(near(weight), near(gain), *after)
            columns[6] = swap(columns_for(6, blocks, after + [own_gain, columns[2]]), 6)
        for u in range(4):
            if last and u == 0:
                after = after + [columns[6]]
            needs = grads[u - 1 : u + 1] if u % 2 else grads[u : u + 1]
            late = []
            if last and u == 1:
                late = [done[0][1], done[0][0]]
            if last and u == 3:
                late = [done[2][1], done[2][0], done[0][0], done[1][0], done[1][1]]
                first_rows, far_first = swap(done[1][2], 2), swap(done[1][1], 6)
                columns[4] = swap(columns_for(4, blocks, [], [done[1][1]]), 4)
            done.append(
                tick_step(
                    tick, needs, blocks[u // 2], turned, gain, kept[u] if last else (), late,
                    after, name=UNITS[u],
                )
            )
            after = [done[u][0]]
            kept[u].append(done[u])
            if tick == layers - 3 and u == 1:
                columns = {2: swap(columns_for(2, blocks, after), 2)}
    own_value, own_values, *rows = done[3]
    rows = [rows[0]] + [swap(rows[k], k) for k in range(1, half)]
    far_value, across_value = swap(own_value, 6), swap(own_value, 4)
    columns[0], handed = columns_for(0, blocks, [own_value, columns[4], far_first, far_value], [first_rows])
    handed = swap(handed, 1)
    values = [own_values, first_rows, rows[2], across_value, far_first, far_value]
    other = partial_sums(shares, piece, True, columns, values)
    own = partial_sums(shares, piece, False, columns, values, [other])
    other = swap(other, 1)
    input_grad, token = pl.pallas_call(
        functools.partial(rows_kernel, half),
        out_shape=(
            jax.ShapeDtypeStruct((tokens, model_width), bf16),
            jax.ShapeDtypeStruct((8, 128), jnp.float32),
        ),
        in_specs=[VMEM] * (2 + half),
        out_specs=(VMEM, VMEM),
        name="rows",
        **params(2.5),
    )(first_rows, handed, *rows)
    weight_grad, gain_grad = pl.pallas_call(
        finish_kernel,
        out_shape=(
            jax.ShapeDtypeStruct((shares, kv_width), jnp.float32),
            jax.ShapeDtypeStruct((1, shares), jnp.float32),
        ),
        in_specs=[VMEM] * 4 + [ANY],
        out_specs=(VMEM, VMEM),
        name="finish",
        **params(0.0),
    )(own, other, own_weight, own_gain, token)
    return input_grad[None], weight_grad[None], gain_grad


def weight_kernel(scale, columns_ref, value_ref, weight_ref, gain_ref, out_ref, gain_out_ref):
    total = lax.dot_general(
        columns_ref[...], value_ref[...], (((0,), (0,)), ((), ())),
        preferred_element_type=jnp.float32,
    ) * scale
    out_ref[...] = total * gain_ref[...]
    product = total * weight_ref[...].astype(jnp.float32)
    sums = lax.dot_general(
        jnp.ones((8, product.shape[1]), jnp.float32), product, (((1,), (1,)), ((), ())),
        preferred_element_type=jnp.float32, precision=lax.Precision.HIGHEST,
    )
    gain_out_ref[...] = sums[:1]


def grouped(hidden, query, key, segments, weight, norm_gain, upstream):
    tokens, model_width = hidden.shape
    kv_width = key.shape[1]
    replicas = lax.axis_size("dp")
    layers = lax.axis_size("section")
    half = replicas // 2
    me = lax.axis_index("dp")
    section = lax.axis_index("section")
    side = me // half
    groups = [list(range(half)), list(range(half, replicas))]
    across = [(i, (i + half) % replicas) for i in range(replicas)]
    shares = model_width // replicas

    def rows_of(array, which, axis=0):
        at = side if which == 0 else 1 - side
        return lax.dynamic_slice_in_dim(array, at * BLOCK, BLOCK, axis)

    def regroup(array):
        return lax.all_to_all(
            array, "dp", split_axis=0, concat_axis=0, axis_index_groups=groups, tiled=True
        )

    def spread(array):
        return lax.all_to_all(array, "dp", split_axis=0, concat_axis=0, tiled=True)

    turned = turn(weight)
    blocks, grads = [], []
    for which in range(2):
        up = rows_of(upstream, which)
        seg = jnp.broadcast_to(segments, (16, 2 * BLOCK)).astype(jnp.bfloat16)
        if which == 1:
            up = lax.ppermute(up, "dp", across)
            seg = lax.ppermute(seg, "dp", across)
        packed = jnp.concatenate(
            [rows_of(query, which), rows_of(key, which), rows_of(hidden, which)], axis=1
        )
        blocks.append(block_probs([regroup(packed)], seg, 0, model_width, kv_width))
        grads.append(up)

    def layer(tick, which, grad, kept):
        live = (section == layers - 1 - tick).astype(jnp.int32)[None]
        return layer_step(live, grad, blocks[which], turned, norm_gain, kept)

    held = [layer(0, which, grads[which], ()) for which in range(2)]
    hops = [(i, i - 1) for i in range(1, layers)]

    def step(tick, held):
        grads = [lax.ppermute(kept[0], "section", hops) for kept in held]
        return [layer(tick, which, grads[which], held[which]) for which in range(2)]

    held = lax.fori_loop(1, layers, step, held)

    columns, values, stored = [], [], []
    for which in range(2):
        block = blocks[which][3].reshape(BLOCK, replicas, shares).transpose(1, 0, 2)
        columns.append(spread(block.reshape(replicas * BLOCK, shares)))
        out, value = held[which]
        stored.append(regroup(out))
        values.append(spread(jnp.tile(value, (replicas, 1))))
    ordered = jnp.where(
        side == 0, jnp.concatenate(stored, axis=0), jnp.concatenate(stored[::-1], axis=0)
    )
    own_weight = lax.dynamic_slice_in_dim(weight, me * shares, shares, 0)
    own_gain = lax.dynamic_slice_in_dim(norm_gain[0], me * shares, shares, 0)
    scale = float(tokens * replicas) ** (-0.5)
    weight_grad, gain_grad = pl.pallas_call(
        functools.partial(weight_kernel, scale),
        out_shape=(
            jax.ShapeDtypeStruct((shares, kv_width), jnp.float32),
            jax.ShapeDtypeStruct((1, shares), jnp.float32),
        ),
        in_specs=[VMEM] * 4,
        out_specs=(VMEM, VMEM),
        name="weight_grad",
    )(
        jnp.concatenate(columns, axis=0),
        jnp.concatenate(values, axis=0),
        own_weight,
        own_gain[:, None],
    )
    return ordered[None], weight_grad[None], gain_grad


def on_device(hidden_in, queries, keys, segments, value_weight, norm_gain, upstream):
    replicas = lax.axis_size("dp")
    piece = hidden_in.shape[1] // replicas
    plan = direct if piece % 16 == 0 and replicas == 8 else grouped
    return plan(
        hidden_in[0], queries[0], keys[0], segments, value_weight[0], norm_gain, upstream
    )


def solution(mesh):
    in_specs = (
        P("section", "dp", None),
        P("section", "dp", None),
        P("section", "dp", None),
        P("dp", None),
        P("section", None, None),
        P("section", None),
        P("dp", None),
    )
    out_specs = (P("section", "dp", None), P("section", "dp", None), P("section", "dp"))
    return jax.shard_map(
        on_device, mesh=mesh, in_specs=in_specs, out_specs=out_specs, check_vma=False
    )
```

```python
import functools

import jax
import jax.numpy as jnp
from jax import lax
from jax.experimental import pallas as pl
from jax.experimental.pallas import tpu as pltpu
from jax.sharding import PartitionSpec as P

HEAD_FEATURES = 128
BLOCK = 64
UNIT = 32
EPSILON = 1e-06
MASKED = -1e30
OUTS = {2: 3, 5: 6}
UNITS = ("a_late", "a_early", "b_late", "b_early")
VMEM = pl.BlockSpec(memory_space=pltpu.VMEM)
SMEM = pl.BlockSpec(memory_space=pltpu.SMEM)


ANY = pl.BlockSpec(memory_space=pl.ANY)


LATE, EARLY = slice(UNIT, BLOCK), slice(0, UNIT)


def params(microseconds):
    flops = int(microseconds * 1.15e9)
    return dict(
        compiler_params=pltpu.CompilerParams(vmem_limit_bytes=16 << 20),
        cost_estimate=pl.CostEstimate(flops=flops, bytes_accessed=0, transcendentals=0),
    )


def near(array):
    return pltpu.with_memory_space_constraint(array, pltpu.VMEM)


def place():
    half = lax.axis_size("dp") // 2
    me = lax.axis_index("dp")
    return lax.div(me, half), lax.rem(me, half), me


def probs_kernel(count, seg_row, model_width, kv_width, *refs):
    pieces, seg_ref = refs[:count], refs[count]
    late_ref, early_ref, inv_ref, x_ref, rows_ref = refs[-5:]
    heads = model_width // kv_width
    rows = BLOCK // count
    side, at, _ = place()
    for k, piece in enumerate(pieces):
        if count == 1:
            rows_ref[...] = piece[...]
        else:
            first = pl.multiple_of(lax.bitwise_xor(at, k) * rows, rows)
            rows_ref[pl.ds(first, rows), :] = piece[...]

    def iota(shape, axis):
        return lax.broadcasted_iota(jnp.int32, shape, axis)

    seg = seg_ref[seg_row : seg_row + 16, : 2 * BLOCK].astype(jnp.float32)[:1]
    shape = (BLOCK, 2 * BLOCK)
    wanted = iota(shape, 1) == side * BLOCK + iota(shape, 0)
    ids = jnp.sum(jnp.where(wanted, seg, 0.0), axis=1, keepdims=True)
    key_code = ids * BLOCK + iota((BLOCK, 1), 0).astype(jnp.float32)
    list_start = ids * BLOCK
    shape = (BLOCK, heads * BLOCK)
    column = iota(shape, 1)
    query_at = lax.rem(column, UNIT) + jnp.where(column < heads * UNIT, UNIT, 0)
    same = iota(shape, 0) == query_at
    query_code = jnp.sum(jnp.where(same, key_code, 0.0), axis=0, keepdims=True)
    query_start = jnp.sum(jnp.where(same, list_start, 0.0), axis=0, keepdims=True)
    allowed = (key_code <= query_code) & (key_code >= query_start)
    for c in range(kv_width // HEAD_FEATURES):
        first = c * heads * HEAD_FEATURES
        query_stack = jnp.concatenate(
            [
                rows_ref[part, first + h * HEAD_FEATURES : first + (h + 1) * HEAD_FEATURES]
                for part in (LATE, EARLY)
                for h in range(heads)
            ],
            axis=0,
        )
        key_first = model_width + c * HEAD_FEATURES
        keys = rows_ref[:, key_first : key_first + HEAD_FEATURES]
        scores = lax.dot_general(
            keys, query_stack, (((1,), (1,)), ((), ())), preferred_element_type=jnp.float32
        ) * HEAD_FEATURES ** (-0.5)
        scores = jnp.where(allowed, scores, MASKED)
        exp_scores = jnp.exp(scores - jnp.max(scores, axis=0, keepdims=True))
        total = jnp.sum(exp_scores, axis=0, keepdims=True)
        probs = (exp_scores / total).astype(jnp.bfloat16)
        late_ref[c] = probs[LATE, : heads * UNIT]
        early_ref[c] = probs[EARLY]
    hidden = rows_ref[:, model_width + kv_width :]
    x_ref[...] = hidden
    x = hidden.astype(jnp.float32)
    mean_square = jnp.mean(x * x, axis=1, keepdims=True)
    inv_ref[...] = jnp.broadcast_to(lax.rsqrt(mean_square + EPSILON), inv_ref.shape)


def block_probs(pieces, seg, seg_row, model_width, kv_width, after=()):
    heads = model_width // kv_width
    key_heads = kv_width // HEAD_FEATURES
    operands = [near(piece) for piece in pieces] + [near(seg)]
    specs = [VMEM] * len(operands) + [ANY] * len(after)
    operands += after
    return pl.pallas_call(
        functools.partial(probs_kernel, len(pieces), seg_row, model_width, kv_width),
        out_shape=(
            jax.ShapeDtypeStruct((key_heads, UNIT, heads * UNIT), jnp.bfloat16),
            jax.ShapeDtypeStruct((key_heads, UNIT, heads * BLOCK), jnp.bfloat16),
            jax.ShapeDtypeStruct((BLOCK, 128), jnp.float32),
            jax.ShapeDtypeStruct((BLOCK, model_width), jnp.bfloat16),
        ),
        in_specs=specs,
        out_specs=(VMEM,) * 4,
        scratch_shapes=[pltpu.VMEM((BLOCK, 2 * model_width + kv_width), jnp.bfloat16)],
        name="probs",
        **params(0.35 if after else 2.0),
    )(*operands)


def unit_math(rows, grads, probs_ref, x_ref, inv_ref, turned_ref, gain_ref, scaled_ref, store, value_ref):
    kv_width, model_width = turned_ref.shape
    heads = model_width // kv_width
    chunk = min(512, model_width)
    inv = inv_ref[rows, :1]
    values = []
    for c in range(kv_width // HEAD_FEATURES):
        first = c * heads * HEAD_FEATURES
        grad_stack = jnp.concatenate(
            [
                grad_ref[part, first + h * HEAD_FEATURES : first + (h + 1) * HEAD_FEATURES]
                for grad_ref, part in grads
                for h in range(heads)
            ],
            axis=0,
        )
        values.append(
            jnp.dot(probs_ref[c], grad_stack, preferred_element_type=jnp.float32).astype(
                jnp.bfloat16
            )
        )
    value = jnp.concatenate(values, axis=1)
    value_ref[...] = (value.astype(jnp.float32) * inv).astype(jnp.bfloat16)
    inner = jnp.zeros((UNIT, 1), jnp.float32)
    for first in range(0, model_width, chunk):
        columns = slice(first, first + chunk)
        normed_grad = jnp.dot(value, turned_ref[:, columns], preferred_element_type=jnp.float32)
        scaled = normed_grad * gain_ref[:, columns]
        scaled_ref[:, columns] = scaled
        x = x_ref[rows, columns].astype(jnp.float32)
        inner = inner + jnp.sum(x * scaled, axis=1, keepdims=True)
    pull = inner * (inv * inv / model_width)
    grad_ref, part = grads[-1]
    for first in range(0, model_width, chunk):
        columns = slice(first, first + chunk)
        x = x_ref[rows, columns].astype(jnp.float32)
        change = inv * (scaled_ref[:, columns] - x * pull)
        grad = grad_ref[part, columns].astype(jnp.float32)
        store(columns, (grad + change).astype(jnp.bfloat16))


def turn_kernel(weight_ref, *refs):
    turned_ref = refs[-1]
    step = min(256, weight_ref.shape[0])
    for first in range(0, weight_ref.shape[0], step):
        turned_ref[:, first : first + step] = weight_ref[first : first + step, :].T


def turn(weight, after=()):
    return pl.pallas_call(
        turn_kernel,
        out_shape=jax.ShapeDtypeStruct(weight.shape[::-1], weight.dtype),
        in_specs=[VMEM] + [ANY] * len(after),
        out_specs=VMEM,
        name="turn",
        **params(1.5),
    )(near(weight), *after)


def layer_kernel(
    live_ref, grad_ref, late_ref, early_ref, inv_ref, x_ref, turned_ref, gain_ref, *rest
):
    out_ref, value_ref, scaled_ref = rest[-3:]
    if len(rest) == 5:

        @pl.when(live_ref[0] == 0)
        def _():
            out_ref[...] = rest[0][...]
            value_ref[...] = rest[1][...]

    @pl.when(live_ref[0] == 1)
    def _():
        for rows, parts, probs_ref in ((LATE, [LATE], late_ref), (EARLY, [LATE, EARLY], early_ref)):

            def store(columns, part, rows=rows):
                out_ref[rows, columns] = part

            grads = [(grad_ref, part) for part in parts]
            unit_math(
                rows, grads, probs_ref, x_ref, inv_ref, turned_ref, gain_ref, scaled_ref, store,
                value_ref.at[rows],
            )


def layer_step(live, grad, block, turned, gain, held=()):
    kv_width, model_width = turned.shape
    operands = [live, grad, *block, turned, gain, *held]
    return pl.pallas_call(
        layer_kernel,
        out_shape=(
            jax.ShapeDtypeStruct((BLOCK, model_width), jnp.bfloat16),
            jax.ShapeDtypeStruct((BLOCK, kv_width), jnp.bfloat16),
        ),
        in_specs=[SMEM] + [VMEM] * (len(operands) - 1),
        out_specs=(VMEM, VMEM),
        scratch_shapes=[pltpu.VMEM((UNIT, model_width), jnp.float32)],
        name="layer",
        **params(1.1),
    )(*operands)


def tick_kernel(tick, rows, parts, kept, late, *refs):
    grads = list(zip(refs, parts))
    probs_ref, inv_ref, x_ref, turned_ref, gain_ref = refs[len(parts) : len(parts) + 5]
    refs = refs[len(parts) + 5 :]
    earlier, refs = refs[: 2 * kept], refs[2 * kept :]
    late_refs = refs[:late]
    kv_width, model_width = turned_ref.shape
    turn = lax.axis_size("section") - 1 - lax.axis_index("section")
    if late:
        outs, (scaled_ref, blocks_ref, value_ref) = refs[late : -3], refs[-3:]
        outs = outs[len(outs) - OUTS[late] :]
    else:
        outs, scaled_ref = refs[-3:-1], refs[-1]
        value_ref = outs[1]
    first_row = BLOCK if late > 2 else 0

    def store(columns, part):
        if late:
            blocks_ref[first_row : first_row + UNIT, columns] = part
        if late <= 2:
            outs[0][:, columns] = part

    @pl.when(turn == tick)
    def _():
        unit_math(
            rows, grads, probs_ref, x_ref, inv_ref, turned_ref, gain_ref, scaled_ref, store,
            value_ref,
        )

    for at in range(kept):

        @pl.when(turn == at)
        def _(at=at):
            store(slice(None), earlier[2 * at][...])
            value_ref[...] = earlier[2 * at + 1][...]

    if not late:
        return
    values = jnp.concatenate([value_ref[...], late_refs[0][...]], axis=0)
    blocks_ref[first_row + UNIT : first_row + BLOCK, :] = late_refs[1][...]
    outs[1 if late == 2 else 0][...] = values
    if late > 2:
        late_a_ref, early_a_ref, value_a_ref = late_refs[2:]
        outs[1][:BLOCK, :] = value_a_ref[...]
        outs[1][BLOCK:, :] = values
        blocks_ref[EARLY, :] = early_a_ref[...]
        blocks_ref[LATE, :] = late_a_ref[...]
    at = place()[1]
    pieces = {2: outs[2]} if late == 2 else dict(enumerate(outs[2:]))
    piece = BLOCK * kv_width // model_width

    def rows_for(k, block):
        first = pl.multiple_of(lax.bitwise_xor(at, k) * piece, piece)
        return blocks_ref[pl.ds(block * BLOCK + first, piece), :]

    block = 0 if late == 2 else 1
    for k, out_ref in pieces.items():
        if k == 2:
            out_ref[:piece, :] = rows_for(2, block)
            for g in range(model_width // kv_width):
                out_ref[piece : 2 * piece, g * kv_width : (g + 1) * kv_width] = values[
                    g * piece : (g + 1) * piece
                ]
            if block == 0:
                out_ref[2 * piece :, :] = rows_for(3, 0)
        elif k == 3:
            out_ref[...] = rows_for(3, 1)
        else:
            out_ref[:piece, :] = rows_for(k, 0)
            out_ref[piece:, :] = rows_for(k, 1)


def tick_step(tick, grads, block, turned, gain, kept=(), late=(), after=(), name=""):
    kv_width, model_width = turned.shape
    low = len(grads) == 2
    arrays = [grad for grad, _ in grads]
    arrays += [block[1] if low else block[0], block[2], block[3], turned, gain]
    arrays += [array for pair in kept for array in pair]
    arrays += late
    operands = [near(array) for array in arrays]
    specs = [VMEM] * len(operands) + [ANY] * len(after)
    bf16 = jnp.bfloat16
    scratch = [pltpu.VMEM((UNIT, model_width), jnp.float32)]
    rows, value = (UNIT, model_width), (UNIT, kv_width)
    shapes = [rows, value]
    if late:
        half = lax.axis_size("dp") // 2
        scratch += [pltpu.VMEM((2 * BLOCK, model_width), bf16), pltpu.VMEM(value, bf16)]
        piece = BLOCK // half
        shapes = [rows, (BLOCK, kv_width), (3 * piece, model_width)]
    if len(late) > 2:
        shapes = [(BLOCK, kv_width), (2 * BLOCK, kv_width)]
        shapes += [(2 * piece, model_width)] * 3 + [(piece, model_width)]
    parts = [part for _, part in grads]
    return pl.pallas_call(
        functools.partial(
            tick_kernel, tick, EARLY if low else LATE, parts, len(kept), len(late)
        ),
        out_shape=tuple(jax.ShapeDtypeStruct(shape, bf16) for shape in shapes),
        in_specs=specs,
        out_specs=(VMEM,) * len(shapes),
        scratch_shapes=scratch,
        name=f"tick{tick}_{name}",
        **params(1.0 if kept else 0.0),
    )(*operands, *after)


def pack_kernel(block, half, piece, query_ref, key_ref, hidden_ref, up_ref, seg_ref, *rest):
    up_out_ref, seg_in_ref, rows_ref, sems = rest[-4:]
    packed = rest[-4 - half : -4]
    side, at, _ = place()
    there = side if block == 0 else 1 - side
    rows = pl.ds(pl.multiple_of(there * BLOCK, BLOCK), BLOCK)
    copies = []

    def copy(source, target):
        made = pltpu.make_async_copy(source, target, sems.at[len(copies)])
        made.start()
        copies.append(made)

    first = 0
    for source in (query_ref, key_ref, hidden_ref):
        width = source.shape[1]
        copy(source.at[rows], rows_ref.at[:, pl.ds(first, width)])
        first += width
    copy(seg_ref, seg_in_ref)
    copy(up_ref.at[rows], up_out_ref.at[pl.ds(0, BLOCK)])
    up_out_ref[BLOCK:, :] = jnp.zeros((16, up_out_ref.shape[1]), jnp.bfloat16)
    if block == 1:
        rest[2][...] = rest[1][...]
        turn_kernel(rest[0], rest[3])
    for made in copies[:4]:
        made.wait()
    ids = seg_in_ref[...].astype(jnp.float32)
    up_out_ref[BLOCK:, : ids.shape[1]] = jnp.broadcast_to(ids, (16, ids.shape[1])).astype(
        jnp.bfloat16
    )
    for k in range(half):
        first = pl.multiple_of(lax.bitwise_xor(at, k) * piece, piece)
        packed[k][...] = rows_ref[pl.ds(first, piece), :]
    copies[4].wait()


def pack(block, half, piece, sources, weight=None, gain=None):
    model_width = sources[0].shape[1]
    width = sum(source.shape[1] for source in sources[:3])
    bf16 = jnp.bfloat16
    operands = [pltpu.with_memory_space_constraint(array, pltpu.HBM) for array in sources]
    specs = [pl.BlockSpec(memory_space=pltpu.HBM)] * len(sources)
    outs = [jax.ShapeDtypeStruct((piece, width), bf16)] * half
    outs.append(jax.ShapeDtypeStruct((BLOCK + 16, model_width), bf16))
    if weight is not None:
        operands += [near(weight), gain]
        specs += [VMEM, VMEM]
        outs = [
            jax.ShapeDtypeStruct(gain.shape, gain.dtype),
            jax.ShapeDtypeStruct(weight.shape[::-1], bf16),
        ] + outs
    return pl.pallas_call(
        functools.partial(pack_kernel, block, half, piece),
        out_shape=tuple(outs),
        in_specs=specs,
        out_specs=(VMEM,) * len(outs),
        scratch_shapes=[
            pltpu.VMEM(sources[-1].shape, jnp.int32),
            pltpu.VMEM((BLOCK, width), bf16),
            pltpu.SemaphoreType.DMA((5,)),
        ],
        name="pack",
        **params(1.2),
    )(*operands)


def columns_kernel(width, distance, first_ref, second_ref, *refs):
    out_ref = refs[-1]
    if distance == 0:
        came_ref, out_ref, handed_ref = refs[0], refs[-2], refs[-1]
        handed_ref[...] = came_ref[came_ref.shape[0] - handed_ref.shape[0] :, :]
    there = lax.div(lax.bitwise_xor(place()[2], distance), 2)
    out_ref[:BLOCK, :] = first_ref[:, columns_of(there, width)]
    out_ref[BLOCK : 2 * BLOCK, :] = second_ref[:, columns_of(there, width)]


def columns_for(distance, blocks, after, came=()):
    model_width = blocks[0][3].shape[1]
    width = 2 * model_width // lax.axis_size("dp")
    shapes = [(2 * BLOCK, width)]
    if distance == 0:
        shapes.append((came[0].shape[0] // 3, model_width))
    outs = [jax.ShapeDtypeStruct(shape, jnp.bfloat16) for shape in shapes]
    results = pl.pallas_call(
        functools.partial(columns_kernel, width, distance),
        out_shape=tuple(outs),
        in_specs=[VMEM] * (2 + len(came)) + [ANY] * len(after),
        out_specs=(VMEM,) * len(outs),
        name=f"columns{distance}",
        **params(0.0 if distance else 0.8),
    )(blocks[0][3], blocks[1][3], *came, *after)
    return results if distance == 0 else results[0]


def own_kernel(scale, weight_ref, gain_ref, after_ref, weight_out_ref, gain_out_ref):
    shares = weight_out_ref.shape[0]
    first = pl.multiple_of(place()[2] * shares, shares)
    weight_out_ref[...] = weight_ref[pl.ds(first, shares), :].astype(jnp.float32) * scale
    gain = gain_ref[:, pl.ds(first, shares)]
    column = jnp.sum(jnp.where(diagonal(shares), gain, 0.0), axis=1, keepdims=True)
    gain_out_ref[...] = jnp.broadcast_to(column * scale, gain_out_ref.shape)


def columns_of(pair, width):
    return pl.ds(pl.multiple_of(pair * width, width), width)


def partial_kernel(shares, first, for_other, *refs):
    columns, values, out_ref = refs[:4], refs[4:10], refs[-1]
    kv_width = out_ref.shape[1]
    parts = []
    for ref in values:
        beside = ref.shape[1] > kv_width
        rows = slice(first, 2 * first) if beside else slice(0, ref.shape[0])
        parts += [ref[rows, at : at + kv_width] for at in range(0, ref.shape[1], kv_width)]
    value = jnp.concatenate(parts, axis=0)
    mine = lax.rem(place()[2], 2)
    core = 1 - mine if for_other else mine
    at = pl.ds(pl.multiple_of(core * shares, shares), shares)
    rows = jnp.concatenate([ref[: 2 * BLOCK, at] for ref in columns], axis=0)
    out_ref[...] = lax.dot_general(
        rows, value, (((0,), (0,)), ((), ())), preferred_element_type=jnp.float32
    ).astype(out_ref.dtype)


def partial_sums(shares, piece, for_other, columns, values, after=()):
    kv_width = values[0].shape[1]
    return pl.pallas_call(
        functools.partial(partial_kernel, shares, piece, for_other),
        out_shape=jax.ShapeDtypeStruct(
            (shares, kv_width), jnp.bfloat16 if for_other else jnp.float32
        ),
        in_specs=[VMEM] * 10 + [ANY] * len(after),
        out_specs=VMEM,
        name="partial_other" if for_other else "partial_own",
        **params(0.0 if for_other else 0.5),
    )(*[columns[k] for k in (0, 2, 4, 6)], *values, *after)


def diagonal(size):
    return lax.broadcasted_iota(jnp.int32, (size, size), 0) == lax.broadcasted_iota(
        jnp.int32, (size, size), 1
    )


def rows_kernel(half, first_rows_ref, handed_ref, *refs):
    pieces = refs[:half]
    rows_ref, token_ref = refs[half:]
    side, at, _ = place()
    piece = BLOCK // half
    for block in range(2):
        for k in range(half):
            replica = (side if block == 0 else 1 - side) * half + lax.bitwise_xor(at, k)
            rows = pl.ds(pl.multiple_of(replica * piece, piece), piece)
            source, first = pieces[k], block * piece
            if k == 2:
                source, first = (pieces[k] if block else first_rows_ref), 0
            if k == 3:
                source, first = (pieces[k] if block else handed_ref), 0
            rows_ref[rows, :] = source[first : first + piece, :]
    token_ref[...] = jnp.zeros_like(token_ref)


def finish_kernel(
    own_ref, other_ref, weight_ref, gain_ref, after_ref, out_ref, gain_out_ref
):
    total = own_ref[...] + other_ref[...].astype(jnp.float32)
    out_ref[...] = total * gain_ref[:, :1]
    sums = jnp.sum(total * weight_ref[...], axis=1, keepdims=True)
    gain_out_ref[...] = jnp.sum(
        jnp.where(diagonal(total.shape[0]), sums, 0.0), axis=0, keepdims=True
    )


def direct(hidden, query, key, segments, weight, norm_gain, upstream):
    tokens, model_width = hidden.shape
    kv_width = key.shape[1]
    replicas = lax.axis_size("dp")
    layers = lax.axis_size("section")
    half = replicas // 2
    piece = tokens // replicas
    shares = model_width // replicas

    def swap(array, k):
        return lax.ppermute(array, "dp", [(i, i ^ k) for i in range(replicas)])

    count = 2 * half
    bf16 = jnp.bfloat16
    sources = (query, key, hidden, upstream, segments)
    pieces, ups = [], []
    for b in range(2):
        extra = (weight, norm_gain) if b else ()
        *packed, up = pack(b, half, piece, sources, *extra)
        if b:
            gain, turned, *packed = packed
        pieces.append([packed[0]] + [swap(packed[k], k) for k in range(1, half)])
        ups.append(swap(up, half) if b else up)
    whole = slice(0, UNIT)
    scale = float(tokens * replicas) ** (-0.5)
    blocks, kept, after = [], [], []
    for b in range(2):
        block = block_probs(pieces[b], ups[b], BLOCK, model_width, kv_width, after)
        late, early = (ups[b], LATE), (ups[b], EARLY)
        first = tick_step(0, [late], block, turned, gain, name=UNITS[2 * b])
        second = tick_step(
            0, [late, early], block, turned, gain, after=[first[0]], name=UNITS[2 * b + 1]
        )
        blocks.append(block)
        kept += [[first], [second]]
        after = [second[0]]

    for tick in range(1, layers):
        hop = [(layers - tick, layers - 1 - tick)]
        grads = [(lax.ppermute(unit[-1][0], "section", hop), whole) for unit in kept]
        last = tick == layers - 1
        after, done = [kept[3][-1][0]], []
        if tick == layers - 2:
            own_weight, own_gain = pl.pallas_call(
                functools.partial(own_kernel, scale),
                out_shape=(
                    jax.ShapeDtypeStruct((shares, kv_width), jnp.float32),
                    jax.ShapeDtypeStruct((shares, 128), jnp.float32),
                ),
                in_specs=[VMEM, VMEM, ANY],
                out_specs=(VMEM, VMEM),
                name="own",
                **params(0.0),
            )(near(weight), near(gain), *after)
            columns = {6: swap(columns_for(6, blocks, after + [own_gain]), 6)}
        if last:
            columns[2] = swap(columns_for(2, blocks, after + [columns[6]]), 2)
        for u in range(4):
            needs = grads[u - 1 : u + 1] if u % 2 else grads[u : u + 1]
            late = []
            if last and u == 1:
                late = [done[0][1], done[0][0]]
            if last and u == 3:
                late = [done[2][1], done[2][0], done[0][0], done[1][0], done[1][1]]
                first_rows, far_first = swap(done[1][2], 2), swap(done[1][1], 6)
                columns[4] = swap(columns_for(4, blocks, [done[1][0]]), 4)
                after = after + [columns[2]]
            done.append(
                tick_step(
                    tick, needs, blocks[u // 2], turned, gain, kept[u] if last else (), late,
                    after, name=UNITS[u],
                )
            )
            after = [done[u][0]]
            kept[u].append(done[u])
    own_value, own_values, *rows = done[3]
    rows = [rows[0]] + [swap(rows[k], k) for k in range(1, half)]
    far_value, across_value = swap(own_value, 6), swap(own_values, 4)
    columns[0], handed = columns_for(0, blocks, [own_value, columns[4], far_first, far_value], [first_rows])
    handed = swap(handed, 1)
    values = [own_values, first_rows, rows[2], across_value, far_first, far_value]
    other = partial_sums(shares, piece, True, columns, values)
    own = partial_sums(shares, piece, False, columns, values, [other])
    other = swap(other, 1)
    input_grad, token = pl.pallas_call(
        functools.partial(rows_kernel, half),
        out_shape=(
            jax.ShapeDtypeStruct((tokens, model_width), bf16),
            jax.ShapeDtypeStruct((8, 128), jnp.float32),
        ),
        in_specs=[VMEM] * (2 + half),
        out_specs=(VMEM, VMEM),
        name="rows",
        **params(2.5),
    )(first_rows, handed, *rows)
    weight_grad, gain_grad = pl.pallas_call(
        finish_kernel,
        out_shape=(
            jax.ShapeDtypeStruct((shares, kv_width), jnp.float32),
            jax.ShapeDtypeStruct((1, shares), jnp.float32),
        ),
        in_specs=[VMEM] * 4 + [ANY],
        out_specs=(VMEM, VMEM),
        name="finish",
        **params(0.0),
    )(own, other, own_weight, own_gain, token)
    return input_grad[None], weight_grad[None], gain_grad


def weight_kernel(scale, columns_ref, value_ref, weight_ref, gain_ref, out_ref, gain_out_ref):
    total = lax.dot_general(
        columns_ref[...], value_ref[...], (((0,), (0,)), ((), ())),
        preferred_element_type=jnp.float32,
    ) * scale
    out_ref[...] = total * gain_ref[...]
    product = total * weight_ref[...].astype(jnp.float32)
    sums = lax.dot_general(
        jnp.ones((8, product.shape[1]), jnp.float32), product, (((1,), (1,)), ((), ())),
        preferred_element_type=jnp.float32, precision=lax.Precision.HIGHEST,
    )
    gain_out_ref[...] = sums[:1]


def grouped(hidden, query, key, segments, weight, norm_gain, upstream):
    tokens, model_width = hidden.shape
    kv_width = key.shape[1]
    replicas = lax.axis_size("dp")
    layers = lax.axis_size("section")
    half = replicas // 2
    me = lax.axis_index("dp")
    section = lax.axis_index("section")
    side = me // half
    groups = [list(range(half)), list(range(half, replicas))]
    across = [(i, (i + half) % replicas) for i in range(replicas)]
    shares = model_width // replicas

    def rows_of(array, which, axis=0):
        at = side if which == 0 else 1 - side
        return lax.dynamic_slice_in_dim(array, at * BLOCK, BLOCK, axis)

    def regroup(array):
        return lax.all_to_all(
            array, "dp", split_axis=0, concat_axis=0, axis_index_groups=groups, tiled=True
        )

    def spread(array):
        return lax.all_to_all(array, "dp", split_axis=0, concat_axis=0, tiled=True)

    turned = turn(weight)
    blocks, grads = [], []
    for which in range(2):
        up = rows_of(upstream, which)
        seg = jnp.broadcast_to(segments, (16, 2 * BLOCK)).astype(jnp.bfloat16)
        if which == 1:
            up = lax.ppermute(up, "dp", across)
            seg = lax.ppermute(seg, "dp", across)
        packed = jnp.concatenate(
            [rows_of(query, which), rows_of(key, which), rows_of(hidden, which)], axis=1
        )
        blocks.append(block_probs([regroup(packed)], seg, 0, model_width, kv_width))
        grads.append(up)

    def layer(tick, which, grad, kept):
        live = (section == layers - 1 - tick).astype(jnp.int32)[None]
        return layer_step(live, grad, blocks[which], turned, norm_gain, kept)

    held = [layer(0, which, grads[which], ()) for which in range(2)]
    hops = [(i, i - 1) for i in range(1, layers)]

    def step(tick, held):
        grads = [lax.ppermute(kept[0], "section", hops) for kept in held]
        return [layer(tick, which, grads[which], held[which]) for which in range(2)]

    held = lax.fori_loop(1, layers, step, held)

    columns, values, stored = [], [], []
    for which in range(2):
        block = blocks[which][3].reshape(BLOCK, replicas, shares).transpose(1, 0, 2)
        columns.append(spread(block.reshape(replicas * BLOCK, shares)))
        out, value = held[which]
        stored.append(regroup(out))
        values.append(spread(jnp.tile(value, (replicas, 1))))
    ordered = jnp.where(
        side == 0, jnp.concatenate(stored, axis=0), jnp.concatenate(stored[::-1], axis=0)
    )
    own_weight = lax.dynamic_slice_in_dim(weight, me * shares, shares, 0)
    own_gain = lax.dynamic_slice_in_dim(norm_gain[0], me * shares, shares, 0)
    scale = float(tokens * replicas) ** (-0.5)
    weight_grad, gain_grad = pl.pallas_call(
        functools.partial(weight_kernel, scale),
        out_shape=(
            jax.ShapeDtypeStruct((shares, kv_width), jnp.float32),
            jax.ShapeDtypeStruct((1, shares), jnp.float32),
        ),
        in_specs=[VMEM] * 4,
        out_specs=(VMEM, VMEM),
        name="weight_grad",
    )(
        jnp.concatenate(columns, axis=0),
        jnp.concatenate(values, axis=0),
        own_weight,
        own_gain[:, None],
    )
    return ordered[None], weight_grad[None], gain_grad


def on_device(hidden_in, queries, keys, segments, value_weight, norm_gain, upstream):
    replicas = lax.axis_size("dp")
    piece = hidden_in.shape[1] // replicas
    plan = direct if piece % 16 == 0 and replicas == 8 else grouped
    return plan(
        hidden_in[0], queries[0], keys[0], segments, value_weight[0], norm_gain, upstream
    )


def solution(mesh):
    in_specs = (
        P("section", "dp", None),
        P("section", "dp", None),
        P("section", "dp", None),
        P("dp", None),
        P("section", None, None),
        P("section", None),
        P("dp", None),
    )
    out_specs = (P("section", "dp", None), P("section", "dp", None), P("section", "dp"))
    return jax.shard_map(
        on_device, mesh=mesh, in_specs=in_specs, out_specs=out_specs, check_vma=False
    )
```

```python
import functools

import jax
import jax.numpy as jnp
from jax import lax
from jax.experimental import pallas as pl
from jax.experimental.pallas import tpu as pltpu
from jax.sharding import PartitionSpec as P

HEAD_FEATURES = 128
BLOCK = 64
UNIT = 32
EPSILON = 1e-06
MASKED = -1e30
OUTS = {2: 3, 5: 6}
UNITS = ("a_late", "a_early", "b_late", "b_early")
VMEM = pl.BlockSpec(memory_space=pltpu.VMEM)
SMEM = pl.BlockSpec(memory_space=pltpu.SMEM)


ANY = pl.BlockSpec(memory_space=pl.ANY)


LATE, EARLY = slice(UNIT, BLOCK), slice(0, UNIT)


def params(microseconds):
    flops = int(microseconds * 1.15e9)
    return dict(
        compiler_params=pltpu.CompilerParams(vmem_limit_bytes=16 << 20),
        cost_estimate=pl.CostEstimate(flops=flops, bytes_accessed=0, transcendentals=0),
    )


def near(array):
    return pltpu.with_memory_space_constraint(array, pltpu.VMEM)


def place():
    half = lax.axis_size("dp") // 2
    me = lax.axis_index("dp")
    return lax.div(me, half), lax.rem(me, half), me


def probs_kernel(count, seg_row, model_width, kv_width, *refs):
    pieces, seg_ref = refs[:count], refs[count]
    late_ref, early_ref, inv_ref, x_ref, rows_ref = refs[-5:]
    heads = model_width // kv_width
    rows = BLOCK // count
    side, at, _ = place()
    for k, piece in enumerate(pieces):
        if count == 1:
            rows_ref[...] = piece[...]
        else:
            first = pl.multiple_of(lax.bitwise_xor(at, k) * rows, rows)
            rows_ref[pl.ds(first, rows), :] = piece[...]

    def iota(shape, axis):
        return lax.broadcasted_iota(jnp.int32, shape, axis)

    seg = seg_ref[seg_row : seg_row + 16, : 2 * BLOCK].astype(jnp.float32)[:1]
    shape = (BLOCK, 2 * BLOCK)
    wanted = iota(shape, 1) == side * BLOCK + iota(shape, 0)
    ids = jnp.sum(jnp.where(wanted, seg, 0.0), axis=1, keepdims=True)
    key_code = ids * BLOCK + iota((BLOCK, 1), 0).astype(jnp.float32)
    list_start = ids * BLOCK
    shape = (BLOCK, heads * BLOCK)
    column = iota(shape, 1)
    query_at = lax.rem(column, UNIT) + jnp.where(column < heads * UNIT, UNIT, 0)
    same = iota(shape, 0) == query_at
    query_code = jnp.sum(jnp.where(same, key_code, 0.0), axis=0, keepdims=True)
    query_start = jnp.sum(jnp.where(same, list_start, 0.0), axis=0, keepdims=True)
    allowed = (key_code <= query_code) & (key_code >= query_start)
    for c in range(kv_width // HEAD_FEATURES):
        first = c * heads * HEAD_FEATURES
        query_stack = jnp.concatenate(
            [
                rows_ref[part, first + h * HEAD_FEATURES : first + (h + 1) * HEAD_FEATURES]
                for part in (LATE, EARLY)
                for h in range(heads)
            ],
            axis=0,
        )
        key_first = model_width + c * HEAD_FEATURES
        keys = rows_ref[:, key_first : key_first + HEAD_FEATURES]
        scores = lax.dot_general(
            keys, query_stack, (((1,), (1,)), ((), ())), preferred_element_type=jnp.float32
        ) * HEAD_FEATURES ** (-0.5)
        scores = jnp.where(allowed, scores, MASKED)
        exp_scores = jnp.exp(scores - jnp.max(scores, axis=0, keepdims=True))
        total = jnp.sum(exp_scores, axis=0, keepdims=True)
        probs = (exp_scores / total).astype(jnp.bfloat16)
        late_ref[c] = probs[LATE, : heads * UNIT]
        early_ref[c] = probs[EARLY]
    hidden = rows_ref[:, model_width + kv_width :]
    x_ref[...] = hidden
    x = hidden.astype(jnp.float32)
    mean_square = jnp.mean(x * x, axis=1, keepdims=True)
    inv_ref[...] = jnp.broadcast_to(lax.rsqrt(mean_square + EPSILON), inv_ref.shape)


def block_probs(pieces, seg, seg_row, model_width, kv_width, after=()):
    heads = model_width // kv_width
    key_heads = kv_width // HEAD_FEATURES
    operands = [near(piece) for piece in pieces] + [near(seg)]
    specs = [VMEM] * len(operands) + [ANY] * len(after)
    operands += after
    return pl.pallas_call(
        functools.partial(probs_kernel, len(pieces), seg_row, model_width, kv_width),
        out_shape=(
            jax.ShapeDtypeStruct((key_heads, UNIT, heads * UNIT), jnp.bfloat16),
            jax.ShapeDtypeStruct((key_heads, UNIT, heads * BLOCK), jnp.bfloat16),
            jax.ShapeDtypeStruct((BLOCK, 128), jnp.float32),
            jax.ShapeDtypeStruct((BLOCK, model_width), jnp.bfloat16),
        ),
        in_specs=specs,
        out_specs=(VMEM,) * 4,
        scratch_shapes=[pltpu.VMEM((BLOCK, 2 * model_width + kv_width), jnp.bfloat16)],
        name="probs",
        **params(0.35 if after else 2.0),
    )(*operands)


def unit_math(rows, grads, probs_ref, x_ref, inv_ref, turned_ref, gain_ref, scaled_ref, store, value_ref):
    kv_width, model_width = turned_ref.shape
    heads = model_width // kv_width
    chunk = min(512, model_width)
    inv = inv_ref[rows, :1]
    values = []
    for c in range(kv_width // HEAD_FEATURES):
        first = c * heads * HEAD_FEATURES
        grad_stack = jnp.concatenate(
            [
                grad_ref[part, first + h * HEAD_FEATURES : first + (h + 1) * HEAD_FEATURES]
                for grad_ref, part in grads
                for h in range(heads)
            ],
            axis=0,
        )
        values.append(
            jnp.dot(probs_ref[c], grad_stack, preferred_element_type=jnp.float32).astype(
                jnp.bfloat16
            )
        )
    value = jnp.concatenate(values, axis=1)
    value_ref[...] = (value.astype(jnp.float32) * inv).astype(jnp.bfloat16)
    inner = jnp.zeros((UNIT, 1), jnp.float32)
    for first in range(0, model_width, chunk):
        columns = slice(first, first + chunk)
        normed_grad = jnp.dot(value, turned_ref[:, columns], preferred_element_type=jnp.float32)
        scaled = normed_grad * gain_ref[:, columns]
        scaled_ref[:, columns] = scaled
        x = x_ref[rows, columns].astype(jnp.float32)
        inner = inner + jnp.sum(x * scaled, axis=1, keepdims=True)
    pull = inner * (inv * inv / model_width)
    grad_ref, part = grads[-1]
    for first in range(0, model_width, chunk):
        columns = slice(first, first + chunk)
        x = x_ref[rows, columns].astype(jnp.float32)
        change = inv * (scaled_ref[:, columns] - x * pull)
        grad = grad_ref[part, columns].astype(jnp.float32)
        store(columns, (grad + change).astype(jnp.bfloat16))


def turn_kernel(weight_ref, *refs):
    turned_ref = refs[-1]
    step = min(256, weight_ref.shape[0])
    for first in range(0, weight_ref.shape[0], step):
        turned_ref[:, first : first + step] = weight_ref[first : first + step, :].T


def turn(weight, after=()):
    return pl.pallas_call(
        turn_kernel,
        out_shape=jax.ShapeDtypeStruct(weight.shape[::-1], weight.dtype),
        in_specs=[VMEM] + [ANY] * len(after),
        out_specs=VMEM,
        name="turn",
        **params(1.5),
    )(near(weight), *after)


def layer_kernel(
    live_ref, grad_ref, late_ref, early_ref, inv_ref, x_ref, turned_ref, gain_ref, *rest
):
    out_ref, value_ref, scaled_ref = rest[-3:]
    if len(rest) == 5:

        @pl.when(live_ref[0] == 0)
        def _():
            out_ref[...] = rest[0][...]
            value_ref[...] = rest[1][...]

    @pl.when(live_ref[0] == 1)
    def _():
        for rows, parts, probs_ref in ((LATE, [LATE], late_ref), (EARLY, [LATE, EARLY], early_ref)):

            def store(columns, part, rows=rows):
                out_ref[rows, columns] = part

            grads = [(grad_ref, part) for part in parts]
            unit_math(
                rows, grads, probs_ref, x_ref, inv_ref, turned_ref, gain_ref, scaled_ref, store,
                value_ref.at[rows],
            )


def layer_step(live, grad, block, turned, gain, held=()):
    kv_width, model_width = turned.shape
    operands = [live, grad, *block, turned, gain, *held]
    return pl.pallas_call(
        layer_kernel,
        out_shape=(
            jax.ShapeDtypeStruct((BLOCK, model_width), jnp.bfloat16),
            jax.ShapeDtypeStruct((BLOCK, kv_width), jnp.bfloat16),
        ),
        in_specs=[SMEM] + [VMEM] * (len(operands) - 1),
        out_specs=(VMEM, VMEM),
        scratch_shapes=[pltpu.VMEM((UNIT, model_width), jnp.float32)],
        name="layer",
        **params(1.1),
    )(*operands)


def tick_kernel(tick, rows, parts, kept, late, *refs):
    grads = list(zip(refs, parts))
    probs_ref, inv_ref, x_ref, turned_ref, gain_ref = refs[len(parts) : len(parts) + 5]
    refs = refs[len(parts) + 5 :]
    earlier, refs = refs[: 2 * kept], refs[2 * kept :]
    late_refs = refs[:late]
    kv_width, model_width = turned_ref.shape
    turn = lax.axis_size("section") - 1 - lax.axis_index("section")
    if late:
        outs, (scaled_ref, blocks_ref, value_ref) = refs[late : -3], refs[-3:]
        outs = outs[len(outs) - OUTS[late] :]
    else:
        outs, scaled_ref = refs[-3:-1], refs[-1]
        value_ref = outs[1]
    first_row = BLOCK if late > 2 else 0

    def store(columns, part):
        if late:
            blocks_ref[first_row : first_row + UNIT, columns] = part
        if late <= 2:
            outs[0][:, columns] = part

    @pl.when(turn == tick)
    def _():
        unit_math(
            rows, grads, probs_ref, x_ref, inv_ref, turned_ref, gain_ref, scaled_ref, store,
            value_ref,
        )

    for at in range(kept):

        @pl.when(turn == at)
        def _(at=at):
            store(slice(None), earlier[2 * at][...])
            value_ref[...] = earlier[2 * at + 1][...]

    if not late:
        return
    values = jnp.concatenate([value_ref[...], late_refs[0][...]], axis=0)
    blocks_ref[first_row + UNIT : first_row + BLOCK, :] = late_refs[1][...]
    outs[1 if late == 2 else 0][...] = values
    if late > 2:
        late_a_ref, early_a_ref, value_a_ref = late_refs[2:]
        outs[1][:BLOCK, :] = value_a_ref[...]
        outs[1][BLOCK:, :] = values
        blocks_ref[EARLY, :] = early_a_ref[...]
        blocks_ref[LATE, :] = late_a_ref[...]
    at = place()[1]
    pieces = {2: outs[2]} if late == 2 else dict(enumerate(outs[2:]))
    piece = BLOCK * kv_width // model_width

    def rows_for(k, block):
        first = pl.multiple_of(lax.bitwise_xor(at, k) * piece, piece)
        return blocks_ref[pl.ds(block * BLOCK + first, piece), :]

    block = 0 if late == 2 else 1
    for k, out_ref in pieces.items():
        if k == 2:
            out_ref[:piece, :] = rows_for(2, block)
            for g in range(model_width // kv_width):
                out_ref[piece : 2 * piece, g * kv_width : (g + 1) * kv_width] = values[
                    g * piece : (g + 1) * piece
                ]
            if block == 0:
                out_ref[2 * piece :, :] = rows_for(3, 0)
        elif k == 3:
            out_ref[...] = rows_for(3, 1)
        else:
            out_ref[:piece, :] = rows_for(k, 0)
            out_ref[piece:, :] = rows_for(k, 1)


def tick_step(tick, grads, block, turned, gain, kept=(), late=(), after=(), name=""):
    kv_width, model_width = turned.shape
    low = len(grads) == 2
    arrays = [grad for grad, _ in grads]
    arrays += [block[1] if low else block[0], block[2], block[3], turned, gain]
    arrays += [array for pair in kept for array in pair]
    arrays += late
    operands = [near(array) for array in arrays]
    specs = [VMEM] * len(operands) + [ANY] * len(after)
    bf16 = jnp.bfloat16
    scratch = [pltpu.VMEM((UNIT, model_width), jnp.float32)]
    rows, value = (UNIT, model_width), (UNIT, kv_width)
    shapes = [rows, value]
    if late:
        half = lax.axis_size("dp") // 2
        scratch += [pltpu.VMEM((2 * BLOCK, model_width), bf16), pltpu.VMEM(value, bf16)]
        piece = BLOCK // half
        shapes = [rows, (BLOCK, kv_width), (3 * piece, model_width)]
    if len(late) > 2:
        shapes = [(BLOCK, kv_width), (2 * BLOCK, kv_width)]
        shapes += [(2 * piece, model_width)] * 3 + [(piece, model_width)]
    parts = [part for _, part in grads]
    return pl.pallas_call(
        functools.partial(
            tick_kernel, tick, EARLY if low else LATE, parts, len(kept), len(late)
        ),
        out_shape=tuple(jax.ShapeDtypeStruct(shape, bf16) for shape in shapes),
        in_specs=specs,
        out_specs=(VMEM,) * len(shapes),
        scratch_shapes=scratch,
        name=f"tick{tick}_{name}",
        **params(1.0 if kept else 0.0),
    )(*operands, *after)


def pack_kernel(block, half, piece, query_ref, key_ref, hidden_ref, up_ref, seg_ref, *rest):
    up_out_ref, seg_in_ref, rows_ref, sems = rest[-4:]
    packed = rest[-4 - half : -4]
    side, at, _ = place()
    there = side if block == 0 else 1 - side
    rows = pl.ds(pl.multiple_of(there * BLOCK, BLOCK), BLOCK)
    copies = []

    def copy(source, target):
        made = pltpu.make_async_copy(source, target, sems.at[len(copies)])
        made.start()
        copies.append(made)

    first = 0
    for source in (query_ref, key_ref, hidden_ref):
        width = source.shape[1]
        copy(source.at[rows], rows_ref.at[:, pl.ds(first, width)])
        first += width
    copy(seg_ref, seg_in_ref)
    copy(up_ref.at[rows], up_out_ref.at[pl.ds(0, BLOCK)])
    up_out_ref[BLOCK:, :] = jnp.zeros((16, up_out_ref.shape[1]), jnp.bfloat16)
    if block == 1:
        copy(rest[1], rest[2])
        turn_kernel(rest[0], rest[3])
    for made in copies[:4]:
        made.wait()
    ids = seg_in_ref[...].astype(jnp.float32)
    up_out_ref[BLOCK:, : ids.shape[1]] = jnp.broadcast_to(ids, (16, ids.shape[1])).astype(
        jnp.bfloat16
    )
    for k in range(half):
        first = pl.multiple_of(lax.bitwise_xor(at, k) * piece, piece)
        packed[k][...] = rows_ref[pl.ds(first, piece), :]
    for made in copies[4:]:
        made.wait()


def pack(block, half, piece, sources, weight=None, gain=None):
    model_width = sources[0].shape[1]
    width = sum(source.shape[1] for source in sources[:3])
    bf16 = jnp.bfloat16
    operands = [pltpu.with_memory_space_constraint(array, pltpu.HBM) for array in sources]
    specs = [pl.BlockSpec(memory_space=pltpu.HBM)] * len(sources)
    outs = [jax.ShapeDtypeStruct((piece, width), bf16)] * half
    outs.append(jax.ShapeDtypeStruct((BLOCK + 16, model_width), bf16))
    if weight is not None:
        operands += [near(weight), pltpu.with_memory_space_constraint(gain, pltpu.HBM)]
        specs += [VMEM, pl.BlockSpec(memory_space=pltpu.HBM)]
        outs = [
            jax.ShapeDtypeStruct(gain.shape, gain.dtype),
            jax.ShapeDtypeStruct(weight.shape[::-1], bf16),
        ] + outs
    return pl.pallas_call(
        functools.partial(pack_kernel, block, half, piece),
        out_shape=tuple(outs),
        in_specs=specs,
        out_specs=(VMEM,) * len(outs),
        scratch_shapes=[
            pltpu.VMEM(sources[-1].shape, jnp.int32),
            pltpu.VMEM((BLOCK, width), bf16),
            pltpu.SemaphoreType.DMA((6,)),
        ],
        name="pack",
        **params(1.2),
    )(*operands)


def columns_kernel(width, distance, first_ref, second_ref, *refs):
    out_ref = refs[-1]
    if distance == 0:
        came_ref, out_ref, handed_ref = refs[0], refs[-2], refs[-1]
        handed_ref[...] = came_ref[came_ref.shape[0] - handed_ref.shape[0] :, :]
    if distance == 4:
        out_ref[2 * BLOCK :, :] = refs[0][...]
    there = lax.div(lax.bitwise_xor(place()[2], distance), 2)
    out_ref[:BLOCK, :] = first_ref[:, columns_of(there, width)]
    out_ref[BLOCK : 2 * BLOCK, :] = second_ref[:, columns_of(there, width)]


def columns_for(distance, blocks, after, came=()):
    model_width = blocks[0][3].shape[1]
    width = 2 * model_width // lax.axis_size("dp")
    shapes = [(2 * BLOCK, width)]
    if distance == 0:
        shapes.append((came[0].shape[0] // 3, model_width))
    if distance == 4:
        shapes = [(3 * BLOCK, width)]
    outs = [jax.ShapeDtypeStruct(shape, jnp.bfloat16) for shape in shapes]
    results = pl.pallas_call(
        functools.partial(columns_kernel, width, distance),
        out_shape=tuple(outs),
        in_specs=[VMEM] * (2 + len(came)) + [ANY] * len(after),
        out_specs=(VMEM,) * len(outs),
        name=f"columns{distance}",
        **params(0.0 if distance else 0.8),
    )(blocks[0][3], blocks[1][3], *came, *after)
    return results if distance == 0 else results[0]


def own_kernel(scale, weight_ref, gain_ref, after_ref, weight_out_ref, gain_out_ref):
    shares = weight_out_ref.shape[0]
    first = pl.multiple_of(place()[2] * shares, shares)
    weight_out_ref[...] = weight_ref[pl.ds(first, shares), :].astype(jnp.float32) * scale
    gain = gain_ref[:, pl.ds(first, shares)]
    column = jnp.sum(jnp.where(diagonal(shares), gain, 0.0), axis=1, keepdims=True)
    gain_out_ref[...] = jnp.broadcast_to(column * scale, gain_out_ref.shape)


def columns_of(pair, width):
    return pl.ds(pl.multiple_of(pair * width, width), width)


def partial_kernel(shares, first, for_other, *refs):
    columns, values, out_ref = refs[:4], refs[4:10], refs[-1]
    kv_width = out_ref.shape[1]
    parts = []
    for ref in values:
        beside = ref.shape[1] > kv_width
        rows = slice(first, 2 * first) if beside else slice(0, ref.shape[0])
        parts += [ref[rows, at : at + kv_width] for at in range(0, ref.shape[1], kv_width)]
    parts.insert(len(parts) - 3, columns[2][2 * BLOCK :, :])
    value = jnp.concatenate(parts, axis=0)
    mine = lax.rem(place()[2], 2)
    core = 1 - mine if for_other else mine
    at = pl.ds(pl.multiple_of(core * shares, shares), shares)
    rows = jnp.concatenate([ref[: 2 * BLOCK, at] for ref in columns], axis=0)
    out_ref[...] = lax.dot_general(
        rows, value, (((0,), (0,)), ((), ())), preferred_element_type=jnp.float32
    ).astype(out_ref.dtype)


def partial_sums(shares, piece, for_other, columns, values, after=()):
    kv_width = values[0].shape[1]
    return pl.pallas_call(
        functools.partial(partial_kernel, shares, piece, for_other),
        out_shape=jax.ShapeDtypeStruct(
            (shares, kv_width), jnp.bfloat16 if for_other else jnp.float32
        ),
        in_specs=[VMEM] * 10 + [ANY] * len(after),
        out_specs=VMEM,
        name="partial_other" if for_other else "partial_own",
        **params(0.0 if for_other else 0.5),
    )(*[columns[k] for k in (0, 2, 4, 6)], *values, *after)


def diagonal(size):
    return lax.broadcasted_iota(jnp.int32, (size, size), 0) == lax.broadcasted_iota(
        jnp.int32, (size, size), 1
    )


def rows_kernel(half, first_rows_ref, handed_ref, *refs):
    pieces = refs[:half]
    rows_ref, token_ref = refs[half:]
    side, at, _ = place()
    piece = BLOCK // half
    for block in range(2):
        for k in range(half):
            replica = (side if block == 0 else 1 - side) * half + lax.bitwise_xor(at, k)
            rows = pl.ds(pl.multiple_of(replica * piece, piece), piece)
            source, first = pieces[k], block * piece
            if k == 2:
                source, first = (pieces[k] if block else first_rows_ref), 0
            if k == 3:
                source, first = (pieces[k] if block else handed_ref), 0
            rows_ref[rows, :] = source[first : first + piece, :]
    token_ref[...] = jnp.zeros_like(token_ref)


def finish_kernel(
    own_ref, other_ref, weight_ref, gain_ref, after_ref, out_ref, gain_out_ref
):
    total = own_ref[...] + other_ref[...].astype(jnp.float32)
    out_ref[...] = total * gain_ref[:, :1]
    sums = jnp.sum(total * weight_ref[...], axis=1, keepdims=True)
    gain_out_ref[...] = jnp.sum(
        jnp.where(diagonal(total.shape[0]), sums, 0.0), axis=0, keepdims=True
    )


def direct(hidden, query, key, segments, weight, norm_gain, upstream):
    tokens, model_width = hidden.shape
    kv_width = key.shape[1]
    replicas = lax.axis_size("dp")
    layers = lax.axis_size("section")
    half = replicas // 2
    piece = tokens // replicas
    shares = model_width // replicas

    def swap(array, k):
        return lax.ppermute(array, "dp", [(i, i ^ k) for i in range(replicas)])

    count = 2 * half
    bf16 = jnp.bfloat16
    sources = (query, key, hidden, upstream, segments)
    pieces, ups = [], []
    for b in range(2):
        extra = (weight, norm_gain) if b else ()
        *packed, up = pack(b, half, piece, sources, *extra)
        if b:
            gain, turned, *packed = packed
        pieces.append([packed[0]] + [swap(packed[k], k) for k in range(1, half)])
        ups.append(swap(up, half) if b else up)
    whole = slice(0, UNIT)
    scale = float(tokens * replicas) ** (-0.5)
    blocks, kept, after = [], [], []
    for b in range(2):
        block = block_probs(pieces[b], ups[b], BLOCK, model_width, kv_width, after)
        late, early = (ups[b], LATE), (ups[b], EARLY)
        first = tick_step(0, [late], block, turned, gain, name=UNITS[2 * b])
        second = tick_step(
            0, [late, early], block, turned, gain, after=[first[0]], name=UNITS[2 * b + 1]
        )
        blocks.append(block)
        kept += [[first], [second]]
        after = [second[0]]

    for tick in range(1, layers):
        hop = [(layers - tick, layers - 1 - tick)]
        grads = [(lax.ppermute(unit[-1][0], "section", hop), whole) for unit in kept]
        last = tick == layers - 1
        after, done = [kept[3][-1][0]], []
        if tick == layers - 2:
            own_weight, own_gain = pl.pallas_call(
                functools.partial(own_kernel, scale),
                out_shape=(
                    jax.ShapeDtypeStruct((shares, kv_width), jnp.float32),
                    jax.ShapeDtypeStruct((shares, 128), jnp.float32),
                ),
                in_specs=[VMEM, VMEM, ANY],
                out_specs=(VMEM, VMEM),
                name="own",
                **params(0.0),
            )(near(weight), near(gain), *after)
            columns = {6: swap(columns_for(6, blocks, after + [own_gain]), 6)}
        if last:
            columns[2] = swap(columns_for(2, blocks, after + [columns[6]]), 2)
        for u in range(4):
            needs = grads[u - 1 : u + 1] if u % 2 else grads[u : u + 1]
            late = []
            if last and u == 1:
                late = [done[0][1], done[0][0]]
            if last and u == 3:
                late = [done[2][1], done[2][0], done[0][0], done[1][0], done[1][1]]
                first_rows, far_first = swap(done[1][2], 2), swap(done[1][1], 6)
                columns[4] = swap(columns_for(4, blocks, [], [done[1][1]]), 4)
                after = after + [columns[2]]
            done.append(
                tick_step(
                    tick, needs, blocks[u // 2], turned, gain, kept[u] if last else (), late,
                    after, name=UNITS[u],
                )
            )
            after = [done[u][0]]
            kept[u].append(done[u])
    own_value, own_values, *rows = done[3]
    rows = [rows[0]] + [swap(rows[k], k) for k in range(1, half)]
    far_value, across_value = swap(own_value, 6), swap(own_value, 4)
    columns[0], handed = columns_for(0, blocks, [own_value, columns[4], far_first, far_value], [first_rows])
    handed = swap(handed, 1)
    values = [own_values, first_rows, rows[2], across_value, far_first, far_value]
    other = partial_sums(shares, piece, True, columns, values)
    own = partial_sums(shares, piece, False, columns, values, [other])
    other = swap(other, 1)
    input_grad, token = pl.pallas_call(
        functools.partial(rows_kernel, half),
        out_shape=(
            jax.ShapeDtypeStruct((tokens, model_width), bf16),
            jax.ShapeDtypeStruct((8, 128), jnp.float32),
        ),
        in_specs=[VMEM] * (2 + half),
        out_specs=(VMEM, VMEM),
        name="rows",
        **params(2.5),
    )(first_rows, handed, *rows)
    weight_grad, gain_grad = pl.pallas_call(
        finish_kernel,
        out_shape=(
            jax.ShapeDtypeStruct((shares, kv_width), jnp.float32),
            jax.ShapeDtypeStruct((1, shares), jnp.float32),
        ),
        in_specs=[VMEM] * 4 + [ANY],
        out_specs=(VMEM, VMEM),
        name="finish",
        **params(0.0),
    )(own, other, own_weight, own_gain, token)
    return input_grad[None], weight_grad[None], gain_grad


def weight_kernel(scale, columns_ref, value_ref, weight_ref, gain_ref, out_ref, gain_out_ref):
    total = lax.dot_general(
        columns_ref[...], value_ref[...], (((0,), (0,)), ((), ())),
        preferred_element_type=jnp.float32,
    ) * scale
    out_ref[...] = total * gain_ref[...]
    product = total * weight_ref[...].astype(jnp.float32)
    sums = lax.dot_general(
        jnp.ones((8, product.shape[1]), jnp.float32), product, (((1,), (1,)), ((), ())),
        preferred_element_type=jnp.float32, precision=lax.Precision.HIGHEST,
    )
    gain_out_ref[...] = sums[:1]


def grouped(hidden, query, key, segments, weight, norm_gain, upstream):
    tokens, model_width = hidden.shape
    kv_width = key.shape[1]
    replicas = lax.axis_size("dp")
    layers = lax.axis_size("section")
    half = replicas // 2
    me = lax.axis_index("dp")
    section = lax.axis_index("section")
    side = me // half
    groups = [list(range(half)), list(range(half, replicas))]
    across = [(i, (i + half) % replicas) for i in range(replicas)]
    shares = model_width // replicas

    def rows_of(array, which, axis=0):
        at = side if which == 0 else 1 - side
        return lax.dynamic_slice_in_dim(array, at * BLOCK, BLOCK, axis)

    def regroup(array):
        return lax.all_to_all(
            array, "dp", split_axis=0, concat_axis=0, axis_index_groups=groups, tiled=True
        )

    def spread(array):
        return lax.all_to_all(array, "dp", split_axis=0, concat_axis=0, tiled=True)

    turned = turn(weight)
    blocks, grads = [], []
    for which in range(2):
        up = rows_of(upstream, which)
        seg = jnp.broadcast_to(segments, (16, 2 * BLOCK)).astype(jnp.bfloat16)
        if which == 1:
            up = lax.ppermute(up, "dp", across)
            seg = lax.ppermute(seg, "dp", across)
        packed = jnp.concatenate(
            [rows_of(query, which), rows_of(key, which), rows_of(hidden, which)], axis=1
        )
        blocks.append(block_probs([regroup(packed)], seg, 0, model_width, kv_width))
        grads.append(up)

    def layer(tick, which, grad, kept):
        live = (section == layers - 1 - tick).astype(jnp.int32)[None]
        return layer_step(live, grad, blocks[which], turned, norm_gain, kept)

    held = [layer(0, which, grads[which], ()) for which in range(2)]
    hops = [(i, i - 1) for i in range(1, layers)]

    def step(tick, held):
        grads = [lax.ppermute(kept[0], "section", hops) for kept in held]
        return [layer(tick, which, grads[which], held[which]) for which in range(2)]

    held = lax.fori_loop(1, layers, step, held)

    columns, values, stored = [], [], []
    for which in range(2):
        block = blocks[which][3].reshape(BLOCK, replicas, shares).transpose(1, 0, 2)
        columns.append(spread(block.reshape(replicas * BLOCK, shares)))
        out, value = held[which]
        stored.append(regroup(out))
        values.append(spread(jnp.tile(value, (replicas, 1))))
    ordered = jnp.where(
        side == 0, jnp.concatenate(stored, axis=0), jnp.concatenate(stored[::-1], axis=0)
    )
    own_weight = lax.dynamic_slice_in_dim(weight, me * shares, shares, 0)
    own_gain = lax.dynamic_slice_in_dim(norm_gain[0], me * shares, shares, 0)
    scale = float(tokens * replicas) ** (-0.5)
    weight_grad, gain_grad = pl.pallas_call(
        functools.partial(weight_kernel, scale),
        out_shape=(
            jax.ShapeDtypeStruct((shares, kv_width), jnp.float32),
            jax.ShapeDtypeStruct((1, shares), jnp.float32),
        ),
        in_specs=[VMEM] * 4,
        out_specs=(VMEM, VMEM),
        name="weight_grad",
    )(
        jnp.concatenate(columns, axis=0),
        jnp.concatenate(values, axis=0),
        own_weight,
        own_gain[:, None],
    )
    return ordered[None], weight_grad[None], gain_grad


def on_device(hidden_in, queries, keys, segments, value_weight, norm_gain, upstream):
    replicas = lax.axis_size("dp")
    piece = hidden_in.shape[1] // replicas
    plan = direct if piece % 16 == 0 and replicas == 8 else grouped
    return plan(
        hidden_in[0], queries[0], keys[0], segments, value_weight[0], norm_gain, upstream
    )


def solution(mesh):
    in_specs = (
        P("section", "dp", None),
        P("section", "dp", None),
        P("section", "dp", None),
        P("dp", None),
        P("section", None, None),
        P("section", None),
        P("dp", None),
    )
    out_specs = (P("section", "dp", None), P("section", "dp", None), P("section", "dp"))
    return jax.shard_map(
        on_device, mesh=mesh, in_specs=in_specs, out_specs=out_specs, check_vma=False
    )
```
